32 devices in a mesh: groups: 2 (over y), clip: 4 (over z), strip: 4 (over x, core).
Axes of the slice: x: 2, y: 2, z: 4, core: 2. Of those that a mesh axis runs over, the one named last changes fastest.
Arguments:
- latents: bfloat16 [32, 20, 64, 320], P(('groups', 'clip'), 'strip'), parts along dimension 0, may hold values from -6 to 6
- anchor_index: int32 [8, 1], P(('groups', 'clip')), parts along dimension 0, may hold values from 0 to 3
- window: int32 [1], replicated, may hold values from 2 to 4
- gain_one: float32 [320], replicated, may hold values from 0.5 to 1.5
- spatial_w: bfloat16 [3, 3, 320, 320], replicated, may hold values from -0.109375 to 0.109375
- gain_two: float32 [320], replicated, may hold values from 0.5 to 1.5
- temporal_w: bfloat16 [3, 320, 320], replicated, may hold values from -0.1875 to 0.1875
- gain_three: float32 [320], replicated, may hold values from 0.5 to 1.5
- w_query: bfloat16 [320, 320], replicated
- w_keyval: bfloat16 [320, 640], replicated
- w_out: bfloat16 [320, 320], replicated, may hold values from -0.3125 to 0.3125
Outputs:
- block_out: bfloat16 [32, 20, 64, 320], P(('groups', 'clip'), 'strip'), parts along dimension 0
The draws below stay inside these ranges and needn't reach their ends.
There are 2 independent parts, one for each index of `groups`. The reference program is written for one: setup_inputs(seed, part) draws one part's arguments, and reference() takes and returns one part's arrays. A program takes and returns all parts, laid end to end along the dimension named above; an argument that names none is the same for every part. Nothing has to cross between parts.
Inputs may be any that keep to these rules, and one draw needn't show every extreme that they name: `anchor_index`: indices of anchor frames within their clip of 4 frames. Frames closer than window[0] within one clip attend to each other.
All inputs are finite; a program needn't handle non-finite values.
Results may differ from the reference program's by a relative error of at most 0.0085.
Values may be sent and summed in bfloat16 or wider, within the bound.
No kernel may reach another device: no remote copies, remote signals or barrier semaphores. Data moves between devices by JAX's collectives and lax.ppermute only.
A program may use at most 128 MiB of HBM per device.

```python
import math
import jax
import jax.numpy as jnp
from jax import lax

C = 320
HEADS = 5
HEAD_DIM = 64
FR_DEV = 4
WIDTH = 64
NANC = 1
CLIPS = 4
FRAMES = 16
HEIGHT = 20


def query_key_parts(key):
    own_query = jax.random.normal(jax.random.fold_in(key, 12), (C, C), jnp.float32)
    own_key = jax.random.normal(jax.random.fold_in(key, 13), (C, C), jnp.float32)
    query_part = own_query
    key_part = own_key
    return (query_part / math.sqrt(C), key_part / math.sqrt(C))


def draw_w_query(key, part):
    return query_key_parts(key)[0].astype(jnp.bfloat16)


def draw_w_keyval(key, part):
    key_part = query_key_parts(key)[1]
    value_part = jax.random.normal(jax.random.fold_in(key, 14), (C, C), jnp.float32) / math.sqrt(C)
    return jnp.concatenate([key_part, value_part], axis=1).astype(jnp.bfloat16)


def with_ends(result, key, least, largest):
    extent = result.shape
    spot = [jax.random.randint(jax.random.fold_in(key, axis), (), 0, extent[axis]) for axis in range(len(extent))]
    result = result.at[tuple(spot)].set(least)
    longest = extent.index(max(extent))
    spot[longest] = (spot[longest] + 1) % extent[longest]
    return result.at[tuple(spot)].set(largest)


def shard_levels(key, dims, cuts, least, high):
    def one(dim, shards_of):
        steps = jax.random.uniform(jax.random.fold_in(jax.random.fold_in(key, 6), dim), (shards_of,), jnp.float32, least / len(cuts), high / len(cuts))
        return jnp.repeat(jnp.exp(steps), dims[dim] // shards_of).reshape((-1,) + (1,) * (len(dims) - dim - 1))

    loudness = one(*cuts[0])
    for cut in cuts[1:]:
        loudness = loudness * one(*cut)
    return loudness


def noise(rng, extent, spread, bound, pieces=(), kind=jnp.bfloat16):
    level = shard_levels(rng, extent, pieces, -0.22, 0.18) if pieces else 1.0
    entries = jax.random.normal(rng, extent, jnp.float32) * spread * level
    return jnp.minimum(jnp.maximum(entries, -bound), bound).astype(kind)


def setup_inputs(seed: int = 0, part: int = 0) -> dict:
    keys = jax.random.split(jax.random.key(seed), 12)
    part_splits = jax.random.split(jax.random.fold_in(keys[11], part), 12)
    latents = noise(part_splits[0], (FRAMES, HEIGHT, WIDTH, C), 1.0, 6.0, ((0, 4), (1, 4)))
    anchor_index = with_ends(jax.random.randint(part_splits[1], (CLIPS, NANC), 0, FR_DEV), jax.random.fold_in(part_splits[1], 1), 0, FR_DEV - 1).astype(jnp.int32)
    window = jax.random.randint(keys[2], (1,), 2, FR_DEV + 1).astype(jnp.int32)
    gain_one = jnp.clip(jax.random.uniform(keys[3], (C,), jnp.float32, 0.5, 1.5), 0.5, 1.5)
    spatial_w = noise(keys[4], (3, 3, C, C), (9 * C) ** -0.5, 0.109375)
    gain_two = jnp.clip(jax.random.uniform(keys[5], (C,), jnp.float32, 0.5, 1.5), 0.5, 1.5)
    temporal_w = noise(keys[6], (3, C, C), (3 * C) ** -0.5, 0.1875)
    gain_three = jnp.clip(jax.random.uniform(keys[7], (C,), jnp.float32, 0.5, 1.5), 0.5, 1.5)
    w_query = draw_w_query(jax.random.fold_in(keys[11], 71), part)
    w_keyval = draw_w_keyval(jax.random.fold_in(keys[11], 71), part)
    w_out = noise(keys[10], (C, C), C ** -0.5, 0.3125)
    return dict(latents=latents, anchor_index=anchor_index, window=window, gain_one=gain_one, spatial_w=spatial_w, gain_two=gain_two, temporal_w=temporal_w, gain_three=gain_three, w_query=w_query, w_keyval=w_keyval, w_out=w_out)


def layer_norm(values, gain):
    widened = values.astype(jnp.float32)
    centred = widened - lax.optimization_barrier(jnp.mean(widened, axis=-1, keepdims=True))
    variance = lax.optimization_barrier(jnp.mean(centred * centred, axis=-1, keepdims=True))
    return centred * lax.rsqrt(variance + 1e-05) * gain

def reference(latents, anchor_index, window, gain_one, spatial_w, gain_two, temporal_w, gain_three, w_query, w_keyval, w_out):
    frames, height, columns, channels = latents.shape
    hidden_one = jax.nn.silu(layer_norm(latents, gain_one)).astype(jnp.bfloat16)
    padded = jnp.pad(hidden_one, ((0, 0), (1, 1), (1, 1), (0, 0)))
    summed = jnp.zeros(latents.shape, jnp.float32)
    for row_tap in range(3):
        for col_tap in range(3):
            summed = summed + jnp.dot(padded[:, row_tap:row_tap + height, col_tap:col_tap + columns, :], spatial_w[row_tap, col_tap], preferred_element_type=jnp.float32)
    spatial = (latents.astype(jnp.float32) + summed).astype(jnp.bfloat16)
    hidden_two = jax.nn.silu(layer_norm(spatial, gain_two)).astype(jnp.bfloat16)
    padded_two = jnp.pad(hidden_two, ((1, 1), (0, 0), (0, 0), (0, 0)))
    summed = jnp.zeros(latents.shape, jnp.float32)
    for frame_tap in range(3):
        summed = summed + jnp.dot(padded_two[frame_tap:frame_tap + frames], temporal_w[frame_tap], preferred_element_type=jnp.float32)
    temporal = (spatial.astype(jnp.float32) + summed).astype(jnp.bfloat16)
    normed = layer_norm(temporal, gain_three).astype(jnp.bfloat16)
    query = lax.optimization_barrier(jnp.dot(normed, w_query, preferred_element_type=jnp.float32).astype(jnp.bfloat16))
    keyval = lax.optimization_barrier(jnp.dot(normed, w_keyval, preferred_element_type=jnp.float32).astype(jnp.bfloat16))
    clips = anchor_index.shape[0]
    per_clip = frames // clips
    pixels = height * columns
    global_frames = (anchor_index + per_clip * jnp.arange(clips, dtype=jnp.int32)[:, None]).reshape(-1).astype(jnp.int32)
    anchors = jnp.take(keyval, global_frames, axis=0).reshape(-1, pixels, 2, HEADS, HEAD_DIM).astype(jnp.float32)
    anchor_keys = anchors[:, :, 0]
    anchor_values = anchors[:, :, 1]
    query_clips = query.reshape(clips, per_clip, pixels, HEADS, HEAD_DIM)
    keyval_clips = keyval.reshape(clips, per_clip, pixels, 2, HEADS, HEAD_DIM)
    score_scale = 1.0 / math.sqrt(HEAD_DIM)
    places = jnp.arange(per_clip, dtype=jnp.int32)
    inside = jnp.abs(places[:, None] - places[None, :]) < window[0]

    def one_clip(inputs):
        query_part, keyval_part = inputs
        query_wide = query_part.astype(jnp.float32)
        key_wide = keyval_part[:, :, 0].astype(jnp.float32)
        value_wide = keyval_part[:, :, 1].astype(jnp.float32)
        nearby = jnp.einsum('iphd,jphd->phij', query_wide, key_wide) * score_scale
        nearby = jnp.where(inside, nearby, -jnp.inf)
        remote = jnp.einsum('iphd,aphd->phia', query_wide, anchor_keys) * score_scale
        scores = jnp.concatenate([nearby, remote], axis=-1)
        maxima = lax.optimization_barrier(jnp.max(scores, axis=-1, keepdims=True))
        weights = jnp.exp(scores - maxima)
        probs = lax.optimization_barrier((weights / lax.optimization_barrier(jnp.sum(weights, axis=-1, keepdims=True))).astype(jnp.bfloat16)).astype(jnp.float32)
        mixed = jnp.einsum('phij,jphd->iphd', probs[..., :per_clip], value_wide) + jnp.einsum('phia,aphd->iphd', probs[..., per_clip:], anchor_values)
        return mixed.astype(jnp.bfloat16)
    attended = lax.map(one_clip, (query_clips, keyval_clips))
    attended = attended.reshape(frames, height, columns, channels)
    block_out = temporal.astype(jnp.float32) + jnp.dot(attended, w_out, preferred_element_type=jnp.float32)
    return block_out.astype(jnp.bfloat16)
```

```python
import functools
import math

import jax
import jax.numpy as jnp
from jax import lax
from jax.experimental import pallas as pl
from jax.experimental.pallas import tpu as pltpu
from jax.sharding import PartitionSpec as P

HEADS = 5
HEAD_DIM = 64
LANES = 128
BF = jnp.bfloat16
F32 = jnp.float32
VMEM = pl.BlockSpec(memory_space=pltpu.VMEM)
SMEM = pl.BlockSpec(memory_space=pltpu.SMEM)
MIB = 1 << 20


def call(body, outs, specs, scratch=(), flops=0, limit=24):
    return pl.pallas_call(
        body,
        out_shape=tuple(jax.ShapeDtypeStruct(s, d) for s, d in outs),
        in_specs=specs,
        out_specs=tuple(VMEM for _ in outs),
        scratch_shapes=list(scratch),
        cost_estimate=pl.CostEstimate(flops=flops, bytes_accessed=2 * MIB, transcendentals=0),
        compiler_params=pltpu.CompilerParams(vmem_limit_bytes=limit * MIB),
    )


def norm(v, gain):
    centred = v - jnp.mean(v, axis=-1, keepdims=True)
    variance = jnp.mean(centred * centred, axis=-1, keepdims=True)
    return centred * lax.rsqrt(variance + 1e-05) * gain


def silu(u):
    half = 0.5 * u
    return half + half * jnp.tanh(half)


def dot(a, b):
    return jnp.dot(a, b, preferred_element_type=F32)


def pack_into(ref, h):
    cells, channels = h.shape
    full = channels // LANES
    for t in range(full):
        ref[t * cells : (t + 1) * cells, :] = h[:, t * LANES : (t + 1) * LANES]
    rest = channels - full * LANES
    if rest:
        share = LANES // rest
        part = cells // share
        ref[full * cells :, :] = jnp.concatenate(
            [h[s * part : (s + 1) * part, full * LANES :] for s in range(share)], axis=1
        )


def unpacked(p, channels):
    cells = p.shape[0] * LANES // channels
    full = channels // LANES
    pieces = [p[t * cells : (t + 1) * cells, :] for t in range(full)]
    rest = channels - full * LANES
    if rest:
        share = LANES // rest
        tail = p[full * cells :, :]
        pieces.append(
            jnp.concatenate([tail[:, s * rest : (s + 1) * rest] for s in range(share)], axis=0)
        )
    return jnp.concatenate(pieces, axis=1)


def columns(h, width):
    cells = h.shape[0]
    place = lax.rem(lax.broadcasted_iota(jnp.int32, h.shape, 0), width)
    left = jnp.where(place == 0, 0.0, pltpu.roll(h, 1, 0))
    right = jnp.where(place == width - 1, 0.0, pltpu.roll(h, cells - 1, 0))
    return jnp.concatenate([left.astype(BF), h.astype(BF), right.astype(BF)], axis=1)


def edge_kernel(x_ref, g_ref, top_ref, bottom_ref):
    frames, height, width, channels = x_ref.shape
    for row, ref in ((0, top_ref), (height - 1, bottom_ref)):
        v = x_ref[:, row].reshape(frames * width, channels).astype(F32)
        pack_into(ref, silu(norm(v, g_ref[...])).astype(BF))


def spatial_kernel(x_ref, g1_ref, g2_ref, w_ref, mid_ref, mid2_ref, edge_ref, col_ref, rem_ref):
    frames, height, width, channels = x_ref.shape
    cells = height * width
    full = channels // 256 * 256
    rest = channels - full
    for a in range(3):
        rem_ref[:, a * rest : (a + 1) * rest] = w_ref[a, :, full:]

    def frame(f, _):
        v = x_ref[f].reshape(cells, channels).astype(F32)
        col_ref[...] = columns(silu(norm(v, g1_ref[...])), width)
        col = col_ref[...]
        main = [
            dot(col[: cells - width], w_ref[0, :, :full]),
            dot(col, w_ref[1, :, :full]),
            dot(col[width:], w_ref[2, :, :full]),
        ]
        tails = dot(col, rem_ref[...])
        for row in range(height):
            lo, hi = row * width, (row + 1) * width
            wide = main[1][lo:hi]
            tail = tails[lo:hi, rest : 2 * rest]
            if row > 0:
                wide = wide + main[0][lo - width : lo]
                tail = tail + tails[lo - width : lo, :rest]
            if row < height - 1:
                wide = wide + main[2][lo:hi]
                tail = tail + tails[hi : hi + width, 2 * rest : 3 * rest]
            total = x_ref[f, row].astype(F32) + jnp.concatenate([wide, tail], axis=1)
            if 0 < row < height - 1:
                rounded = total.astype(BF)
                mid_ref[f, row - 1] = rounded
                mid2_ref[f, row - 1] = silu(norm(rounded.astype(F32), g2_ref[...])).astype(BF)
            else:
                edge_ref[f, 0 if row == 0 else 1] = total
        return 0

    lax.fori_loop(0, frames, frame, 0)


def spatial_edge_kernel(
    acc_ref, above_ref, below_ref, g2_ref, w_ref, mid2_ref, edge_ref, edge2_ref, first_ref, last_ref
):
    frames, _, width, channels = acc_ref.shape
    for side, halo_ref, a in ((0, above_ref, 0), (1, below_ref, 2)):
        halo = unpacked(halo_ref[...], channels).astype(F32)
        add = dot(columns(halo, width), w_ref[a])
        total = acc_ref[:, side].reshape(frames * width, channels) + add
        rounded = total.astype(BF)
        hidden = silu(norm(rounded.astype(F32), g2_ref[...])).astype(BF)
        edge_ref[:, side] = rounded.reshape(frames, width, channels)
        edge2_ref[:, side] = hidden.reshape(frames, width, channels)
    for f, ref in ((0, first_ref), (frames - 1, last_ref)):
        pack_into(ref, whole_frame(mid2_ref, edge2_ref, f))


def whole_frame(mid_ref, edge_ref, f):
    rows, width, channels = mid_ref.shape[1:]
    mid = mid_ref[f].reshape(rows * width, channels)
    return jnp.concatenate([edge_ref[f, 0], mid, edge_ref[f, 1]], axis=0)


def temporal_kernel(
    mid_ref, edge_ref, mid2_ref, edge2_ref, g3_ref, w_ref, wq_ref, wkv_ref,
    inner_ref, normed_ref, query_ref, keyval_ref, outer_ref,
):
    frames = mid_ref.shape[0]
    hidden = [whole_frame(mid2_ref, edge2_ref, f) for f in range(frames)]
    for f in range(frames):
        taps = [k for k in range(3) if 0 <= f + k - 1 < frames]
        total = whole_frame(mid_ref, edge_ref, f).astype(F32)
        for k in taps:
            total = total + dot(hidden[f + k - 1], w_ref[k])
        if len(taps) == 3:
            rounded = total.astype(BF)
            inner_ref[f - 1] = rounded
            normed = norm(rounded.astype(F32), g3_ref[...]).astype(BF)
            normed_ref[f - 1] = normed
            query_ref[f - 1] = dot(normed, wq_ref[...]).astype(BF)
            keyval_ref[f - 1] = dot(normed, wkv_ref[...]).astype(BF)
        else:
            outer_ref[0 if f == 0 else 1] = total


def temporal_edge_kernel(
    picks_ref, outer_ref, before_ref, after_ref, g3_ref, w_ref, inner_normed_ref,
    outer_out_ref, outer_normed_ref, chosen_ref, all_ref,
):
    channels = outer_ref.shape[-1]
    frames = all_ref.shape[0]
    all_ref[1 : frames - 1] = inner_normed_ref[...]
    for side, halo_ref, k in ((0, before_ref, 0), (1, after_ref, 2)):
        total = outer_ref[side] + dot(unpacked(halo_ref[...], channels), w_ref[k])
        rounded = total.astype(BF)
        outer_out_ref[side] = rounded
        normed = norm(rounded.astype(F32), g3_ref[...]).astype(BF)
        outer_normed_ref[side] = normed
        all_ref[0 if side == 0 else frames - 1] = normed
    for n in range(chosen_ref.shape[0]):
        pack_into(chosen_ref.at[n], all_ref[picks_ref[0, n]])


def head_map(channels):
    c = lax.broadcasted_iota(jnp.int32, (channels, LANES), 0)
    h = lax.broadcasted_iota(jnp.int32, (channels, LANES), 1)
    inside = (c >= h * HEAD_DIM) & (c < (h + 1) * HEAD_DIM)
    return jnp.where(inside, 1.0 / math.sqrt(HEAD_DIM), 0.0).astype(BF)


def head_spread(channels):
    h = lax.broadcasted_iota(jnp.int32, (LANES, channels), 0)
    c = lax.broadcasted_iota(jnp.int32, (LANES, channels), 1)
    inside = (c >= h * HEAD_DIM) & (c < (h + 1) * HEAD_DIM)
    return jnp.where(inside, 1.0, 0.0).astype(BF)


def local_kernel(
    picks_ref, window_ref, inner_query_ref, inner_keyval_ref, outer_normed_ref, wq_ref, wkv_ref,
    query_ref, top_ref, sum_ref, mix_ref, keyval_ref,
):
    frames, cells, channels = query_ref.shape
    count = picks_ref.shape[1]
    query_ref[1 : frames - 1] = inner_query_ref[...]
    keyval_ref[1 : frames - 1] = inner_keyval_ref[...]
    for side, f in ((0, 0), (1, frames - 1)):
        query_ref[f] = dot(outer_normed_ref[side], wq_ref[...]).astype(BF)
        keyval_ref[f] = dot(outer_normed_ref[side], wkv_ref[...]).astype(BF)
    gather = head_map(channels)
    spread = head_spread(channels)
    step = cells // 5 if cells % 5 == 0 else cells
    window = window_ref[0]

    def chunk(t, _):
        rows = pl.ds(pl.multiple_of(t * step, 16), step)
        sources = list(range(frames)) + [picks_ref[0, n] for n in range(count)]
        keyvals = [keyval_ref[j, rows, :] for j in sources]
        for i in range(frames):
            q = query_ref[i, rows, :]
            products = jnp.concatenate([q * kv[:, :channels] for kv in keyvals], axis=0)
            scores = dot(products, gather)
            parts = []
            for j in range(len(sources)):
                s = scores[j * step : (j + 1) * step]
                if j < frames and j != i:
                    s = jnp.where(abs(i - j) < window, s, -jnp.inf)
                parts.append(s)
            top = functools.reduce(jnp.maximum, parts)
            weights = [jnp.exp(s - top) for s in parts]
            total = functools.reduce(jnp.add, weights)
            wide = dot(jnp.concatenate([w.astype(BF) for w in weights], axis=0), spread)
            mixed = 0.0
            for j in range(len(sources)):
                mixed = mixed + wide[j * step : (j + 1) * step] * keyvals[j][:, channels:].astype(F32)
            top_ref[i, rows, :] = top
            sum_ref[i, rows, :] = total
            mix_ref[i, rows, :] = mixed
        return 0

    lax.fori_loop(0, cells // step, chunk, 0)


def updated(anchor_ref, wkv_ref, query_ref, top_ref, sum_ref, mix_ref, put):
    frames, cells, channels = query_ref.shape
    gather = head_map(channels)
    spread = head_spread(channels)
    count = anchor_ref.shape[0]
    keyvals = [
        dot(unpacked(anchor_ref[n], channels), wkv_ref[...]).astype(BF) for n in range(count)
    ]
    for i in range(frames):
        q = query_ref[i]
        scores = dot(
            jnp.concatenate([q * kv[:, :channels] for kv in keyvals], axis=0), gather
        )
        parts = [scores[n * cells : (n + 1) * cells] for n in range(count)]
        before = top_ref[i]
        top = functools.reduce(jnp.maximum, parts, before)
        weights = [jnp.exp(s - top) for s in parts]
        fade = jnp.exp(before - top).astype(BF)
        total = functools.reduce(jnp.add, weights, sum_ref[i] * fade.astype(F32))
        wide = dot(jnp.concatenate([fade] + [w.astype(BF) for w in weights], axis=0), spread)
        mixed = mix_ref[i] * wide[:cells]
        for n in range(count):
            mixed = mixed + wide[(n + 1) * cells : (n + 2) * cells] * keyvals[n][:, channels:].astype(F32)
        put(i, top, total, mixed, spread)


def anchor_kernel(
    anchor_ref, wkv_ref, query_ref, top_ref, sum_ref, mix_ref, top_out_ref, sum_out_ref, mix_out_ref
):
    def put(i, top, total, mixed, spread):
        top_out_ref[i] = top
        sum_out_ref[i] = total
        mix_out_ref[i] = mixed

    updated(anchor_ref, wkv_ref, query_ref, top_ref, sum_ref, mix_ref, put)


def last_kernel(
    anchor_ref, wkv_ref, query_ref, top_ref, sum_ref, mix_ref, inner_ref, outer_ref, wo_ref, out_ref
):
    frames = query_ref.shape[0]
    height, width, channels = out_ref.shape[1:]

    def put(i, top, total, mixed, spread):
        share = dot((1.0 / total).astype(BF), spread)
        attended = (mixed * share).astype(BF)
        if 0 < i < frames - 1:
            temporal = inner_ref[i - 1]
        else:
            temporal = outer_ref[0 if i == 0 else 1]
        result = temporal.astype(F32) + dot(attended, wo_ref[...])
        out_ref[i] = result.astype(BF).reshape(height, width, channels)

    updated(anchor_ref, wkv_ref, query_ref, top_ref, sum_ref, mix_ref, put)


def neighbours(leading, last, axis):
    count = lax.axis_size(axis)
    up = [(i, i + 1) for i in range(count - 1)]
    down = [(i + 1, i) for i in range(count - 1)]
    return lax.ppermute(last, axis, up), lax.ppermute(leading, axis, down)


def on_device(
    latents, anchor_index, window, gain_one, spatial_w, gain_two, temporal_w, gain_three,
    w_query, w_keyval, w_out,
):
    frames, height, width, channels = latents.shape
    cells = height * width
    count = anchor_index.shape[1]
    g1, g2, g3 = (g.reshape(1, channels) for g in (gain_one, gain_two, gain_three))
    ws = spatial_w.reshape(3, 3 * channels, channels)
    one = 2 * channels * channels
    packed = cells * channels // LANES
    edge_packed = frames * width * channels // LANES

    top, bottom = call(
        edge_kernel, [((edge_packed, LANES), BF)] * 2, [VMEM] * 2, flops=one * 100
    )(latents, g1)
    above, below = neighbours(top, bottom, "strip")
    mid, mid2, edge_sum = call(
        spatial_kernel,
        [
            ((frames, height - 2, width, channels), BF),
            ((frames, height - 2, width, channels), BF),
            ((frames, 2, width, channels), F32),
        ],
        [VMEM] * 4,
        [pltpu.VMEM((cells, 3 * channels), BF), pltpu.VMEM((3 * channels, 3 * (channels % 256)), BF)],
        flops=9 * frames * cells * one,
    )(latents, g1, g2, ws)
    edge, edge2, first, last = call(
        spatial_edge_kernel,
        [
            ((frames, 2, width, channels), BF),
            ((frames, 2, width, channels), BF),
            ((packed, LANES), BF),
            ((packed, LANES), BF),
        ],
        [VMEM] * 6,
        flops=6 * frames * width * one,
    )(edge_sum, above, below, g2, ws, mid2)
    before, after = neighbours(first, last, "clip")
    inner, inner_normed, inner_query, inner_keyval, outer_sum = call(
        temporal_kernel,
        [
            ((frames - 2, cells, channels), BF),
            ((frames - 2, cells, channels), BF),
            ((frames - 2, cells, channels), BF),
            ((frames - 2, cells, 2 * channels), BF),
            ((2, cells, channels), F32),
        ],
        [VMEM] * 8,
        flops=(3 + 2) * frames * cells * one,
    )(mid, edge, mid2, edge2, g3, temporal_w, w_query, w_keyval)
    outer, outer_normed, chosen = call(
        temporal_edge_kernel,
        [
            ((2, cells, channels), BF),
            ((2, cells, channels), BF),
            ((count, packed, LANES), BF),
        ],
        [SMEM] + [VMEM] * 6,
        [pltpu.VMEM((frames, cells, channels), BF)],
        flops=2 * cells * one,
    )(anchor_index, outer_sum, before, after, g3, temporal_w, inner_normed)
    clips = lax.axis_size("clip")
    arrived = [
        lax.ppermute(chosen, "clip", [(i, (i + s) % clips) for i in range(clips)])
        for s in range(1, clips)
    ]
    query, tops, sums, mixes = call(
        local_kernel,
        [
            ((frames, cells, channels), BF),
            ((frames, cells, LANES), F32),
            ((frames, cells, LANES), F32),
            ((frames, cells, channels), F32),
        ],
        [SMEM] * 2 + [VMEM] * 5,
        [pltpu.VMEM((frames, cells, 2 * channels), BF)],
        flops=10 * frames * cells * one,
    )(anchor_index, window, inner_query, inner_keyval, outer_normed, w_query, w_keyval)
    for arrival in arrived[:-1]:
        tops, sums, mixes = call(
            anchor_kernel,
            [
                ((frames, cells, LANES), F32),
                ((frames, cells, LANES), F32),
                ((frames, cells, channels), F32),
            ],
            [VMEM] * 6,
            flops=4 * frames * cells * one,
        )(arrival, w_keyval, query, tops, sums, mixes)
    (out,) = call(
        last_kernel,
        [((frames, height, width, channels), BF)],
        [VMEM] * 9,
        flops=5 * frames * cells * one,
    )(arrived[-1], w_keyval, query, tops, sums, mixes, inner, outer, w_out)
    return out


def solution(mesh):
    return jax.shard_map(
        on_device,
        mesh=mesh,
        in_specs=(
            P(("groups", "clip"), "strip", None, None),
            P(("groups", "clip"), None),
            P(),
            P(),
            P(),
            P(),
            P(),
            P(),
            P(),
            P(),
            P(),
        ),
        out_specs=P(("groups", "clip"), "strip", None, None),
        check_vma=False,
    )
```

```python
import functools
import math

import jax
import jax.numpy as jnp
from jax import lax
from jax.experimental import pallas as pl
from jax.experimental.pallas import tpu as pltpu
from jax.sharding import PartitionSpec as P

HEADS = 5
HEAD_DIM = 64
LANES = 128
BF = jnp.bfloat16
F32 = jnp.float32
VMEM = pl.BlockSpec(memory_space=pltpu.VMEM)
SMEM = pl.BlockSpec(memory_space=pltpu.SMEM)
ANY = pl.BlockSpec(memory_space=pl.ANY)
MIB = 1 << 20


def call(body, outs, specs, scratch=(), flops=0, limit=24, out_specs=None):
    return pl.pallas_call(
        body,
        out_shape=tuple(jax.ShapeDtypeStruct(s, d) for s, d in outs),
        in_specs=specs,
        out_specs=out_specs or tuple(VMEM for _ in outs),
        scratch_shapes=list(scratch),
        cost_estimate=pl.CostEstimate(flops=flops, bytes_accessed=2 * MIB, transcendentals=0),
        compiler_params=pltpu.CompilerParams(vmem_limit_bytes=limit * MIB),
    )


def dot(a, b):
    return jnp.dot(a, b, preferred_element_type=F32)


def widened(v, channels):
    pieces = [v] * (channels // LANES)
    if channels % LANES:
        pieces.append(v[:, : channels % LANES])
    return jnp.concatenate(pieces, axis=1)


def norm(v, gain_ref):
    channels = v.shape[1]
    ones = jnp.ones((channels, LANES), BF)
    centred = v.astype(F32) - widened(dot(v, ones) * (1.0 / channels), channels)
    variance = dot((centred * centred).astype(BF), ones) * (1.0 / channels)
    gain = gain_ref[...].reshape(1, channels)
    return centred * widened(lax.rsqrt(variance + 1e-05), channels) * gain


def silu(u):
    half = 0.5 * u
    return half + half * jnp.tanh(half)


def pack_into(ref, h):
    cells, channels = h.shape
    full = channels // LANES
    for t in range(full):
        ref[t * cells : (t + 1) * cells, :] = h[:, t * LANES : (t + 1) * LANES]
    rest = channels - full * LANES
    if rest:
        share = LANES // rest
        part = cells // share
        ref[full * cells :, :] = jnp.concatenate(
            [h[s * part : (s + 1) * part, full * LANES :] for s in range(share)], axis=1
        )


def unpacked(p, channels):
    cells = p.shape[0] * LANES // channels
    full = channels // LANES
    pieces = [p[t * cells : (t + 1) * cells, :] for t in range(full)]
    rest = channels - full * LANES
    if rest:
        share = LANES // rest
        tail = p[full * cells :, :]
        pieces.append(
            jnp.concatenate([tail[:, s * rest : (s + 1) * rest] for s in range(share)], axis=0)
        )
    return jnp.concatenate(pieces, axis=1)


def columns(h, width):
    cells = h.shape[0]
    place = lax.rem(lax.broadcasted_iota(jnp.int32, h.shape, 0), width)
    left = jnp.where(place == 0, 0.0, pltpu.roll(h, 1, 0))
    right = jnp.where(place == width - 1, 0.0, pltpu.roll(h, cells - 1, 0))
    return jnp.concatenate([left.astype(BF), h.astype(BF), right.astype(BF)], axis=1)


def edge_kernel(x_ref, g_ref, top_ref, bottom_ref, rows_ref, sems):
    frames, height, width, channels = x_ref.shape
    copies = [
        pltpu.make_async_copy(x_ref.at[:, row], rows_ref.at[side], sems.at[side])
        for side, row in enumerate((0, height - 1))
    ]
    for copy in copies:
        copy.start()
    for side, ref in enumerate((top_ref, bottom_ref)):
        copies[side].wait()
        v = rows_ref[side].reshape(frames * width, channels)
        pack_into(ref, silu(norm(v, g_ref)).astype(BF))


def by_taps(col, w_ref, rem_ref, frames, rows, width):
    full = w_ref.shape[2] // 256 * 256

    def cut(lo, hi):
        part = col.reshape(frames, rows * width, col.shape[1])[:, lo * width : hi * width]
        return part.reshape(frames * (hi - lo) * width, col.shape[1])

    def times(lo, hi, weights):
        return dot(cut(lo, hi), weights).reshape(frames, hi - lo, width, weights.shape[1])

    return times, [w_ref[a, :, :full] for a in range(3)], rem_ref[...]


def outer_kernel(x_ref, g1_ref, g2_ref, w_hbm, mid_ref, mid2_ref, edge_ref, w_ref, rem_ref, x_buf, sems):
    frames, height, width, channels = x_ref.shape
    full = channels // 256 * 256
    rest = channels - full
    fetch_x = [
        pltpu.make_async_copy(x_ref.at[f], x_buf.at[s], sems.at[s])
        for s, f in enumerate((0, frames - 1))
    ]
    fetch_w = [pltpu.make_async_copy(w_hbm.at[a], w_ref.at[a], sems.at[2 + a]) for a in range(3)]
    for copy in fetch_x + fetch_w:
        copy.start()
    for copy in fetch_x:
        copy.wait()
    x = x_buf[...].reshape(2 * height * width, channels)
    col = columns(silu(norm(x, g1_ref)), width)
    for a, copy in enumerate(fetch_w):
        copy.wait()
        rem_ref[:, a * rest : (a + 1) * rest] = w_ref[a, :, full:]
    times, main, rem = by_taps(col, w_ref, rem_ref, 2, height, width)
    centre = times(0, height, main[1])
    above = times(0, height - 1, main[0])
    below = times(1, height, main[2])
    tails = times(0, height, rem)
    for row in range(height):
        wide = centre[:, row]
        tail = tails[:, row, :, rest : 2 * rest]
        if row > 0:
            wide = wide + above[:, row - 1]
            tail = tail + tails[:, row - 1, :, :rest]
        if row < height - 1:
            wide = wide + below[:, row]
            tail = tail + tails[:, row + 1, :, 2 * rest : 3 * rest]
        total = x_buf[:, row].astype(F32) + jnp.concatenate([wide, tail], axis=-1)
        if 0 < row < height - 1:
            rounded = total.astype(BF)
            mid_ref[:, row - 1] = rounded
            hidden = silu(norm(rounded.reshape(2 * width, channels), g2_ref)).astype(BF)
            mid2_ref[:, row - 1] = hidden.reshape(2, width, channels)
        else:
            edge_ref[:, 0 if row == 0 else 1] = total


def outer_edge_kernel(
    acc_ref, above_ref, below_ref, g2_ref, w_ref, mid_ref, mid2_ref,
    spatial_ref, hidden_ref, first_ref, last_ref,
):
    _, rows, width, channels = mid_ref.shape
    cells = (rows + 2) * width
    spatial_ref[:, width : cells - width] = mid_ref[...].reshape(2, rows * width, channels)
    hidden_ref[:, width : cells - width] = mid2_ref[...].reshape(2, rows * width, channels)
    for side, halo_ref, a in ((0, above_ref, 0), (1, below_ref, 2)):
        halo = unpacked(halo_ref[...], channels)
        halo = jnp.concatenate([halo[:width], halo[halo.shape[0] - width :]], axis=0)
        add = dot(columns(halo.astype(F32), width), w_ref[a])
        total = acc_ref[:, side].reshape(2 * width, channels) + add
        rounded = total.astype(BF)
        hidden = silu(norm(rounded, g2_ref)).astype(BF)
        place = pl.ds(0 if side == 0 else cells - width, width)
        spatial_ref[:, place] = rounded.reshape(2, width, channels)
        hidden_ref[:, place] = hidden.reshape(2, width, channels)
    pack_into(first_ref, hidden_ref[0])
    pack_into(last_ref, hidden_ref[1])


def inner_kernel(
    x_ref, above_ref, below_ref, g1_ref, g2_ref, g3_ref, w_ref, rem_ref, spatial_ref, hidden_ref,
    wt_ref, wq_ref, wkv_ref,
    inner_ref, normed_ref, query_ref, keyval_ref, outer_ref,
):
    frames, height, width, channels = x_ref.shape
    inside = frames - 2
    cells = height * width
    full = channels // 256 * 256
    rest = channels - full
    x = x_ref[1 : frames - 1].reshape(inside * cells, channels)
    own = silu(norm(x, g1_ref))
    above = unpacked(above_ref[...], channels).astype(F32)
    below = unpacked(below_ref[...], channels).astype(F32)
    pieces = []
    for f in range(inside):
        pieces.append(above[(f + 1) * width : (f + 2) * width])
        pieces.append(own[f * cells : (f + 1) * cells])
        pieces.append(below[(f + 1) * width : (f + 2) * width])
    col = columns(jnp.concatenate(pieces, axis=0), width)
    times, main, rem = by_taps(col, w_ref, rem_ref, inside, height + 2, width)
    wide = times(0, height, main[0]) + times(1, height + 1, main[1]) + times(2, height + 2, main[2])
    tails = times(0, height + 2, rem)
    tail = (
        tails[:, :height, :, :rest]
        + tails[:, 1 : height + 1, :, rest : 2 * rest]
        + tails[:, 2:, :, 2 * rest : 3 * rest]
    )
    total = x.astype(F32) + jnp.concatenate([wide, tail], axis=-1).reshape(inside * cells, channels)
    rounded = total.astype(BF)
    hidden2 = silu(norm(rounded, g2_ref)).astype(BF)
    sources = jnp.concatenate([hidden_ref[0], hidden2, hidden_ref[1]], axis=0)
    spatial = jnp.concatenate([spatial_ref[0], rounded, spatial_ref[1]], axis=0)
    size = frames * cells
    earlier = dot(sources[: size - cells], wt_ref[0])
    same = dot(sources, wt_ref[1]) + spatial.astype(F32)
    later = dot(sources[cells:], wt_ref[2])
    outer_ref[0] = same[:cells] + later[:cells]
    outer_ref[1] = same[size - cells :] + earlier[size - 2 * cells :]
    temporal = (
        same[cells : size - cells] + later[cells:] + earlier[: size - 2 * cells]
    ).astype(BF)
    normed = norm(temporal, g3_ref).astype(BF)
    shape = (inside, cells, channels)
    inner_ref[...] = temporal.reshape(shape)
    normed_ref[...] = normed.reshape(shape)
    query_ref[...] = dot(normed, wq_ref[...]).astype(BF).reshape(shape)
    keyval_ref[...] = dot(normed, wkv_ref[...]).astype(BF).reshape(inside, cells, 2 * channels)


def temporal_edge_kernel(
    picks_ref, outer_ref, before_ref, after_ref, g3_ref, w_ref, inner_normed_ref,
    outer_out_ref, outer_normed_ref, chosen_ref, all_ref,
):
    channels = outer_ref.shape[-1]
    frames = all_ref.shape[0]
    all_ref[1 : frames - 1] = inner_normed_ref[...]
    for side, halo_ref, k in ((0, before_ref, 0), (1, after_ref, 2)):
        total = outer_ref[side] + dot(unpacked(halo_ref[...], channels), w_ref[k])
        rounded = total.astype(BF)
        outer_out_ref[side] = rounded
        normed = norm(rounded, g3_ref).astype(BF)
        outer_normed_ref[side] = normed
        all_ref[0 if side == 0 else frames - 1] = normed
    for n in range(chosen_ref.shape[0]):
        pack_into(chosen_ref.at[n], all_ref[picks_ref[0, n]])


def lane_map(shape, channel_dim, count, channels, value, everywhere=False):
    full = channels // LANES * LANES
    rest = channels - full
    c = lax.broadcasted_iota(jnp.int32, shape, channel_dim)
    lane = lax.broadcasted_iota(jnp.int32, shape, 1 - channel_dim)
    stride = LANES // 4
    wide = c < count * full
    source = jnp.where(wide, lax.div(c, full), lax.div(c - count * full, max(rest, 1)))
    channel = jnp.where(
        wide, lax.rem(c, full), full + lax.rem(jnp.maximum(c - count * full, 0), max(rest, 1))
    )
    head = lax.div(channel, HEAD_DIM)
    if everywhere:
        hit = lax.rem(lane, stride) == head
    else:
        hit = lane == source * stride + head
    return jnp.where(hit, value, 0.0).astype(BF)


def local_kernel(
    picks_ref, window_ref, inner_query_ref, inner_keyval_ref, outer_normed_ref, wq_ref, wkv_ref,
    query_ref, top_ref, sum_ref, mix_ref,
):
    frames, cells, channels = query_ref.shape
    count = picks_ref.shape[1]
    full = channels // LANES * LANES
    stride = LANES // 4
    outer = outer_normed_ref[...].reshape(2 * cells, channels)
    outer_query = dot(outer, wq_ref[...]).astype(BF)
    outer_keyval = dot(outer, wkv_ref[...]).astype(BF)
    queries = [outer_query[:cells]] + [inner_query_ref[f] for f in range(frames - 2)]
    queries.append(outer_query[cells:])
    keyvals = [outer_keyval[:cells]] + [inner_keyval_ref[f] for f in range(frames - 2)]
    keyvals.append(outer_keyval[cells:])
    for f in range(frames):
        query_ref[f] = queries[f]
    keys = [kv[:, :full] for kv in keyvals] + [
        jnp.concatenate([kv[:, full:channels] for kv in keyvals], axis=1)
    ]
    values = [kv[:, channels : channels + full].astype(F32) for kv in keyvals] + [
        jnp.concatenate([kv[:, channels + full :] for kv in keyvals], axis=1).astype(F32)
    ]
    products = []
    for q in queries:
        again = jnp.concatenate([q[:, full:]] * frames, axis=1)
        row = [q[:, :full] * k for k in keys[:frames]] + [again * keys[frames]]
        products.append(jnp.concatenate(row, axis=1))
    to_lanes = lane_map(
        (frames * channels, LANES), 0, frames, channels, 1.0 / math.sqrt(HEAD_DIM)
    )
    to_channels = lane_map((LANES, frames * channels), 1, frames, channels, 1.0)
    scores = dot(jnp.concatenate(products, axis=0), to_lanes)
    source = lax.div(lax.broadcasted_iota(jnp.int32, (1, LANES), 1), stride)
    window = window_ref[0]
    copies = jnp.zeros((1, LANES), F32)
    for n in range(count):
        copies = copies + jnp.where(source == picks_ref[0, n], 1.0, 0.0)
    weights = []
    for i in range(frames):
        times = copies + jnp.where(jnp.abs(source - i) < window, 1.0, 0.0)
        s = jnp.where(times > 0.0, scores[i * cells : (i + 1) * cells], -jnp.inf)
        top = jnp.maximum(s, pltpu.roll(s, stride, 1))
        top = jnp.maximum(top, pltpu.roll(top, 2 * stride, 1))
        w = jnp.exp(s - top) * times
        total = w + pltpu.roll(w, stride, 1)
        total = total + pltpu.roll(total, 2 * stride, 1)
        top_ref[i] = top
        sum_ref[i] = total
        weights.append(w.astype(BF))
    spread = dot(jnp.concatenate(weights, axis=0), to_channels)
    for i in range(frames):
        part = spread[i * cells : (i + 1) * cells]
        wide = part[:, :full] * values[0]
        for j in range(1, frames):
            wide = wide + part[:, j * full : (j + 1) * full] * values[j]
        tail = part[:, frames * full :] * values[frames]
        tail = tail[:, :LANES] + tail[:, LANES:]
        tail = tail + pltpu.roll(tail, LANES // 2, 1)
        mix_ref[i] = jnp.concatenate([wide, tail], axis=1)


def updated(which, refs, wkv_ref, query_ref, top_ref, sum_ref, mix_ref, last):
    frames, cells, channels = query_ref.shape
    full = channels // LANES * LANES
    count = refs[0].shape[0]
    state = (top_ref[...], sum_ref[...], mix_ref[...])
    size = frames * cells
    top, total, mix = (v.reshape(size, v.shape[-1]) for v in state)
    query = query_ref[...].reshape(size, channels)
    to_lanes = lane_map(
        (channels, LANES), 0, 1, channels, 1.0 / math.sqrt(HEAD_DIM), everywhere=True
    )
    to_channels = lane_map((LANES, 2 * channels), 1, 2, channels, 1.0)
    low = lax.broadcasted_iota(jnp.int32, (1, LANES), 1) < LANES // 4
    for n in range(count):
        anchor = refs[0][n]
        for t in range(1, len(refs)):
            anchor = jnp.where(which == t, refs[t][n], anchor)
        keyval = dot(unpacked(anchor, channels), wkv_ref[...]).astype(BF)
        key = jnp.concatenate([keyval[:, :channels]] * frames, axis=0)
        scores = dot(query * key, to_lanes)
        higher = jnp.maximum(top, scores)
        weight = jnp.exp(scores - higher)
        fade = jnp.exp(top - higher)
        total = total * fade + weight
        both = jnp.where(low, weight, fade)
        if last and n == count - 1:
            both = both / total
        spread = dot(both.astype(BF), to_channels)
        value = keyval[:, channels:].astype(F32)
        value = jnp.concatenate([value] * frames, axis=0)
        wide = spread[:, :full] * value[:, :full] + spread[:, full : 2 * full] * mix[:, :full]
        tail = jnp.concatenate([value[:, full:], mix[:, full + LANES // 2 :]], axis=1)
        tail = spread[:, 2 * full :] * tail
        tail = tail + pltpu.roll(tail, LANES // 2, 1)
        mix = jnp.concatenate([wide, tail], axis=1)
        top = higher
    return top, total, mix


def place_of(table, slot):
    me = lax.axis_index("clip")
    found = 0
    for clip, row in enumerate(table):
        if row[slot]:
            found = jnp.where(me == clip, row[slot], found)
    return found


def anchor_kernel(table, slot, many, *refs):
    wkv_ref, query_ref, top_ref, sum_ref, mix_ref, top_out, sum_out, mix_out = refs[many:]
    new = updated(
        place_of(table, slot), refs[:many], wkv_ref, query_ref, top_ref, sum_ref, mix_ref, False
    )
    for ref, v in zip((top_out, sum_out, mix_out), new):
        ref[...] = v.reshape(ref.shape)


def last_kernel(table, slot, many, *refs):
    (
        wkv_ref, query_ref, top_ref, sum_ref, mix_ref, inner_ref, outer_ref, wo_ref,
        out_ref, out_buf, sems,
    ) = refs[many:]
    frames, cells, channels = query_ref.shape
    height, width = out_ref.shape[1:3]
    _, _, mix = updated(
        place_of(table, slot), refs[:many], wkv_ref, query_ref, top_ref, sum_ref, mix_ref, True
    )
    attended = mix[:, :channels].astype(BF)
    result = dot(attended, wo_ref[...])
    copies = []
    for i in range(frames):
        if 0 < i < frames - 1:
            temporal = inner_ref[i - 1]
        else:
            temporal = outer_ref[0 if i == 0 else 1]
        total = temporal.astype(F32) + result[i * cells : (i + 1) * cells]
        out_buf[i] = total.astype(BF).reshape(height, width, channels)
        copies.append(pltpu.make_async_copy(out_buf.at[i], out_ref.at[i], sems.at[i]))
        copies[i].start()
    for copy in copies:
        copy.wait()


def steps(axis):
    count = lax.axis_size(axis)
    up = [(i, i + 1) for i in range(count - 1)]
    return up, [(j, i) for i, j in up]


def slots(clips):
    names = [[] for _ in range(clips - 1)]
    table = [[0] * (clips - 1) for _ in range(clips)]
    for me in range(clips):
        order = []
        for distance in range(1, clips):
            if me >= distance:
                order.append(("up", distance))
            if me + distance < clips:
                order.append(("down", distance))
        for slot, (way, distance) in enumerate(order):
            name = ("far" if distance == clips - 1 and clips > 2 else way, distance)
            if name not in names[slot]:
                names[slot].append(name)
            table[me][slot] = names[slot].index(name)
    return names, table


def on_device(
    latents, anchor_index, window, gain_one, spatial_w, gain_two, temporal_w, gain_three,
    w_query, w_keyval, w_out,
):
    frames, height, width, channels = latents.shape
    cells = height * width
    count = anchor_index.shape[1]
    ws = spatial_w.reshape(3, 3 * channels, channels)
    one = 2 * channels * channels
    packed = cells * channels // LANES
    edge_packed = frames * width * channels // LANES
    lanes_up = (channels + LANES - 1) // LANES * LANES
    sem = pltpu.SemaphoreType.DMA

    top, bottom = call(
        edge_kernel,
        [((edge_packed, LANES), BF)] * 2,
        [ANY, VMEM],
        [pltpu.VMEM((2, frames, width, channels), BF), sem((2,))],
        flops=one * 100,
    )(latents, gain_one)
    up, down = steps("strip")
    above = lax.ppermute(bottom, "strip", up)
    below = lax.ppermute(top, "strip", down)
    mid, mid2, edge_sum, w_vmem, w_rem = call(
        outer_kernel,
        [
            ((2, height - 2, width, channels), BF),
            ((2, height - 2, width, channels), BF),
            ((2, 2, width, channels), F32),
            ((3, 3 * channels, channels), BF),
            ((3 * channels, 3 * (channels % 256)), BF),
        ],
        [ANY, VMEM, VMEM, ANY],
        [pltpu.VMEM((2, height, width, channels), BF), sem((5,))],
        flops=9 * 2 * cells * one,
        limit=32,
    )(latents, gain_one, gain_two, ws)
    spatial, hidden, first, last = call(
        outer_edge_kernel,
        [
            ((2, cells, channels), BF),
            ((2, cells, channels), BF),
            ((packed, LANES), BF),
            ((packed, LANES), BF),
        ],
        [VMEM] * 7,
        flops=6 * 2 * width * one,
    )(edge_sum, above, below, gain_two, w_vmem, mid, mid2)
    up, down = steps("clip")
    before = lax.ppermute(last, "clip", up)
    after = lax.ppermute(first, "clip", down)
    inner, inner_normed, inner_query, inner_keyval, outer_sum = call(
        inner_kernel,
        [
            ((frames - 2, cells, channels), BF),
            ((frames - 2, cells, channels), BF),
            ((frames - 2, cells, channels), BF),
            ((frames - 2, cells, 2 * channels), BF),
            ((2, cells, channels), F32),
        ],
        [VMEM] * 13,
        flops=(9 + 2 * 3 + 3) * 2 * cells * one,
        limit=32,
    )(
        latents, above, below, gain_one, gain_two, gain_three, w_vmem, w_rem, spatial, hidden,
        temporal_w, w_query, w_keyval,
    )
    outer, outer_normed, chosen = call(
        temporal_edge_kernel,
        [
            ((2, cells, channels), BF),
            ((2, cells, channels), BF),
            ((count, packed, LANES), BF),
        ],
        [SMEM] + [VMEM] * 6,
        [pltpu.VMEM((frames, cells, channels), BF)],
        flops=2 * cells * one,
    )(anchor_index, outer_sum, before, after, gain_three, temporal_w, inner_normed)
    clips = lax.axis_size("clip")
    got = {("up", 0): chosen, ("down", 0): chosen}
    got["up", 1] = lax.ppermute(chosen, "clip", up)
    got["down", 1] = lax.ppermute(chosen, "clip", down)
    if clips > 2:
        ends = [(0, clips - 1), (clips - 1, 0)]
        got["far", clips - 1] = lax.ppermute(chosen, "clip", ends)
    for distance in range(2, clips - 1):
        links = [(i, i + 1) for i in range(distance - 1, clips - 1)]
        got["up", distance] = lax.ppermute(got["up", distance - 1], "clip", links)
        links = [(i + 1, i) for i in range(clips - distance)]
        got["down", distance] = lax.ppermute(got["down", distance - 1], "clip", links)
    query, *state = call(
        local_kernel,
        [
            ((frames, cells, channels), BF),
            ((frames, cells, LANES), F32),
            ((frames, cells, LANES), F32),
            ((frames, cells, lanes_up), F32),
        ],
        [SMEM] * 2 + [VMEM] * 5,
        flops=10 * frames * cells * one,
        limit=32,
    )(anchor_index, window, inner_query, inner_keyval, outer_normed, w_query, w_keyval)
    names, table = slots(clips)
    for slot in range(clips - 1):
        candidates = [got[name] for name in names[slot]]
        many = len(candidates)
        if slot < clips - 2:
            state = call(
                functools.partial(anchor_kernel, table, slot, many),
                [
                    ((frames, cells, LANES), F32),
                    ((frames, cells, LANES), F32),
                    ((frames, cells, lanes_up), F32),
                ],
                [VMEM] * (many + 5),
                flops=4 * frames * cells * one,
                limit=32,
            )(*candidates, w_keyval, query, *state)
        else:
            (out,) = call(
                functools.partial(last_kernel, table, slot, many),
                [((frames, height, width, channels), BF)],
                [VMEM] * (many + 8),
                [pltpu.VMEM((frames, height, width, channels), BF), sem((frames,))],
                flops=5 * frames * cells * one,
                limit=32,
                out_specs=(ANY,),
            )(*candidates, w_keyval, query, *state, inner, outer, w_out)
    return out


def solution(mesh):
    return jax.shard_map(
        on_device,
        mesh=mesh,
        in_specs=(
            P(("groups", "clip"), "strip", None, None),
            P(("groups", "clip"), None),
            P(),
            P(),
            P(),
            P(),
            P(),
            P(),
            P(),
            P(),
            P(),
        ),
        out_specs=P(("groups", "clip"), "strip", None, None),
        check_vma=False,
    )
```

```python
import functools
import math

import jax
import jax.numpy as jnp
from jax import lax
from jax.experimental import pallas as pl
from jax.experimental.pallas import tpu as pltpu
from jax.sharding import PartitionSpec as P

HEADS = 5
HEAD_DIM = 64
LANES = 128
BF = jnp.bfloat16
F32 = jnp.float32
VMEM = pl.BlockSpec(memory_space=pltpu.VMEM)
SMEM = pl.BlockSpec(memory_space=pltpu.SMEM)
HBM = pl.BlockSpec(memory_space=pltpu.HBM)
MIB = 1 << 20


def call(body, outs, specs, scratch=(), flops=0, limit=24, out_specs=None):
    return pl.pallas_call(
        body,
        out_shape=tuple(jax.ShapeDtypeStruct(s, d) for s, d in outs),
        in_specs=specs,
        out_specs=out_specs or tuple(VMEM for _ in outs),
        scratch_shapes=list(scratch),
        cost_estimate=pl.CostEstimate(flops=flops, bytes_accessed=2 * MIB, transcendentals=0),
        compiler_params=pltpu.CompilerParams(vmem_limit_bytes=limit * MIB),
    )


def dot(a, b):
    return jnp.dot(a, b, preferred_element_type=F32)


def norm(v, gain_ref):
    wide = v.astype(F32)
    centred = wide - jnp.mean(wide, axis=-1, keepdims=True)
    variance = jnp.mean(centred * centred, axis=-1, keepdims=True)
    return centred * lax.rsqrt(variance + 1e-05) * gain_ref[...].reshape(1, v.shape[1])


def silu(u):
    half = 0.5 * u
    return half + half * jnp.tanh(half)


def pack_into(ref, h):
    cells, channels = h.shape
    full = channels // LANES
    for t in range(full):
        ref[t * cells : (t + 1) * cells, :] = h[:, t * LANES : (t + 1) * LANES]
    rest = channels - full * LANES
    if rest:
        share = LANES // rest
        part = cells // share
        ref[full * cells :, :] = jnp.concatenate(
            [h[s * part : (s + 1) * part, full * LANES :] for s in range(share)], axis=1
        )


def unpacked(p, channels):
    cells = p.shape[0] * LANES // channels
    full = channels // LANES
    pieces = [p[t * cells : (t + 1) * cells, :] for t in range(full)]
    rest = channels - full * LANES
    if rest:
        share = LANES // rest
        tail = p[full * cells :, :]
        pieces.append(
            jnp.concatenate([tail[:, s * rest : (s + 1) * rest] for s in range(share)], axis=0)
        )
    return jnp.concatenate(pieces, axis=1)


def columns(h, width):
    cells = h.shape[0]
    place = lax.rem(lax.broadcasted_iota(jnp.int32, h.shape, 0), width)
    left = jnp.where(place == 0, 0.0, pltpu.roll(h, 1, 0))
    right = jnp.where(place == width - 1, 0.0, pltpu.roll(h, cells - 1, 0))
    return jnp.concatenate([left.astype(BF), h.astype(BF), right.astype(BF)], axis=1)


def edge_kernel(x_ref, top_ref, bottom_ref):
    frames, height, width, channels = x_ref.shape
    pack_into(top_ref, x_ref[:, 0].reshape(frames * width, channels))
    pack_into(bottom_ref, x_ref[:, height - 1].reshape(frames * width, channels))


def prepare_kernel(x_ref, g1_ref, w_ref, rem_ref, col_ref, order_ref):
    order_ref[...] = jnp.zeros_like(order_ref)
    frames, height, width, channels = x_ref.shape
    full = channels // 256 * 256
    rest = channels - full

    def frame(f, _):
        x = x_ref[f].reshape(height * width, channels)
        col_ref[f] = columns(silu(norm(x, g1_ref)), width)
        return 0

    lax.fori_loop(0, frames, frame, 0)
    for a in range(3):
        rem_ref[:, a * rest : (a + 1) * rest] = w_ref[a, :, full:]


def rim_kernel(x_ref, above_ref, below_ref, order_ref, first_ref, last_ref):
    frames, height, width, channels = x_ref.shape
    above = unpacked(above_ref[...], channels)
    below = unpacked(below_ref[...], channels)
    for f, ref in ((0, first_ref), (frames - 1, last_ref)):
        rows = slice(f * width, (f + 1) * width)
        own = x_ref[f].reshape(height * width, channels)
        pack_into(ref, jnp.concatenate([above[rows], own, below[rows]], axis=0))


def convolved(x, col, w_ref, rem_ref, width):
    count, cells, channels = x.shape
    full = channels // 256 * 256
    rest = channels - full

    def part(a, lo, size):
        return col[:, lo : lo + size].reshape(count * size, 3 * channels)

    wide = 0.0
    for a in range(3):
        wide = wide + dot(part(a, a * width, cells), w_ref[a, :, :full])
    wide = wide.reshape(count, cells, full)
    tails = dot(part(0, 0, cells + 2 * width), rem_ref[...]).reshape(count, cells + 2 * width, 3 * rest)
    tail = (
        tails[:, :cells, :rest]
        + tails[:, width : width + cells, rest : 2 * rest]
        + tails[:, 2 * width :, 2 * rest :]
    )
    return (x.astype(F32) + jnp.concatenate([wide, tail], axis=-1)).astype(BF)


def spatial_kernel(
    x_ref, col_ref, above_ref, below_ref, g1_ref, g2_ref, w_ref, rem_ref,
    spatial_ref, hidden_ref, rims_ref,
):
    frames, height, width, channels = x_ref.shape
    cells = height * width
    for side, ref in enumerate((above_ref, below_ref)):
        rim = silu(norm(unpacked(ref[...], channels), g1_ref))
        rims_ref[side] = columns(rim, width).reshape(frames, width, 3 * channels)
    group = 2 if frames % 2 == 0 else 1

    def some(t, _):
        at = pl.ds(t * group, group)
        x = x_ref[at].reshape(group, cells, channels)
        col = jnp.concatenate([rims_ref[0, at], col_ref[at], rims_ref[1, at]], axis=1)
        spatial = convolved(x, col, w_ref, rem_ref, width)
        spatial_ref[at] = spatial
        hidden = silu(norm(spatial.reshape(group * cells, channels), g2_ref)).astype(BF)
        hidden_ref[at] = hidden.reshape(group, cells, channels)
        return 0

    lax.fori_loop(0, frames // group, some, 0)


def halo_hidden(raw, g1_ref, g2_ref, w_ref, rem_ref, width, channels):
    x = unpacked(raw, channels)
    size = x.shape[0]
    col = columns(silu(norm(x, g1_ref)), width)
    spatial = convolved(x[None, width : size - width], col[None], w_ref, rem_ref, width)[0]
    return silu(norm(spatial, g2_ref)).astype(BF)


def chosen_kernel(
    width, picks_ref, before_ref, after_ref, spatial_ref, hidden_ref,
    g1_ref, g2_ref, g3_ref, w_ref, rem_ref, wt_ref,
    halo_ref, chosen_ref,
):
    frames, cells, channels = spatial_ref.shape
    for n in range(chosen_ref.shape[0]):
        pick = picks_ref[0, n]
        raw = jnp.where(pick == frames - 1, after_ref[...], before_ref[...])
        halo = halo_hidden(raw, g1_ref, g2_ref, w_ref, rem_ref, width, channels)
        halo_ref[n] = halo
        earlier = jnp.where(pick == 0, halo, hidden_ref[jnp.maximum(pick - 1, 0)])
        later = jnp.where(pick == frames - 1, halo, hidden_ref[jnp.minimum(pick + 1, frames - 1)])
        total = spatial_ref[pick].astype(F32) + dot(hidden_ref[pick], wt_ref[1])
        total = total + dot(earlier, wt_ref[0]) + dot(later, wt_ref[2])
        pack_into(chosen_ref.at[n], norm(total.astype(BF), g3_ref).astype(BF))


def temporal_kernel(
    width, picks_ref, before_ref, after_ref, halo_ref, spatial_ref, hidden_ref,
    g1_ref, g2_ref, g3_ref, w_ref, rem_ref, wt_ref, wq_ref, wkv_ref,
    temporal_ref, query_ref, keyval_ref,
):
    frames, cells, channels = spatial_ref.shape
    size = frames * cells
    at_end = picks_ref[0, 0] == frames - 1
    raw = jnp.where(at_end, before_ref[...], after_ref[...])
    other = halo_hidden(raw, g1_ref, g2_ref, w_ref, rem_ref, width, channels)
    halo = halo_ref[0]
    before = jnp.where(at_end, other, halo)
    after = jnp.where(at_end, halo, other)
    hidden = hidden_ref[...].reshape(size, channels)
    total = spatial_ref[...].reshape(size, channels).astype(F32) + dot(hidden, wt_ref[1])
    total = total + dot(jnp.concatenate([before, hidden[: size - cells]], axis=0), wt_ref[0])
    total = total + dot(jnp.concatenate([hidden[cells:], after], axis=0), wt_ref[2])
    temporal = total.astype(BF)
    temporal_ref[...] = temporal.reshape(frames, cells, channels)
    normed = norm(temporal, g3_ref).astype(BF)
    query_ref[...] = dot(normed, wq_ref[...]).astype(BF).reshape(frames, cells, channels)
    keyval_ref[...] = dot(normed, wkv_ref[...]).astype(BF).reshape(frames, cells, 2 * channels)


def lane_map(shape, channel_dim, count, channels, value, everywhere=False):
    full = channels // LANES * LANES
    rest = channels - full
    c = lax.broadcasted_iota(jnp.int32, shape, channel_dim)
    lane = lax.broadcasted_iota(jnp.int32, shape, 1 - channel_dim)
    stride = LANES // 4
    wide = c < count * full
    source = jnp.where(wide, lax.div(c, full), lax.div(c - count * full, max(rest, 1)))
    channel = jnp.where(
        wide, lax.rem(c, full), full + lax.rem(jnp.maximum(c - count * full, 0), max(rest, 1))
    )
    head = lax.div(channel, HEAD_DIM)
    if everywhere:
        hit = lax.rem(lane, stride) == head
    else:
        hit = lane == source * stride + head
    return jnp.where(hit, value, 0.0).astype(BF)


def local_kernel(
    picks_ref, window_ref, query_ref, keyval_ref, top_ref, sum_ref, mix_ref,
):
    frames, cells, channels = query_ref.shape
    count = picks_ref.shape[1]
    full = channels // LANES * LANES
    stride = LANES // 4
    queries = [query_ref[f] for f in range(frames)]
    keyvals = [keyval_ref[f] for f in range(frames)]
    keys = [kv[:, :full] for kv in keyvals] + [
        jnp.concatenate([kv[:, full:channels] for kv in keyvals], axis=1)
    ]
    values = [kv[:, channels : channels + full].astype(F32) for kv in keyvals] + [
        jnp.concatenate([kv[:, channels + full :] for kv in keyvals], axis=1).astype(F32)
    ]
    products = []
    for q in queries:
        again = jnp.concatenate([q[:, full:]] * frames, axis=1)
        row = [q[:, :full] * k for k in keys[:frames]] + [again * keys[frames]]
        products.append(jnp.concatenate(row, axis=1))
    to_lanes = lane_map(
        (frames * channels, LANES), 0, frames, channels, 1.0 / math.sqrt(HEAD_DIM)
    )
    to_channels = lane_map((LANES, frames * channels), 1, frames, channels, 1.0)
    scores = dot(jnp.concatenate(products, axis=0), to_lanes)
    source = lax.div(lax.broadcasted_iota(jnp.int32, (1, LANES), 1), stride)
    window = window_ref[0]
    copies = jnp.zeros((1, LANES), F32)
    for n in range(count):
        copies = copies + jnp.where(source == picks_ref[0, n], 1.0, 0.0)
    weights = []
    for i in range(frames):
        times = copies + jnp.where(jnp.abs(source - i) < window, 1.0, 0.0)
        s = jnp.where(times > 0.0, scores[i * cells : (i + 1) * cells], -jnp.inf)
        top = jnp.maximum(s, pltpu.roll(s, stride, 1))
        top = jnp.maximum(top, pltpu.roll(top, 2 * stride, 1))
        w = jnp.exp(s - top) * times
        total = w + pltpu.roll(w, stride, 1)
        total = total + pltpu.roll(total, 2 * stride, 1)
        top_ref[i] = top
        sum_ref[i] = total
        weights.append(w.astype(BF))
    spread = dot(jnp.concatenate(weights, axis=0), to_channels)
    for i in range(frames):
        part = spread[i * cells : (i + 1) * cells]
        wide = part[:, :full] * values[0]
        for j in range(1, frames):
            wide = wide + part[:, j * full : (j + 1) * full] * values[j]
        tail = part[:, frames * full :] * values[frames]
        tail = tail[:, :LANES] + tail[:, LANES:]
        tail = tail + pltpu.roll(tail, LANES // 2, 1)
        mix_ref[i] = jnp.concatenate([wide, tail], axis=1)


def updated(anchor_ref, wkv_ref, query_ref, top_ref, sum_ref, mix_ref, last):
    frames, cells, channels = query_ref.shape
    full = channels // LANES * LANES
    count = anchor_ref.shape[0]
    state = (top_ref[...], sum_ref[...], mix_ref[...])
    size = frames * cells
    top, total, mix = (v.reshape(size, v.shape[-1]) for v in state)
    query = query_ref[...].reshape(size, channels)
    to_lanes = lane_map(
        (channels, LANES), 0, 1, channels, 1.0 / math.sqrt(HEAD_DIM), everywhere=True
    )
    to_channels = lane_map((LANES, 2 * channels), 1, 2, channels, 1.0)
    low = lax.broadcasted_iota(jnp.int32, (1, LANES), 1) < LANES // 4
    for n in range(count):
        keyval = dot(unpacked(anchor_ref[n], channels), wkv_ref[...]).astype(BF)
        key = jnp.concatenate([keyval[:, :channels]] * frames, axis=0)
        scores = dot(query * key, to_lanes)
        higher = jnp.maximum(top, scores)
        weight = jnp.exp(scores - higher)
        fade = jnp.exp(top - higher)
        total = total * fade + weight
        both = jnp.where(low, weight, fade)
        if last and n == count - 1:
            both = both / total
        spread = dot(both.astype(BF), to_channels)
        value = keyval[:, channels:].astype(F32)
        value = jnp.concatenate([value] * frames, axis=0)
        wide = spread[:, :full] * value[:, :full] + spread[:, full : 2 * full] * mix[:, :full]
        tail = jnp.concatenate([value[:, full:], mix[:, full + LANES // 2 :]], axis=1)
        tail = spread[:, 2 * full :] * tail
        tail = tail + pltpu.roll(tail, LANES // 2, 1)
        mix = jnp.concatenate([wide, tail], axis=1)
        top = higher
    return top, total, mix


def anchor_kernel(
    anchor_ref, wkv_ref, query_ref, top_ref, sum_ref, mix_ref, top_out, sum_out, mix_out
):
    new = updated(anchor_ref, wkv_ref, query_ref, top_ref, sum_ref, mix_ref, False)
    for ref, v in zip((top_out, sum_out, mix_out), new):
        ref[...] = v.reshape(ref.shape)


def last_kernel(
    anchor_ref, wkv_ref, query_ref, top_ref, sum_ref, mix_ref, temporal_ref, wo_ref,
    out_ref, out_buf, sems,
):
    frames, cells, channels = query_ref.shape
    height, width = out_ref.shape[1:3]
    _, _, mix = updated(anchor_ref, wkv_ref, query_ref, top_ref, sum_ref, mix_ref, True)
    attended = mix[:, :channels].astype(BF)
    result = dot(attended, wo_ref[...])
    copies = []
    for i in range(frames):
        total = temporal_ref[i].astype(F32) + result[i * cells : (i + 1) * cells]
        out_buf[i] = total.astype(BF).reshape(height, width, channels)
        copies.append(pltpu.make_async_copy(out_buf.at[i], out_ref.at[i], sems.at[i]))
        copies[i].start()
    for copy in copies:
        copy.wait()


def neighbours(leading, last, axis):
    count = lax.axis_size(axis)
    up = [(i, i + 1) for i in range(count - 1)]
    down = [(j, i) for i, j in up]
    return lax.ppermute(last, axis, up), lax.ppermute(leading, axis, down)


def on_device(
    latents, anchor_index, window, gain_one, spatial_w, gain_two, temporal_w, gain_three,
    w_query, w_keyval, w_out,
):
    frames, height, width, channels = latents.shape
    cells = height * width
    count = anchor_index.shape[1]
    ws = spatial_w.reshape(3, 3 * channels, channels)
    one = 2 * channels * channels
    packed = cells * channels // LANES
    edge_packed = frames * width * channels // LANES
    rim_packed = (cells + 2 * width) * channels // LANES
    lanes_up = (channels + LANES - 1) // LANES * LANES
    sem = pltpu.SemaphoreType.DMA
    some = (frames, cells, channels)

    x, g1, g2, g3, w = latents, gain_one, gain_two, gain_three, ws

    top, bottom = call(
        edge_kernel, [((edge_packed, LANES), BF)] * 2, [VMEM], flops=8 * frames * cells * one
    )(x)
    above, below = neighbours(top, bottom, "strip")
    w_rem, col, order = call(
        prepare_kernel,
        [
            ((3 * channels, 3 * (channels % 256)), BF),
            ((frames, cells, 3 * channels), BF),
            ((8, LANES), F32),
        ],
        [VMEM] * 3,
        flops=4 * frames * cells * one,
    )(x, g1, w)
    first, last = call(
        rim_kernel, [((rim_packed, LANES), BF)] * 2, [VMEM] * 4
    )(x, above, below, order)
    before, after = neighbours(first, last, "clip")
    spatial, hidden = call(
        spatial_kernel,
        [(some, BF), (some, BF)],
        [VMEM] * 8,
        [pltpu.VMEM((2, frames, width, 3 * channels), BF)],
        flops=9 * frames * cells * one,
        limit=32,
    )(x, col, above, below, g1, g2, w, w_rem)
    halo, chosen = call(
        functools.partial(chosen_kernel, width),
        [((count, cells, channels), BF), ((count, packed, LANES), BF)],
        [SMEM] + [VMEM] * 10,
        flops=12 * cells * one,
    )(anchor_index, before, after, spatial, hidden, g1, g2, g3, w, w_rem, temporal_w)
    clips = lax.axis_size("clip")
    arrived = [
        lax.ppermute(chosen, "clip", [(i, (i + s) % clips) for i in range(clips)])
        for s in range(1, clips)
    ]
    temporal, query, keyval = call(
        functools.partial(temporal_kernel, width),
        [(some, BF), (some, BF), ((frames, cells, 2 * channels), BF)],
        [SMEM] + [VMEM] * 13,
        flops=(9 + 6 * frames) * cells * one,
        limit=32,
    )(
        anchor_index, before, after, halo, spatial, hidden, g1, g2, g3, w, w_rem, temporal_w,
        w_query, w_keyval,
    )
    states = [((frames, cells, LANES), F32)] * 2 + [((frames, cells, lanes_up), F32)]
    state = call(
        local_kernel, states, [SMEM] * 2 + [VMEM] * 2, flops=10 * frames * cells * one, limit=32
    )(anchor_index, window, query, keyval)
    for arrival in arrived[:-1]:
        state = call(
            anchor_kernel, states, [VMEM] * 6, flops=4 * frames * cells * one, limit=32
        )(arrival, w_keyval, query, *state)
    (out,) = call(
        last_kernel,
        [(latents.shape, BF)],
        [VMEM] * 8,
        [pltpu.VMEM(latents.shape, BF), sem((frames,))],
        flops=5 * frames * cells * one,
        limit=32,
        out_specs=(HBM,),
    )(arrived[-1], w_keyval, query, *state, temporal, w_out)
    return out


def solution(mesh):
    return jax.shard_map(
        on_device,
        mesh=mesh,
        in_specs=(
            P(("groups", "clip"), "strip", None, None),
            P(("groups", "clip"), None),
            P(),
            P(),
            P(),
            P(),
            P(),
            P(),
            P(),
            P(),
            P(),
        ),
        out_specs=P(("groups", "clip"), "strip", None, None),
        check_vma=False,
    )
```

```python
import functools
import math

import jax
import jax.numpy as jnp
from jax import lax
from jax.experimental import pallas as pl
from jax.experimental.pallas import tpu as pltpu
from jax.sharding import PartitionSpec as P

HEADS = 5
HEAD_DIM = 64
LANES = 128
BF = jnp.bfloat16
F32 = jnp.float32
VMEM = pl.BlockSpec(memory_space=pltpu.VMEM)
HBM = pl.BlockSpec(memory_space=pltpu.HBM)
MIB = 1 << 20


def call(body, outs, specs, scratch=(), flops=0, limit=24, out_specs=None):
    return pl.pallas_call(
        body,
        out_shape=tuple(jax.ShapeDtypeStruct(s, d) for s, d in outs),
        in_specs=specs,
        out_specs=out_specs or tuple(VMEM for _ in outs),
        scratch_shapes=list(scratch),
        cost_estimate=pl.CostEstimate(flops=flops, bytes_accessed=2 * MIB, transcendentals=0),
        compiler_params=pltpu.CompilerParams(vmem_limit_bytes=limit * MIB),
    )


def dot(a, b):
    return jnp.dot(a, b, preferred_element_type=F32)


def norm(v, gain_ref):
    wide = v.astype(F32)
    centred = wide - jnp.mean(wide, axis=-1, keepdims=True)
    variance = jnp.mean(centred * centred, axis=-1, keepdims=True)
    return centred * lax.rsqrt(variance + 1e-05) * gain_ref[...].reshape(1, v.shape[1])


def silu(u):
    half = 0.5 * u
    return half + half * jnp.tanh(half)


def pack_into(ref, h):
    cells, channels = h.shape
    full = channels // LANES
    for t in range(full):
        ref[t * cells : (t + 1) * cells, :] = h[:, t * LANES : (t + 1) * LANES]
    rest = channels - full * LANES
    if rest:
        share = LANES // rest
        part = cells // share
        ref[full * cells :, :] = jnp.concatenate(
            [h[s * part : (s + 1) * part, full * LANES :] for s in range(share)], axis=1
        )


def unpacked(p, channels):
    cells = p.shape[0] * LANES // channels
    full = channels // LANES
    pieces = [p[t * cells : (t + 1) * cells, :] for t in range(full)]
    rest = channels - full * LANES
    if rest:
        share = LANES // rest
        tail = p[full * cells :, :]
        pieces.append(
            jnp.concatenate([tail[:, s * rest : (s + 1) * rest] for s in range(share)], axis=0)
        )
    return jnp.concatenate(pieces, axis=1)


def columns(h, width):
    cells = h.shape[0]
    place = lax.rem(lax.broadcasted_iota(jnp.int32, h.shape, 0), width)
    left = jnp.where(place == 0, 0.0, pltpu.roll(h, 1, 0))
    right = jnp.where(place == width - 1, 0.0, pltpu.roll(h, cells - 1, 0))
    return jnp.concatenate([left.astype(BF), h.astype(BF), right.astype(BF)], axis=1)


def scalar(ref, n):
    values = ref[...].astype(F32)
    place = lax.broadcasted_iota(jnp.int32, values.shape, 1)
    return jnp.sum(jnp.where(place == n, values, 0.0)).astype(jnp.int32)


def edge_kernel(x_ref, first_ref, last_ref, top_ref, bottom_ref):
    frames, height, width, channels = x_ref.shape
    pack_into(first_ref, x_ref[0].reshape(height * width, channels))
    pack_into(last_ref, x_ref[frames - 1].reshape(height * width, channels))
    pack_into(top_ref, x_ref[:, 0].reshape(frames * width, channels))
    pack_into(bottom_ref, x_ref[:, height - 1].reshape(frames * width, channels))


def prepare_kernel(x_ref, g1_ref, w_ref, rem_ref, col_ref):
    frames, height, width, channels = x_ref.shape
    full = channels // 256 * 256
    rest = channels - full

    def frame(f, _):
        x = x_ref[f].reshape(height * width, channels)
        col_ref[f] = columns(silu(norm(x, g1_ref)), width)
        return 0

    lax.fori_loop(0, frames, frame, 0)
    for a in range(3):
        rem_ref[:, a * rest : (a + 1) * rest] = w_ref[a, :, full:]


def rim_kernel(width, before_ref, after_ref, order_ref, top_ref, bottom_ref):
    cells = order_ref.shape[1]
    channels = before_ref.shape[0] * LANES // cells
    frames = [unpacked(ref[...], channels) for ref in (before_ref, after_ref)]
    pack_into(top_ref, jnp.concatenate([f[:width] for f in frames], axis=0))
    pack_into(bottom_ref, jnp.concatenate([f[cells - width :] for f in frames], axis=0))


def convolved(x, col, w_ref, rem_ref, width):
    count, cells, channels = x.shape
    full = channels // 256 * 256
    rest = channels - full

    def part(a, lo, size):
        return col[:, lo : lo + size].reshape(count * size, 3 * channels)

    wide = 0.0
    for a in range(3):
        wide = wide + dot(part(a, a * width, cells), w_ref[a, :, :full])
    wide = wide.reshape(count, cells, full)
    tails = dot(part(0, 0, cells + 2 * width), rem_ref[...]).reshape(count, cells + 2 * width, 3 * rest)
    tail = (
        tails[:, :cells, :rest]
        + tails[:, width : width + cells, rest : 2 * rest]
        + tails[:, 2 * width :, 2 * rest :]
    )
    return (x.astype(F32) + jnp.concatenate([wide, tail], axis=-1)).astype(BF)


def rim_terms(above_ref, below_ref, g1_ref, w_ref, frames, width, channels, add_ref):
    for side, ref, a in ((0, above_ref, 0), (1, below_ref, 2)):
        rim = silu(norm(unpacked(ref[...], channels), g1_ref))
        add = dot(columns(rim, width), w_ref[a])
        add_ref[side] = add.reshape(frames, width, channels)


def spatial_frame(f, x_ref, col_ref, g2_ref, w_ref, rem_ref, add_ref, spatial_ref, hidden_ref, to):
    _, height, width, channels = x_ref.shape
    cells = height * width
    full = channels // 256 * 256
    rest = channels - full
    centre = dot(col_ref[f], w_ref[1, :, :full])
    above = dot(col_ref[f, : cells - width], w_ref[0, :, :full])
    below = dot(col_ref[f, width:], w_ref[2, :, :full])
    tails = dot(col_ref[f], rem_ref[...])
    for row in range(height):
        lo, hi = row * width, (row + 1) * width
        wide = centre[lo:hi]
        tail = tails[lo:hi, rest : 2 * rest]
        if row > 0:
            wide = wide + above[lo - width : lo]
            tail = tail + tails[lo - width : lo, :rest]
        if row < height - 1:
            wide = wide + below[lo:hi]
            tail = tail + tails[hi : hi + width, 2 * rest : 3 * rest]
        total = x_ref[f, row].astype(F32) + jnp.concatenate([wide, tail], axis=1)
        if row == 0:
            total = total + add_ref[0, f]
        if row == height - 1:
            total = total + add_ref[1, f]
        rounded = total.astype(BF)
        spatial_ref[to, lo:hi] = rounded
        hidden_ref[to, lo:hi] = silu(norm(rounded, g2_ref)).astype(BF)


def spatial_kernel(
    x_ref, col_ref, above_ref, below_ref, g1_ref, g2_ref, w_ref, rem_ref,
    spatial_ref, hidden_ref, add_ref, order_ref,
):
    frames, _, width, channels = x_ref.shape
    order_ref[...] = jnp.zeros_like(order_ref)
    rim_terms(above_ref, below_ref, g1_ref, w_ref, frames, width, channels, add_ref)

    def one(f, _):
        spatial_frame(
            f, x_ref, col_ref, g2_ref, w_ref, rem_ref, add_ref, spatial_ref, hidden_ref, f
        )
        return 0

    lax.fori_loop(0, spatial_ref.shape[0], one, 0)


def more_spatial_kernel(
    x_ref, col_ref, add_ref, early_spatial_ref, early_hidden_ref, g2_ref, w_ref, rem_ref,
    spatial_ref, hidden_ref,
):
    early = early_spatial_ref.shape[0]
    spatial_ref[:early] = early_spatial_ref[...]
    hidden_ref[:early] = early_hidden_ref[...]

    def one(f, _):
        spatial_frame(
            f, x_ref, col_ref, g2_ref, w_ref, rem_ref, add_ref, spatial_ref, hidden_ref, f
        )
        return 0

    lax.fori_loop(early, x_ref.shape[0], one, 0)


def halo_hidden(
    after, before_ref, after_ref, above_ref, below_ref, g1_ref, g2_ref, w_ref, rem_ref, width, channels
):
    own = unpacked(jnp.where(after, after_ref[...], before_ref[...]), channels)
    rims = []
    for ref in (above_ref, below_ref):
        rim = unpacked(ref[...], channels)
        rims.append(jnp.where(after, rim[width:], rim[:width]))
    x = jnp.concatenate([rims[0], own, rims[1]], axis=0)
    col = columns(silu(norm(x, g1_ref)), width)
    spatial = convolved(own[None], col[None], w_ref, rem_ref, width)[0]
    return silu(norm(spatial, g2_ref)).astype(BF)


def chosen_kernel(
    width, picks_ref, before_ref, after_ref, above_ref, below_ref, spatial_ref, hidden_ref,
    g1_ref, g2_ref, g3_ref, w_ref, rem_ref, wt_ref,
    halo_ref, chosen_ref,
):
    frames, cells, channels = spatial_ref.shape
    for n in range(chosen_ref.shape[0]):
        pick = scalar(picks_ref, n)
        halo = halo_hidden(
            pick == frames - 1, before_ref, after_ref, above_ref, below_ref,
            g1_ref, g2_ref, w_ref, rem_ref, width, channels,
        )
        halo_ref[n] = halo
        earlier = jnp.where(pick == 0, halo, hidden_ref[jnp.maximum(pick - 1, 0)])
        later = jnp.where(pick == frames - 1, halo, hidden_ref[jnp.minimum(pick + 1, frames - 1)])
        total = spatial_ref[pick].astype(F32) + dot(hidden_ref[pick], wt_ref[1])
        total = total + dot(earlier, wt_ref[0]) + dot(later, wt_ref[2])
        pack_into(chosen_ref.at[n], norm(total.astype(BF), g3_ref).astype(BF))


def temporal_kernel(
    width, picks_ref, before_ref, after_ref, above_ref, below_ref, halo_ref, spatial_ref, hidden_ref,
    g1_ref, g2_ref, g3_ref, w_ref, rem_ref, wt_ref, wq_ref, wkv_ref,
    temporal_ref, query_ref, keyval_ref,
):
    frames, cells, channels = spatial_ref.shape
    size = frames * cells
    at_end = scalar(picks_ref, 0) == frames - 1
    other = halo_hidden(
        jnp.logical_not(at_end), before_ref, after_ref, above_ref, below_ref,
        g1_ref, g2_ref, w_ref, rem_ref, width, channels,
    )
    halo = halo_ref[0]
    before = jnp.where(at_end, other, halo)
    after = jnp.where(at_end, halo, other)
    hidden = hidden_ref[...].reshape(size, channels)
    total = spatial_ref[...].reshape(size, channels).astype(F32) + dot(hidden, wt_ref[1])
    total = total + dot(jnp.concatenate([before, hidden[: size - cells]], axis=0), wt_ref[0])
    total = total + dot(jnp.concatenate([hidden[cells:], after], axis=0), wt_ref[2])
    temporal = total.astype(BF)
    temporal_ref[...] = temporal.reshape(frames, cells, channels)
    normed = norm(temporal, g3_ref).astype(BF)
    query_ref[...] = dot(normed, wq_ref[...]).astype(BF).reshape(frames, cells, channels)
    keyval_ref[...] = dot(normed, wkv_ref[...]).astype(BF).reshape(frames, cells, 2 * channels)


def lane_map(shape, channel_dim, count, channels, value, everywhere=False):
    full = channels // LANES * LANES
    rest = channels - full
    c = lax.broadcasted_iota(jnp.int32, shape, channel_dim)
    lane = lax.broadcasted_iota(jnp.int32, shape, 1 - channel_dim)
    stride = LANES // 4
    wide = c < count * full
    source = jnp.where(wide, lax.div(c, full), lax.div(c - count * full, max(rest, 1)))
    channel = jnp.where(
        wide, lax.rem(c, full), full + lax.rem(jnp.maximum(c - count * full, 0), max(rest, 1))
    )
    head = lax.div(channel, HEAD_DIM)
    if everywhere:
        hit = lax.rem(lane, stride) == head
    else:
        hit = lane == source * stride + head
    return jnp.where(hit, value, 0.0).astype(BF)


def local_kernel(
    picks_ref, window_ref, query_ref, keyval_ref, top_ref, sum_ref, mix_ref,
):
    frames, cells, channels = query_ref.shape
    count = picks_ref.shape[1]
    full = channels // LANES * LANES
    stride = LANES // 4
    queries = [query_ref[f] for f in range(frames)]
    keyvals = [keyval_ref[f] for f in range(frames)]
    keys = [kv[:, :full] for kv in keyvals] + [
        jnp.concatenate([kv[:, full:channels] for kv in keyvals], axis=1)
    ]
    values = [kv[:, channels : channels + full].astype(F32) for kv in keyvals] + [
        jnp.concatenate([kv[:, channels + full :] for kv in keyvals], axis=1).astype(F32)
    ]
    products = []
    for q in queries:
        again = jnp.concatenate([q[:, full:]] * frames, axis=1)
        row = [q[:, :full] * k for k in keys[:frames]] + [again * keys[frames]]
        products.append(jnp.concatenate(row, axis=1))
    to_lanes = lane_map(
        (frames * channels, LANES), 0, frames, channels, 1.0 / math.sqrt(HEAD_DIM)
    )
    to_channels = lane_map((LANES, frames * channels), 1, frames, channels, 1.0)
    scores = dot(jnp.concatenate(products, axis=0), to_lanes)
    source = lax.div(lax.broadcasted_iota(jnp.int32, (1, LANES), 1), stride)
    window = window_ref[...].reshape(1, 1)
    copies = jnp.zeros((1, LANES), F32)
    for n in range(count):
        copies = copies + jnp.where(source == picks_ref[:, n : n + 1], 1.0, 0.0)
    weights = []
    for i in range(frames):
        times = copies + jnp.where(jnp.abs(source - i) < window, 1.0, 0.0)
        s = jnp.where(times > 0.0, scores[i * cells : (i + 1) * cells], -jnp.inf)
        top = jnp.maximum(s, pltpu.roll(s, stride, 1))
        top = jnp.maximum(top, pltpu.roll(top, 2 * stride, 1))
        w = jnp.exp(s - top) * times
        total = w + pltpu.roll(w, stride, 1)
        total = total + pltpu.roll(total, 2 * stride, 1)
        top_ref[i] = top
        sum_ref[i] = total
        weights.append(w.astype(BF))
    spread = dot(jnp.concatenate(weights, axis=0), to_channels)
    for i in range(frames):
        part = spread[i * cells : (i + 1) * cells]
        wide = part[:, :full] * values[0]
        for j in range(1, frames):
            wide = wide + part[:, j * full : (j + 1) * full] * values[j]
        tail = part[:, frames * full :] * values[frames]
        tail = tail[:, :LANES] + tail[:, LANES:]
        tail = tail + pltpu.roll(tail, LANES // 2, 1)
        mix_ref[i] = jnp.concatenate([wide, tail], axis=1)


def updated(anchor_ref, wkv_ref, query_ref, top_ref, sum_ref, mix_ref, last):
    frames, cells, channels = query_ref.shape
    full = channels // LANES * LANES
    count = anchor_ref.shape[0]
    state = (top_ref[...], sum_ref[...], mix_ref[...])
    size = frames * cells
    top, total, mix = (v.reshape(size, v.shape[-1]) for v in state)
    query = query_ref[...].reshape(size, channels)
    to_lanes = lane_map(
        (channels, LANES), 0, 1, channels, 1.0 / math.sqrt(HEAD_DIM), everywhere=True
    )
    to_channels = lane_map((LANES, 2 * channels), 1, 2, channels, 1.0)
    low = lax.broadcasted_iota(jnp.int32, (1, LANES), 1) < LANES // 4
    for n in range(count):
        keyval = dot(unpacked(anchor_ref[n], channels), wkv_ref[...]).astype(BF)
        key = jnp.concatenate([keyval[:, :channels]] * frames, axis=0)
        scores = dot(query * key, to_lanes)
        higher = jnp.maximum(top, scores)
        weight = jnp.exp(scores - higher)
        fade = jnp.exp(top - higher)
        total = total * fade + weight
        both = jnp.where(low, weight, fade)
        if last and n == count - 1:
            both = both / total
        spread = dot(both.astype(BF), to_channels)
        value = keyval[:, channels:].astype(F32)
        value = jnp.concatenate([value] * frames, axis=0)
        wide = spread[:, :full] * value[:, :full] + spread[:, full : 2 * full] * mix[:, :full]
        tail = jnp.concatenate([value[:, full:], mix[:, full + LANES // 2 :]], axis=1)
        tail = spread[:, 2 * full :] * tail
        tail = tail + pltpu.roll(tail, LANES // 2, 1)
        mix = jnp.concatenate([wide, tail], axis=1)
        top = higher
    return top, total, mix


def anchor_kernel(
    anchor_ref, wkv_ref, query_ref, top_ref, sum_ref, mix_ref, top_out, sum_out, mix_out
):
    new = updated(anchor_ref, wkv_ref, query_ref, top_ref, sum_ref, mix_ref, False)
    for ref, v in zip((top_out, sum_out, mix_out), new):
        ref[...] = v.reshape(ref.shape)


def last_kernel(
    anchor_ref, wkv_ref, query_ref, top_ref, sum_ref, mix_ref, temporal_ref, wo_ref,
    out_ref, out_buf, sems,
):
    frames, cells, channels = query_ref.shape
    height, width = out_ref.shape[1:3]
    _, _, mix = updated(anchor_ref, wkv_ref, query_ref, top_ref, sum_ref, mix_ref, True)
    attended = mix[:, :channels].astype(BF)
    result = dot(attended, wo_ref[...])
    copies = []
    for i in range(frames):
        total = temporal_ref[i].astype(F32) + result[i * cells : (i + 1) * cells]
        out_buf[i] = total.astype(BF).reshape(height, width, channels)
        copies.append(pltpu.make_async_copy(out_buf.at[i], out_ref.at[i], sems.at[i]))
        copies[i].start()
    for copy in copies:
        copy.wait()


def neighbours(leading, last, axis):
    count = lax.axis_size(axis)
    up = [(i, i + 1) for i in range(count - 1)]
    down = [(j, i) for i, j in up]
    return lax.ppermute(last, axis, up), lax.ppermute(leading, axis, down)


def on_device(
    latents, anchor_index, window, gain_one, spatial_w, gain_two, temporal_w, gain_three,
    w_query, w_keyval, w_out,
):
    frames, height, width, channels = latents.shape
    cells = height * width
    count = anchor_index.shape[1]
    ws = spatial_w.reshape(3, 3 * channels, channels)
    one = 2 * channels * channels
    packed = cells * channels // LANES
    edge_packed = frames * width * channels // LANES
    rim_packed = 2 * width * channels // LANES
    lanes_up = (channels + LANES - 1) // LANES * LANES
    sem = pltpu.SemaphoreType.DMA
    some = (frames, cells, channels)

    x, g1, g2, g3, w = latents, gain_one, gain_two, gain_three, ws

    first, last, top, bottom = call(
        edge_kernel,
        [((packed, LANES), BF)] * 2 + [((edge_packed, LANES), BF)] * 2,
        [VMEM],
        flops=8 * frames * cells * one,
    )(x)
    before, after = neighbours(first, last, "clip")
    above, below = neighbours(top, bottom, "strip")
    w_rem, col = call(
        prepare_kernel,
        [
            ((3 * channels, 3 * (channels % 256)), BF),
            ((frames, cells, 3 * channels), BF),
        ],
        [VMEM] * 3,
        flops=4 * frames * cells * one,
    )(x, g1, w)
    early = frames // 2
    spatial, hidden, add, order = call(
        spatial_kernel,
        [
            ((early, cells, channels), BF),
            ((early, cells, channels), BF),
            ((2, frames, width, channels), F32),
            ((8, cells), F32),
        ],
        [VMEM] * 8,
        flops=9 * early * cells * one,
    )(x, col, above, below, g1, g2, w, w_rem)
    top, bottom = call(
        functools.partial(rim_kernel, width), [((rim_packed, LANES), BF)] * 2, [VMEM] * 3
    )(before, after, order)
    above, below = neighbours(top, bottom, "strip")
    spatial, hidden = call(
        more_spatial_kernel,
        [(some, BF), (some, BF)],
        [VMEM] * 8,
        flops=9 * (frames - early) * cells * one,
    )(x, col, add, spatial, hidden, g2, w, w_rem)
    halo, chosen = call(
        functools.partial(chosen_kernel, width),
        [((count, cells, channels), BF), ((count, packed, LANES), BF)],
        [VMEM] * 13,
        flops=12 * cells * one,
    )(
        anchor_index, before, after, above, below, spatial, hidden, g1, g2, g3, w, w_rem,
        temporal_w,
    )
    clips = lax.axis_size("clip")
    arrived = [
        lax.ppermute(chosen, "clip", [(i, (i + s) % clips) for i in range(clips)])
        for s in range(1, clips)
    ]
    temporal, query, keyval = call(
        functools.partial(temporal_kernel, width),
        [(some, BF), (some, BF), ((frames, cells, 2 * channels), BF)],
        [VMEM] * 16,
        flops=(9 + 6 * frames) * cells * one,
        limit=32,
    )(
        anchor_index, before, after, above, below, halo, spatial, hidden, g1, g2, g3, w, w_rem,
        temporal_w, w_query, w_keyval,
    )
    states = [((frames, cells, LANES), F32)] * 2 + [((frames, cells, lanes_up), F32)]
    state = call(
        local_kernel, states, [VMEM] * 4, flops=10 * frames * cells * one, limit=32
    )(anchor_index, window, query, keyval)
    for arrival in arrived[:-1]:
        state = call(
            anchor_kernel, states, [VMEM] * 6, flops=4 * frames * cells * one, limit=32
        )(arrival, w_keyval, query, *state)
    (out,) = call(
        last_kernel,
        [(latents.shape, BF)],
        [VMEM] * 8,
        [pltpu.VMEM(latents.shape, BF), sem((frames,))],
        flops=5 * frames * cells * one,
        limit=32,
        out_specs=(HBM,),
    )(arrived[-1], w_keyval, query, *state, temporal, w_out)
    return out


def solution(mesh):
    return jax.shard_map(
        on_device,
        mesh=mesh,
        in_specs=(
            P(("groups", "clip"), "strip", None, None),
            P(("groups", "clip"), None),
            P(),
            P(),
            P(),
            P(),
            P(),
            P(),
            P(),
            P(),
            P(),
        ),
        out_specs=P(("groups", "clip"), "strip", None, None),
        check_vma=False,
    )
```

```python
import functools
import math

import jax
import jax.numpy as jnp
from jax import lax
from jax.experimental import pallas as pl
from jax.experimental.pallas import tpu as pltpu
from jax.sharding import PartitionSpec as P

HEADS = 5
HEAD_DIM = 64
LANES = 128
BF = jnp.bfloat16
F32 = jnp.float32
VMEM = pl.BlockSpec(memory_space=pltpu.VMEM)
HBM = pl.BlockSpec(memory_space=pltpu.HBM)
MIB = 1 << 20


def call(body, outs, specs, scratch=(), flops=0, limit=24, out_specs=None):
    return pl.pallas_call(
        body,
        out_shape=tuple(jax.ShapeDtypeStruct(s, d) for s, d in outs),
        in_specs=specs,
        out_specs=out_specs or tuple(VMEM for _ in outs),
        scratch_shapes=list(scratch),
        cost_estimate=pl.CostEstimate(flops=flops, bytes_accessed=2 * MIB, transcendentals=0),
        compiler_params=pltpu.CompilerParams(vmem_limit_bytes=limit * MIB),
    )


def dot(a, b):
    return jnp.dot(a, b, preferred_element_type=F32)


def norm(v, gain_ref):
    wide = v.astype(F32)
    centred = wide - jnp.mean(wide, axis=-1, keepdims=True)
    variance = jnp.mean(centred * centred, axis=-1, keepdims=True)
    return centred * lax.rsqrt(variance + 1e-05) * gain_ref[...].reshape(1, v.shape[1])


def silu(u):
    half = 0.5 * u
    return half + half * jnp.tanh(half)


def pack_into(ref, h):
    cells, channels = h.shape
    full = channels // LANES
    for t in range(full):
        ref[t * cells : (t + 1) * cells, :] = h[:, t * LANES : (t + 1) * LANES]
    rest = channels - full * LANES
    if rest:
        share = LANES // rest
        part = cells // share
        ref[full * cells :, :] = jnp.concatenate(
            [h[s * part : (s + 1) * part, full * LANES :] for s in range(share)], axis=1
        )


def unpacked(p, channels):
    cells = p.shape[0] * LANES // channels
    full = channels // LANES
    pieces = [p[t * cells : (t + 1) * cells, :] for t in range(full)]
    rest = channels - full * LANES
    if rest:
        share = LANES // rest
        tail = p[full * cells :, :]
        pieces.append(
            jnp.concatenate([tail[:, s * rest : (s + 1) * rest] for s in range(share)], axis=0)
        )
    return jnp.concatenate(pieces, axis=1)


def columns(h, width):
    cells = h.shape[0]
    place = lax.rem(lax.broadcasted_iota(jnp.int32, h.shape, 0), width)
    left = jnp.where(place == 0, 0.0, pltpu.roll(h, 1, 0))
    right = jnp.where(place == width - 1, 0.0, pltpu.roll(h, cells - 1, 0))
    return jnp.concatenate([left.astype(BF), h.astype(BF), right.astype(BF)], axis=1)


def scalar(ref, n):
    values = ref[...].astype(F32)
    place = lax.broadcasted_iota(jnp.int32, values.shape, 1)
    return jnp.sum(jnp.where(place == n, values, 0.0)).astype(jnp.int32)


def edge_kernel(x_ref, top_ref, bottom_ref):
    frames, height, width, channels = x_ref.shape
    pack_into(top_ref, x_ref[:, 0].reshape(frames * width, channels))
    pack_into(bottom_ref, x_ref[:, height - 1].reshape(frames * width, channels))


def rests_into(rem_ref, w_ref):
    full = w_ref.shape[2] // 256 * 256
    rest = w_ref.shape[2] - full
    for a in range(3):
        rem_ref[:, a * rest : (a + 1) * rest] = w_ref[a, :, full:]


def frame_rows(f, x_ref, col_ref, g1_ref, w_ref, rem_ref):
    _, height, width, channels = x_ref.shape
    cells = height * width
    full = channels // 256 * 256
    rest = channels - full
    col_ref[...] = columns(silu(norm(x_ref[f].reshape(cells, channels), g1_ref)), width)
    centre = dot(col_ref[...], w_ref[1, :, :full])
    above = dot(col_ref[: cells - width], w_ref[0, :, :full])
    below = dot(col_ref[width:], w_ref[2, :, :full])
    tails = dot(col_ref[...], rem_ref[...])
    rows = []
    for row in range(height):
        lo, hi = row * width, (row + 1) * width
        wide = centre[lo:hi]
        tail = tails[lo:hi, rest : 2 * rest]
        if row > 0:
            wide = wide + above[lo - width : lo]
            tail = tail + tails[lo - width : lo, :rest]
        if row < height - 1:
            wide = wide + below[lo:hi]
            tail = tail + tails[hi : hi + width, 2 * rest : 3 * rest]
        rows.append(x_ref[f, row].astype(F32) + jnp.concatenate([wide, tail], axis=1))
    return rows


def rim_terms(refs, frames, width, channels, g1_ref, w_ref):
    terms = []
    for ref, a in zip(refs, (0, 2)):
        rows = unpacked(ref[...], channels)
        rows = jnp.concatenate([rows[f * width : (f + 1) * width] for f in frames], axis=0)
        terms.append(dot(columns(silu(norm(rows, g1_ref)), width), w_ref[a]))
    return terms


def outer_kernel(x_ref, g1_ref, g2_ref, w_ref, mid_ref, mid2_ref, edge_ref, rem_ref, order_ref, col_ref):
    frames, height, width, channels = x_ref.shape
    order_ref[...] = jnp.zeros_like(order_ref)
    rests_into(rem_ref, w_ref)

    def frame(s, _):
        rows = frame_rows(s * (frames - 1), x_ref, col_ref, g1_ref, w_ref, rem_ref)
        edge_ref[s, 0] = rows[0]
        edge_ref[s, 1] = rows[-1]
        for row, total in enumerate(rows[1:-1]):
            rounded = total.astype(BF)
            mid_ref[s, row * width : (row + 1) * width] = rounded
            hidden = silu(norm(rounded, g2_ref)).astype(BF)
            mid2_ref[s, row * width : (row + 1) * width] = hidden
        return 0

    lax.fori_loop(0, 2, frame, 0)


def outer_edge_kernel(
    frames, edge_ref, above_ref, below_ref, order_ref, mid_ref, mid2_ref, g1_ref, g2_ref, w_ref,
    spatial_ref, hidden_ref, first_ref, last_ref,
):
    _, cells, channels = spatial_ref.shape
    width = edge_ref.shape[2]
    spatial_ref[:, width : cells - width] = mid_ref[...]
    hidden_ref[:, width : cells - width] = mid2_ref[...]
    terms = rim_terms((above_ref, below_ref), (0, frames - 1), width, channels, g1_ref, w_ref)
    for side, lo in ((0, 0), (1, cells - width)):
        rounded = (edge_ref[:, side].reshape(2 * width, channels) + terms[side]).astype(BF)
        hidden = silu(norm(rounded, g2_ref)).astype(BF)
        spatial_ref[:, lo : lo + width] = rounded.reshape(2, width, channels)
        hidden_ref[:, lo : lo + width] = hidden.reshape(2, width, channels)
    pack_into(first_ref, hidden_ref[0])
    pack_into(last_ref, hidden_ref[1])


def inner_kernel(
    x_ref, above_ref, below_ref, g1_ref, g2_ref, w_ref, rem_ref, outer_spatial_ref, outer_hidden_ref,
    spatial_ref, hidden_ref, col_ref, add_ref,
):
    frames, height, width, channels = x_ref.shape
    for s, f in ((0, 0), (1, frames - 1)):
        spatial_ref[f] = outer_spatial_ref[s]
        hidden_ref[f] = outer_hidden_ref[s]
    inside = range(1, frames - 1)
    terms = rim_terms((above_ref, below_ref), inside, width, channels, g1_ref, w_ref)
    for side in range(2):
        add_ref[side, 1 : frames - 1] = terms[side].reshape(frames - 2, width, channels)

    def frame(f, _):
        rows = frame_rows(f, x_ref, col_ref, g1_ref, w_ref, rem_ref)
        rows[0] = rows[0] + add_ref[0, f]
        rows[-1] = rows[-1] + add_ref[1, f]
        for row, total in enumerate(rows):
            rounded = total.astype(BF)
            spatial_ref[f, row * width : (row + 1) * width] = rounded
            hidden = silu(norm(rounded, g2_ref)).astype(BF)
            hidden_ref[f, row * width : (row + 1) * width] = hidden
        return 0

    lax.fori_loop(1, frames - 1, frame, 0)


def chosen_kernel(
    picks_ref, before_ref, after_ref, spatial_ref, hidden_ref, g3_ref, wt_ref, chosen_ref
):
    frames, cells, channels = spatial_ref.shape
    before = unpacked(before_ref[...], channels)
    after = unpacked(after_ref[...], channels)
    for n in range(chosen_ref.shape[0]):
        pick = scalar(picks_ref, n)
        earlier = jnp.where(pick == 0, before, hidden_ref[jnp.maximum(pick - 1, 0)])
        later = jnp.where(pick == frames - 1, after, hidden_ref[jnp.minimum(pick + 1, frames - 1)])
        total = spatial_ref[pick].astype(F32) + dot(hidden_ref[pick], wt_ref[1])
        total = total + dot(earlier, wt_ref[0]) + dot(later, wt_ref[2])
        pack_into(chosen_ref.at[n], norm(total.astype(BF), g3_ref).astype(BF))


def temporal_kernel(
    before_ref, after_ref, spatial_ref, hidden_ref, g3_ref, wt_ref, wq_ref, wkv_ref,
    temporal_ref, query_ref, keyval_ref,
):
    frames, cells, channels = spatial_ref.shape
    size = frames * cells
    before = unpacked(before_ref[...], channels)
    after = unpacked(after_ref[...], channels)
    hidden = hidden_ref[...].reshape(size, channels)
    total = spatial_ref[...].reshape(size, channels).astype(F32) + dot(hidden, wt_ref[1])
    total = total + dot(jnp.concatenate([before, hidden[: size - cells]], axis=0), wt_ref[0])
    total = total + dot(jnp.concatenate([hidden[cells:], after], axis=0), wt_ref[2])
    temporal = total.astype(BF)
    temporal_ref[...] = temporal.reshape(frames, cells, channels)
    normed = norm(temporal, g3_ref).astype(BF)
    query_ref[...] = dot(normed, wq_ref[...]).astype(BF).reshape(frames, cells, channels)
    keyval_ref[...] = dot(normed, wkv_ref[...]).astype(BF).reshape(frames, cells, 2 * channels)


def lane_map(shape, channel_dim, count, channels, value, everywhere=False):
    full = channels // LANES * LANES
    rest = channels - full
    c = lax.broadcasted_iota(jnp.int32, shape, channel_dim)
    lane = lax.broadcasted_iota(jnp.int32, shape, 1 - channel_dim)
    stride = LANES // 4
    wide = c < count * full
    source = jnp.where(wide, lax.div(c, full), lax.div(c - count * full, max(rest, 1)))
    channel = jnp.where(
        wide, lax.rem(c, full), full + lax.rem(jnp.maximum(c - count * full, 0), max(rest, 1))
    )
    head = lax.div(channel, HEAD_DIM)
    if everywhere:
        hit = lax.rem(lane, stride) == head
    else:
        hit = lane == source * stride + head
    return jnp.where(hit, value, 0.0).astype(BF)


def local_kernel(
    picks_ref, window_ref, query_ref, keyval_ref, top_ref, sum_ref, mix_ref,
):
    frames, cells, channels = query_ref.shape
    count = picks_ref.shape[1]
    full = channels // LANES * LANES
    stride = LANES // 4
    queries = [query_ref[f] for f in range(frames)]
    keyvals = [keyval_ref[f] for f in range(frames)]
    keys = [kv[:, :full] for kv in keyvals] + [
        jnp.concatenate([kv[:, full:channels] for kv in keyvals], axis=1)
    ]
    values = [kv[:, channels : channels + full].astype(F32) for kv in keyvals] + [
        jnp.concatenate([kv[:, channels + full :] for kv in keyvals], axis=1).astype(F32)
    ]
    products = []
    for q in queries:
        again = jnp.concatenate([q[:, full:]] * frames, axis=1)
        row = [q[:, :full] * k for k in keys[:frames]] + [again * keys[frames]]
        products.append(jnp.concatenate(row, axis=1))
    to_lanes = lane_map(
        (frames * channels, LANES), 0, frames, channels, 1.0 / math.sqrt(HEAD_DIM)
    )
    to_channels = lane_map((LANES, frames * channels), 1, frames, channels, 1.0)
    scores = dot(jnp.concatenate(products, axis=0), to_lanes)
    source = lax.div(lax.broadcasted_iota(jnp.int32, (1, LANES), 1), stride)
    window = window_ref[...].reshape(1, 1)
    copies = jnp.zeros((1, LANES), F32)
    for n in range(count):
        copies = copies + jnp.where(source == picks_ref[:, n : n + 1], 1.0, 0.0)
    weights = []
    for i in range(frames):
        times = copies + jnp.where(jnp.abs(source - i) < window, 1.0, 0.0)
        s = jnp.where(times > 0.0, scores[i * cells : (i + 1) * cells], -jnp.inf)
        top = jnp.maximum(s, pltpu.roll(s, stride, 1))
        top = jnp.maximum(top, pltpu.roll(top, 2 * stride, 1))
        w = jnp.exp(s - top) * times
        total = w + pltpu.roll(w, stride, 1)
        total = total + pltpu.roll(total, 2 * stride, 1)
        top_ref[i] = top
        sum_ref[i] = total
        weights.append(w.astype(BF))
    spread = dot(jnp.concatenate(weights, axis=0), to_channels)
    for i in range(frames):
        part = spread[i * cells : (i + 1) * cells]
        wide = part[:, :full] * values[0]
        for j in range(1, frames):
            wide = wide + part[:, j * full : (j + 1) * full] * values[j]
        tail = part[:, frames * full :] * values[frames]
        tail = tail[:, :LANES] + tail[:, LANES:]
        tail = tail + pltpu.roll(tail, LANES // 2, 1)
        mix_ref[i] = jnp.concatenate([wide, tail], axis=1)


def updated(anchor_ref, wkv_ref, query_ref, top_ref, sum_ref, mix_ref, last):
    frames, cells, channels = query_ref.shape
    full = channels // LANES * LANES
    count = anchor_ref.shape[0]
    state = (top_ref[...], sum_ref[...], mix_ref[...])
    size = frames * cells
    top, total, mix = (v.reshape(size, v.shape[-1]) for v in state)
    query = query_ref[...].reshape(size, channels)
    to_lanes = lane_map(
        (channels, LANES), 0, 1, channels, 1.0 / math.sqrt(HEAD_DIM), everywhere=True
    )
    to_channels = lane_map((LANES, 2 * channels), 1, 2, channels, 1.0)
    low = lax.broadcasted_iota(jnp.int32, (1, LANES), 1) < LANES // 4
    for n in range(count):
        keyval = dot(unpacked(anchor_ref[n], channels), wkv_ref[...]).astype(BF)
        key = jnp.concatenate([keyval[:, :channels]] * frames, axis=0)
        scores = dot(query * key, to_lanes)
        higher = jnp.maximum(top, scores)
        weight = jnp.exp(scores - higher)
        fade = jnp.exp(top - higher)
        total = total * fade + weight
        both = jnp.where(low, weight, fade)
        if last and n == count - 1:
            both = both / total
        spread = dot(both.astype(BF), to_channels)
        value = keyval[:, channels:].astype(F32)
        value = jnp.concatenate([value] * frames, axis=0)
        wide = spread[:, :full] * value[:, :full] + spread[:, full : 2 * full] * mix[:, :full]
        tail = jnp.concatenate([value[:, full:], mix[:, full + LANES // 2 :]], axis=1)
        tail = spread[:, 2 * full :] * tail
        tail = tail + pltpu.roll(tail, LANES // 2, 1)
        mix = jnp.concatenate([wide, tail], axis=1)
        top = higher
    return top, total, mix


def anchor_kernel(
    anchor_ref, wkv_ref, query_ref, top_ref, sum_ref, mix_ref, top_out, sum_out, mix_out
):
    new = updated(anchor_ref, wkv_ref, query_ref, top_ref, sum_ref, mix_ref, False)
    for ref, v in zip((top_out, sum_out, mix_out), new):
        ref[...] = v.reshape(ref.shape)


def last_kernel(
    anchor_ref, wkv_ref, query_ref, top_ref, sum_ref, mix_ref, temporal_ref, wo_ref,
    out_ref, out_buf, sems,
):
    frames, cells, channels = query_ref.shape
    height, width = out_ref.shape[1:3]
    _, _, mix = updated(anchor_ref, wkv_ref, query_ref, top_ref, sum_ref, mix_ref, True)
    attended = mix[:, :channels].astype(BF)
    result = dot(attended, wo_ref[...])
    copies = []
    for i in range(frames):
        total = temporal_ref[i].astype(F32) + result[i * cells : (i + 1) * cells]
        out_buf[i] = total.astype(BF).reshape(height, width, channels)
        copies.append(pltpu.make_async_copy(out_buf.at[i], out_ref.at[i], sems.at[i]))
        copies[i].start()
    for copy in copies:
        copy.wait()


def neighbours(leading, last, axis):
    count = lax.axis_size(axis)
    up = [(i, i + 1) for i in range(count - 1)]
    down = [(j, i) for i, j in up]
    return lax.ppermute(last, axis, up), lax.ppermute(leading, axis, down)


def on_device(
    latents, anchor_index, window, gain_one, spatial_w, gain_two, temporal_w, gain_three,
    w_query, w_keyval, w_out,
):
    frames, height, width, channels = latents.shape
    cells = height * width
    count = anchor_index.shape[1]
    ws = spatial_w.reshape(3, 3 * channels, channels)
    one = 2 * channels * channels
    packed = cells * channels // LANES
    edge_packed = frames * width * channels // LANES
    lanes_up = (channels + LANES - 1) // LANES * LANES
    sem = pltpu.SemaphoreType.DMA
    some = (frames, cells, channels)

    x, g1, g2, g3, w = latents, gain_one, gain_two, gain_three, ws

    top, bottom = call(
        edge_kernel, [((edge_packed, LANES), BF)] * 2, [VMEM], flops=8 * frames * cells * one
    )(x)
    above, below = neighbours(top, bottom, "strip")
    col = pltpu.VMEM((cells, 3 * channels), BF)
    middle = (2, cells - 2 * width, channels)
    mid, mid2, edge, w_rem, order = call(
        outer_kernel,
        [
            (middle, BF),
            (middle, BF),
            ((2, 2, width, channels), F32),
            ((3 * channels, 3 * (channels % 256)), BF),
            ((8, LANES), F32),
        ],
        [VMEM] * 4,
        [col],
        flops=9 * 2 * cells * one,
    )(x, g1, g2, w)
    outer_spatial, outer_hidden, first, last = call(
        functools.partial(outer_edge_kernel, frames),
        [((2, cells, channels), BF)] * 2 + [((packed, LANES), BF)] * 2,
        [VMEM] * 9,
        flops=6 * 2 * width * one,
    )(edge, above, below, order, mid, mid2, g1, g2, w)
    before, after = neighbours(first, last, "clip")
    spatial, hidden = call(
        inner_kernel,
        [(some, BF), (some, BF)],
        [VMEM] * 9,
        [col, pltpu.VMEM((2, frames, width, channels), F32)],
        flops=9 * (frames - 2) * cells * one,
    )(x, above, below, g1, g2, w, w_rem, outer_spatial, outer_hidden)
    (chosen,) = call(
        chosen_kernel, [((count, packed, LANES), BF)], [VMEM] * 7, flops=3 * cells * one
    )(anchor_index, before, after, spatial, hidden, g3, temporal_w)
    clips = lax.axis_size("clip")
    arrived = [
        lax.ppermute(chosen, "clip", [(i, (i + s) % clips) for i in range(clips)])
        for s in range(1, clips)
    ]
    temporal, query, keyval = call(
        temporal_kernel,
        [(some, BF), (some, BF), ((frames, cells, 2 * channels), BF)],
        [VMEM] * 8,
        flops=6 * frames * cells * one,
        limit=32,
    )(before, after, spatial, hidden, g3, temporal_w, w_query, w_keyval)
    states = [((frames, cells, LANES), F32)] * 2 + [((frames, cells, lanes_up), F32)]
    state = call(
        local_kernel, states, [VMEM] * 4, flops=10 * frames * cells * one, limit=32
    )(anchor_index, window, query, keyval)
    for arrival in arrived[:-1]:
        state = call(
            anchor_kernel, states, [VMEM] * 6, flops=4 * frames * cells * one, limit=32
        )(arrival, w_keyval, query, *state)
    (out,) = call(
        last_kernel,
        [(latents.shape, BF)],
        [VMEM] * 8,
        [pltpu.VMEM(latents.shape, BF), sem((frames,))],
        flops=5 * frames * cells * one,
        limit=32,
        out_specs=(HBM,),
    )(arrived[-1], w_keyval, query, *state, temporal, w_out)
    return out


def solution(mesh):
    return jax.shard_map(
        on_device,
        mesh=mesh,
        in_specs=(
            P(("groups", "clip"), "strip", None, None),
            P(("groups", "clip"), None),
            P(),
            P(),
            P(),
            P(),
            P(),
            P(),
            P(),
            P(),
            P(),
        ),
        out_specs=P(("groups", "clip"), "strip", None, None),
        check_vma=False,
    )
```

```python
import functools
import math

import jax
import jax.numpy as jnp
from jax import lax
from jax.experimental import pallas as pl
from jax.experimental.pallas import tpu as pltpu
from jax.sharding import PartitionSpec as P

HEADS = 5
HEAD_DIM = 64
LANES = 128
BF = jnp.bfloat16
F32 = jnp.float32
VMEM = pl.BlockSpec(memory_space=pltpu.VMEM)
HBM = pl.BlockSpec(memory_space=pltpu.HBM)
MIB = 1 << 20


def call(body, outs, specs, scratch=(), flops=0, limit=24, out_specs=None):
    return pl.pallas_call(
        body,
        out_shape=tuple(jax.ShapeDtypeStruct(s, d) for s, d in outs),
        in_specs=specs,
        out_specs=out_specs or tuple(VMEM for _ in outs),
        scratch_shapes=list(scratch),
        cost_estimate=pl.CostEstimate(flops=flops, bytes_accessed=2 * MIB, transcendentals=0),
        compiler_params=pltpu.CompilerParams(vmem_limit_bytes=limit * MIB),
    )


def dot(a, b):
    return jnp.dot(a, b, preferred_element_type=F32)


def norm(v, gain_ref):
    wide = v.astype(F32)
    centred = wide - jnp.mean(wide, axis=-1, keepdims=True)
    variance = jnp.mean(centred * centred, axis=-1, keepdims=True)
    return centred * lax.rsqrt(variance + 1e-05) * gain_ref[...].reshape(1, v.shape[1])


def silu(u):
    half = 0.5 * u
    return half + half * jnp.tanh(half)


def pack_into(ref, h):
    cells, channels = h.shape
    full = channels // LANES
    for t in range(full):
        ref[t * cells : (t + 1) * cells, :] = h[:, t * LANES : (t + 1) * LANES]
    rest = channels - full * LANES
    if rest:
        share = LANES // rest
        part = cells // share
        ref[full * cells :, :] = jnp.concatenate(
            [h[s * part : (s + 1) * part, full * LANES :] for s in range(share)], axis=1
        )


def unpacked(p, channels):
    cells = p.shape[0] * LANES // channels
    full = channels // LANES
    pieces = [p[t * cells : (t + 1) * cells, :] for t in range(full)]
    rest = channels - full * LANES
    if rest:
        share = LANES // rest
        tail = p[full * cells :, :]
        pieces.append(
            jnp.concatenate([tail[:, s * rest : (s + 1) * rest] for s in range(share)], axis=0)
        )
    return jnp.concatenate(pieces, axis=1)


def columns(h, width):
    cells = h.shape[0]
    place = lax.rem(lax.broadcasted_iota(jnp.int32, h.shape, 0), width)
    left = jnp.where(place == 0, 0.0, pltpu.roll(h, 1, 0))
    right = jnp.where(place == width - 1, 0.0, pltpu.roll(h, cells - 1, 0))
    return jnp.concatenate([left.astype(BF), h.astype(BF), right.astype(BF)], axis=1)


def scalar(ref, n):
    values = ref[...].astype(F32)
    place = lax.broadcasted_iota(jnp.int32, values.shape, 1)
    return jnp.sum(jnp.where(place == n, values, 0.0)).astype(jnp.int32)


def edge_kernel(x_ref, top_ref, bottom_ref):
    frames, height, width, channels = x_ref.shape
    pack_into(top_ref, x_ref[:, 0].reshape(frames * width, channels))
    pack_into(bottom_ref, x_ref[:, height - 1].reshape(frames * width, channels))


def rests_into(rem_ref, w_ref):
    full = w_ref.shape[2] // 256 * 256
    rest = w_ref.shape[2] - full
    for a in range(3):
        rem_ref[:, a * rest : (a + 1) * rest] = w_ref[a, :, full:]


def hidden_columns(v, g1_ref, width):
    return columns(silu(norm(v, g1_ref)), width)


def stacked_rows(col_ref, count, height, width, w_ref, rem_ref):
    cells = height * width
    rims = (col_ref.shape[0] - count * cells) // 2
    channels = w_ref.shape[2]
    full = channels // 256 * 256
    rest = channels - full
    size = count * cells
    above = dot(col_ref[: rims + size], w_ref[0, :, :full])
    centre = dot(col_ref[rims : rims + size], w_ref[1, :, :full])
    below = dot(col_ref[rims:], w_ref[2, :, :full])
    tails = dot(col_ref[...], rem_ref[...])

    def terms(place, row):
        own = place * cells + row * width
        wide = centre[own : own + width]
        tail = tails[rims + own : rims + own + width, rest : 2 * rest]
        if row > 0 or rims:
            at = rims + own - width if row > 0 else place * width
            wide = wide + above[at : at + width]
            tail = tail + tails[at : at + width, :rest]
        if row < height - 1 or rims:
            at = own + width if row < height - 1 else size + place * width
            wide = wide + below[at : at + width]
            tail = tail + tails[rims + at : rims + at + width, 2 * rest :]
        return jnp.concatenate([wide, tail], axis=1)

    return terms


def rim_rows(ref, frames, width, channels):
    rows = unpacked(ref[...], channels)
    return jnp.concatenate([rows[f * width : (f + 1) * width] for f in frames], axis=0)


def outer_kernel(x_ref, g1_ref, g2_ref, w_ref, mid_ref, mid2_ref, edge_ref, rem_ref, order_ref, col_ref):
    frames, height, width, channels = x_ref.shape
    cells = height * width
    order_ref[...] = jnp.zeros_like(order_ref)
    rests_into(rem_ref, w_ref)
    outer = (0, frames - 1)
    for s, f in enumerate(outer):
        x = x_ref[f].reshape(cells, channels)
        col_ref[s * cells : (s + 1) * cells] = hidden_columns(x, g1_ref, width)
    terms = stacked_rows(col_ref, 2, height, width, w_ref, rem_ref)
    for s, f in enumerate(outer):
        for row in range(height):
            total = x_ref[f, row].astype(F32) + terms(s, row)
            if 0 < row < height - 1:
                rounded = total.astype(BF)
                lo = (row - 1) * width
                mid_ref[s, lo : lo + width] = rounded
                mid2_ref[s, lo : lo + width] = silu(norm(rounded, g2_ref)).astype(BF)
            else:
                edge_ref[s, 0 if row == 0 else 1] = total


def outer_edge_kernel(
    frames, edge_ref, above_ref, below_ref, order_ref, mid_ref, mid2_ref, g1_ref, g2_ref, w_ref, rem_ref,
    spatial_ref, hidden_ref, first_ref, last_ref,
):
    _, cells, channels = spatial_ref.shape
    width = edge_ref.shape[2]
    full = channels // 256 * 256
    rest = channels - full
    spatial_ref[:, width : cells - width] = mid_ref[...]
    hidden_ref[:, width : cells - width] = mid2_ref[...]
    cols = [
        hidden_columns(rim_rows(ref, (0, frames - 1), width, channels), g1_ref, width)
        for ref in (above_ref, below_ref)
    ]
    tails = dot(jnp.concatenate(cols, axis=0), rem_ref[...])
    size = 2 * width
    for side, lo in ((0, 0), (1, cells - width)):
        tail = tails[:size, :rest] if side == 0 else tails[size:, 2 * rest :]
        wide = dot(cols[side], w_ref[2 * side, :, :full])
        term = jnp.concatenate([wide, tail], axis=1)
        rounded = (edge_ref[:, side].reshape(size, channels) + term).astype(BF)
        hidden = silu(norm(rounded, g2_ref)).astype(BF)
        spatial_ref[:, lo : lo + width] = rounded.reshape(2, width, channels)
        hidden_ref[:, lo : lo + width] = hidden.reshape(2, width, channels)
    pack_into(first_ref, hidden_ref[0])
    pack_into(last_ref, hidden_ref[1])


def inner_kernel(
    x_ref, above_ref, below_ref, g1_ref, g2_ref, w_ref, rem_ref, outer_spatial_ref, outer_hidden_ref,
    spatial_ref, hidden_ref, col_ref,
):
    frames, height, width, channels = x_ref.shape
    cells = height * width
    for s, f in ((0, 0), (1, frames - 1)):
        spatial_ref[f] = outer_spatial_ref[s]
        hidden_ref[f] = outer_hidden_ref[s]
    inside = range(1, frames - 1)
    rims = len(inside) * width
    end = rims + len(inside) * cells
    col_ref[:rims] = hidden_columns(rim_rows(above_ref, inside, width, channels), g1_ref, width)
    for s, f in enumerate(inside):
        x = x_ref[f].reshape(cells, channels)
        lo = rims + s * cells
        col_ref[lo : lo + cells] = hidden_columns(x, g1_ref, width)
    col_ref[end:] = hidden_columns(rim_rows(below_ref, inside, width, channels), g1_ref, width)
    terms = stacked_rows(col_ref, len(inside), height, width, w_ref, rem_ref)
    for s, f in enumerate(inside):
        for row in range(height):
            rounded = (x_ref[f, row].astype(F32) + terms(s, row)).astype(BF)
            lo = row * width
            spatial_ref[f, lo : lo + width] = rounded
            hidden_ref[f, lo : lo + width] = silu(norm(rounded, g2_ref)).astype(BF)


def chosen_kernel(
    picks_ref, before_ref, after_ref, spatial_ref, hidden_ref, g3_ref, wt_ref, chosen_ref
):
    frames, cells, channels = spatial_ref.shape
    before = unpacked(before_ref[...], channels)
    after = unpacked(after_ref[...], channels)
    for n in range(chosen_ref.shape[0]):
        pick = scalar(picks_ref, n)
        earlier = jnp.where(pick == 0, before, hidden_ref[jnp.maximum(pick - 1, 0)])
        later = jnp.where(pick == frames - 1, after, hidden_ref[jnp.minimum(pick + 1, frames - 1)])
        total = spatial_ref[pick].astype(F32) + dot(hidden_ref[pick], wt_ref[1])
        total = total + dot(earlier, wt_ref[0]) + dot(later, wt_ref[2])
        pack_into(chosen_ref.at[n], norm(total.astype(BF), g3_ref).astype(BF))


def temporal_kernel(
    before_ref, after_ref, spatial_ref, hidden_ref, g3_ref, wt_ref, wq_ref, wkv_ref,
    temporal_ref, query_ref, keyval_ref,
):
    frames, cells, channels = spatial_ref.shape
    size = frames * cells
    before = unpacked(before_ref[...], channels)
    after = unpacked(after_ref[...], channels)
    hidden = hidden_ref[...].reshape(size, channels)
    total = spatial_ref[...].reshape(size, channels).astype(F32) + dot(hidden, wt_ref[1])
    total = total + dot(jnp.concatenate([before, hidden[: size - cells]], axis=0), wt_ref[0])
    total = total + dot(jnp.concatenate([hidden[cells:], after], axis=0), wt_ref[2])
    temporal = total.astype(BF)
    temporal_ref[...] = temporal.reshape(frames, cells, channels)
    normed = norm(temporal, g3_ref).astype(BF)
    query_ref[...] = dot(normed, wq_ref[...]).astype(BF).reshape(frames, cells, channels)
    keyval_ref[...] = dot(normed, wkv_ref[...]).astype(BF).reshape(frames, cells, 2 * channels)


def lane_map(shape, channel_dim, count, channels, value, everywhere=False):
    full = channels // LANES * LANES
    rest = channels - full
    c = lax.broadcasted_iota(jnp.int32, shape, channel_dim)
    lane = lax.broadcasted_iota(jnp.int32, shape, 1 - channel_dim)
    stride = LANES // 4
    wide = c < count * full
    source = jnp.where(wide, lax.div(c, full), lax.div(c - count * full, max(rest, 1)))
    channel = jnp.where(
        wide, lax.rem(c, full), full + lax.rem(jnp.maximum(c - count * full, 0), max(rest, 1))
    )
    head = lax.div(channel, HEAD_DIM)
    if everywhere:
        hit = lax.rem(lane, stride) == head
    else:
        hit = lane == source * stride + head
    return jnp.where(hit, value, 0.0).astype(BF)


def local_kernel(
    picks_ref, window_ref, query_ref, keyval_ref, top_ref, sum_ref, mix_ref,
):
    frames, cells, channels = query_ref.shape
    count = picks_ref.shape[1]
    full = channels // LANES * LANES
    stride = LANES // 4
    queries = [query_ref[f] for f in range(frames)]
    keyvals = [keyval_ref[f] for f in range(frames)]
    keys = [kv[:, :full] for kv in keyvals] + [
        jnp.concatenate([kv[:, full:channels] for kv in keyvals], axis=1)
    ]
    values = [kv[:, channels : channels + full].astype(F32) for kv in keyvals] + [
        jnp.concatenate([kv[:, channels + full :] for kv in keyvals], axis=1).astype(F32)
    ]
    products = []
    for q in queries:
        again = jnp.concatenate([q[:, full:]] * frames, axis=1)
        row = [q[:, :full] * k for k in keys[:frames]] + [again * keys[frames]]
        products.append(jnp.concatenate(row, axis=1))
    to_lanes = lane_map(
        (frames * channels, LANES), 0, frames, channels, 1.0 / math.sqrt(HEAD_DIM)
    )
    to_channels = lane_map((LANES, frames * channels), 1, frames, channels, 1.0)
    scores = dot(jnp.concatenate(products, axis=0), to_lanes)
    source = lax.div(lax.broadcasted_iota(jnp.int32, (1, LANES), 1), stride)
    window = window_ref[...].reshape(1, 1)
    copies = jnp.zeros((1, LANES), F32)
    for n in range(count):
        copies = copies + jnp.where(source == picks_ref[:, n : n + 1], 1.0, 0.0)
    weights = []
    for i in range(frames):
        times = copies + jnp.where(jnp.abs(source - i) < window, 1.0, 0.0)
        s = jnp.where(times > 0.0, scores[i * cells : (i + 1) * cells], -jnp.inf)
        top = jnp.maximum(s, pltpu.roll(s, stride, 1))
        top = jnp.maximum(top, pltpu.roll(top, 2 * stride, 1))
        w = jnp.exp(s - top) * times
        total = w + pltpu.roll(w, stride, 1)
        total = total + pltpu.roll(total, 2 * stride, 1)
        top_ref[i] = top
        sum_ref[i] = total
        weights.append(w.astype(BF))
    spread = dot(jnp.concatenate(weights, axis=0), to_channels)
    for i in range(frames):
        part = spread[i * cells : (i + 1) * cells]
        wide = part[:, :full] * values[0]
        for j in range(1, frames):
            wide = wide + part[:, j * full : (j + 1) * full] * values[j]
        tail = part[:, frames * full :] * values[frames]
        tail = tail[:, :LANES] + tail[:, LANES:]
        tail = tail + pltpu.roll(tail, LANES // 2, 1)
        mix_ref[i] = jnp.concatenate([wide, tail], axis=1)


def updated(anchor_ref, wkv_ref, query_ref, top_ref, sum_ref, mix_ref, last):
    frames, cells, channels = query_ref.shape
    full = channels // LANES * LANES
    count = anchor_ref.shape[0]
    state = (top_ref[...], sum_ref[...], mix_ref[...])
    size = frames * cells
    top, total, mix = (v.reshape(size, v.shape[-1]) for v in state)
    query = query_ref[...].reshape(size, channels)
    to_lanes = lane_map(
        (channels, LANES), 0, 1, channels, 1.0 / math.sqrt(HEAD_DIM), everywhere=True
    )
    to_channels = lane_map((LANES, 2 * channels), 1, 2, channels, 1.0)
    low = lax.broadcasted_iota(jnp.int32, (1, LANES), 1) < LANES // 4
    for n in range(count):
        keyval = dot(unpacked(anchor_ref[n], channels), wkv_ref[...]).astype(BF)
        key = jnp.concatenate([keyval[:, :channels]] * frames, axis=0)
        scores = dot(query * key, to_lanes)
        higher = jnp.maximum(top, scores)
        weight = jnp.exp(scores - higher)
        fade = jnp.exp(top - higher)
        total = total * fade + weight
        both = jnp.where(low, weight, fade)
        if last and n == count - 1:
            both = both / total
        spread = dot(both.astype(BF), to_channels)
        value = keyval[:, channels:].astype(F32)
        value = jnp.concatenate([value] * frames, axis=0)
        wide = spread[:, :full] * value[:, :full] + spread[:, full : 2 * full] * mix[:, :full]
        tail = jnp.concatenate([value[:, full:], mix[:, full + LANES // 2 :]], axis=1)
        tail = spread[:, 2 * full :] * tail
        tail = tail + pltpu.roll(tail, LANES // 2, 1)
        mix = jnp.concatenate([wide, tail], axis=1)
        top = higher
    return top, total, mix


def anchor_kernel(
    anchor_ref, wkv_ref, query_ref, top_ref, sum_ref, mix_ref, top_out, sum_out, mix_out
):
    new = updated(anchor_ref, wkv_ref, query_ref, top_ref, sum_ref, mix_ref, False)
    for ref, v in zip((top_out, sum_out, mix_out), new):
        ref[...] = v.reshape(ref.shape)


def last_kernel(
    anchor_ref, wkv_ref, query_ref, top_ref, sum_ref, mix_ref, temporal_ref, wo_ref,
    out_ref, out_buf, sems,
):
    frames, cells, channels = query_ref.shape
    height, width = out_ref.shape[1:3]
    _, _, mix = updated(anchor_ref, wkv_ref, query_ref, top_ref, sum_ref, mix_ref, True)
    attended = mix[:, :channels].astype(BF)
    result = dot(attended, wo_ref[...])
    copies = []
    for i in range(frames):
        total = temporal_ref[i].astype(F32) + result[i * cells : (i + 1) * cells]
        out_buf[i] = total.astype(BF).reshape(height, width, channels)
        copies.append(pltpu.make_async_copy(out_buf.at[i], out_ref.at[i], sems.at[i]))
        copies[i].start()
    for copy in copies:
        copy.wait()


def neighbours(leading, last, axis):
    count = lax.axis_size(axis)
    up = [(i, i + 1) for i in range(count - 1)]
    down = [(j, i) for i, j in up]
    return lax.ppermute(last, axis, up), lax.ppermute(leading, axis, down)


def on_device(
    latents, anchor_index, window, gain_one, spatial_w, gain_two, temporal_w, gain_three,
    w_query, w_keyval, w_out,
):
    frames, height, width, channels = latents.shape
    cells = height * width
    count = anchor_index.shape[1]
    ws = spatial_w.reshape(3, 3 * channels, channels)
    one = 2 * channels * channels
    packed = cells * channels // LANES
    edge_packed = frames * width * channels // LANES
    lanes_up = (channels + LANES - 1) // LANES * LANES
    sem = pltpu.SemaphoreType.DMA
    some = (frames, cells, channels)

    x, g1, g2, g3, w = latents, gain_one, gain_two, gain_three, ws

    top, bottom = call(
        edge_kernel, [((edge_packed, LANES), BF)] * 2, [VMEM], flops=8 * frames * cells * one
    )(x)
    above, below = neighbours(top, bottom, "strip")
    outer_col = pltpu.VMEM((2 * cells, 3 * channels), BF)
    inner_col = pltpu.VMEM(((frames - 2) * (cells + 2 * width), 3 * channels), BF)
    middle = (2, cells - 2 * width, channels)
    mid, mid2, edge, w_rem, order = call(
        outer_kernel,
        [
            (middle, BF),
            (middle, BF),
            ((2, 2, width, channels), F32),
            ((3 * channels, 3 * (channels % 256)), BF),
            ((8, LANES), F32),
        ],
        [VMEM] * 4,
        [outer_col],
        flops=9 * 2 * cells * one,
    )(x, g1, g2, w)
    outer_spatial, outer_hidden, first, last = call(
        functools.partial(outer_edge_kernel, frames),
        [((2, cells, channels), BF)] * 2 + [((packed, LANES), BF)] * 2,
        [VMEM] * 10,
        flops=6 * 2 * width * one,
    )(edge, above, below, order, mid, mid2, g1, g2, w, w_rem)
    before, after = neighbours(first, last, "clip")
    spatial, hidden = call(
        inner_kernel,
        [(some, BF), (some, BF)],
        [VMEM] * 9,
        [inner_col],
        flops=9 * (frames - 2) * cells * one,
    )(x, above, below, g1, g2, w, w_rem, outer_spatial, outer_hidden)
    (chosen,) = call(
        chosen_kernel, [((count, packed, LANES), BF)], [VMEM] * 7, flops=3 * cells * one
    )(anchor_index, before, after, spatial, hidden, g3, temporal_w)
    clips = lax.axis_size("clip")
    arrived = [
        lax.ppermute(chosen, "clip", [(i, (i + s) % clips) for i in range(clips)])
        for s in range(1, clips)
    ]
    temporal, query, keyval = call(
        temporal_kernel,
        [(some, BF), (some, BF), ((frames, cells, 2 * channels), BF)],
        [VMEM] * 8,
        flops=6 * frames * cells * one,
        limit=32,
    )(before, after, spatial, hidden, g3, temporal_w, w_query, w_keyval)
    states = [((frames, cells, LANES), F32)] * 2 + [((frames, cells, lanes_up), F32)]
    state = call(
        local_kernel, states, [VMEM] * 4, flops=10 * frames * cells * one, limit=32
    )(anchor_index, window, query, keyval)
    for arrival in arrived[:-1]:
        state = call(
            anchor_kernel, states, [VMEM] * 6, flops=4 * frames * cells * one, limit=32
        )(arrival, w_keyval, query, *state)
    (out,) = call(
        last_kernel,
        [(latents.shape, BF)],
        [VMEM] * 8,
        [pltpu.VMEM(latents.shape, BF), sem((frames,))],
        flops=5 * frames * cells * one,
        limit=32,
        out_specs=(HBM,),
    )(arrived[-1], w_keyval, query, *state, temporal, w_out)
    return out


def solution(mesh):
    return jax.shard_map(
        on_device,
        mesh=mesh,
        in_specs=(
            P(("groups", "clip"), "strip", None, None),
            P(("groups", "clip"), None),
            P(),
            P(),
            P(),
            P(),
            P(),
            P(),
            P(),
            P(),
            P(),
        ),
        out_specs=P(("groups", "clip"), "strip", None, None),
        check_vma=False,
    )
```

```python
import functools
import math

import jax
import jax.numpy as jnp
import numpy as np
from jax import lax
from jax.experimental import pallas as pl
from jax.experimental.pallas import tpu as pltpu
from jax.sharding import PartitionSpec as P

HEADS = 5
HEAD_DIM = 64
LANES = 128
BF = jnp.bfloat16
F32 = jnp.float32
VMEM = pl.BlockSpec(memory_space=pltpu.VMEM)
HBM = pl.BlockSpec(memory_space=pltpu.HBM)
MIB = 1 << 20


def call(body, outs, specs, scratch=(), flops=0, limit=24, out_specs=None):
    return pl.pallas_call(
        body,
        out_shape=tuple(jax.ShapeDtypeStruct(s, d) for s, d in outs),
        in_specs=specs,
        out_specs=out_specs or tuple(VMEM for _ in outs),
        scratch_shapes=list(scratch),
        cost_estimate=pl.CostEstimate(flops=flops, bytes_accessed=2 * MIB, transcendentals=0),
        compiler_params=pltpu.CompilerParams(vmem_limit_bytes=limit * MIB),
    )


def dot(a, b):
    return jnp.dot(a, b, preferred_element_type=F32)


def norm(v, gain_ref):
    wide = v.astype(F32)
    centred = wide - jnp.mean(wide, axis=-1, keepdims=True)
    variance = jnp.mean(centred * centred, axis=-1, keepdims=True)
    return centred * lax.rsqrt(variance + 1e-05) * gain_ref[...].reshape(1, v.shape[1])


def silu(u):
    half = 0.5 * u
    return half + half * jnp.tanh(half)


def pack_into(ref, h):
    cells, channels = h.shape
    full = channels // LANES
    for t in range(full):
        ref[t * cells : (t + 1) * cells, :] = h[:, t * LANES : (t + 1) * LANES]
    rest = channels - full * LANES
    if rest:
        share = LANES // rest
        part = cells // share
        ref[full * cells :, :] = jnp.concatenate(
            [h[s * part : (s + 1) * part, full * LANES :] for s in range(share)], axis=1
        )


def unpacked(p, channels):
    cells = p.shape[0] * LANES // channels
    full = channels // LANES
    pieces = [p[t * cells : (t + 1) * cells, :] for t in range(full)]
    rest = channels - full * LANES
    if rest:
        share = LANES // rest
        tail = p[full * cells :, :]
        pieces.append(
            jnp.concatenate([tail[:, s * rest : (s + 1) * rest] for s in range(share)], axis=0)
        )
    return jnp.concatenate(pieces, axis=1)


def columns(h, width):
    cells, channels = h.shape
    left = pltpu.roll(h, 1, 0)
    right = pltpu.roll(h, cells - 1, 0)
    place = lax.broadcasted_iota(jnp.int32, (8, channels), 0)
    lefts, rights = [], []
    for lo in range(0, cells, width):
        hi = lo + width
        lefts += [jnp.where(place == 0, 0.0, left[lo : lo + 8]), left[lo + 8 : hi]]
        rights += [right[lo : hi - 8], jnp.where(place == 7, 0.0, right[hi - 8 : hi])]
    sides = [jnp.concatenate(lefts, axis=0), h, jnp.concatenate(rights, axis=0)]
    return jnp.concatenate([v.astype(BF) for v in sides], axis=1)


def scalar(ref, n):
    values = ref[...].astype(F32)
    place = lax.broadcasted_iota(jnp.int32, values.shape, 1)
    return jnp.sum(jnp.where(place == n, values, 0.0)).astype(jnp.int32)


def edge_kernel(x_ref, top_ref, bottom_ref):
    frames, height, width, channels = x_ref.shape
    pack_into(top_ref, x_ref[:, 0].reshape(frames * width, channels))
    pack_into(bottom_ref, x_ref[:, height - 1].reshape(frames * width, channels))


def rests_into(rem_ref, w_ref):
    full = w_ref.shape[2] // 256 * 256
    rest = w_ref.shape[2] - full
    for a in range(3):
        rem_ref[:, a * rest : (a + 1) * rest] = w_ref[a, :, full:]


def hidden_columns(v, g1_ref, width):
    return columns(silu(norm(v, g1_ref)), width)


def stacked_rows(col_ref, count, height, width, w_ref, rem_ref):
    cells = height * width
    rims = (col_ref.shape[0] - count * cells) // 2
    channels = w_ref.shape[2]
    full = channels // 256 * 256
    rest = channels - full
    size = count * cells
    above = dot(col_ref[: rims + size], w_ref[0, :, :full])
    centre = dot(col_ref[rims : rims + size], w_ref[1, :, :full])
    below = dot(col_ref[rims:], w_ref[2, :, :full])
    tails = dot(col_ref[...], rem_ref[...])

    def terms(place, row):
        own = place * cells + row * width
        wide = centre[own : own + width]
        tail = tails[rims + own : rims + own + width, rest : 2 * rest]
        if row > 0 or rims:
            at = rims + own - width if row > 0 else place * width
            wide = wide + above[at : at + width]
            tail = tail + tails[at : at + width, :rest]
        if row < height - 1 or rims:
            at = own + width if row < height - 1 else size + place * width
            wide = wide + below[at : at + width]
            tail = tail + tails[rims + at : rims + at + width, 2 * rest :]
        return jnp.concatenate([wide, tail], axis=1)

    return terms


def rim_rows(ref, frames, width, channels):
    rows = unpacked(ref[...], channels)
    return jnp.concatenate([rows[f * width : (f + 1) * width] for f in frames], axis=0)


def outer_kernel(x_ref, g1_ref, g2_ref, w_ref, mid_ref, mid2_ref, edge_ref, rem_ref, order_ref, col_ref):
    frames, height, width, channels = x_ref.shape
    cells = height * width
    order_ref[...] = jnp.zeros_like(order_ref)
    rests_into(rem_ref, w_ref)
    outer = (0, frames - 1)
    for s, f in enumerate(outer):
        x = x_ref[f].reshape(cells, channels)
        col_ref[s * cells : (s + 1) * cells] = hidden_columns(x, g1_ref, width)
    terms = stacked_rows(col_ref, 2, height, width, w_ref, rem_ref)
    for s, f in enumerate(outer):
        for row in range(height):
            total = x_ref[f, row].astype(F32) + terms(s, row)
            if 0 < row < height - 1:
                rounded = total.astype(BF)
                lo = (row - 1) * width
                mid_ref[s, lo : lo + width] = rounded
                mid2_ref[s, lo : lo + width] = silu(norm(rounded, g2_ref)).astype(BF)
            else:
                edge_ref[s, 0 if row == 0 else 1] = total


def outer_edge_kernel(
    frames, edge_ref, above_ref, below_ref, order_ref, mid_ref, mid2_ref, g1_ref, g2_ref, w_ref, rem_ref,
    spatial_ref, hidden_ref, first_ref, last_ref,
):
    _, cells, channels = spatial_ref.shape
    width = edge_ref.shape[2]
    full = channels // 256 * 256
    rest = channels - full
    spatial_ref[:, width : cells - width] = mid_ref[...]
    hidden_ref[:, width : cells - width] = mid2_ref[...]
    cols = [
        hidden_columns(rim_rows(ref, (0, frames - 1), width, channels), g1_ref, width)
        for ref in (above_ref, below_ref)
    ]
    tails = dot(jnp.concatenate(cols, axis=0), rem_ref[...])
    size = 2 * width
    for side, lo in ((0, 0), (1, cells - width)):
        tail = tails[:size, :rest] if side == 0 else tails[size:, 2 * rest :]
        wide = dot(cols[side], w_ref[2 * side, :, :full])
        term = jnp.concatenate([wide, tail], axis=1)
        rounded = (edge_ref[:, side].reshape(size, channels) + term).astype(BF)
        hidden = silu(norm(rounded, g2_ref)).astype(BF)
        spatial_ref[:, lo : lo + width] = rounded.reshape(2, width, channels)
        hidden_ref[:, lo : lo + width] = hidden.reshape(2, width, channels)
    pack_into(first_ref, hidden_ref[0])
    pack_into(last_ref, hidden_ref[1])


def inner_kernel(
    x_ref, above_ref, below_ref, g1_ref, g2_ref, w_ref, rem_ref, outer_spatial_ref, outer_hidden_ref,
    spatial_ref, hidden_ref, col_ref,
):
    frames, height, width, channels = x_ref.shape
    cells = height * width
    for s, f in ((0, 0), (1, frames - 1)):
        spatial_ref[f] = outer_spatial_ref[s]
        hidden_ref[f] = outer_hidden_ref[s]
    inside = range(1, frames - 1)
    rims = len(inside) * width
    end = rims + len(inside) * cells
    col_ref[:rims] = hidden_columns(rim_rows(above_ref, inside, width, channels), g1_ref, width)
    for s, f in enumerate(inside):
        x = x_ref[f].reshape(cells, channels)
        lo = rims + s * cells
        col_ref[lo : lo + cells] = hidden_columns(x, g1_ref, width)
    col_ref[end:] = hidden_columns(rim_rows(below_ref, inside, width, channels), g1_ref, width)
    terms = stacked_rows(col_ref, len(inside), height, width, w_ref, rem_ref)
    for s, f in enumerate(inside):
        for row in range(height):
            rounded = (x_ref[f, row].astype(F32) + terms(s, row)).astype(BF)
            lo = row * width
            spatial_ref[f, lo : lo + width] = rounded
            hidden_ref[f, lo : lo + width] = silu(norm(rounded, g2_ref)).astype(BF)


def chosen_kernel(
    picks_ref, before_ref, after_ref, spatial_ref, hidden_ref, g3_ref, wt_ref, chosen_ref
):
    frames, cells, channels = spatial_ref.shape
    before = unpacked(before_ref[...], channels)
    after = unpacked(after_ref[...], channels)
    for n in range(chosen_ref.shape[0]):
        pick = scalar(picks_ref, n)
        earlier = jnp.where(pick == 0, before, hidden_ref[jnp.maximum(pick - 1, 0)])
        later = jnp.where(pick == frames - 1, after, hidden_ref[jnp.minimum(pick + 1, frames - 1)])
        total = spatial_ref[pick].astype(F32) + dot(hidden_ref[pick], wt_ref[1])
        total = total + dot(earlier, wt_ref[0]) + dot(later, wt_ref[2])
        pack_into(chosen_ref.at[n], norm(total.astype(BF), g3_ref).astype(BF))


def temporal_kernel(
    before_ref, after_ref, spatial_ref, hidden_ref, g3_ref, wt_ref, wq_ref, wkv_ref,
    temporal_ref, query_ref, keyval_ref,
):
    frames, cells, channels = spatial_ref.shape
    size = frames * cells
    before = unpacked(before_ref[...], channels)
    after = unpacked(after_ref[...], channels)
    hidden = hidden_ref[...].reshape(size, channels)
    total = spatial_ref[...].reshape(size, channels).astype(F32) + dot(hidden, wt_ref[1])
    total = total + dot(jnp.concatenate([before, hidden[: size - cells]], axis=0), wt_ref[0])
    total = total + dot(jnp.concatenate([hidden[cells:], after], axis=0), wt_ref[2])
    temporal = total.astype(BF)
    temporal_ref[...] = temporal.reshape(frames, cells, channels)
    normed = norm(temporal, g3_ref).astype(BF)
    query_ref[...] = dot(normed, wq_ref[...]).astype(BF).reshape(frames, cells, channels)
    keyval_ref[...] = dot(normed, wkv_ref[...]).astype(BF).reshape(frames, cells, 2 * channels)


def head_maps(count, channels, everywhere=False):
    full = channels // LANES * LANES
    rest = channels - full
    stride = LANES // 4
    hits = np.zeros((count * channels, LANES), np.float32)
    for j in range(count):
        for c in range(channels):
            at = j * full + c if c < full else count * full + j * rest + c - full
            lanes = range(0, LANES, stride) if everywhere else (j * stride,)
            for lane in lanes:
                hits[at, lane + c // HEAD_DIM] = 1.0
    padded = np.zeros((-(-hits.shape[0] // LANES) * LANES, LANES), np.float32)
    padded[: hits.shape[0]] = hits
    blocks = padded.reshape(-1, LANES, LANES).transpose(0, 2, 1).reshape(-1, LANES)
    return jnp.asarray(hits / math.sqrt(HEAD_DIM), BF), jnp.asarray(blocks, BF)


def beside(ref):
    count = ref.shape[0] // LANES
    return jnp.concatenate([ref[b * LANES : (b + 1) * LANES] for b in range(count)], axis=1)


def local_kernel(
    picks_ref, window_ref, query_ref, keyval_ref, to_lanes_ref, to_channels_ref,
    top_ref, sum_ref, mix_ref,
):
    frames, cells, channels = query_ref.shape
    count = picks_ref.shape[1]
    full = channels // LANES * LANES
    stride = LANES // 4
    queries = [query_ref[f] for f in range(frames)]
    keyvals = [keyval_ref[f] for f in range(frames)]
    keys = [kv[:, :full] for kv in keyvals] + [
        jnp.concatenate([kv[:, full:channels] for kv in keyvals], axis=1)
    ]
    values = [kv[:, channels : channels + full].astype(F32) for kv in keyvals] + [
        jnp.concatenate([kv[:, channels + full :] for kv in keyvals], axis=1).astype(F32)
    ]
    products = []
    for q in queries:
        again = jnp.concatenate([q[:, full:]] * frames, axis=1)
        row = [q[:, :full] * k for k in keys[:frames]] + [again * keys[frames]]
        products.append(jnp.concatenate(row, axis=1))
    scores = dot(jnp.concatenate(products, axis=0), to_lanes_ref[...])
    source = lax.div(lax.broadcasted_iota(jnp.int32, (1, LANES), 1), stride)
    window = window_ref[...].reshape(1, 1)
    copies = jnp.zeros((1, LANES), F32)
    for n in range(count):
        copies = copies + jnp.where(source == picks_ref[:, n : n + 1], 1.0, 0.0)
    weights = []
    for i in range(frames):
        times = copies + jnp.where(jnp.abs(source - i) < window, 1.0, 0.0)
        s = jnp.where(times > 0.0, scores[i * cells : (i + 1) * cells], -jnp.inf)
        top = jnp.maximum(s, pltpu.roll(s, stride, 1))
        top = jnp.maximum(top, pltpu.roll(top, 2 * stride, 1))
        w = jnp.exp(s - top) * times
        total = w + pltpu.roll(w, stride, 1)
        total = total + pltpu.roll(total, 2 * stride, 1)
        top_ref[i] = top
        sum_ref[i] = total
        weights.append(w.astype(BF))
    spread = dot(jnp.concatenate(weights, axis=0), beside(to_channels_ref))
    for i in range(frames):
        part = spread[i * cells : (i + 1) * cells]
        wide = part[:, :full] * values[0]
        for j in range(1, frames):
            wide = wide + part[:, j * full : (j + 1) * full] * values[j]
        tail = part[:, frames * full :] * values[frames]
        tail = tail[:, :LANES] + tail[:, LANES:]
        tail = tail + pltpu.roll(tail, LANES // 2, 1)
        mix_ref[i] = jnp.concatenate([wide, tail], axis=1)


def updated(
    anchor_ref, wkv_ref, to_lanes_ref, to_channels_ref, query_ref, top_ref, sum_ref, mix_ref, last
):
    frames, cells, channels = query_ref.shape
    full = channels // LANES * LANES
    count = anchor_ref.shape[0]
    state = (top_ref[...], sum_ref[...], mix_ref[...])
    size = frames * cells
    top, total, mix = (v.reshape(size, v.shape[-1]) for v in state)
    query = query_ref[...].reshape(size, channels)
    low = lax.broadcasted_iota(jnp.int32, (1, LANES), 1) < LANES // 4
    for n in range(count):
        keyval = dot(unpacked(anchor_ref[n], channels), wkv_ref[...]).astype(BF)
        key = jnp.concatenate([keyval[:, :channels]] * frames, axis=0)
        scores = dot(query * key, to_lanes_ref[...])
        higher = jnp.maximum(top, scores)
        weight = jnp.exp(scores - higher)
        fade = jnp.exp(top - higher)
        total = total * fade + weight
        both = jnp.where(low, weight, fade)
        if last and n == count - 1:
            both = both / total
        spread = dot(both.astype(BF), beside(to_channels_ref))
        value = keyval[:, channels:].astype(F32)
        value = jnp.concatenate([value] * frames, axis=0)
        wide = spread[:, :full] * value[:, :full] + spread[:, full : 2 * full] * mix[:, :full]
        tail = jnp.concatenate([value[:, full:], mix[:, full + LANES // 2 :]], axis=1)
        tail = spread[:, 2 * full :] * tail
        tail = tail + pltpu.roll(tail, LANES // 2, 1)
        mix = jnp.concatenate([wide, tail], axis=1)
        top = higher
    return top, total, mix


def anchor_kernel(
    anchor_ref, wkv_ref, to_lanes_ref, to_channels_ref, query_ref, top_ref, sum_ref, mix_ref,
    top_out, sum_out, mix_out,
):
    new = updated(
        anchor_ref, wkv_ref, to_lanes_ref, to_channels_ref, query_ref, top_ref, sum_ref, mix_ref, False
    )
    for ref, v in zip((top_out, sum_out, mix_out), new):
        ref[...] = v.reshape(ref.shape)


def last_kernel(
    anchor_ref, wkv_ref, to_lanes_ref, to_channels_ref, query_ref, top_ref, sum_ref, mix_ref,
    temporal_ref, wo_ref, out_ref, out_buf, sems,
):
    frames, cells, channels = query_ref.shape
    height, width = out_ref.shape[1:3]
    _, _, mix = updated(
        anchor_ref, wkv_ref, to_lanes_ref, to_channels_ref, query_ref, top_ref, sum_ref, mix_ref, True
    )
    attended = mix[:, :channels].astype(BF)
    result = dot(attended, wo_ref[...])
    copies = []
    for i in range(frames):
        total = temporal_ref[i].astype(F32) + result[i * cells : (i + 1) * cells]
        out_buf[i] = total.astype(BF).reshape(height, width, channels)
        copies.append(pltpu.make_async_copy(out_buf.at[i], out_ref.at[i], sems.at[i]))
        copies[i].start()
    for copy in copies:
        copy.wait()


def neighbours(leading, last, axis):
    count = lax.axis_size(axis)
    up = [(i, i + 1) for i in range(count - 1)]
    down = [(j, i) for i, j in up]
    return lax.ppermute(last, axis, up), lax.ppermute(leading, axis, down)


def on_device(
    latents, anchor_index, window, gain_one, spatial_w, gain_two, temporal_w, gain_three,
    w_query, w_keyval, w_out,
):
    frames, height, width, channels = latents.shape
    cells = height * width
    count = anchor_index.shape[1]
    ws = spatial_w.reshape(3, 3 * channels, channels)
    one = 2 * channels * channels
    packed = cells * channels // LANES
    edge_packed = frames * width * channels // LANES
    lanes_up = (channels + LANES - 1) // LANES * LANES
    sem = pltpu.SemaphoreType.DMA
    some = (frames, cells, channels)

    x, g1, g2, g3, w = latents, gain_one, gain_two, gain_three, ws

    top, bottom = call(
        edge_kernel, [((edge_packed, LANES), BF)] * 2, [VMEM], flops=8 * frames * cells * one
    )(x)
    above, below = neighbours(top, bottom, "strip")
    outer_col = pltpu.VMEM((2 * cells, 3 * channels), BF)
    inner_col = pltpu.VMEM(((frames - 2) * (cells + 2 * width), 3 * channels), BF)
    middle = (2, cells - 2 * width, channels)
    mid, mid2, edge, w_rem, order = call(
        outer_kernel,
        [
            (middle, BF),
            (middle, BF),
            ((2, 2, width, channels), F32),
            ((3 * channels, 3 * (channels % 256)), BF),
            ((8, LANES), F32),
        ],
        [VMEM] * 4,
        [outer_col],
        flops=9 * 2 * cells * one,
    )(x, g1, g2, w)
    outer_spatial, outer_hidden, first, last = call(
        functools.partial(outer_edge_kernel, frames),
        [((2, cells, channels), BF)] * 2 + [((packed, LANES), BF)] * 2,
        [VMEM] * 10,
        flops=6 * 2 * width * one,
    )(edge, above, below, order, mid, mid2, g1, g2, w, w_rem)
    before, after = neighbours(first, last, "clip")
    spatial, hidden = call(
        inner_kernel,
        [(some, BF), (some, BF)],
        [VMEM] * 9,
        [inner_col],
        flops=9 * (frames - 2) * cells * one,
    )(x, above, below, g1, g2, w, w_rem, outer_spatial, outer_hidden)
    (chosen,) = call(
        chosen_kernel, [((count, packed, LANES), BF)], [VMEM] * 7, flops=3 * cells * one
    )(anchor_index, before, after, spatial, hidden, g3, temporal_w)
    clips = lax.axis_size("clip")
    arrived = [
        lax.ppermute(chosen, "clip", [(i, (i + s) % clips) for i in range(clips)])
        for s in range(1, clips)
    ]
    temporal, query, keyval = call(
        temporal_kernel,
        [(some, BF), (some, BF), ((frames, cells, 2 * channels), BF)],
        [VMEM] * 8,
        flops=6 * frames * cells * one,
        limit=32,
    )(before, after, spatial, hidden, g3, temporal_w, w_query, w_keyval)
    states = [((frames, cells, LANES), F32)] * 2 + [((frames, cells, lanes_up), F32)]
    state = call(
        local_kernel, states, [VMEM] * 6, flops=10 * frames * cells * one, limit=32
    )(anchor_index, window, query, keyval, *head_maps(frames, channels))
    to_lanes, _ = head_maps(1, channels, everywhere=True)
    _, to_channels = head_maps(2, channels)
    for arrival in arrived[:-1]:
        state = call(
            anchor_kernel, states, [VMEM] * 8, flops=4 * frames * cells * one, limit=32
        )(arrival, w_keyval, to_lanes, to_channels, query, *state)
    (out,) = call(
        last_kernel,
        [(latents.shape, BF)],
        [VMEM] * 10,
        [pltpu.VMEM(latents.shape, BF), sem((frames,))],
        flops=5 * frames * cells * one,
        limit=32,
        out_specs=(HBM,),
    )(arrived[-1], w_keyval, to_lanes, to_channels, query, *state, temporal, w_out)
    return out


def solution(mesh):
    return jax.shard_map(
        on_device,
        mesh=mesh,
        in_specs=(
            P(("groups", "clip"), "strip", None, None),
            P(("groups", "clip"), None),
            P(),
            P(),
            P(),
            P(),
            P(),
            P(),
            P(),
            P(),
            P(),
        ),
        out_specs=P(("groups", "clip"), "strip", None, None),
        check_vma=False,
    )
```

```python
import functools
import math

import jax
import jax.numpy as jnp
import numpy as np
from jax import lax
from jax.experimental import pallas as pl
from jax.experimental.pallas import tpu as pltpu
from jax.sharding import PartitionSpec as P

HEADS = 5
HEAD_DIM = 64
LANES = 128
BF = jnp.bfloat16
F32 = jnp.float32
VMEM = pl.BlockSpec(memory_space=pltpu.VMEM)
HBM = pl.BlockSpec(memory_space=pltpu.HBM)
MIB = 1 << 20


def call(body, outs, specs, scratch=(), flops=0, limit=24, out_specs=None):
    return pl.pallas_call(
        body,
        out_shape=tuple(jax.ShapeDtypeStruct(s, d) for s, d in outs),
        in_specs=specs,
        out_specs=out_specs or tuple(VMEM for _ in outs),
        scratch_shapes=list(scratch),
        cost_estimate=pl.CostEstimate(flops=flops, bytes_accessed=2 * MIB, transcendentals=0),
        compiler_params=pltpu.CompilerParams(vmem_limit_bytes=limit * MIB),
    )


def dot(a, b):
    return jnp.dot(a, b, preferred_element_type=F32)


def norm(v, gain_ref):
    wide = v.astype(F32)
    centred = wide - jnp.mean(wide, axis=-1, keepdims=True)
    variance = jnp.mean(centred * centred, axis=-1, keepdims=True)
    return centred * lax.rsqrt(variance + 1e-05) * gain_ref[...].reshape(1, v.shape[1])


def silu(u):
    half = 0.5 * u
    return half + half * jnp.tanh(half)


def pack_into(ref, h):
    cells, channels = h.shape
    full = channels // LANES
    for t in range(full):
        ref[t * cells : (t + 1) * cells, :] = h[:, t * LANES : (t + 1) * LANES]
    rest = channels - full * LANES
    if rest:
        share = LANES // rest
        part = cells // share
        ref[full * cells :, :] = jnp.concatenate(
            [h[s * part : (s + 1) * part, full * LANES :] for s in range(share)], axis=1
        )


def unpacked(p, channels):
    cells = p.shape[0] * LANES // channels
    full = channels // LANES
    pieces = [p[t * cells : (t + 1) * cells, :] for t in range(full)]
    rest = channels - full * LANES
    if rest:
        share = LANES // rest
        tail = p[full * cells :, :]
        pieces.append(
            jnp.concatenate([tail[:, s * rest : (s + 1) * rest] for s in range(share)], axis=0)
        )
    return jnp.concatenate(pieces, axis=1)


def columns(h, width):
    cells, channels = h.shape
    left = pltpu.roll(h, 1, 0)
    right = pltpu.roll(h, cells - 1, 0)
    place = lax.broadcasted_iota(jnp.int32, (8, channels), 0)
    lefts, rights = [], []
    for lo in range(0, cells, width):
        hi = lo + width
        lefts += [jnp.where(place == 0, 0.0, left[lo : lo + 8]), left[lo + 8 : hi]]
        rights += [right[lo : hi - 8], jnp.where(place == 7, 0.0, right[hi - 8 : hi])]
    sides = [jnp.concatenate(lefts, axis=0), h, jnp.concatenate(rights, axis=0)]
    return jnp.concatenate([v.astype(BF) for v in sides], axis=1)


def scalar(ref, n):
    values = ref[...].astype(F32)
    place = lax.broadcasted_iota(jnp.int32, values.shape, 1)
    return jnp.sum(jnp.where(place == n, values, 0.0)).astype(jnp.int32)


def edge_kernel(x_ref, top_ref, bottom_ref):
    frames, height, width, channels = x_ref.shape
    pack_into(top_ref, x_ref[:, 0].reshape(frames * width, channels))
    pack_into(bottom_ref, x_ref[:, height - 1].reshape(frames * width, channels))


def rests_into(rem_ref, w_ref):
    full = w_ref.shape[2] // 256 * 256
    rest = w_ref.shape[2] - full
    for a in range(3):
        rem_ref[:, a * rest : (a + 1) * rest] = w_ref[a, :, full:]


def hidden_columns(v, g1_ref, width):
    return columns(silu(norm(v, g1_ref)), width)


def stacked_rows(col_ref, count, height, width, w_ref, rem_ref):
    cells = height * width
    rims = (col_ref.shape[0] - count * cells) // 2
    channels = w_ref.shape[2]
    full = channels // 256 * 256
    rest = channels - full
    size = count * cells
    above = dot(col_ref[: rims + size], w_ref[0, :, :full])
    centre = dot(col_ref[rims : rims + size], w_ref[1, :, :full])
    below = dot(col_ref[rims:], w_ref[2, :, :full])
    tails = dot(col_ref[...], rem_ref[...])

    def terms(place, row):
        own = place * cells + row * width
        wide = centre[own : own + width]
        tail = tails[rims + own : rims + own + width, rest : 2 * rest]
        if row > 0 or rims:
            at = rims + own - width if row > 0 else place * width
            wide = wide + above[at : at + width]
            tail = tail + tails[at : at + width, :rest]
        if row < height - 1 or rims:
            at = own + width if row < height - 1 else size + place * width
            wide = wide + below[at : at + width]
            tail = tail + tails[rims + at : rims + at + width, 2 * rest :]
        return jnp.concatenate([wide, tail], axis=1)

    return terms


def rim_rows(ref, frames, width, channels):
    rows = unpacked(ref[...], channels)
    return jnp.concatenate([rows[f * width : (f + 1) * width] for f in frames], axis=0)


def outer_kernel(x_ref, g1_ref, g2_ref, w_ref, mid_ref, mid2_ref, edge_ref, rem_ref, order_ref, col_ref):
    frames, height, width, channels = x_ref.shape
    cells = height * width
    order_ref[...] = jnp.zeros_like(order_ref)
    rests_into(rem_ref, w_ref)
    outer = (0, frames - 1)
    for s, f in enumerate(outer):
        x = x_ref[f].reshape(cells, channels)
        col_ref[s * cells : (s + 1) * cells] = hidden_columns(x, g1_ref, width)
    terms = stacked_rows(col_ref, 2, height, width, w_ref, rem_ref)
    for s, f in enumerate(outer):
        for row in range(height):
            total = x_ref[f, row].astype(F32) + terms(s, row)
            if 0 < row < height - 1:
                rounded = total.astype(BF)
                lo = (row - 1) * width
                mid_ref[s, lo : lo + width] = rounded
                mid2_ref[s, lo : lo + width] = silu(norm(rounded, g2_ref)).astype(BF)
            else:
                edge_ref[s, 0 if row == 0 else 1] = total


def outer_edge_kernel(
    frames, edge_ref, above_ref, below_ref, order_ref, mid_ref, mid2_ref, g1_ref, g2_ref, w_ref, rem_ref,
    spatial_ref, hidden_ref, first_ref, last_ref,
):
    _, cells, channels = spatial_ref.shape
    width = edge_ref.shape[2]
    full = channels // 256 * 256
    rest = channels - full
    spatial_ref[:, width : cells - width] = mid_ref[...]
    hidden_ref[:, width : cells - width] = mid2_ref[...]
    cols = [
        hidden_columns(rim_rows(ref, (0, frames - 1), width, channels), g1_ref, width)
        for ref in (above_ref, below_ref)
    ]
    tails = dot(jnp.concatenate(cols, axis=0), rem_ref[...])
    size = 2 * width
    for side, lo in ((0, 0), (1, cells - width)):
        tail = tails[:size, :rest] if side == 0 else tails[size:, 2 * rest :]
        wide = dot(cols[side], w_ref[2 * side, :, :full])
        term = jnp.concatenate([wide, tail], axis=1)
        rounded = (edge_ref[:, side].reshape(size, channels) + term).astype(BF)
        hidden = silu(norm(rounded, g2_ref)).astype(BF)
        spatial_ref[:, lo : lo + width] = rounded.reshape(2, width, channels)
        hidden_ref[:, lo : lo + width] = hidden.reshape(2, width, channels)
    pack_into(first_ref, hidden_ref[0])
    pack_into(last_ref, hidden_ref[1])


def inner_kernel(
    x_ref, above_ref, below_ref, g1_ref, g2_ref, w_ref, rem_ref, outer_spatial_ref, outer_hidden_ref,
    spatial_ref, hidden_ref, col_ref,
):
    frames, height, width, channels = x_ref.shape
    cells = height * width
    for s, f in ((0, 0), (1, frames - 1)):
        spatial_ref[f] = outer_spatial_ref[s]
        hidden_ref[f] = outer_hidden_ref[s]
    inside = range(1, frames - 1)
    rims = len(inside) * width
    end = rims + len(inside) * cells
    col_ref[:rims] = hidden_columns(rim_rows(above_ref, inside, width, channels), g1_ref, width)
    for s, f in enumerate(inside):
        x = x_ref[f].reshape(cells, channels)
        lo = rims + s * cells
        col_ref[lo : lo + cells] = hidden_columns(x, g1_ref, width)
    col_ref[end:] = hidden_columns(rim_rows(below_ref, inside, width, channels), g1_ref, width)
    terms = stacked_rows(col_ref, len(inside), height, width, w_ref, rem_ref)
    for s, f in enumerate(inside):
        for row in range(height):
            rounded = (x_ref[f, row].astype(F32) + terms(s, row)).astype(BF)
            lo = row * width
            spatial_ref[f, lo : lo + width] = rounded
            hidden_ref[f, lo : lo + width] = silu(norm(rounded, g2_ref)).astype(BF)


def chosen_kernel(
    picks_ref, before_ref, after_ref, spatial_ref, hidden_ref, g3_ref, wt_ref, chosen_ref
):
    frames, cells, channels = spatial_ref.shape
    before = unpacked(before_ref[...], channels)
    after = unpacked(after_ref[...], channels)
    for n in range(chosen_ref.shape[0]):
        pick = scalar(picks_ref, n)
        earlier = jnp.where(pick == 0, before, hidden_ref[jnp.maximum(pick - 1, 0)])
        later = jnp.where(pick == frames - 1, after, hidden_ref[jnp.minimum(pick + 1, frames - 1)])
        total = spatial_ref[pick].astype(F32) + dot(hidden_ref[pick], wt_ref[1])
        total = total + dot(earlier, wt_ref[0]) + dot(later, wt_ref[2])
        pack_into(chosen_ref.at[n], norm(total.astype(BF), g3_ref).astype(BF))


def temporal_kernel(
    before_ref, after_ref, spatial_ref, hidden_ref, g3_ref, wt_ref, wq_ref, wkv_ref,
    temporal_ref, query_ref, keyval_ref,
):
    frames, cells, channels = spatial_ref.shape
    size = frames * cells
    before = unpacked(before_ref[...], channels)
    after = unpacked(after_ref[...], channels)
    hidden = hidden_ref[...].reshape(size, channels)
    total = spatial_ref[...].reshape(size, channels).astype(F32) + dot(hidden, wt_ref[1])
    total = total + dot(jnp.concatenate([before, hidden[: size - cells]], axis=0), wt_ref[0])
    total = total + dot(jnp.concatenate([hidden[cells:], after], axis=0), wt_ref[2])
    temporal = total.astype(BF)
    temporal_ref[...] = temporal.reshape(frames, cells, channels)
    normed = norm(temporal, g3_ref).astype(BF)
    query_ref[...] = dot(normed, wq_ref[...]).astype(BF).reshape(frames, cells, channels)
    keyval_ref[...] = dot(normed, wkv_ref[...]).astype(BF).reshape(frames, cells, 2 * channels)


def head_maps(count, channels, everywhere=False):
    full = channels // LANES * LANES
    rest = channels - full
    stride = LANES // 4
    hits = np.zeros((count * channels, LANES), np.float32)
    for j in range(count):
        for c in range(channels):
            at = j * full + c if c < full else count * full + j * rest + c - full
            lanes = range(0, LANES, stride) if everywhere else (j * stride,)
            for lane in lanes:
                hits[at, lane + c // HEAD_DIM] = 1.0
    padded = np.zeros((-(-hits.shape[0] // LANES) * LANES, LANES), np.float32)
    padded[: hits.shape[0]] = hits
    blocks = padded.reshape(-1, LANES, LANES).transpose(0, 2, 1).reshape(-1, LANES)
    return jnp.asarray(hits / math.sqrt(HEAD_DIM), BF), jnp.asarray(blocks, BF)


def beside(ref):
    count = ref.shape[0] // LANES
    return jnp.concatenate([ref[b * LANES : (b + 1) * LANES] for b in range(count)], axis=1)


def local_kernel(
    picks_ref, window_ref, query_ref, keyval_ref, to_lanes_ref, to_channels_ref,
    top_ref, sum_ref, mix_ref,
):
    frames, cells, channels = query_ref.shape
    count = picks_ref.shape[1]
    full = channels // LANES * LANES
    stride = LANES // 4
    queries = [query_ref[f] for f in range(frames)]
    keyvals = [keyval_ref[f] for f in range(frames)]
    keys = [kv[:, :full] for kv in keyvals] + [
        jnp.concatenate([kv[:, full:channels] for kv in keyvals], axis=1)
    ]
    values = [kv[:, channels : channels + full].astype(F32) for kv in keyvals] + [
        jnp.concatenate([kv[:, channels + full :] for kv in keyvals], axis=1).astype(F32)
    ]
    products = []
    for q in queries:
        again = jnp.concatenate([q[:, full:]] * frames, axis=1)
        row = [q[:, :full] * k for k in keys[:frames]] + [again * keys[frames]]
        products.append(jnp.concatenate(row, axis=1))
    scores = dot(jnp.concatenate(products, axis=0), to_lanes_ref[...])
    source = lax.div(lax.broadcasted_iota(jnp.int32, (1, LANES), 1), stride)
    window = window_ref[...].reshape(1, 1)
    copies = jnp.zeros((1, LANES), F32)
    for n in range(count):
        copies = copies + jnp.where(source == picks_ref[:, n : n + 1], 1.0, 0.0)
    weights = []
    for i in range(frames):
        times = copies + jnp.where(jnp.abs(source - i) < window, 1.0, 0.0)
        s = jnp.where(times > 0.0, scores[i * cells : (i + 1) * cells], -jnp.inf)
        top = jnp.maximum(s, pltpu.roll(s, stride, 1))
        top = jnp.maximum(top, pltpu.roll(top, 2 * stride, 1))
        w = jnp.exp(s - top) * times
        total = w + pltpu.roll(w, stride, 1)
        total = total + pltpu.roll(total, 2 * stride, 1)
        top_ref[i] = top
        sum_ref[i] = total
        weights.append(w.astype(BF))
    spread = dot(jnp.concatenate(weights, axis=0), beside(to_channels_ref))
    for i in range(frames):
        part = spread[i * cells : (i + 1) * cells]
        wide = part[:, :full] * values[0]
        for j in range(1, frames):
            wide = wide + part[:, j * full : (j + 1) * full] * values[j]
        tail = part[:, frames * full :] * values[frames]
        tail = tail[:, :LANES] + tail[:, LANES:]
        tail = tail + pltpu.roll(tail, LANES // 2, 1)
        mix_ref[i] = jnp.concatenate([wide, tail], axis=1)


def updated(
    anchor_ref, wkv_ref, to_lanes_ref, to_channels_ref, query_ref, top_ref, sum_ref, mix_ref, last
):
    frames, cells, channels = query_ref.shape
    full = channels // LANES * LANES
    count = anchor_ref.shape[0]
    state = (top_ref[...], sum_ref[...], mix_ref[...])
    size = frames * cells
    top, total, mix = (v.reshape(size, v.shape[-1]) for v in state)
    query = query_ref[...].reshape(size, channels)
    low = lax.broadcasted_iota(jnp.int32, (1, LANES), 1) < LANES // 4
    for n in range(count):
        keyval = dot(unpacked(anchor_ref[n], channels), wkv_ref[...]).astype(BF)
        key = jnp.concatenate([keyval[:, :channels]] * frames, axis=0)
        scores = dot(query * key, to_lanes_ref[...])
        higher = jnp.maximum(top, scores)
        weight = jnp.exp(scores - higher)
        fade = jnp.exp(top - higher)
        total = total * fade + weight
        both = jnp.where(low, weight, fade)
        if last and n == count - 1:
            both = both / total
        spread = dot(both.astype(BF), beside(to_channels_ref))
        value = keyval[:, channels:].astype(F32)
        value = jnp.concatenate([value] * frames, axis=0)
        wide = spread[:, :full] * value[:, :full] + spread[:, full : 2 * full] * mix[:, :full]
        tail = jnp.concatenate([value[:, full:], mix[:, full + LANES // 2 :]], axis=1)
        tail = spread[:, 2 * full :] * tail
        tail = tail + pltpu.roll(tail, LANES // 2, 1)
        mix = jnp.concatenate([wide, tail], axis=1)
        top = higher
    return top, total, mix


def relay_kernel(from_below_ref, from_above_ref, out_ref, order_ref):
    even = lax.rem(lax.axis_index("clip"), 2) == 0
    out_ref[...] = jnp.where(even, from_below_ref[...], from_above_ref[...])
    order_ref[...] = jnp.zeros_like(order_ref)


def anchor_kernel(
    anchor_ref, wkv_ref, to_lanes_ref, to_channels_ref, query_ref, top_ref, sum_ref, mix_ref,
    order_ref, top_out, sum_out, mix_out,
):
    new = updated(
        anchor_ref, wkv_ref, to_lanes_ref, to_channels_ref, query_ref, top_ref, sum_ref, mix_ref, False
    )
    for ref, v in zip((top_out, sum_out, mix_out), new):
        ref[...] = v.reshape(ref.shape)


def last_kernel(
    anchor_ref, wkv_ref, to_lanes_ref, to_channels_ref, query_ref, top_ref, sum_ref, mix_ref,
    temporal_ref, wo_ref, out_ref, out_buf, sems,
):
    frames, cells, channels = query_ref.shape
    height, width = out_ref.shape[1:3]
    _, _, mix = updated(
        anchor_ref, wkv_ref, to_lanes_ref, to_channels_ref, query_ref, top_ref, sum_ref, mix_ref, True
    )
    attended = mix[:, :channels].astype(BF)
    result = dot(attended, wo_ref[...])
    copies = []
    for i in range(frames):
        total = temporal_ref[i].astype(F32) + result[i * cells : (i + 1) * cells]
        out_buf[i] = total.astype(BF).reshape(height, width, channels)
        copies.append(pltpu.make_async_copy(out_buf.at[i], out_ref.at[i], sems.at[i]))
        copies[i].start()
    for copy in copies:
        copy.wait()


def neighbours(leading, last, axis):
    count = lax.axis_size(axis)
    up = [(i, i + 1) for i in range(count - 1)]
    down = [(j, i) for i, j in up]
    return lax.ppermute(last, axis, up), lax.ppermute(leading, axis, down)


def on_device(
    latents, anchor_index, window, gain_one, spatial_w, gain_two, temporal_w, gain_three,
    w_query, w_keyval, w_out,
):
    frames, height, width, channels = latents.shape
    cells = height * width
    count = anchor_index.shape[1]
    ws = spatial_w.reshape(3, 3 * channels, channels)
    one = 2 * channels * channels
    packed = cells * channels // LANES
    edge_packed = frames * width * channels // LANES
    lanes_up = (channels + LANES - 1) // LANES * LANES
    sem = pltpu.SemaphoreType.DMA
    some = (frames, cells, channels)

    x, g1, g2, g3, w = latents, gain_one, gain_two, gain_three, ws

    top, bottom = call(
        edge_kernel, [((edge_packed, LANES), BF)] * 2, [VMEM], flops=8 * frames * cells * one
    )(x)
    above, below = neighbours(top, bottom, "strip")
    outer_col = pltpu.VMEM((2 * cells, 3 * channels), BF)
    inner_col = pltpu.VMEM(((frames - 2) * (cells + 2 * width), 3 * channels), BF)
    middle = (2, cells - 2 * width, channels)
    mid, mid2, edge, w_rem, order = call(
        outer_kernel,
        [
            (middle, BF),
            (middle, BF),
            ((2, 2, width, channels), F32),
            ((3 * channels, 3 * (channels % 256)), BF),
            ((8, LANES), F32),
        ],
        [VMEM] * 4,
        [outer_col],
        flops=9 * 2 * cells * one,
    )(x, g1, g2, w)
    outer_spatial, outer_hidden, first, last = call(
        functools.partial(outer_edge_kernel, frames),
        [((2, cells, channels), BF)] * 2 + [((packed, LANES), BF)] * 2,
        [VMEM] * 10,
        flops=6 * 2 * width * one,
    )(edge, above, below, order, mid, mid2, g1, g2, w, w_rem)
    before, after = neighbours(first, last, "clip")
    spatial, hidden = call(
        inner_kernel,
        [(some, BF), (some, BF)],
        [VMEM] * 9,
        [inner_col],
        flops=9 * (frames - 2) * cells * one,
    )(x, above, below, g1, g2, w, w_rem, outer_spatial, outer_hidden)
    (chosen,) = call(
        chosen_kernel, [((count, packed, LANES), BF)], [VMEM] * 7, flops=3 * cells * one
    )(anchor_index, before, after, spatial, hidden, g3, temporal_w)
    clips = lax.axis_size("clip")

    def rotated(step):
        return lax.ppermute(chosen, "clip", [(i, (i + step) % clips) for i in range(clips)])

    if clips == 4:
        arrived = [rotated(1), rotated(clips - 1)]
        relayed, anchors_order = call(
            relay_kernel, [(chosen.shape, BF), ((8, LANES), F32)], [VMEM] * 2
        )(*arrived)
        pairs = [(i, i + 1 - 2 * (i % 2)) for i in range(clips)]
        arrived.append(lax.ppermute(relayed, "clip", pairs))
    else:
        arrived = [rotated(s) for s in range(1, clips)]
        anchors_order = order
    temporal, query, keyval = call(
        temporal_kernel,
        [(some, BF), (some, BF), ((frames, cells, 2 * channels), BF)],
        [VMEM] * 8,
        flops=6 * frames * cells * one,
        limit=32,
    )(before, after, spatial, hidden, g3, temporal_w, w_query, w_keyval)
    states = [((frames, cells, LANES), F32)] * 2 + [((frames, cells, lanes_up), F32)]
    state = call(
        local_kernel, states, [VMEM] * 6, flops=10 * frames * cells * one, limit=32
    )(anchor_index, window, query, keyval, *head_maps(frames, channels))
    to_lanes, _ = head_maps(1, channels, everywhere=True)
    _, to_channels = head_maps(2, channels)
    for arrival in arrived[:-1]:
        state = call(
            anchor_kernel, states, [VMEM] * 9, flops=4 * frames * cells * one, limit=32
        )(arrival, w_keyval, to_lanes, to_channels, query, *state, anchors_order)
    (out,) = call(
        last_kernel,
        [(latents.shape, BF)],
        [VMEM] * 10,
        [pltpu.VMEM(latents.shape, BF), sem((frames,))],
        flops=5 * frames * cells * one,
        limit=32,
        out_specs=(HBM,),
    )(arrived[-1], w_keyval, to_lanes, to_channels, query, *state, temporal, w_out)
    return out


def solution(mesh):
    return jax.shard_map(
        on_device,
        mesh=mesh,
        in_specs=(
            P(("groups", "clip"), "strip", None, None),
            P(("groups", "clip"), None),
            P(),
            P(),
            P(),
            P(),
            P(),
            P(),
            P(),
            P(),
            P(),
        ),
        out_specs=P(("groups", "clip"), "strip", None, None),
        check_vma=False,
    )
```

```python
import functools
import math

import jax
import jax.numpy as jnp
import numpy as np
from jax import lax
from jax.experimental import pallas as pl
from jax.experimental.pallas import tpu as pltpu
from jax.sharding import PartitionSpec as P

HEADS = 5
HEAD_DIM = 64
LANES = 128
BF = jnp.bfloat16
F32 = jnp.float32
VMEM = pl.BlockSpec(memory_space=pltpu.VMEM)
HBM = pl.BlockSpec(memory_space=pltpu.HBM)
MIB = 1 << 20


def call(body, outs, specs, scratch=(), flops=0, limit=24, out_specs=None):
    return pl.pallas_call(
        body,
        out_shape=tuple(jax.ShapeDtypeStruct(s, d) for s, d in outs),
        in_specs=specs,
        out_specs=out_specs or tuple(VMEM for _ in outs),
        scratch_shapes=list(scratch),
        cost_estimate=pl.CostEstimate(flops=flops, bytes_accessed=2 * MIB, transcendentals=0),
        compiler_params=pltpu.CompilerParams(vmem_limit_bytes=limit * MIB),
    )


def dot(a, b):
    return jnp.dot(a, b, preferred_element_type=F32)


def norm(v, gain_ref):
    wide = v.astype(F32)
    centred = wide - jnp.mean(wide, axis=-1, keepdims=True)
    variance = jnp.mean(centred * centred, axis=-1, keepdims=True)
    return centred * lax.rsqrt(variance + 1e-05) * gain_ref[...].reshape(1, v.shape[1])


def silu(u):
    half = 0.5 * u
    return half + half * jnp.tanh(half)


def pack_into(ref, h):
    cells, channels = h.shape
    full = channels // LANES
    for t in range(full):
        ref[t * cells : (t + 1) * cells, :] = h[:, t * LANES : (t + 1) * LANES]
    rest = channels - full * LANES
    if rest:
        share = LANES // rest
        part = cells // share
        ref[full * cells :, :] = jnp.concatenate(
            [h[s * part : (s + 1) * part, full * LANES :] for s in range(share)], axis=1
        )


def unpacked(p, channels):
    cells = p.shape[0] * LANES // channels
    full = channels // LANES
    pieces = [p[t * cells : (t + 1) * cells, :] for t in range(full)]
    rest = channels - full * LANES
    if rest:
        share = LANES // rest
        tail = p[full * cells :, :]
        pieces.append(
            jnp.concatenate([tail[:, s * rest : (s + 1) * rest] for s in range(share)], axis=0)
        )
    return jnp.concatenate(pieces, axis=1)


def columns(h, width):
    cells, channels = h.shape
    left = pltpu.roll(h, 1, 0)
    right = pltpu.roll(h, cells - 1, 0)
    place = lax.broadcasted_iota(jnp.int32, (8, channels), 0)
    lefts, rights = [], []
    for lo in range(0, cells, width):
        hi = lo + width
        lefts += [jnp.where(place == 0, 0.0, left[lo : lo + 8]), left[lo + 8 : hi]]
        rights += [right[lo : hi - 8], jnp.where(place == 7, 0.0, right[hi - 8 : hi])]
    sides = [jnp.concatenate(lefts, axis=0), h, jnp.concatenate(rights, axis=0)]
    return jnp.concatenate([v.astype(BF) for v in sides], axis=1)


def scalar(ref, n):
    values = ref[...].astype(F32)
    place = lax.broadcasted_iota(jnp.int32, values.shape, 1)
    return jnp.sum(jnp.where(place == n, values, 0.0)).astype(jnp.int32)


def edge_kernel(x_ref, top_ref, bottom_ref):
    frames, height, width, channels = x_ref.shape
    pack_into(top_ref, x_ref[:, 0].reshape(frames * width, channels))
    pack_into(bottom_ref, x_ref[:, height - 1].reshape(frames * width, channels))


def rests_into(rem_ref, w_ref):
    full = w_ref.shape[2] // 256 * 256
    rest = w_ref.shape[2] - full
    for a in range(3):
        rem_ref[:, a * rest : (a + 1) * rest] = w_ref[a, :, full:]


def hidden_columns(v, g1_ref, width):
    return columns(silu(norm(v, g1_ref)), width)


def stacked_rows(col_ref, count, height, width, w_ref, rem_ref):
    cells = height * width
    rims = (col_ref.shape[0] - count * cells) // 2
    channels = w_ref.shape[2]
    full = channels // 256 * 256
    rest = channels - full
    size = count * cells
    above = dot(col_ref[: rims + size], w_ref[0, :, :full])
    centre = dot(col_ref[rims : rims + size], w_ref[1, :, :full])
    below = dot(col_ref[rims:], w_ref[2, :, :full])
    tails = dot(col_ref[...], rem_ref[...])

    def terms(place, row):
        own = place * cells + row * width
        wide = centre[own : own + width]
        tail = tails[rims + own : rims + own + width, rest : 2 * rest]
        if row > 0 or rims:
            at = rims + own - width if row > 0 else place * width
            wide = wide + above[at : at + width]
            tail = tail + tails[at : at + width, :rest]
        if row < height - 1 or rims:
            at = own + width if row < height - 1 else size + place * width
            wide = wide + below[at : at + width]
            tail = tail + tails[rims + at : rims + at + width, 2 * rest :]
        return jnp.concatenate([wide, tail], axis=1)

    return terms


def rim_rows(ref, frames, width, channels):
    rows = unpacked(ref[...], channels)
    return jnp.concatenate([rows[f * width : (f + 1) * width] for f in frames], axis=0)


def outer_kernel(x_ref, g1_ref, g2_ref, w_ref, mid_ref, mid2_ref, edge_ref, rem_ref, order_ref, col_ref):
    frames, height, width, channels = x_ref.shape
    cells = height * width
    order_ref[...] = jnp.zeros_like(order_ref)
    rests_into(rem_ref, w_ref)
    outer = (0, frames - 1)
    for s, f in enumerate(outer):
        x = x_ref[f].reshape(cells, channels)
        col_ref[s * cells : (s + 1) * cells] = hidden_columns(x, g1_ref, width)
    terms = stacked_rows(col_ref, 2, height, width, w_ref, rem_ref)
    for s, f in enumerate(outer):
        for row in range(height):
            total = x_ref[f, row].astype(F32) + terms(s, row)
            if 0 < row < height - 1:
                rounded = total.astype(BF)
                lo = (row - 1) * width
                mid_ref[s, lo : lo + width] = rounded
                mid2_ref[s, lo : lo + width] = silu(norm(rounded, g2_ref)).astype(BF)
            else:
                edge_ref[s, 0 if row == 0 else 1] = total


def outer_edge_kernel(
    frames, edge_ref, above_ref, below_ref, order_ref, mid_ref, mid2_ref, g1_ref, g2_ref, w_ref, rem_ref,
    spatial_ref, hidden_ref, first_ref, last_ref,
):
    _, cells, channels = spatial_ref.shape
    width = edge_ref.shape[2]
    full = channels // 256 * 256
    rest = channels - full
    spatial_ref[:, width : cells - width] = mid_ref[...]
    hidden_ref[:, width : cells - width] = mid2_ref[...]
    cols = [
        hidden_columns(rim_rows(ref, (0, frames - 1), width, channels), g1_ref, width)
        for ref in (above_ref, below_ref)
    ]
    tails = dot(jnp.concatenate(cols, axis=0), rem_ref[...])
    size = 2 * width
    for side, lo in ((0, 0), (1, cells - width)):
        tail = tails[:size, :rest] if side == 0 else tails[size:, 2 * rest :]
        wide = dot(cols[side], w_ref[2 * side, :, :full])
        term = jnp.concatenate([wide, tail], axis=1)
        rounded = (edge_ref[:, side].reshape(size, channels) + term).astype(BF)
        hidden = silu(norm(rounded, g2_ref)).astype(BF)
        spatial_ref[:, lo : lo + width] = rounded.reshape(2, width, channels)
        hidden_ref[:, lo : lo + width] = hidden.reshape(2, width, channels)
    pack_into(first_ref, hidden_ref[0])
    pack_into(last_ref, hidden_ref[1])


def inner_kernel(
    x_ref, above_ref, below_ref, g1_ref, g2_ref, w_ref, rem_ref, outer_spatial_ref, outer_hidden_ref,
    spatial_ref, hidden_ref, col_ref,
):
    frames, height, width, channels = x_ref.shape
    cells = height * width
    for s, f in ((0, 0), (1, frames - 1)):
        spatial_ref[f] = outer_spatial_ref[s]
        hidden_ref[f] = outer_hidden_ref[s]
    inside = range(1, frames - 1)
    rims = len(inside) * width
    end = rims + len(inside) * cells
    col_ref[:rims] = hidden_columns(rim_rows(above_ref, inside, width, channels), g1_ref, width)
    for s, f in enumerate(inside):
        x = x_ref[f].reshape(cells, channels)
        lo = rims + s * cells
        col_ref[lo : lo + cells] = hidden_columns(x, g1_ref, width)
    col_ref[end:] = hidden_columns(rim_rows(below_ref, inside, width, channels), g1_ref, width)
    terms = stacked_rows(col_ref, len(inside), height, width, w_ref, rem_ref)
    for s, f in enumerate(inside):
        for row in range(height):
            rounded = (x_ref[f, row].astype(F32) + terms(s, row)).astype(BF)
            lo = row * width
            spatial_ref[f, lo : lo + width] = rounded
            hidden_ref[f, lo : lo + width] = silu(norm(rounded, g2_ref)).astype(BF)


def chosen_kernel(
    picks_ref, before_ref, after_ref, spatial_ref, hidden_ref, g3_ref, wt_ref, chosen_ref
):
    frames, cells, channels = spatial_ref.shape
    before = unpacked(before_ref[...], channels)
    after = unpacked(after_ref[...], channels)
    for n in range(chosen_ref.shape[0]):
        pick = scalar(picks_ref, n)
        earlier = jnp.where(pick == 0, before, hidden_ref[jnp.maximum(pick - 1, 0)])
        later = jnp.where(pick == frames - 1, after, hidden_ref[jnp.minimum(pick + 1, frames - 1)])
        total = spatial_ref[pick].astype(F32) + dot(hidden_ref[pick], wt_ref[1])
        total = total + dot(earlier, wt_ref[0]) + dot(later, wt_ref[2])
        pack_into(chosen_ref.at[n], norm(total.astype(BF), g3_ref).astype(BF))


def temporal_kernel(
    before_ref, after_ref, spatial_ref, hidden_ref, g3_ref, wt_ref, wq_ref, wkv_ref,
    temporal_ref, query_ref, keyval_ref,
):
    frames, cells, channels = spatial_ref.shape
    size = frames * cells
    before = unpacked(before_ref[...], channels)
    after = unpacked(after_ref[...], channels)
    hidden = hidden_ref[...].reshape(size, channels)
    total = spatial_ref[...].reshape(size, channels).astype(F32) + dot(hidden, wt_ref[1])
    total = total + dot(jnp.concatenate([before, hidden[: size - cells]], axis=0), wt_ref[0])
    total = total + dot(jnp.concatenate([hidden[cells:], after], axis=0), wt_ref[2])
    temporal = total.astype(BF)
    temporal_ref[...] = temporal.reshape(frames, cells, channels)
    normed = norm(temporal, g3_ref).astype(BF)
    query_ref[...] = dot(normed, wq_ref[...]).astype(BF).reshape(frames, cells, channels)
    keyval_ref[...] = dot(normed, wkv_ref[...]).astype(BF).reshape(frames, cells, 2 * channels)


def head_maps(count, channels, everywhere=False):
    full = channels // LANES * LANES
    rest = channels - full
    stride = LANES // 4
    hits = np.zeros((count * channels, LANES), np.float32)
    for j in range(count):
        for c in range(channels):
            at = j * full + c if c < full else count * full + j * rest + c - full
            lanes = range(0, LANES, stride) if everywhere else (j * stride,)
            for lane in lanes:
                hits[at, lane + c // HEAD_DIM] = 1.0
    padded = np.zeros((-(-hits.shape[0] // LANES) * LANES, LANES), np.float32)
    padded[: hits.shape[0]] = hits
    blocks = padded.reshape(-1, LANES, LANES).transpose(0, 2, 1).reshape(-1, LANES)
    return jnp.asarray(hits / math.sqrt(HEAD_DIM), BF), jnp.asarray(blocks, BF)


def beside(ref):
    count = ref.shape[0] // LANES
    return jnp.concatenate([ref[b * LANES : (b + 1) * LANES] for b in range(count)], axis=1)


def local_kernel(
    picks_ref, window_ref, query_ref, keyval_ref, to_lanes_ref, to_channels_ref,
    top_ref, sum_ref, mix_ref,
):
    frames, cells, channels = query_ref.shape
    count = picks_ref.shape[1]
    full = channels // LANES * LANES
    stride = LANES // 4
    queries = [query_ref[f] for f in range(frames)]
    keyvals = [keyval_ref[f] for f in range(frames)]
    keys = [kv[:, :full] for kv in keyvals] + [
        jnp.concatenate([kv[:, full:channels] for kv in keyvals], axis=1)
    ]
    values = [kv[:, channels : channels + full].astype(F32) for kv in keyvals] + [
        jnp.concatenate([kv[:, channels + full :] for kv in keyvals], axis=1).astype(F32)
    ]
    products = []
    for q in queries:
        again = jnp.concatenate([q[:, full:]] * frames, axis=1)
        row = [q[:, :full] * k for k in keys[:frames]] + [again * keys[frames]]
        products.append(jnp.concatenate(row, axis=1))
    scores = dot(jnp.concatenate(products, axis=0), to_lanes_ref[...])
    source = lax.div(lax.broadcasted_iota(jnp.int32, (1, LANES), 1), stride)
    window = window_ref[...].reshape(1, 1)
    copies = jnp.zeros((1, LANES), F32)
    for n in range(count):
        copies = copies + jnp.where(source == picks_ref[:, n : n + 1], 1.0, 0.0)
    weights = []
    for i in range(frames):
        times = copies + jnp.where(jnp.abs(source - i) < window, 1.0, 0.0)
        s = jnp.where(times > 0.0, scores[i * cells : (i + 1) * cells], -jnp.inf)
        top = jnp.maximum(s, pltpu.roll(s, stride, 1))
        top = jnp.maximum(top, pltpu.roll(top, 2 * stride, 1))
        w = jnp.exp(s - top) * times
        total = w + pltpu.roll(w, stride, 1)
        total = total + pltpu.roll(total, 2 * stride, 1)
        top_ref[i] = top
        sum_ref[i] = total
        weights.append(w.astype(BF))
    spread = dot(jnp.concatenate(weights, axis=0), beside(to_channels_ref))
    for i in range(frames):
        part = spread[i * cells : (i + 1) * cells]
        wide = part[:, :full] * values[0]
        for j in range(1, frames):
            wide = wide + part[:, j * full : (j + 1) * full] * values[j]
        tail = part[:, frames * full :] * values[frames]
        tail = tail[:, :LANES] + tail[:, LANES:]
        tail = tail + pltpu.roll(tail, LANES // 2, 1)
        mix_ref[i] = jnp.concatenate([wide, tail], axis=1)


def keys_and_values(anchor_ref, wkv_ref, channels):
    return [
        dot(unpacked(anchor_ref[n], channels), wkv_ref[...]).astype(BF)
        for n in range(anchor_ref.shape[0])
    ]


def updated(keyvals, to_lanes_ref, to_channels_ref, query, top, total, mix, last):
    frames, cells, channels = query.shape
    full = channels // LANES * LANES
    size = frames * cells
    query, top, total, mix = (v.reshape(size, v.shape[-1]) for v in (query, top, total, mix))
    low = lax.broadcasted_iota(jnp.int32, (1, LANES), 1) < LANES // 4
    for n, keyval in enumerate(keyvals):
        key = jnp.concatenate([keyval[:, :channels]] * frames, axis=0)
        scores = dot(query * key, to_lanes_ref[...])
        higher = jnp.maximum(top, scores)
        weight = jnp.exp(scores - higher)
        fade = jnp.exp(top - higher)
        total = total * fade + weight
        both = jnp.where(low, weight, fade)
        if last and n == len(keyvals) - 1:
            both = both / total
        spread = dot(both.astype(BF), beside(to_channels_ref))
        value = keyval[:, channels:].astype(F32)
        value = jnp.concatenate([value] * frames, axis=0)
        wide = spread[:, :full] * value[:, :full] + spread[:, full : 2 * full] * mix[:, :full]
        tail = jnp.concatenate([value[:, full:], mix[:, full + LANES // 2 :]], axis=1)
        tail = spread[:, 2 * full :] * tail
        tail = tail + pltpu.roll(tail, LANES // 2, 1)
        mix = jnp.concatenate([wide, tail], axis=1)
        top = higher
    return top, total, mix


def anchor_kernel(
    anchor_ref, wkv_ref, to_lanes_ref, to_channels_ref, query_ref, top_ref, sum_ref, mix_ref,
    top_out, sum_out, mix_out,
):
    new = updated(
        keys_and_values(anchor_ref, wkv_ref, query_ref.shape[2]), to_lanes_ref, to_channels_ref,
        query_ref[...], top_ref[...], sum_ref[...], mix_ref[...], False,
    )
    for ref, v in zip((top_out, sum_out, mix_out), new):
        ref[...] = v.reshape(ref.shape)


def last_kernel(
    anchor_ref, wkv_ref, to_lanes_ref, to_channels_ref, query_ref, top_ref, sum_ref, mix_ref,
    temporal_ref, wo_ref, out_ref, out_buf, sems,
):
    frames, cells, channels = query_ref.shape
    height, width = out_ref.shape[1:3]
    keyvals = keys_and_values(anchor_ref, wkv_ref, channels)
    copies = []
    group = 2 if frames % 2 == 0 else 1
    for lo in range(0, frames, group):
        at = slice(lo, lo + group)
        _, _, mix = updated(
            keyvals, to_lanes_ref, to_channels_ref,
            query_ref[at], top_ref[at], sum_ref[at], mix_ref[at], True,
        )
        result = dot(mix[:, :channels].astype(BF), wo_ref[...])
        total = temporal_ref[at].astype(F32) + result.reshape(group, cells, channels)
        out_buf[at] = total.astype(BF).reshape(group, height, width, channels)
        copies.append(pltpu.make_async_copy(out_buf.at[at], out_ref.at[at], sems.at[lo // group]))
        copies[-1].start()
    for copy in copies:
        copy.wait()


def neighbours(leading, last, axis):
    count = lax.axis_size(axis)
    up = [(i, i + 1) for i in range(count - 1)]
    down = [(j, i) for i, j in up]
    return lax.ppermute(last, axis, up), lax.ppermute(leading, axis, down)


def on_device(
    latents, anchor_index, window, gain_one, spatial_w, gain_two, temporal_w, gain_three,
    w_query, w_keyval, w_out,
):
    frames, height, width, channels = latents.shape
    cells = height * width
    count = anchor_index.shape[1]
    ws = spatial_w.reshape(3, 3 * channels, channels)
    one = 2 * channels * channels
    packed = cells * channels // LANES
    edge_packed = frames * width * channels // LANES
    lanes_up = (channels + LANES - 1) // LANES * LANES
    sem = pltpu.SemaphoreType.DMA
    some = (frames, cells, channels)

    x, g1, g2, g3, w = latents, gain_one, gain_two, gain_three, ws

    top, bottom = call(
        edge_kernel, [((edge_packed, LANES), BF)] * 2, [VMEM], flops=8 * frames * cells * one
    )(x)
    above, below = neighbours(top, bottom, "strip")
    outer_col = pltpu.VMEM((2 * cells, 3 * channels), BF)
    inner_col = pltpu.VMEM(((frames - 2) * (cells + 2 * width), 3 * channels), BF)
    middle = (2, cells - 2 * width, channels)
    mid, mid2, edge, w_rem, order = call(
        outer_kernel,
        [
            (middle, BF),
            (middle, BF),
            ((2, 2, width, channels), F32),
            ((3 * channels, 3 * (channels % 256)), BF),
            ((8, LANES), F32),
        ],
        [VMEM] * 4,
        [outer_col],
        flops=9 * 2 * cells * one,
    )(x, g1, g2, w)
    outer_spatial, outer_hidden, first, last = call(
        functools.partial(outer_edge_kernel, frames),
        [((2, cells, channels), BF)] * 2 + [((packed, LANES), BF)] * 2,
        [VMEM] * 10,
        flops=6 * 2 * width * one,
    )(edge, above, below, order, mid, mid2, g1, g2, w, w_rem)
    before, after = neighbours(first, last, "clip")
    spatial, hidden = call(
        inner_kernel,
        [(some, BF), (some, BF)],
        [VMEM] * 9,
        [inner_col],
        flops=9 * (frames - 2) * cells * one,
    )(x, above, below, g1, g2, w, w_rem, outer_spatial, outer_hidden)
    (chosen,) = call(
        chosen_kernel, [((count, packed, LANES), BF)], [VMEM] * 7, flops=3 * cells * one
    )(anchor_index, before, after, spatial, hidden, g3, temporal_w)
    clips = lax.axis_size("clip")
    arrived = [
        lax.ppermute(chosen, "clip", [(i, (i + s) % clips) for i in range(clips)])
        for s in range(1, clips)
    ]
    temporal, query, keyval = call(
        temporal_kernel,
        [(some, BF), (some, BF), ((frames, cells, 2 * channels), BF)],
        [VMEM] * 8,
        flops=6 * frames * cells * one,
        limit=32,
    )(before, after, spatial, hidden, g3, temporal_w, w_query, w_keyval)
    states = [((frames, cells, LANES), F32)] * 2 + [((frames, cells, lanes_up), F32)]
    state = call(
        local_kernel, states, [VMEM] * 6, flops=10 * frames * cells * one, limit=32
    )(anchor_index, window, query, keyval, *head_maps(frames, channels))
    to_lanes, _ = head_maps(1, channels, everywhere=True)
    _, to_channels = head_maps(2, channels)
    for arrival in arrived[:-1]:
        state = call(
            anchor_kernel, states, [VMEM] * 8, flops=4 * frames * cells * one, limit=32
        )(arrival, w_keyval, to_lanes, to_channels, query, *state)
    (out,) = call(
        last_kernel,
        [(latents.shape, BF)],
        [VMEM] * 10,
        [pltpu.VMEM(latents.shape, BF), sem((frames,))],
        flops=5 * frames * cells * one,
        limit=32,
        out_specs=(HBM,),
    )(arrived[-1], w_keyval, to_lanes, to_channels, query, *state, temporal, w_out)
    return out


def solution(mesh):
    return jax.shard_map(
        on_device,
        mesh=mesh,
        in_specs=(
            P(("groups", "clip"), "strip", None, None),
            P(("groups", "clip"), None),
            P(),
            P(),
            P(),
            P(),
            P(),
            P(),
            P(),
            P(),
            P(),
        ),
        out_specs=P(("groups", "clip"), "strip", None, None),
        check_vma=False,
    )
```

```python
import functools
import math

import jax
import jax.numpy as jnp
import numpy as np
from jax import lax
from jax.experimental import pallas as pl
from jax.experimental.pallas import tpu as pltpu
from jax.sharding import PartitionSpec as P

HEADS = 5
HEAD_DIM = 64
LANES = 128
BF = jnp.bfloat16
F32 = jnp.float32
VMEM = pl.BlockSpec(memory_space=pltpu.VMEM)
HBM = pl.BlockSpec(memory_space=pltpu.HBM)
MIB = 1 << 20


def call(body, outs, specs, scratch=(), flops=0, limit=24, out_specs=None):
    return pl.pallas_call(
        body,
        out_shape=tuple(jax.ShapeDtypeStruct(s, d) for s, d in outs),
        in_specs=specs,
        out_specs=out_specs or tuple(VMEM for _ in outs),
        scratch_shapes=list(scratch),
        cost_estimate=pl.CostEstimate(flops=flops, bytes_accessed=2 * MIB, transcendentals=0),
        compiler_params=pltpu.CompilerParams(vmem_limit_bytes=limit * MIB),
    )


def dot(a, b):
    return jnp.dot(a, b, preferred_element_type=F32)


def norm(v, gain_ref):
    wide = v.astype(F32)
    centred = wide - jnp.mean(wide, axis=-1, keepdims=True)
    variance = jnp.mean(centred * centred, axis=-1, keepdims=True)
    return centred * lax.rsqrt(variance + 1e-05) * gain_ref[...].reshape(1, v.shape[1])


def silu(u):
    half = 0.5 * u
    return half + half * jnp.tanh(half)


def pack_into(ref, h):
    cells, channels = h.shape
    full = channels // LANES
    for t in range(full):
        ref[t * cells : (t + 1) * cells, :] = h[:, t * LANES : (t + 1) * LANES]
    rest = channels - full * LANES
    if rest:
        share = LANES // rest
        part = cells // share
        ref[full * cells :, :] = jnp.concatenate(
            [h[s * part : (s + 1) * part, full * LANES :] for s in range(share)], axis=1
        )


def unpacked(p, channels):
    cells = p.shape[0] * LANES // channels
    full = channels // LANES
    pieces = [p[t * cells : (t + 1) * cells, :] for t in range(full)]
    rest = channels - full * LANES
    if rest:
        share = LANES // rest
        tail = p[full * cells :, :]
        pieces.append(
            jnp.concatenate([tail[:, s * rest : (s + 1) * rest] for s in range(share)], axis=0)
        )
    return jnp.concatenate(pieces, axis=1)


def columns(h, width):
    cells, channels = h.shape
    left = pltpu.roll(h, 1, 0)
    right = pltpu.roll(h, cells - 1, 0)
    place = lax.broadcasted_iota(jnp.int32, (8, channels), 0)
    lefts, rights = [], []
    for lo in range(0, cells, width):
        hi = lo + width
        lefts += [jnp.where(place == 0, 0.0, left[lo : lo + 8]), left[lo + 8 : hi]]
        rights += [right[lo : hi - 8], jnp.where(place == 7, 0.0, right[hi - 8 : hi])]
    sides = [jnp.concatenate(lefts, axis=0), h, jnp.concatenate(rights, axis=0)]
    return jnp.concatenate([v.astype(BF) for v in sides], axis=1)


def scalar(ref, n):
    values = ref[...].astype(F32)
    place = lax.broadcasted_iota(jnp.int32, values.shape, 1)
    return jnp.sum(jnp.where(place == n, values, 0.0)).astype(jnp.int32)


def at_odd(axis):
    return lax.rem(lax.axis_index(axis), 2) == 1


def sorted_pair(odd_ref, even_ref, axis):
    odd = at_odd(axis)
    first, second = odd_ref[...], even_ref[...]
    return jnp.where(odd, second, first), jnp.where(odd, first, second)


def edge_kernel(x_ref, odd_ref, even_ref):
    frames, height, width, channels = x_ref.shape
    odd = at_odd("strip")
    top = x_ref[:, 0].reshape(frames * width, channels)
    bottom = x_ref[:, height - 1].reshape(frames * width, channels)
    pack_into(odd_ref, jnp.where(odd, bottom, top))
    pack_into(even_ref, jnp.where(odd, top, bottom))


def rests_into(rem_ref, w_ref):
    full = w_ref.shape[2] // 256 * 256
    rest = w_ref.shape[2] - full
    for a in range(3):
        rem_ref[:, a * rest : (a + 1) * rest] = w_ref[a, :, full:]


def hidden_columns(v, g1_ref, width):
    return columns(silu(norm(v, g1_ref)), width)


def stacked_rows(col_ref, count, height, width, w_ref, rem_ref):
    cells = height * width
    rims = (col_ref.shape[0] - count * cells) // 2
    channels = w_ref.shape[2]
    full = channels // 256 * 256
    rest = channels - full
    size = count * cells
    above = dot(col_ref[: rims + size], w_ref[0, :, :full])
    centre = dot(col_ref[rims : rims + size], w_ref[1, :, :full])
    below = dot(col_ref[rims:], w_ref[2, :, :full])
    tails = dot(col_ref[...], rem_ref[...])

    def terms(place, row):
        own = place * cells + row * width
        wide = centre[own : own + width]
        tail = tails[rims + own : rims + own + width, rest : 2 * rest]
        if row > 0 or rims:
            at = rims + own - width if row > 0 else place * width
            wide = wide + above[at : at + width]
            tail = tail + tails[at : at + width, :rest]
        if row < height - 1 or rims:
            at = own + width if row < height - 1 else size + place * width
            wide = wide + below[at : at + width]
            tail = tail + tails[rims + at : rims + at + width, 2 * rest :]
        return jnp.concatenate([wide, tail], axis=1)

    return terms


def rim_rows(packed, frames, width, channels):
    rows = unpacked(packed, channels)
    return jnp.concatenate([rows[f * width : (f + 1) * width] for f in frames], axis=0)


def outer_kernel(x_ref, g1_ref, g2_ref, w_ref, mid_ref, mid2_ref, edge_ref, rem_ref, order_ref, col_ref):
    frames, height, width, channels = x_ref.shape
    cells = height * width
    order_ref[...] = jnp.zeros_like(order_ref)
    rests_into(rem_ref, w_ref)
    outer = (0, frames - 1)
    for s, f in enumerate(outer):
        x = x_ref[f].reshape(cells, channels)
        col_ref[s * cells : (s + 1) * cells] = hidden_columns(x, g1_ref, width)
    terms = stacked_rows(col_ref, 2, height, width, w_ref, rem_ref)
    for s, f in enumerate(outer):
        for row in range(height):
            total = x_ref[f, row].astype(F32) + terms(s, row)
            if 0 < row < height - 1:
                rounded = total.astype(BF)
                lo = (row - 1) * width
                mid_ref[s, lo : lo + width] = rounded
                mid2_ref[s, lo : lo + width] = silu(norm(rounded, g2_ref)).astype(BF)
            else:
                edge_ref[s, 0 if row == 0 else 1] = total


def outer_edge_kernel(
    frames, edge_ref, odd_ref, even_ref, order_ref, mid_ref, mid2_ref, g1_ref, g2_ref, w_ref, rem_ref,
    spatial_ref, hidden_ref, odd_clip_ref, even_clip_ref,
):
    _, cells, channels = spatial_ref.shape
    width = edge_ref.shape[2]
    full = channels // 256 * 256
    rest = channels - full
    spatial_ref[:, width : cells - width] = mid_ref[...]
    hidden_ref[:, width : cells - width] = mid2_ref[...]
    cols = [
        hidden_columns(rim_rows(packed, (0, frames - 1), width, channels), g1_ref, width)
        for packed in sorted_pair(odd_ref, even_ref, "strip")
    ]
    tails = dot(jnp.concatenate(cols, axis=0), rem_ref[...])
    size = 2 * width
    for side, lo in ((0, 0), (1, cells - width)):
        tail = tails[:size, :rest] if side == 0 else tails[size:, 2 * rest :]
        wide = dot(cols[side], w_ref[2 * side, :, :full])
        term = jnp.concatenate([wide, tail], axis=1)
        rounded = (edge_ref[:, side].reshape(size, channels) + term).astype(BF)
        hidden = silu(norm(rounded, g2_ref)).astype(BF)
        spatial_ref[:, lo : lo + width] = rounded.reshape(2, width, channels)
        hidden_ref[:, lo : lo + width] = hidden.reshape(2, width, channels)
    odd = at_odd("clip")
    pack_into(odd_clip_ref, jnp.where(odd, hidden_ref[1], hidden_ref[0]))
    pack_into(even_clip_ref, jnp.where(odd, hidden_ref[0], hidden_ref[1]))


def inner_kernel(
    x_ref, odd_ref, even_ref, g1_ref, g2_ref, w_ref, rem_ref, outer_spatial_ref, outer_hidden_ref,
    spatial_ref, hidden_ref, col_ref,
):
    frames, height, width, channels = x_ref.shape
    cells = height * width
    for s, f in ((0, 0), (1, frames - 1)):
        spatial_ref[f] = outer_spatial_ref[s]
        hidden_ref[f] = outer_hidden_ref[s]
    inside = range(1, frames - 1)
    above, below = sorted_pair(odd_ref, even_ref, "strip")
    rims = len(inside) * width
    end = rims + len(inside) * cells
    col_ref[:rims] = hidden_columns(rim_rows(above, inside, width, channels), g1_ref, width)
    for s, f in enumerate(inside):
        x = x_ref[f].reshape(cells, channels)
        lo = rims + s * cells
        col_ref[lo : lo + cells] = hidden_columns(x, g1_ref, width)
    col_ref[end:] = hidden_columns(rim_rows(below, inside, width, channels), g1_ref, width)
    terms = stacked_rows(col_ref, len(inside), height, width, w_ref, rem_ref)
    for s, f in enumerate(inside):
        for row in range(height):
            rounded = (x_ref[f, row].astype(F32) + terms(s, row)).astype(BF)
            lo = row * width
            spatial_ref[f, lo : lo + width] = rounded
            hidden_ref[f, lo : lo + width] = silu(norm(rounded, g2_ref)).astype(BF)


def chosen_kernel(
    picks_ref, odd_ref, even_ref, spatial_ref, hidden_ref, g3_ref, wt_ref, chosen_ref
):
    frames, cells, channels = spatial_ref.shape
    before, after = (unpacked(v, channels) for v in sorted_pair(odd_ref, even_ref, "clip"))
    for n in range(chosen_ref.shape[0]):
        pick = scalar(picks_ref, n)
        earlier = jnp.where(pick == 0, before, hidden_ref[jnp.maximum(pick - 1, 0)])
        later = jnp.where(pick == frames - 1, after, hidden_ref[jnp.minimum(pick + 1, frames - 1)])
        total = spatial_ref[pick].astype(F32) + dot(hidden_ref[pick], wt_ref[1])
        total = total + dot(earlier, wt_ref[0]) + dot(later, wt_ref[2])
        pack_into(chosen_ref.at[n], norm(total.astype(BF), g3_ref).astype(BF))


def temporal_kernel(
    odd_ref, even_ref, spatial_ref, hidden_ref, g3_ref, wt_ref, wq_ref, wkv_ref,
    temporal_ref, query_ref, keyval_ref,
):
    frames, cells, channels = spatial_ref.shape
    size = frames * cells
    before, after = (unpacked(v, channels) for v in sorted_pair(odd_ref, even_ref, "clip"))
    hidden = hidden_ref[...].reshape(size, channels)
    total = spatial_ref[...].reshape(size, channels).astype(F32) + dot(hidden, wt_ref[1])
    total = total + dot(jnp.concatenate([before, hidden[: size - cells]], axis=0), wt_ref[0])
    total = total + dot(jnp.concatenate([hidden[cells:], after], axis=0), wt_ref[2])
    temporal = total.astype(BF)
    temporal_ref[...] = temporal.reshape(frames, cells, channels)
    normed = norm(temporal, g3_ref).astype(BF)
    query_ref[...] = dot(normed, wq_ref[...]).astype(BF).reshape(frames, cells, channels)
    keyval_ref[...] = dot(normed, wkv_ref[...]).astype(BF).reshape(frames, cells, 2 * channels)


def head_maps(count, channels, everywhere=False):
    full = channels // LANES * LANES
    rest = channels - full
    stride = LANES // 4
    hits = np.zeros((count * channels, LANES), np.float32)
    for j in range(count):
        for c in range(channels):
            at = j * full + c if c < full else count * full + j * rest + c - full
            lanes = range(0, LANES, stride) if everywhere else (j * stride,)
            for lane in lanes:
                hits[at, lane + c // HEAD_DIM] = 1.0
    padded = np.zeros((-(-hits.shape[0] // LANES) * LANES, LANES), np.float32)
    padded[: hits.shape[0]] = hits
    blocks = padded.reshape(-1, LANES, LANES).transpose(0, 2, 1).reshape(-1, LANES)
    return jnp.asarray(hits / math.sqrt(HEAD_DIM), BF), jnp.asarray(blocks, BF)


def beside(ref):
    count = ref.shape[0] // LANES
    return jnp.concatenate([ref[b * LANES : (b + 1) * LANES] for b in range(count)], axis=1)


def local_kernel(
    picks_ref, window_ref, query_ref, keyval_ref, to_lanes_ref, to_channels_ref,
    top_ref, sum_ref, mix_ref,
):
    frames, cells, channels = query_ref.shape
    count = picks_ref.shape[1]
    full = channels // LANES * LANES
    stride = LANES // 4
    queries = [query_ref[f] for f in range(frames)]
    keyvals = [keyval_ref[f] for f in range(frames)]
    keys = [kv[:, :full] for kv in keyvals] + [
        jnp.concatenate([kv[:, full:channels] for kv in keyvals], axis=1)
    ]
    values = [kv[:, channels : channels + full].astype(F32) for kv in keyvals] + [
        jnp.concatenate([kv[:, channels + full :] for kv in keyvals], axis=1).astype(F32)
    ]
    products = []
    for q in queries:
        again = jnp.concatenate([q[:, full:]] * frames, axis=1)
        row = [q[:, :full] * k for k in keys[:frames]] + [again * keys[frames]]
        products.append(jnp.concatenate(row, axis=1))
    scores = dot(jnp.concatenate(products, axis=0), to_lanes_ref[...])
    source = lax.div(lax.broadcasted_iota(jnp.int32, (1, LANES), 1), stride)
    window = window_ref[...].reshape(1, 1)
    copies = jnp.zeros((1, LANES), F32)
    for n in range(count):
        copies = copies + jnp.where(source == picks_ref[:, n : n + 1], 1.0, 0.0)
    weights = []
    for i in range(frames):
        times = copies + jnp.where(jnp.abs(source - i) < window, 1.0, 0.0)
        s = jnp.where(times > 0.0, scores[i * cells : (i + 1) * cells], -jnp.inf)
        top = jnp.maximum(s, pltpu.roll(s, stride, 1))
        top = jnp.maximum(top, pltpu.roll(top, 2 * stride, 1))
        w = jnp.exp(s - top) * times
        total = w + pltpu.roll(w, stride, 1)
        total = total + pltpu.roll(total, 2 * stride, 1)
        top_ref[i] = top
        sum_ref[i] = total
        weights.append(w.astype(BF))
    spread = dot(jnp.concatenate(weights, axis=0), beside(to_channels_ref))
    for i in range(frames):
        part = spread[i * cells : (i + 1) * cells]
        wide = part[:, :full] * values[0]
        for j in range(1, frames):
            wide = wide + part[:, j * full : (j + 1) * full] * values[j]
        tail = part[:, frames * full :] * values[frames]
        tail = tail[:, :LANES] + tail[:, LANES:]
        tail = tail + pltpu.roll(tail, LANES // 2, 1)
        mix_ref[i] = jnp.concatenate([wide, tail], axis=1)


def keys_and_values(anchor_ref, wkv_ref, channels):
    return [
        dot(unpacked(anchor_ref[n], channels), wkv_ref[...]).astype(BF)
        for n in range(anchor_ref.shape[0])
    ]


def updated(keyvals, to_lanes_ref, to_channels_ref, query, top, total, mix, last):
    frames, cells, channels = query.shape
    full = channels // LANES * LANES
    size = frames * cells
    query, top, total, mix = (v.reshape(size, v.shape[-1]) for v in (query, top, total, mix))
    low = lax.broadcasted_iota(jnp.int32, (1, LANES), 1) < LANES // 4
    for n, keyval in enumerate(keyvals):
        key = jnp.concatenate([keyval[:, :channels]] * frames, axis=0)
        scores = dot(query * key, to_lanes_ref[...])
        higher = jnp.maximum(top, scores)
        weight = jnp.exp(scores - higher)
        fade = jnp.exp(top - higher)
        total = total * fade + weight
        both = jnp.where(low, weight, fade)
        if last and n == len(keyvals) - 1:
            both = both / total
        spread = dot(both.astype(BF), beside(to_channels_ref))
        value = keyval[:, channels:].astype(F32)
        value = jnp.concatenate([value] * frames, axis=0)
        wide = spread[:, :full] * value[:, :full] + spread[:, full : 2 * full] * mix[:, :full]
        tail = jnp.concatenate([value[:, full:], mix[:, full + LANES // 2 :]], axis=1)
        tail = spread[:, 2 * full :] * tail
        tail = tail + pltpu.roll(tail, LANES // 2, 1)
        mix = jnp.concatenate([wide, tail], axis=1)
        top = higher
    return top, total, mix


def anchor_kernel(
    anchor_ref, wkv_ref, to_lanes_ref, to_channels_ref, query_ref, top_ref, sum_ref, mix_ref,
    top_out, sum_out, mix_out,
):
    new = updated(
        keys_and_values(anchor_ref, wkv_ref, query_ref.shape[2]), to_lanes_ref, to_channels_ref,
        query_ref[...], top_ref[...], sum_ref[...], mix_ref[...], False,
    )
    for ref, v in zip((top_out, sum_out, mix_out), new):
        ref[...] = v.reshape(ref.shape)


def last_kernel(
    anchor_ref, wkv_ref, to_lanes_ref, to_channels_ref, query_ref, top_ref, sum_ref, mix_ref,
    temporal_ref, wo_ref, out_ref, out_buf, sems,
):
    frames, cells, channels = query_ref.shape
    height, width = out_ref.shape[1:3]
    keyvals = keys_and_values(anchor_ref, wkv_ref, channels)
    copies = []
    group = 2 if frames % 2 == 0 else 1
    for lo in range(0, frames, group):
        at = slice(lo, lo + group)
        _, _, mix = updated(
            keyvals, to_lanes_ref, to_channels_ref,
            query_ref[at], top_ref[at], sum_ref[at], mix_ref[at], True,
        )
        result = dot(mix[:, :channels].astype(BF), wo_ref[...])
        total = temporal_ref[at].astype(F32) + result.reshape(group, cells, channels)
        out_buf[at] = total.astype(BF).reshape(group, height, width, channels)
        copies.append(pltpu.make_async_copy(out_buf.at[at], out_ref.at[at], sems.at[lo // group]))
        copies[-1].start()
    for copy in copies:
        copy.wait()


def swapped(odd, even, axis):
    count = lax.axis_size(axis)
    pairs = [[(i, i + 1) for i in range(start, count - 1, 2)] for start in (1, 0)]
    pairs = [up + [(j, i) for i, j in up] for up in pairs]
    return lax.ppermute(odd, axis, pairs[0]), lax.ppermute(even, axis, pairs[1])


def on_device(
    latents, anchor_index, window, gain_one, spatial_w, gain_two, temporal_w, gain_three,
    w_query, w_keyval, w_out,
):
    frames, height, width, channels = latents.shape
    cells = height * width
    count = anchor_index.shape[1]
    ws = spatial_w.reshape(3, 3 * channels, channels)
    one = 2 * channels * channels
    packed = cells * channels // LANES
    edge_packed = frames * width * channels // LANES
    lanes_up = (channels + LANES - 1) // LANES * LANES
    sem = pltpu.SemaphoreType.DMA
    some = (frames, cells, channels)

    x, g1, g2, g3, w = latents, gain_one, gain_two, gain_three, ws

    strip_odd, strip_even = call(
        edge_kernel, [((edge_packed, LANES), BF)] * 2, [VMEM], flops=8 * frames * cells * one
    )(x)
    strip_odd, strip_even = swapped(strip_odd, strip_even, "strip")
    outer_col = pltpu.VMEM((2 * cells, 3 * channels), BF)
    inner_col = pltpu.VMEM(((frames - 2) * (cells + 2 * width), 3 * channels), BF)
    middle = (2, cells - 2 * width, channels)
    mid, mid2, edge, w_rem, order = call(
        outer_kernel,
        [
            (middle, BF),
            (middle, BF),
            ((2, 2, width, channels), F32),
            ((3 * channels, 3 * (channels % 256)), BF),
            ((8, LANES), F32),
        ],
        [VMEM] * 4,
        [outer_col],
        flops=9 * 2 * cells * one,
    )(x, g1, g2, w)
    outer_spatial, outer_hidden, clip_odd, clip_even = call(
        functools.partial(outer_edge_kernel, frames),
        [((2, cells, channels), BF)] * 2 + [((packed, LANES), BF)] * 2,
        [VMEM] * 10,
        flops=6 * 2 * width * one,
    )(edge, strip_odd, strip_even, order, mid, mid2, g1, g2, w, w_rem)
    clip_odd, clip_even = swapped(clip_odd, clip_even, "clip")
    spatial, hidden = call(
        inner_kernel,
        [(some, BF), (some, BF)],
        [VMEM] * 9,
        [inner_col],
        flops=9 * (frames - 2) * cells * one,
    )(x, strip_odd, strip_even, g1, g2, w, w_rem, outer_spatial, outer_hidden)
    (chosen,) = call(
        chosen_kernel, [((count, packed, LANES), BF)], [VMEM] * 7, flops=3 * cells * one
    )(anchor_index, clip_odd, clip_even, spatial, hidden, g3, temporal_w)
    clips = lax.axis_size("clip")
    arrived = [
        lax.ppermute(chosen, "clip", [(i, (i + s) % clips) for i in range(clips)])
        for s in range(1, clips)
    ]
    temporal, query, keyval = call(
        temporal_kernel,
        [(some, BF), (some, BF), ((frames, cells, 2 * channels), BF)],
        [VMEM] * 8,
        flops=6 * frames * cells * one,
        limit=32,
    )(clip_odd, clip_even, spatial, hidden, g3, temporal_w, w_query, w_keyval)
    states = [((frames, cells, LANES), F32)] * 2 + [((frames, cells, lanes_up), F32)]
    state = call(
        local_kernel, states, [VMEM] * 6, flops=10 * frames * cells * one, limit=32
    )(anchor_index, window, query, keyval, *head_maps(frames, channels))
    to_lanes, _ = head_maps(1, channels, everywhere=True)
    _, to_channels = head_maps(2, channels)
    for arrival in arrived[:-1]:
        state = call(
            anchor_kernel, states, [VMEM] * 8, flops=4 * frames * cells * one, limit=32
        )(arrival, w_keyval, to_lanes, to_channels, query, *state)
    (out,) = call(
        last_kernel,
        [(latents.shape, BF)],
        [VMEM] * 10,
        [pltpu.VMEM(latents.shape, BF), sem((frames,))],
        flops=5 * frames * cells * one,
        limit=32,
        out_specs=(HBM,),
    )(arrived[-1], w_keyval, to_lanes, to_channels, query, *state, temporal, w_out)
    return out


def solution(mesh):
    return jax.shard_map(
        on_device,
        mesh=mesh,
        in_specs=(
            P(("groups", "clip"), "strip", None, None),
            P(("groups", "clip"), None),
            P(),
            P(),
            P(),
            P(),
            P(),
            P(),
            P(),
            P(),
            P(),
        ),
        out_specs=P(("groups", "clip"), "strip", None, None),
        check_vma=False,
    )
```

```python
import functools
import math

import jax
import jax.numpy as jnp
import numpy as np
from jax import lax
from jax.experimental import pallas as pl
from jax.experimental.pallas import tpu as pltpu
from jax.sharding import PartitionSpec as P

HEADS = 5
HEAD_DIM = 64
LANES = 128
BF = jnp.bfloat16
F32 = jnp.float32
VMEM = pl.BlockSpec(memory_space=pltpu.VMEM)
HBM = pl.BlockSpec(memory_space=pltpu.HBM)
MIB = 1 << 20


def call(body, outs, specs, scratch=(), flops=0, limit=24, out_specs=None):
    return pl.pallas_call(
        body,
        out_shape=tuple(jax.ShapeDtypeStruct(s, d) for s, d in outs),
        in_specs=specs,
        out_specs=out_specs or tuple(VMEM for _ in outs),
        scratch_shapes=list(scratch),
        cost_estimate=pl.CostEstimate(flops=flops, bytes_accessed=2 * MIB, transcendentals=0),
        compiler_params=pltpu.CompilerParams(vmem_limit_bytes=limit * MIB),
    )


def dot(a, b):
    return jnp.dot(a, b, preferred_element_type=F32)


def norm(v, gain_ref):
    wide = v.astype(F32)
    centred = wide - jnp.mean(wide, axis=-1, keepdims=True)
    variance = jnp.mean(centred * centred, axis=-1, keepdims=True)
    return centred * lax.rsqrt(variance + 1e-05) * gain_ref[...].reshape(1, v.shape[1])


def silu(u):
    half = 0.5 * u
    return half + half * jnp.tanh(half)


def pack_into(ref, h):
    cells, channels = h.shape
    full = channels // LANES
    for t in range(full):
        ref[t * cells : (t + 1) * cells, :] = h[:, t * LANES : (t + 1) * LANES]
    rest = channels - full * LANES
    if rest:
        share = LANES // rest
        part = cells // share
        ref[full * cells :, :] = jnp.concatenate(
            [h[s * part : (s + 1) * part, full * LANES :] for s in range(share)], axis=1
        )


def unpacked(p, channels):
    cells = p.shape[0] * LANES // channels
    full = channels // LANES
    pieces = [p[t * cells : (t + 1) * cells, :] for t in range(full)]
    rest = channels - full * LANES
    if rest:
        share = LANES // rest
        tail = p[full * cells :, :]
        pieces.append(
            jnp.concatenate([tail[:, s * rest : (s + 1) * rest] for s in range(share)], axis=0)
        )
    return jnp.concatenate(pieces, axis=1)


def columns(h, width):
    cells, channels = h.shape
    left = pltpu.roll(h, 1, 0)
    right = pltpu.roll(h, cells - 1, 0)
    place = lax.broadcasted_iota(jnp.int32, (8, channels), 0)
    lefts, rights = [], []
    for lo in range(0, cells, width):
        hi = lo + width
        lefts += [jnp.where(place == 0, 0.0, left[lo : lo + 8]), left[lo + 8 : hi]]
        rights += [right[lo : hi - 8], jnp.where(place == 7, 0.0, right[hi - 8 : hi])]
    sides = [jnp.concatenate(lefts, axis=0), h, jnp.concatenate(rights, axis=0)]
    return jnp.concatenate([v.astype(BF) for v in sides], axis=1)


def scalar(ref, n):
    values = ref[...].astype(F32)
    place = lax.broadcasted_iota(jnp.int32, values.shape, 1)
    return jnp.sum(jnp.where(place == n, values, 0.0)).astype(jnp.int32)


def at_odd(axis):
    return lax.rem(lax.axis_index(axis), 2) == 1


def sorted_pair(odd_ref, even_ref, axis):
    odd = at_odd(axis)
    first, second = odd_ref[...], even_ref[...]
    return jnp.where(odd, second, first), jnp.where(odd, first, second)


def edge_kernel(x_ref, odd_ref, even_ref):
    frames, height, width, channels = x_ref.shape
    odd = at_odd("strip")
    top = x_ref[:, 0].reshape(frames * width, channels)
    bottom = x_ref[:, height - 1].reshape(frames * width, channels)
    pack_into(odd_ref, jnp.where(odd, bottom, top))
    pack_into(even_ref, jnp.where(odd, top, bottom))


def rests_into(rem_ref, w_ref):
    full = w_ref.shape[2] // 256 * 256
    rest = w_ref.shape[2] - full
    for a in range(3):
        rem_ref[:, a * rest : (a + 1) * rest] = w_ref[a, :, full:]


def hidden_columns(v, g1_ref, width):
    return columns(silu(norm(v, g1_ref)), width)


def stacked_rows(col_ref, count, height, width, w_ref, rem_ref):
    cells = height * width
    rims = (col_ref.shape[0] - count * cells) // 2
    channels = w_ref.shape[2]
    full = channels // 256 * 256
    rest = channels - full
    size = count * cells
    above = dot(col_ref[: rims + size], w_ref[0, :, :full])
    centre = dot(col_ref[rims : rims + size], w_ref[1, :, :full])
    below = dot(col_ref[rims:], w_ref[2, :, :full])
    tails = dot(col_ref[...], rem_ref[...])

    def terms(place, row):
        own = place * cells + row * width
        wide = centre[own : own + width]
        tail = tails[rims + own : rims + own + width, rest : 2 * rest]
        if row > 0 or rims:
            at = rims + own - width if row > 0 else place * width
            wide = wide + above[at : at + width]
            tail = tail + tails[at : at + width, :rest]
        if row < height - 1 or rims:
            at = own + width if row < height - 1 else size + place * width
            wide = wide + below[at : at + width]
            tail = tail + tails[rims + at : rims + at + width, 2 * rest :]
        return jnp.concatenate([wide, tail], axis=1)

    return terms


def rim_rows(packed, frames, width, channels):
    rows = unpacked(packed, channels)
    return jnp.concatenate([rows[f * width : (f + 1) * width] for f in frames], axis=0)


def outer_kernel(x_ref, g1_ref, g2_ref, w_ref, mid_ref, mid2_ref, edge_ref, rem_ref, order_ref, col_ref):
    frames, height, width, channels = x_ref.shape
    cells = height * width
    order_ref[...] = jnp.zeros_like(order_ref)
    rests_into(rem_ref, w_ref)
    outer = (0, frames - 1)
    for s, f in enumerate(outer):
        x = x_ref[f].reshape(cells, channels)
        col_ref[s * cells : (s + 1) * cells] = hidden_columns(x, g1_ref, width)
    terms = stacked_rows(col_ref, 2, height, width, w_ref, rem_ref)
    for s, f in enumerate(outer):
        for row in range(height):
            total = x_ref[f, row].astype(F32) + terms(s, row)
            if 0 < row < height - 1:
                rounded = total.astype(BF)
                lo = (row - 1) * width
                mid_ref[s, lo : lo + width] = rounded
                mid2_ref[s, lo : lo + width] = silu(norm(rounded, g2_ref)).astype(BF)
            else:
                edge_ref[s, 0 if row == 0 else 1] = total


def outer_edge_kernel(
    frames, edge_ref, odd_ref, even_ref, order_ref, mid_ref, mid2_ref, g1_ref, g2_ref, w_ref, rem_ref,
    spatial_ref, hidden_ref, odd_clip_ref, even_clip_ref,
):
    _, cells, channels = spatial_ref.shape
    width = edge_ref.shape[2]
    full = channels // 256 * 256
    rest = channels - full
    spatial_ref[:, width : cells - width] = mid_ref[...]
    hidden_ref[:, width : cells - width] = mid2_ref[...]
    cols = [
        hidden_columns(rim_rows(packed, (0, frames - 1), width, channels), g1_ref, width)
        for packed in sorted_pair(odd_ref, even_ref, "strip")
    ]
    tails = dot(jnp.concatenate(cols, axis=0), rem_ref[...])
    size = 2 * width
    for side, lo in ((0, 0), (1, cells - width)):
        tail = tails[:size, :rest] if side == 0 else tails[size:, 2 * rest :]
        wide = dot(cols[side], w_ref[2 * side, :, :full])
        term = jnp.concatenate([wide, tail], axis=1)
        rounded = (edge_ref[:, side].reshape(size, channels) + term).astype(BF)
        hidden = silu(norm(rounded, g2_ref)).astype(BF)
        spatial_ref[:, lo : lo + width] = rounded.reshape(2, width, channels)
        hidden_ref[:, lo : lo + width] = hidden.reshape(2, width, channels)
    odd = at_odd("clip")
    pack_into(odd_clip_ref, jnp.where(odd, hidden_ref[1], hidden_ref[0]))
    pack_into(even_clip_ref, jnp.where(odd, hidden_ref[0], hidden_ref[1]))


def inner_kernel(
    x_ref, odd_ref, even_ref, g1_ref, g2_ref, w_ref, rem_ref, outer_spatial_ref, outer_hidden_ref,
    spatial_ref, hidden_ref, col_ref,
):
    frames, height, width, channels = x_ref.shape
    cells = height * width
    for s, f in ((0, 0), (1, frames - 1)):
        spatial_ref[f] = outer_spatial_ref[s]
        hidden_ref[f] = outer_hidden_ref[s]
    inside = range(1, frames - 1)
    above, below = sorted_pair(odd_ref, even_ref, "strip")
    rims = len(inside) * width
    end = rims + len(inside) * cells
    col_ref[:rims] = hidden_columns(rim_rows(above, inside, width, channels), g1_ref, width)
    for s, f in enumerate(inside):
        x = x_ref[f].reshape(cells, channels)
        lo = rims + s * cells
        col_ref[lo : lo + cells] = hidden_columns(x, g1_ref, width)
    col_ref[end:] = hidden_columns(rim_rows(below, inside, width, channels), g1_ref, width)
    terms = stacked_rows(col_ref, len(inside), height, width, w_ref, rem_ref)
    for s, f in enumerate(inside):
        for row in range(height):
            rounded = (x_ref[f, row].astype(F32) + terms(s, row)).astype(BF)
            lo = row * width
            spatial_ref[f, lo : lo + width] = rounded
            hidden_ref[f, lo : lo + width] = silu(norm(rounded, g2_ref)).astype(BF)


def chosen_kernel(
    picks_ref, odd_ref, even_ref, spatial_ref, hidden_ref, g3_ref, wt_ref, chosen_ref
):
    frames, cells, channels = spatial_ref.shape
    before, after = (unpacked(v, channels) for v in sorted_pair(odd_ref, even_ref, "clip"))
    for n in range(chosen_ref.shape[0]):
        pick = scalar(picks_ref, n)
        earlier = jnp.where(pick == 0, before, hidden_ref[jnp.maximum(pick - 1, 0)])
        later = jnp.where(pick == frames - 1, after, hidden_ref[jnp.minimum(pick + 1, frames - 1)])
        total = spatial_ref[pick].astype(F32) + dot(hidden_ref[pick], wt_ref[1])
        total = total + dot(earlier, wt_ref[0]) + dot(later, wt_ref[2])
        pack_into(chosen_ref.at[n], norm(total.astype(BF), g3_ref).astype(BF))


def temporal_kernel(
    odd_ref, even_ref, spatial_ref, hidden_ref, g3_ref, wt_ref, wq_ref, wkv_ref,
    temporal_ref, query_ref, keyval_ref,
):
    frames, cells, channels = spatial_ref.shape
    size = frames * cells
    before, after = (unpacked(v, channels) for v in sorted_pair(odd_ref, even_ref, "clip"))
    hidden = hidden_ref[...].reshape(size, channels)
    total = spatial_ref[...].reshape(size, channels).astype(F32) + dot(hidden, wt_ref[1])
    total = total + dot(jnp.concatenate([before, hidden[: size - cells]], axis=0), wt_ref[0])
    total = total + dot(jnp.concatenate([hidden[cells:], after], axis=0), wt_ref[2])
    temporal = total.astype(BF)
    temporal_ref[...] = temporal.reshape(frames, cells, channels)
    normed = norm(temporal, g3_ref).astype(BF)
    query_ref[...] = dot(normed, wq_ref[...]).astype(BF).reshape(frames, cells, channels)
    keyval_ref[...] = dot(normed, wkv_ref[...]).astype(BF).reshape(frames, cells, 2 * channels)


def head_maps(count, channels, everywhere=False):
    full = channels // LANES * LANES
    rest = channels - full
    stride = LANES // 4
    hits = np.zeros((count * channels, LANES), np.float32)
    for j in range(count):
        for c in range(channels):
            at = j * full + c if c < full else count * full + j * rest + c - full
            lanes = range(0, LANES, stride) if everywhere else (j * stride,)
            for lane in lanes:
                hits[at, lane + c // HEAD_DIM] = 1.0
    padded = np.zeros((-(-hits.shape[0] // LANES) * LANES, LANES), np.float32)
    padded[: hits.shape[0]] = hits
    blocks = padded.reshape(-1, LANES, LANES).transpose(0, 2, 1).reshape(-1, LANES)
    return jnp.asarray(hits / math.sqrt(HEAD_DIM), BF), jnp.asarray(blocks, BF)


def beside(ref):
    count = ref.shape[0] // LANES
    return jnp.concatenate([ref[b * LANES : (b + 1) * LANES] for b in range(count)], axis=1)


def local_kernel(
    picks_ref, window_ref, query_ref, keyval_ref, to_lanes_ref, to_channels_ref,
    top_ref, sum_ref, mix_ref,
):
    frames, cells, channels = query_ref.shape
    count = picks_ref.shape[1]
    full = channels // LANES * LANES
    stride = LANES // 4
    queries = [query_ref[f] for f in range(frames)]
    keyvals = [keyval_ref[f] for f in range(frames)]
    keys = [kv[:, :full] for kv in keyvals] + [
        jnp.concatenate([kv[:, full:channels] for kv in keyvals], axis=1)
    ]
    values = [kv[:, channels : channels + full].astype(F32) for kv in keyvals] + [
        jnp.concatenate([kv[:, channels + full :] for kv in keyvals], axis=1).astype(F32)
    ]
    products = []
    for q in queries:
        again = jnp.concatenate([q[:, full:]] * frames, axis=1)
        row = [q[:, :full] * k for k in keys[:frames]] + [again * keys[frames]]
        products.append(jnp.concatenate(row, axis=1))
    scores = dot(jnp.concatenate(products, axis=0), to_lanes_ref[...])
    source = lax.div(lax.broadcasted_iota(jnp.int32, (1, LANES), 1), stride)
    window = window_ref[...].reshape(1, 1)
    copies = jnp.zeros((1, LANES), F32)
    for n in range(count):
        copies = copies + jnp.where(source == picks_ref[:, n : n + 1], 1.0, 0.0)
    weights = []
    for i in range(frames):
        times = copies + jnp.where(jnp.abs(source - i) < window, 1.0, 0.0)
        s = jnp.where(times > 0.0, scores[i * cells : (i + 1) * cells], -jnp.inf)
        top = jnp.maximum(s, pltpu.roll(s, stride, 1))
        top = jnp.maximum(top, pltpu.roll(top, 2 * stride, 1))
        w = jnp.exp(s - top) * times
        total = w + pltpu.roll(w, stride, 1)
        total = total + pltpu.roll(total, 2 * stride, 1)
        top_ref[i] = top
        sum_ref[i] = total
        weights.append(w.astype(BF))
    spread = dot(jnp.concatenate(weights, axis=0), beside(to_channels_ref))
    for i in range(frames):
        part = spread[i * cells : (i + 1) * cells]
        wide = part[:, :full] * values[0]
        for j in range(1, frames):
            wide = wide + part[:, j * full : (j + 1) * full] * values[j]
        tail = part[:, frames * full :] * values[frames]
        tail = tail[:, :LANES] + tail[:, LANES:]
        tail = tail + pltpu.roll(tail, LANES // 2, 1)
        mix_ref[i] = jnp.concatenate([wide, tail], axis=1)


def keys_and_values(anchor_ref, wkv_ref, channels):
    return [
        dot(unpacked(anchor_ref[n], channels), wkv_ref[...]).astype(BF)
        for n in range(anchor_ref.shape[0])
    ]


def updated(keyvals, to_lanes_ref, to_channels_ref, query, top, total, mix, last):
    frames, cells, channels = query.shape
    full = channels // LANES * LANES
    size = frames * cells
    query, top, total, mix = (v.reshape(size, v.shape[-1]) for v in (query, top, total, mix))
    low = lax.broadcasted_iota(jnp.int32, (1, LANES), 1) < LANES // 4
    for n, keyval in enumerate(keyvals):
        key = jnp.concatenate([keyval[:, :channels]] * frames, axis=0)
        scores = dot(query * key, to_lanes_ref[...])
        higher = jnp.maximum(top, scores)
        weight = jnp.exp(scores - higher)
        fade = jnp.exp(top - higher)
        total = total * fade + weight
        both = jnp.where(low, weight, fade)
        if last and n == len(keyvals) - 1:
            both = both / total
        spread = dot(both.astype(BF), beside(to_channels_ref))
        value = keyval[:, channels:].astype(F32)
        value = jnp.concatenate([value] * frames, axis=0)
        wide = spread[:, :full] * value[:, :full] + spread[:, full : 2 * full] * mix[:, :full]
        tail = jnp.concatenate([value[:, full:], mix[:, full + LANES // 2 :]], axis=1)
        tail = spread[:, 2 * full :] * tail
        tail = tail + pltpu.roll(tail, LANES // 2, 1)
        mix = jnp.concatenate([wide, tail], axis=1)
        top = higher
    return top, total, mix


def anchor_kernel(
    anchor_ref, wkv_ref, to_lanes_ref, to_channels_ref, query_ref, top_ref, sum_ref, mix_ref,
    top_out, sum_out, mix_out,
):
    new = updated(
        keys_and_values(anchor_ref, wkv_ref, query_ref.shape[2]), to_lanes_ref, to_channels_ref,
        query_ref[...], top_ref[...], sum_ref[...], mix_ref[...], False,
    )
    for ref, v in zip((top_out, sum_out, mix_out), new):
        ref[...] = v.reshape(ref.shape)


def last_kernel(
    anchor_ref, wkv_ref, to_lanes_ref, to_channels_ref, query_ref, top_ref, sum_ref, mix_ref,
    temporal_ref, wo_ref, out_ref, out_buf, sems,
):
    frames, cells, channels = query_ref.shape
    height, width = out_ref.shape[1:3]
    keyvals = keys_and_values(anchor_ref, wkv_ref, channels)
    copies = []
    group = 2 if frames % 2 == 0 else 1
    for lo in range(0, frames, group):
        at = slice(lo, lo + group)
        _, _, mix = updated(
            keyvals, to_lanes_ref, to_channels_ref,
            query_ref[at], top_ref[at], sum_ref[at], mix_ref[at], True,
        )
        result = dot(mix[:, :channels].astype(BF), wo_ref[...])
        total = temporal_ref[at].astype(F32) + result.reshape(group, cells, channels)
        out_buf[at] = total.astype(BF).reshape(group, height, width, channels)
        copies.append(pltpu.make_async_copy(out_buf.at[at], out_ref.at[at], sems.at[lo // group]))
        copies[-1].start()
    for copy in copies:
        copy.wait()


def swapped(odd, even, axis):
    count = lax.axis_size(axis)
    pairs = [[(i, i + 1) for i in range(start, count - 1, 2)] for start in (1, 0)]
    pairs = [up + [(j, i) for i, j in up] for up in pairs]
    return lax.ppermute(odd, axis, pairs[0]), lax.ppermute(even, axis, pairs[1])


def swap_order(s):
    return (s.bit_length(), -s)


def on_device(
    latents, anchor_index, window, gain_one, spatial_w, gain_two, temporal_w, gain_three,
    w_query, w_keyval, w_out,
):
    frames, height, width, channels = latents.shape
    cells = height * width
    count = anchor_index.shape[1]
    ws = spatial_w.reshape(3, 3 * channels, channels)
    one = 2 * channels * channels
    packed = cells * channels // LANES
    edge_packed = frames * width * channels // LANES
    lanes_up = (channels + LANES - 1) // LANES * LANES
    sem = pltpu.SemaphoreType.DMA
    some = (frames, cells, channels)

    x, g1, g2, g3, w = latents, gain_one, gain_two, gain_three, ws

    strip_odd, strip_even = call(
        edge_kernel, [((edge_packed, LANES), BF)] * 2, [VMEM], flops=8 * frames * cells * one
    )(x)
    strip_odd, strip_even = swapped(strip_odd, strip_even, "strip")
    outer_col = pltpu.VMEM((2 * cells, 3 * channels), BF)
    inner_col = pltpu.VMEM(((frames - 2) * (cells + 2 * width), 3 * channels), BF)
    middle = (2, cells - 2 * width, channels)
    mid, mid2, edge, w_rem, order = call(
        outer_kernel,
        [
            (middle, BF),
            (middle, BF),
            ((2, 2, width, channels), F32),
            ((3 * channels, 3 * (channels % 256)), BF),
            ((8, LANES), F32),
        ],
        [VMEM] * 4,
        [outer_col],
        flops=9 * 2 * cells * one,
    )(x, g1, g2, w)
    outer_spatial, outer_hidden, clip_odd, clip_even = call(
        functools.partial(outer_edge_kernel, frames),
        [((2, cells, channels), BF)] * 2 + [((packed, LANES), BF)] * 2,
        [VMEM] * 10,
        flops=6 * 2 * width * one,
    )(edge, strip_odd, strip_even, order, mid, mid2, g1, g2, w, w_rem)
    clip_odd, clip_even = swapped(clip_odd, clip_even, "clip")
    spatial, hidden = call(
        inner_kernel,
        [(some, BF), (some, BF)],
        [VMEM] * 9,
        [inner_col],
        flops=9 * (frames - 2) * cells * one,
    )(x, strip_odd, strip_even, g1, g2, w, w_rem, outer_spatial, outer_hidden)
    (chosen,) = call(
        chosen_kernel, [((count, packed, LANES), BF)], [VMEM] * 7, flops=3 * cells * one
    )(anchor_index, clip_odd, clip_even, spatial, hidden, g3, temporal_w)
    clips = lax.axis_size("clip")
    if clips & (clips - 1) == 0:
        routes = [[(i, i ^ s) for i in range(clips)] for s in sorted(range(1, clips), key=swap_order)]
    else:
        routes = [[(i, (i + s) % clips) for i in range(clips)] for s in range(1, clips)]
    arrived = [lax.ppermute(chosen, "clip", route) for route in routes]
    temporal, query, keyval = call(
        temporal_kernel,
        [(some, BF), (some, BF), ((frames, cells, 2 * channels), BF)],
        [VMEM] * 8,
        flops=6 * frames * cells * one,
        limit=32,
    )(clip_odd, clip_even, spatial, hidden, g3, temporal_w, w_query, w_keyval)
    states = [((frames, cells, LANES), F32)] * 2 + [((frames, cells, lanes_up), F32)]
    state = call(
        local_kernel, states, [VMEM] * 6, flops=10 * frames * cells * one, limit=32
    )(anchor_index, window, query, keyval, *head_maps(frames, channels))
    to_lanes, _ = head_maps(1, channels, everywhere=True)
    _, to_channels = head_maps(2, channels)
    for arrival in arrived[:-1]:
        state = call(
            anchor_kernel, states, [VMEM] * 8, flops=4 * frames * cells * one, limit=32
        )(arrival, w_keyval, to_lanes, to_channels, query, *state)
    (out,) = call(
        last_kernel,
        [(latents.shape, BF)],
        [VMEM] * 10,
        [pltpu.VMEM(latents.shape, BF), sem((frames,))],
        flops=5 * frames * cells * one,
        limit=32,
        out_specs=(HBM,),
    )(arrived[-1], w_keyval, to_lanes, to_channels, query, *state, temporal, w_out)
    return out


def solution(mesh):
    return jax.shard_map(
        on_device,
        mesh=mesh,
        in_specs=(
            P(("groups", "clip"), "strip", None, None),
            P(("groups", "clip"), None),
            P(),
            P(),
            P(),
            P(),
            P(),
            P(),
            P(),
            P(),
            P(),
        ),
        out_specs=P(("groups", "clip"), "strip", None, None),
        check_vma=False,
    )
```

```python
import functools
import math

import jax
import jax.numpy as jnp
import numpy as np
from jax import lax
from jax.experimental import pallas as pl
from jax.experimental.pallas import tpu as pltpu
from jax.sharding import PartitionSpec as P

HEADS = 5
HEAD_DIM = 64
LANES = 128
BF = jnp.bfloat16
F32 = jnp.float32
VMEM = pl.BlockSpec(memory_space=pltpu.VMEM)
HBM = pl.BlockSpec(memory_space=pltpu.HBM)
MIB = 1 << 20


def call(body, outs, specs, scratch=(), flops=0, limit=24, out_specs=None):
    return pl.pallas_call(
        body,
        out_shape=tuple(jax.ShapeDtypeStruct(s, d) for s, d in outs),
        in_specs=specs,
        out_specs=out_specs or tuple(VMEM for _ in outs),
        scratch_shapes=list(scratch),
        cost_estimate=pl.CostEstimate(flops=flops, bytes_accessed=2 * MIB, transcendentals=0),
        compiler_params=pltpu.CompilerParams(vmem_limit_bytes=limit * MIB),
    )


def dot(a, b):
    return jnp.dot(a, b, preferred_element_type=F32)


def norm(v, gain_ref):
    wide = v.astype(F32)
    centred = wide - jnp.mean(wide, axis=-1, keepdims=True)
    variance = jnp.mean(centred * centred, axis=-1, keepdims=True)
    return centred * lax.rsqrt(variance + 1e-05) * gain_ref[...].reshape(1, v.shape[1])


def silu(u):
    half = 0.5 * u
    return half + half * jnp.tanh(half)


def pack_into(ref, h):
    cells, channels = h.shape
    full = channels // LANES
    for t in range(full):
        ref[t * cells : (t + 1) * cells, :] = h[:, t * LANES : (t + 1) * LANES]
    rest = channels - full * LANES
    if rest:
        share = LANES // rest
        part = cells // share
        ref[full * cells :, :] = jnp.concatenate(
            [h[s * part : (s + 1) * part, full * LANES :] for s in range(share)], axis=1
        )


def unpacked(p, channels):
    cells = p.shape[0] * LANES // channels
    full = channels // LANES
    pieces = [p[t * cells : (t + 1) * cells, :] for t in range(full)]
    rest = channels - full * LANES
    if rest:
        share = LANES // rest
        tail = p[full * cells :, :]
        pieces.append(
            jnp.concatenate([tail[:, s * rest : (s + 1) * rest] for s in range(share)], axis=0)
        )
    return jnp.concatenate(pieces, axis=1)


def columns(h, width):
    cells, channels = h.shape
    left = pltpu.roll(h, 1, 0)
    right = pltpu.roll(h, cells - 1, 0)
    place = lax.broadcasted_iota(jnp.int32, (8, channels), 0)
    lefts, rights = [], []
    for lo in range(0, cells, width):
        hi = lo + width
        lefts += [jnp.where(place == 0, 0.0, left[lo : lo + 8]), left[lo + 8 : hi]]
        rights += [right[lo : hi - 8], jnp.where(place == 7, 0.0, right[hi - 8 : hi])]
    sides = [jnp.concatenate(lefts, axis=0), h, jnp.concatenate(rights, axis=0)]
    return jnp.concatenate([v.astype(BF) for v in sides], axis=1)


def scalar(ref, n):
    values = ref[...].astype(F32)
    place = lax.broadcasted_iota(jnp.int32, values.shape, 1)
    return jnp.sum(jnp.where(place == n, values, 0.0)).astype(jnp.int32)


def at_odd(axis):
    return lax.rem(lax.axis_index(axis), 2) == 1


def sorted_pair(odd_ref, even_ref, axis):
    odd = at_odd(axis)
    first, second = odd_ref[...], even_ref[...]
    return jnp.where(odd, second, first), jnp.where(odd, first, second)


def edge_kernel(x_ref, odd_ref, even_ref):
    frames, height, width, channels = x_ref.shape
    odd = at_odd("strip")
    top = x_ref[:, 0].reshape(frames * width, channels)
    bottom = x_ref[:, height - 1].reshape(frames * width, channels)
    pack_into(odd_ref, jnp.where(odd, bottom, top))
    pack_into(even_ref, jnp.where(odd, top, bottom))


def rests_into(rem_ref, w_ref):
    full = w_ref.shape[2] // 256 * 256
    rest = w_ref.shape[2] - full
    for a in range(3):
        rem_ref[:, a * rest : (a + 1) * rest] = w_ref[a, :, full:]


def hidden_columns(v, g1_ref, width):
    return columns(silu(norm(v, g1_ref)), width)


def stacked_rows(col_ref, count, height, width, w_ref, rem_ref):
    cells = height * width
    rims = (col_ref.shape[0] - count * cells) // 2
    channels = w_ref.shape[2]
    full = channels // 256 * 256
    rest = channels - full
    size = count * cells
    above = dot(col_ref[: rims + size], w_ref[0, :, :full])
    centre = dot(col_ref[rims : rims + size], w_ref[1, :, :full])
    below = dot(col_ref[rims:], w_ref[2, :, :full])
    tails = dot(col_ref[...], rem_ref[...])

    def terms(place, row):
        own = place * cells + row * width
        wide = centre[own : own + width]
        tail = tails[rims + own : rims + own + width, rest : 2 * rest]
        if row > 0 or rims:
            at = rims + own - width if row > 0 else place * width
            wide = wide + above[at : at + width]
            tail = tail + tails[at : at + width, :rest]
        if row < height - 1 or rims:
            at = own + width if row < height - 1 else size + place * width
            wide = wide + below[at : at + width]
            tail = tail + tails[rims + at : rims + at + width, 2 * rest :]
        return jnp.concatenate([wide, tail], axis=1)

    return terms


def rim_rows(packed, frames, width, channels):
    rows = unpacked(packed, channels)
    return jnp.concatenate([rows[f * width : (f + 1) * width] for f in frames], axis=0)


def outer_kernel(x_ref, g1_ref, g2_ref, w_ref, mid_ref, mid2_ref, edge_ref, rem_ref, order_ref, col_ref):
    frames, height, width, channels = x_ref.shape
    cells = height * width
    order_ref[...] = jnp.zeros_like(order_ref)
    rests_into(rem_ref, w_ref)
    outer = (0, frames - 1)
    for s, f in enumerate(outer):
        x = x_ref[f].reshape(cells, channels)
        col_ref[s * cells : (s + 1) * cells] = hidden_columns(x, g1_ref, width)
    terms = stacked_rows(col_ref, 2, height, width, w_ref, rem_ref)
    for s, f in enumerate(outer):
        for row in range(height):
            total = x_ref[f, row].astype(F32) + terms(s, row)
            if 0 < row < height - 1:
                rounded = total.astype(BF)
                lo = (row - 1) * width
                mid_ref[s, lo : lo + width] = rounded
                mid2_ref[s, lo : lo + width] = silu(norm(rounded, g2_ref)).astype(BF)
            else:
                edge_ref[s, 0 if row == 0 else 1] = total


def outer_edge_kernel(
    frames, edge_ref, odd_ref, even_ref, order_ref, mid_ref, mid2_ref, g1_ref, g2_ref, w_ref, rem_ref,
    spatial_ref, hidden_ref, odd_clip_ref, even_clip_ref,
):
    _, cells, channels = spatial_ref.shape
    width = edge_ref.shape[2]
    full = channels // 256 * 256
    rest = channels - full
    spatial_ref[:, width : cells - width] = mid_ref[...]
    hidden_ref[:, width : cells - width] = mid2_ref[...]
    cols = [
        hidden_columns(rim_rows(packed, (0, frames - 1), width, channels), g1_ref, width)
        for packed in sorted_pair(odd_ref, even_ref, "strip")
    ]
    tails = dot(jnp.concatenate(cols, axis=0), rem_ref[...])
    size = 2 * width
    for side, lo in ((0, 0), (1, cells - width)):
        tail = tails[:size, :rest] if side == 0 else tails[size:, 2 * rest :]
        wide = dot(cols[side], w_ref[2 * side, :, :full])
        term = jnp.concatenate([wide, tail], axis=1)
        rounded = (edge_ref[:, side].reshape(size, channels) + term).astype(BF)
        hidden = silu(norm(rounded, g2_ref)).astype(BF)
        spatial_ref[:, lo : lo + width] = rounded.reshape(2, width, channels)
        hidden_ref[:, lo : lo + width] = hidden.reshape(2, width, channels)
    odd = at_odd("clip")
    pack_into(odd_clip_ref, jnp.where(odd, hidden_ref[1], hidden_ref[0]))
    pack_into(even_clip_ref, jnp.where(odd, hidden_ref[0], hidden_ref[1]))


def inner_kernel(
    x_ref, odd_ref, even_ref, g1_ref, g2_ref, w_ref, rem_ref, outer_spatial_ref, outer_hidden_ref,
    spatial_ref, hidden_ref, col_ref,
):
    frames, height, width, channels = x_ref.shape
    cells = height * width
    for s, f in ((0, 0), (1, frames - 1)):
        spatial_ref[f] = outer_spatial_ref[s]
        hidden_ref[f] = outer_hidden_ref[s]
    inside = range(1, frames - 1)
    above, below = sorted_pair(odd_ref, even_ref, "strip")
    rims = len(inside) * width
    end = rims + len(inside) * cells
    col_ref[:rims] = hidden_columns(rim_rows(above, inside, width, channels), g1_ref, width)
    for s, f in enumerate(inside):
        x = x_ref[f].reshape(cells, channels)
        lo = rims + s * cells
        col_ref[lo : lo + cells] = hidden_columns(x, g1_ref, width)
    col_ref[end:] = hidden_columns(rim_rows(below, inside, width, channels), g1_ref, width)
    terms = stacked_rows(col_ref, len(inside), height, width, w_ref, rem_ref)
    for s, f in enumerate(inside):
        for row in range(height):
            rounded = (x_ref[f, row].astype(F32) + terms(s, row)).astype(BF)
            lo = row * width
            spatial_ref[f, lo : lo + width] = rounded
            hidden_ref[f, lo : lo + width] = silu(norm(rounded, g2_ref)).astype(BF)


def chosen_kernel(
    picks_ref, odd_ref, even_ref, spatial_ref, hidden_ref, g3_ref, wt_ref, chosen_ref
):
    frames, cells, channels = spatial_ref.shape
    before, after = (unpacked(v, channels) for v in sorted_pair(odd_ref, even_ref, "clip"))
    for n in range(chosen_ref.shape[0]):
        pick = scalar(picks_ref, n)
        earlier = jnp.where(pick == 0, before, hidden_ref[jnp.maximum(pick - 1, 0)])
        later = jnp.where(pick == frames - 1, after, hidden_ref[jnp.minimum(pick + 1, frames - 1)])
        total = spatial_ref[pick].astype(F32) + dot(hidden_ref[pick], wt_ref[1])
        total = total + dot(earlier, wt_ref[0]) + dot(later, wt_ref[2])
        pack_into(chosen_ref.at[n], norm(total.astype(BF), g3_ref).astype(BF))


def temporal_kernel(
    odd_ref, even_ref, spatial_ref, hidden_ref, g3_ref, wt_ref, wq_ref, wkv_ref,
    temporal_ref, query_ref, keyval_ref,
):
    frames, cells, channels = spatial_ref.shape
    size = frames * cells
    before, after = (unpacked(v, channels) for v in sorted_pair(odd_ref, even_ref, "clip"))
    hidden = hidden_ref[...].reshape(size, channels)
    total = spatial_ref[...].reshape(size, channels).astype(F32) + dot(hidden, wt_ref[1])
    total = total + dot(jnp.concatenate([before, hidden[: size - cells]], axis=0), wt_ref[0])
    total = total + dot(jnp.concatenate([hidden[cells:], after], axis=0), wt_ref[2])
    temporal = total.astype(BF)
    temporal_ref[...] = temporal.reshape(frames, cells, channels)
    normed = norm(temporal, g3_ref).astype(BF)
    query_ref[...] = dot(normed, wq_ref[...]).astype(BF).reshape(frames, cells, channels)
    keyval_ref[...] = dot(normed, wkv_ref[...]).astype(BF).reshape(frames, cells, 2 * channels)


def head_maps(count, channels, everywhere=False):
    full = channels // LANES * LANES
    rest = channels - full
    stride = LANES // 4
    hits = np.zeros((count * channels, LANES), np.float32)
    for j in range(count):
        for c in range(channels):
            at = j * full + c if c < full else count * full + j * rest + c - full
            lanes = range(0, LANES, stride) if everywhere else (j * stride,)
            for lane in lanes:
                hits[at, lane + c // HEAD_DIM] = 1.0
    padded = np.zeros((-(-hits.shape[0] // LANES) * LANES, LANES), np.float32)
    padded[: hits.shape[0]] = hits
    blocks = padded.reshape(-1, LANES, LANES).transpose(0, 2, 1).reshape(-1, LANES)
    return jnp.asarray(hits / math.sqrt(HEAD_DIM), BF), jnp.asarray(blocks, BF)


def beside(ref):
    count = ref.shape[0] // LANES
    return jnp.concatenate([ref[b * LANES : (b + 1) * LANES] for b in range(count)], axis=1)


def local_kernel(
    picks_ref, window_ref, query_ref, keyval_ref, to_lanes_ref, to_channels_ref,
    top_ref, sum_ref, mix_ref,
):
    frames, cells, channels = query_ref.shape
    count = picks_ref.shape[1]
    full = channels // LANES * LANES
    stride = LANES // 4
    queries = [query_ref[f] for f in range(frames)]
    keyvals = [keyval_ref[f] for f in range(frames)]
    keys = [kv[:, :full] for kv in keyvals] + [
        jnp.concatenate([kv[:, full:channels] for kv in keyvals], axis=1)
    ]
    values = [kv[:, channels : channels + full].astype(F32) for kv in keyvals] + [
        jnp.concatenate([kv[:, channels + full :] for kv in keyvals], axis=1).astype(F32)
    ]
    products = []
    for q in queries:
        again = jnp.concatenate([q[:, full:]] * frames, axis=1)
        row = [q[:, :full] * k for k in keys[:frames]] + [again * keys[frames]]
        products.append(jnp.concatenate(row, axis=1))
    scores = dot(jnp.concatenate(products, axis=0), to_lanes_ref[...])
    source = lax.div(lax.broadcasted_iota(jnp.int32, (1, LANES), 1), stride)
    window = window_ref[...].reshape(1, 1)
    copies = jnp.zeros((1, LANES), F32)
    for n in range(count):
        copies = copies + jnp.where(source == picks_ref[:, n : n + 1], 1.0, 0.0)
    weights = []
    for i in range(frames):
        times = copies + jnp.where(jnp.abs(source - i) < window, 1.0, 0.0)
        s = jnp.where(times > 0.0, scores[i * cells : (i + 1) * cells], -jnp.inf)
        top = jnp.maximum(s, pltpu.roll(s, stride, 1))
        top = jnp.maximum(top, pltpu.roll(top, 2 * stride, 1))
        w = jnp.exp(s - top) * times
        total = w + pltpu.roll(w, stride, 1)
        total = total + pltpu.roll(total, 2 * stride, 1)
        top_ref[i] = top
        sum_ref[i] = total
        weights.append(w.astype(BF))
    spread = dot(jnp.concatenate(weights, axis=0), beside(to_channels_ref))
    for i in range(frames):
        part = spread[i * cells : (i + 1) * cells]
        wide = part[:, :full] * values[0]
        for j in range(1, frames):
            wide = wide + part[:, j * full : (j + 1) * full] * values[j]
        tail = part[:, frames * full :] * values[frames]
        tail = tail[:, :LANES] + tail[:, LANES:]
        tail = tail + pltpu.roll(tail, LANES // 2, 1)
        mix_ref[i] = jnp.concatenate([wide, tail], axis=1)


def keys_and_values(anchor_ref, wkv_ref, channels):
    return [
        dot(unpacked(anchor_ref[n], channels), wkv_ref[...]).astype(BF)
        for n in range(anchor_ref.shape[0])
    ]


def updated(keyvals, to_lanes_ref, to_channels_ref, query, top, total, mix, last):
    frames, cells, channels = query.shape
    full = channels // LANES * LANES
    size = frames * cells
    query, top, total, mix = (v.reshape(size, v.shape[-1]) for v in (query, top, total, mix))
    low = lax.broadcasted_iota(jnp.int32, (1, LANES), 1) < LANES // 4
    for n, keyval in enumerate(keyvals):
        key = jnp.concatenate([keyval[:, :channels]] * frames, axis=0)
        scores = dot(query * key, to_lanes_ref[...])
        higher = jnp.maximum(top, scores)
        weight = jnp.exp(scores - higher)
        fade = jnp.exp(top - higher)
        total = total * fade + weight
        both = jnp.where(low, weight, fade)
        if last and n == len(keyvals) - 1:
            both = both / total
        spread = dot(both.astype(BF), beside(to_channels_ref))
        value = keyval[:, channels:].astype(F32)
        value = jnp.concatenate([value] * frames, axis=0)
        wide = spread[:, :full] * value[:, :full] + spread[:, full : 2 * full] * mix[:, :full]
        tail = jnp.concatenate([value[:, full:], mix[:, full + LANES // 2 :]], axis=1)
        tail = spread[:, 2 * full :] * tail
        tail = tail + pltpu.roll(tail, LANES // 2, 1)
        mix = jnp.concatenate([wide, tail], axis=1)
        top = higher
    return top, total, mix


def relay_kernel(*refs):
    count = len(refs) // 2
    for n in range(count):
        refs[count + n][...] = refs[n][...]
    refs[-1][...] = jnp.zeros_like(refs[-1])


def anchor_kernel(
    anchor_ref, wkv_ref, to_lanes_ref, to_channels_ref, query_ref, top_ref, sum_ref, mix_ref,
    order_ref, top_out, sum_out, mix_out,
):
    new = updated(
        keys_and_values(anchor_ref, wkv_ref, query_ref.shape[2]), to_lanes_ref, to_channels_ref,
        query_ref[...], top_ref[...], sum_ref[...], mix_ref[...], False,
    )
    for ref, v in zip((top_out, sum_out, mix_out), new):
        ref[...] = v.reshape(ref.shape)


def last_kernel(
    anchor_ref, wkv_ref, to_lanes_ref, to_channels_ref, query_ref, top_ref, sum_ref, mix_ref,
    temporal_ref, wo_ref, out_ref, out_buf, sems,
):
    frames, cells, channels = query_ref.shape
    height, width = out_ref.shape[1:3]
    keyvals = keys_and_values(anchor_ref, wkv_ref, channels)
    copies = []
    group = 2 if frames % 2 == 0 else 1
    for lo in range(0, frames, group):
        at = slice(lo, lo + group)
        _, _, mix = updated(
            keyvals, to_lanes_ref, to_channels_ref,
            query_ref[at], top_ref[at], sum_ref[at], mix_ref[at], True,
        )
        result = dot(mix[:, :channels].astype(BF), wo_ref[...])
        total = temporal_ref[at].astype(F32) + result.reshape(group, cells, channels)
        out_buf[at] = total.astype(BF).reshape(group, height, width, channels)
        copies.append(pltpu.make_async_copy(out_buf.at[at], out_ref.at[at], sems.at[lo // group]))
        copies[-1].start()
    for copy in copies:
        copy.wait()


def swapped(odd, even, axis):
    count = lax.axis_size(axis)
    pairs = [[(i, i + 1) for i in range(start, count - 1, 2)] for start in (1, 0)]
    pairs = [up + [(j, i) for i, j in up] for up in pairs]
    return lax.ppermute(odd, axis, pairs[0]), lax.ppermute(even, axis, pairs[1])


def on_device(
    latents, anchor_index, window, gain_one, spatial_w, gain_two, temporal_w, gain_three,
    w_query, w_keyval, w_out,
):
    frames, height, width, channels = latents.shape
    cells = height * width
    count = anchor_index.shape[1]
    ws = spatial_w.reshape(3, 3 * channels, channels)
    one = 2 * channels * channels
    packed = cells * channels // LANES
    edge_packed = frames * width * channels // LANES
    lanes_up = (channels + LANES - 1) // LANES * LANES
    sem = pltpu.SemaphoreType.DMA
    some = (frames, cells, channels)

    x, g1, g2, g3, w = latents, gain_one, gain_two, gain_three, ws

    strip_odd, strip_even = call(
        edge_kernel, [((edge_packed, LANES), BF)] * 2, [VMEM], flops=8 * frames * cells * one
    )(x)
    strip_odd, strip_even = swapped(strip_odd, strip_even, "strip")
    outer_col = pltpu.VMEM((2 * cells, 3 * channels), BF)
    inner_col = pltpu.VMEM(((frames - 2) * (cells + 2 * width), 3 * channels), BF)
    middle = (2, cells - 2 * width, channels)
    mid, mid2, edge, w_rem, order = call(
        outer_kernel,
        [
            (middle, BF),
            (middle, BF),
            ((2, 2, width, channels), F32),
            ((3 * channels, 3 * (channels % 256)), BF),
            ((8, LANES), F32),
        ],
        [VMEM] * 4,
        [outer_col],
        flops=9 * 2 * cells * one,
    )(x, g1, g2, w)
    outer_spatial, outer_hidden, clip_odd, clip_even = call(
        functools.partial(outer_edge_kernel, frames),
        [((2, cells, channels), BF)] * 2 + [((packed, LANES), BF)] * 2,
        [VMEM] * 10,
        flops=6 * 2 * width * one,
    )(edge, strip_odd, strip_even, order, mid, mid2, g1, g2, w, w_rem)
    clip_odd, clip_even = swapped(clip_odd, clip_even, "clip")
    spatial, hidden = call(
        inner_kernel,
        [(some, BF), (some, BF)],
        [VMEM] * 9,
        [inner_col],
        flops=9 * (frames - 2) * cells * one,
    )(x, strip_odd, strip_even, g1, g2, w, w_rem, outer_spatial, outer_hidden)
    (chosen,) = call(
        chosen_kernel, [((count, packed, LANES), BF)], [VMEM] * 7, flops=3 * cells * one
    )(anchor_index, clip_odd, clip_even, spatial, hidden, g3, temporal_w)
    clips = lax.axis_size("clip")
    anchors_order = order
    if clips & (clips - 1) == 0:
        routes = [[(i, i ^ s) for i in range(clips)] for s in range(1, clips, 2)]
        arrived = [lax.ppermute(chosen, "clip", route) for route in routes]
        *relayed, anchors_order = call(
            relay_kernel,
            [(chosen.shape, BF)] * (clips // 2 - 1) + [((8, LANES), F32)],
            [VMEM] * (clips // 2 - 1),
        )(*arrived[1:])
        arrived += [lax.ppermute(v, "clip", routes[0]) for v in relayed]
    else:
        routes = [[(i, (i + s) % clips) for i in range(clips)] for s in range(1, clips)]
        arrived = [lax.ppermute(chosen, "clip", route) for route in routes]
    temporal, query, keyval = call(
        temporal_kernel,
        [(some, BF), (some, BF), ((frames, cells, 2 * channels), BF)],
        [VMEM] * 8,
        flops=6 * frames * cells * one,
        limit=32,
    )(clip_odd, clip_even, spatial, hidden, g3, temporal_w, w_query, w_keyval)
    states = [((frames, cells, LANES), F32)] * 2 + [((frames, cells, lanes_up), F32)]
    state = call(
        local_kernel, states, [VMEM] * 6, flops=10 * frames * cells * one, limit=32
    )(anchor_index, window, query, keyval, *head_maps(frames, channels))
    to_lanes, _ = head_maps(1, channels, everywhere=True)
    _, to_channels = head_maps(2, channels)
    for arrival in arrived[:-1]:
        state = call(
            anchor_kernel, states, [VMEM] * 9, flops=4 * frames * cells * one, limit=32
        )(arrival, w_keyval, to_lanes, to_channels, query, *state, anchors_order)
    (out,) = call(
        last_kernel,
        [(latents.shape, BF)],
        [VMEM] * 10,
        [pltpu.VMEM(latents.shape, BF), sem((frames,))],
        flops=5 * frames * cells * one,
        limit=32,
        out_specs=(HBM,),
    )(arrived[-1], w_keyval, to_lanes, to_channels, query, *state, temporal, w_out)
    return out


def solution(mesh):
    return jax.shard_map(
        on_device,
        mesh=mesh,
        in_specs=(
            P(("groups", "clip"), "strip", None, None),
            P(("groups", "clip"), None),
            P(),
            P(),
            P(),
            P(),
            P(),
            P(),
            P(),
            P(),
            P(),
        ),
        out_specs=P(("groups", "clip"), "strip", None, None),
        check_vma=False,
    )
```

```python
import functools
import math

import jax
import jax.numpy as jnp
import numpy as np
from jax import lax
from jax.experimental import pallas as pl
from jax.experimental.pallas import tpu as pltpu
from jax.sharding import PartitionSpec as P

HEADS = 5
HEAD_DIM = 64
LANES = 128
BF = jnp.bfloat16
F32 = jnp.float32
VMEM = pl.BlockSpec(memory_space=pltpu.VMEM)
HBM = pl.BlockSpec(memory_space=pltpu.HBM)
MIB = 1 << 20


def call(body, outs, specs, scratch=(), flops=0, limit=24, out_specs=None):
    return pl.pallas_call(
        body,
        out_shape=tuple(jax.ShapeDtypeStruct(s, d) for s, d in outs),
        in_specs=specs,
        out_specs=out_specs or tuple(VMEM for _ in outs),
        scratch_shapes=list(scratch),
        cost_estimate=pl.CostEstimate(flops=flops, bytes_accessed=2 * MIB, transcendentals=0),
        compiler_params=pltpu.CompilerParams(vmem_limit_bytes=limit * MIB),
    )


def dot(a, b):
    return jnp.dot(a, b, preferred_element_type=F32)


def norm(v, gain_ref):
    wide = v.astype(F32)
    centred = wide - jnp.mean(wide, axis=-1, keepdims=True)
    variance = jnp.mean(centred * centred, axis=-1, keepdims=True)
    return centred * lax.rsqrt(variance + 1e-05) * gain_ref[...].reshape(1, v.shape[1])


def silu(u):
    half = 0.5 * u
    return half + half * jnp.tanh(half)


def pack_into(ref, h):
    cells, channels = h.shape
    full = channels // LANES
    for t in range(full):
        ref[t * cells : (t + 1) * cells, :] = h[:, t * LANES : (t + 1) * LANES]
    rest = channels - full * LANES
    if rest:
        share = LANES // rest
        part = cells // share
        ref[full * cells :, :] = jnp.concatenate(
            [h[s * part : (s + 1) * part, full * LANES :] for s in range(share)], axis=1
        )


def unpacked(p, channels):
    cells = p.shape[0] * LANES // channels
    full = channels // LANES
    pieces = [p[t * cells : (t + 1) * cells, :] for t in range(full)]
    rest = channels - full * LANES
    if rest:
        share = LANES // rest
        tail = p[full * cells :, :]
        pieces.append(
            jnp.concatenate([tail[:, s * rest : (s + 1) * rest] for s in range(share)], axis=0)
        )
    return jnp.concatenate(pieces, axis=1)


def columns(h, width):
    cells, channels = h.shape
    left = pltpu.roll(h, 1, 0)
    right = pltpu.roll(h, cells - 1, 0)
    place = lax.broadcasted_iota(jnp.int32, (8, channels), 0)
    lefts, rights = [], []
    for lo in range(0, cells, width):
        hi = lo + width
        lefts += [jnp.where(place == 0, 0.0, left[lo : lo + 8]), left[lo + 8 : hi]]
        rights += [right[lo : hi - 8], jnp.where(place == 7, 0.0, right[hi - 8 : hi])]
    sides = [jnp.concatenate(lefts, axis=0), h, jnp.concatenate(rights, axis=0)]
    return jnp.concatenate([v.astype(BF) for v in sides], axis=1)


def scalar(ref, n):
    values = ref[...].astype(F32)
    place = lax.broadcasted_iota(jnp.int32, values.shape, 1)
    return jnp.sum(jnp.where(place == n, values, 0.0)).astype(jnp.int32)


def at_odd(axis):
    return lax.rem(lax.axis_index(axis), 2) == 1


def sorted_pair(odd_ref, even_ref, axis):
    odd = at_odd(axis)
    first, second = odd_ref[...], even_ref[...]
    return jnp.where(odd, second, first), jnp.where(odd, first, second)


def edge_kernel(x_ref, odd_ref, even_ref):
    frames, height, width, channels = x_ref.shape
    odd = at_odd("strip")
    top = x_ref[:, 0].reshape(frames * width, channels)
    bottom = x_ref[:, height - 1].reshape(frames * width, channels)
    pack_into(odd_ref, jnp.where(odd, bottom, top))
    pack_into(even_ref, jnp.where(odd, top, bottom))


def rests_into(rem_ref, w_ref):
    full = w_ref.shape[2] // 256 * 256
    rest = w_ref.shape[2] - full
    for a in range(3):
        rem_ref[:, a * rest : (a + 1) * rest] = w_ref[a, :, full:]


def hidden_columns(v, g1_ref, width):
    return columns(silu(norm(v, g1_ref)), width)


def stacked_rows(col_ref, count, height, width, w_ref, rem_ref):
    cells = height * width
    rims = (col_ref.shape[0] - count * cells) // 2
    channels = w_ref.shape[2]
    full = channels // 256 * 256
    rest = channels - full
    size = count * cells
    above = dot(col_ref[: rims + size], w_ref[0, :, :full])
    centre = dot(col_ref[rims : rims + size], w_ref[1, :, :full])
    below = dot(col_ref[rims:], w_ref[2, :, :full])
    tails = dot(col_ref[...], rem_ref[...])

    def terms(place, row):
        own = place * cells + row * width
        wide = centre[own : own + width]
        tail = tails[rims + own : rims + own + width, rest : 2 * rest]
        if row > 0 or rims:
            at = rims + own - width if row > 0 else place * width
            wide = wide + above[at : at + width]
            tail = tail + tails[at : at + width, :rest]
        if row < height - 1 or rims:
            at = own + width if row < height - 1 else size + place * width
            wide = wide + below[at : at + width]
            tail = tail + tails[rims + at : rims + at + width, 2 * rest :]
        return jnp.concatenate([wide, tail], axis=1)

    return terms


def rim_rows(packed, frames, width, channels):
    rows = unpacked(packed, channels)
    return jnp.concatenate([rows[f * width : (f + 1) * width] for f in frames], axis=0)


def outer_kernel(x_ref, g1_ref, g2_ref, w_ref, mid_ref, mid2_ref, edge_ref, rem_ref, order_ref, col_ref):
    frames, height, width, channels = x_ref.shape
    cells = height * width
    order_ref[...] = jnp.zeros_like(order_ref)
    rests_into(rem_ref, w_ref)
    outer = (0, frames - 1)
    for s, f in enumerate(outer):
        x = x_ref[f].reshape(cells, channels)
        col_ref[s * cells : (s + 1) * cells] = hidden_columns(x, g1_ref, width)
    terms = stacked_rows(col_ref, 2, height, width, w_ref, rem_ref)
    for s, f in enumerate(outer):
        for row in range(height):
            total = x_ref[f, row].astype(F32) + terms(s, row)
            if 0 < row < height - 1:
                rounded = total.astype(BF)
                lo = (row - 1) * width
                mid_ref[s, lo : lo + width] = rounded
                mid2_ref[s, lo : lo + width] = silu(norm(rounded, g2_ref)).astype(BF)
            else:
                edge_ref[s, 0 if row == 0 else 1] = total


def outer_edge_kernel(
    frames, edge_ref, odd_ref, even_ref, order_ref, mid_ref, mid2_ref, g1_ref, g2_ref, w_ref, rem_ref,
    spatial_ref, hidden_ref, odd_clip_ref, even_clip_ref,
):
    _, cells, channels = spatial_ref.shape
    width = edge_ref.shape[2]
    full = channels // 256 * 256
    rest = channels - full
    spatial_ref[:, width : cells - width] = mid_ref[...]
    hidden_ref[:, width : cells - width] = mid2_ref[...]
    cols = [
        hidden_columns(rim_rows(packed, (0, frames - 1), width, channels), g1_ref, width)
        for packed in sorted_pair(odd_ref, even_ref, "strip")
    ]
    tails = dot(jnp.concatenate(cols, axis=0), rem_ref[...])
    size = 2 * width
    for side, lo in ((0, 0), (1, cells - width)):
        tail = tails[:size, :rest] if side == 0 else tails[size:, 2 * rest :]
        wide = dot(cols[side], w_ref[2 * side, :, :full])
        term = jnp.concatenate([wide, tail], axis=1)
        rounded = (edge_ref[:, side].reshape(size, channels) + term).astype(BF)
        hidden = silu(norm(rounded, g2_ref)).astype(BF)
        spatial_ref[:, lo : lo + width] = rounded.reshape(2, width, channels)
        hidden_ref[:, lo : lo + width] = hidden.reshape(2, width, channels)
    odd = at_odd("clip")
    pack_into(odd_clip_ref, jnp.where(odd, hidden_ref[1], hidden_ref[0]))
    pack_into(even_clip_ref, jnp.where(odd, hidden_ref[0], hidden_ref[1]))


def inner_kernel(
    x_ref, odd_ref, even_ref, g1_ref, g2_ref, w_ref, rem_ref, outer_spatial_ref, outer_hidden_ref,
    spatial_ref, hidden_ref, col_ref,
):
    frames, height, width, channels = x_ref.shape
    cells = height * width
    for s, f in ((0, 0), (1, frames - 1)):
        spatial_ref[f] = outer_spatial_ref[s]
        hidden_ref[f] = outer_hidden_ref[s]
    inside = range(1, frames - 1)
    above, below = sorted_pair(odd_ref, even_ref, "strip")
    rims = len(inside) * width
    end = rims + len(inside) * cells
    col_ref[:rims] = hidden_columns(rim_rows(above, inside, width, channels), g1_ref, width)
    for s, f in enumerate(inside):
        x = x_ref[f].reshape(cells, channels)
        lo = rims + s * cells
        col_ref[lo : lo + cells] = hidden_columns(x, g1_ref, width)
    col_ref[end:] = hidden_columns(rim_rows(below, inside, width, channels), g1_ref, width)
    terms = stacked_rows(col_ref, len(inside), height, width, w_ref, rem_ref)
    for s, f in enumerate(inside):
        for row in range(height):
            rounded = (x_ref[f, row].astype(F32) + terms(s, row)).astype(BF)
            lo = row * width
            spatial_ref[f, lo : lo + width] = rounded
            hidden_ref[f, lo : lo + width] = silu(norm(rounded, g2_ref)).astype(BF)


def chosen_kernel(
    picks_ref, odd_ref, even_ref, spatial_ref, hidden_ref, g3_ref, wt_ref, chosen_ref
):
    frames, cells, channels = spatial_ref.shape
    before, after = (unpacked(v, channels) for v in sorted_pair(odd_ref, even_ref, "clip"))
    for n in range(chosen_ref.shape[0]):
        pick = scalar(picks_ref, n)
        earlier = jnp.where(pick == 0, before, hidden_ref[jnp.maximum(pick - 1, 0)])
        later = jnp.where(pick == frames - 1, after, hidden_ref[jnp.minimum(pick + 1, frames - 1)])
        total = spatial_ref[pick].astype(F32) + dot(hidden_ref[pick], wt_ref[1])
        total = total + dot(earlier, wt_ref[0]) + dot(later, wt_ref[2])
        pack_into(chosen_ref.at[n], norm(total.astype(BF), g3_ref).astype(BF))


def temporal_kernel(
    odd_ref, even_ref, spatial_ref, hidden_ref, g3_ref, wt_ref, wq_ref, wkv_ref,
    temporal_ref, query_ref, keyval_ref,
):
    frames, cells, channels = spatial_ref.shape
    size = frames * cells
    before, after = (unpacked(v, channels) for v in sorted_pair(odd_ref, even_ref, "clip"))
    hidden = hidden_ref[...].reshape(size, channels)
    total = spatial_ref[...].reshape(size, channels).astype(F32) + dot(hidden, wt_ref[1])
    total = total + dot(jnp.concatenate([before, hidden[: size - cells]], axis=0), wt_ref[0])
    total = total + dot(jnp.concatenate([hidden[cells:], after], axis=0), wt_ref[2])
    temporal = total.astype(BF)
    temporal_ref[...] = temporal.reshape(frames, cells, channels)
    normed = norm(temporal, g3_ref).astype(BF)
    query_ref[...] = dot(normed, wq_ref[...]).astype(BF).reshape(frames, cells, channels)
    keyval_ref[...] = dot(normed, wkv_ref[...]).astype(BF).reshape(frames, cells, 2 * channels)


def head_maps(count, channels, everywhere=False):
    full = channels // LANES * LANES
    rest = channels - full
    stride = LANES // 4
    hits = np.zeros((count * channels, LANES), np.float32)
    for j in range(count):
        for c in range(channels):
            at = j * full + c if c < full else count * full + j * rest + c - full
            lanes = range(0, LANES, stride) if everywhere else (j * stride,)
            for lane in lanes:
                hits[at, lane + c // HEAD_DIM] = 1.0
    padded = np.zeros((-(-hits.shape[0] // LANES) * LANES, LANES), np.float32)
    padded[: hits.shape[0]] = hits
    blocks = padded.reshape(-1, LANES, LANES).transpose(0, 2, 1).reshape(-1, LANES)
    return jnp.asarray(hits / math.sqrt(HEAD_DIM), BF), jnp.asarray(blocks, BF)


def beside(ref):
    count = ref.shape[0] // LANES
    return jnp.concatenate([ref[b * LANES : (b + 1) * LANES] for b in range(count)], axis=1)


def local_kernel(
    start, picks_ref, window_ref, query_ref, keyval_ref, to_lanes_ref, to_channels_ref, order_ref,
    top_ref, sum_ref, mix_ref, next_ref,
):
    next_ref[...] = jnp.zeros_like(next_ref)
    frames, cells, channels = query_ref.shape
    count = picks_ref.shape[1]
    full = channels // LANES * LANES
    stride = LANES // 4
    part = top_ref.shape[0]
    queries = [query_ref[start + f] for f in range(part)]
    keyvals = [keyval_ref[f] for f in range(frames)]
    keys = [kv[:, :full] for kv in keyvals] + [
        jnp.concatenate([kv[:, full:channels] for kv in keyvals], axis=1)
    ]
    values = [kv[:, channels : channels + full].astype(F32) for kv in keyvals] + [
        jnp.concatenate([kv[:, channels + full :] for kv in keyvals], axis=1).astype(F32)
    ]
    products = []
    for q in queries:
        again = jnp.concatenate([q[:, full:]] * frames, axis=1)
        row = [q[:, :full] * k for k in keys[:frames]] + [again * keys[frames]]
        products.append(jnp.concatenate(row, axis=1))
    scores = dot(jnp.concatenate(products, axis=0), to_lanes_ref[...])
    source = lax.div(lax.broadcasted_iota(jnp.int32, (1, LANES), 1), stride)
    window = window_ref[...].reshape(1, 1)
    copies = jnp.zeros((1, LANES), F32)
    for n in range(count):
        copies = copies + jnp.where(source == picks_ref[:, n : n + 1], 1.0, 0.0)
    weights = []
    for i in range(part):
        times = copies + jnp.where(jnp.abs(source - (start + i)) < window, 1.0, 0.0)
        s = jnp.where(times > 0.0, scores[i * cells : (i + 1) * cells], -jnp.inf)
        top = jnp.maximum(s, pltpu.roll(s, stride, 1))
        top = jnp.maximum(top, pltpu.roll(top, 2 * stride, 1))
        w = jnp.exp(s - top) * times
        total = w + pltpu.roll(w, stride, 1)
        total = total + pltpu.roll(total, 2 * stride, 1)
        top_ref[i] = top
        sum_ref[i] = total
        weights.append(w.astype(BF))
    spread = dot(jnp.concatenate(weights, axis=0), beside(to_channels_ref))
    for i in range(part):
        share = spread[i * cells : (i + 1) * cells]
        wide = share[:, :full] * values[0]
        for j in range(1, frames):
            wide = wide + share[:, j * full : (j + 1) * full] * values[j]
        tail = share[:, frames * full :] * values[frames]
        tail = tail[:, :LANES] + tail[:, LANES:]
        tail = tail + pltpu.roll(tail, LANES // 2, 1)
        mix_ref[i] = jnp.concatenate([wide, tail], axis=1)


def keys_and_values(anchor_ref, wkv_ref, channels):
    return [
        dot(unpacked(anchor_ref[n], channels), wkv_ref[...]).astype(BF)
        for n in range(anchor_ref.shape[0])
    ]


def updated(keyvals, to_lanes_ref, to_channels_ref, query, top, total, mix, last):
    frames, cells, channels = query.shape
    full = channels // LANES * LANES
    size = frames * cells
    query, top, total, mix = (v.reshape(size, v.shape[-1]) for v in (query, top, total, mix))
    low = lax.broadcasted_iota(jnp.int32, (1, LANES), 1) < LANES // 4
    for n, keyval in enumerate(keyvals):
        key = jnp.concatenate([keyval[:, :channels]] * frames, axis=0)
        scores = dot(query * key, to_lanes_ref[...])
        higher = jnp.maximum(top, scores)
        weight = jnp.exp(scores - higher)
        fade = jnp.exp(top - higher)
        total = total * fade + weight
        both = jnp.where(low, weight, fade)
        if last and n == len(keyvals) - 1:
            both = both / total
        spread = dot(both.astype(BF), beside(to_channels_ref))
        value = keyval[:, channels:].astype(F32)
        value = jnp.concatenate([value] * frames, axis=0)
        wide = spread[:, :full] * value[:, :full] + spread[:, full : 2 * full] * mix[:, :full]
        tail = jnp.concatenate([value[:, full:], mix[:, full + LANES // 2 :]], axis=1)
        tail = spread[:, 2 * full :] * tail
        tail = tail + pltpu.roll(tail, LANES // 2, 1)
        mix = jnp.concatenate([wide, tail], axis=1)
        top = higher
    return top, total, mix


def relay_kernel(order_ref, *refs):
    count = len(refs) // 2
    for n in range(count):
        refs[count + n][...] = refs[n][...]
    refs[-1][...] = jnp.zeros_like(refs[-1])


def anchor_kernel(pieces, anchor_ref, wkv_ref, to_lanes_ref, to_channels_ref, query_ref, *refs):
    top, total, mix = (
        jnp.concatenate([ref[...] for ref in refs[v * pieces : (v + 1) * pieces]], axis=0)
        for v in range(3)
    )
    new = updated(
        keys_and_values(anchor_ref, wkv_ref, query_ref.shape[2]), to_lanes_ref, to_channels_ref,
        query_ref[...], top, total, mix, False,
    )
    for ref, v in zip(refs[3 * pieces :], new):
        ref[...] = v.reshape(ref.shape)


def last_kernel(
    anchor_ref, wkv_ref, to_lanes_ref, to_channels_ref, query_ref, top_ref, sum_ref, mix_ref,
    temporal_ref, wo_ref, out_ref, out_buf, sems,
):
    frames, cells, channels = query_ref.shape
    height, width = out_ref.shape[1:3]
    keyvals = keys_and_values(anchor_ref, wkv_ref, channels)
    copies = []
    group = 2 if frames % 2 == 0 else 1
    for lo in range(0, frames, group):
        at = slice(lo, lo + group)
        _, _, mix = updated(
            keyvals, to_lanes_ref, to_channels_ref,
            query_ref[at], top_ref[at], sum_ref[at], mix_ref[at], True,
        )
        result = dot(mix[:, :channels].astype(BF), wo_ref[...])
        total = temporal_ref[at].astype(F32) + result.reshape(group, cells, channels)
        out_buf[at] = total.astype(BF).reshape(group, height, width, channels)
        copies.append(pltpu.make_async_copy(out_buf.at[at], out_ref.at[at], sems.at[lo // group]))
        copies[-1].start()
    for copy in copies:
        copy.wait()


def swapped(odd, even, axis):
    count = lax.axis_size(axis)
    pairs = [[(i, i + 1) for i in range(start, count - 1, 2)] for start in (1, 0)]
    pairs = [up + [(j, i) for i, j in up] for up in pairs]
    return lax.ppermute(odd, axis, pairs[0]), lax.ppermute(even, axis, pairs[1])


def on_device(
    latents, anchor_index, window, gain_one, spatial_w, gain_two, temporal_w, gain_three,
    w_query, w_keyval, w_out,
):
    frames, height, width, channels = latents.shape
    cells = height * width
    count = anchor_index.shape[1]
    ws = spatial_w.reshape(3, 3 * channels, channels)
    one = 2 * channels * channels
    packed = cells * channels // LANES
    edge_packed = frames * width * channels // LANES
    lanes_up = (channels + LANES - 1) // LANES * LANES
    sem = pltpu.SemaphoreType.DMA
    some = (frames, cells, channels)

    x, g1, g2, g3, w = latents, gain_one, gain_two, gain_three, ws

    strip_odd, strip_even = call(
        edge_kernel, [((edge_packed, LANES), BF)] * 2, [VMEM], flops=8 * frames * cells * one
    )(x)
    strip_odd, strip_even = swapped(strip_odd, strip_even, "strip")
    outer_col = pltpu.VMEM((2 * cells, 3 * channels), BF)
    inner_col = pltpu.VMEM(((frames - 2) * (cells + 2 * width), 3 * channels), BF)
    middle = (2, cells - 2 * width, channels)
    mid, mid2, edge, w_rem, order = call(
        outer_kernel,
        [
            (middle, BF),
            (middle, BF),
            ((2, 2, width, channels), F32),
            ((3 * channels, 3 * (channels % 256)), BF),
            ((8, LANES), F32),
        ],
        [VMEM] * 4,
        [outer_col],
        flops=9 * 2 * cells * one,
    )(x, g1, g2, w)
    outer_spatial, outer_hidden, clip_odd, clip_even = call(
        functools.partial(outer_edge_kernel, frames),
        [((2, cells, channels), BF)] * 2 + [((packed, LANES), BF)] * 2,
        [VMEM] * 10,
        flops=6 * 2 * width * one,
    )(edge, strip_odd, strip_even, order, mid, mid2, g1, g2, w, w_rem)
    clip_odd, clip_even = swapped(clip_odd, clip_even, "clip")
    spatial, hidden = call(
        inner_kernel,
        [(some, BF), (some, BF)],
        [VMEM] * 9,
        [inner_col],
        flops=9 * (frames - 2) * cells * one,
    )(x, strip_odd, strip_even, g1, g2, w, w_rem, outer_spatial, outer_hidden)
    (chosen,) = call(
        chosen_kernel, [((count, packed, LANES), BF)], [VMEM] * 7, flops=3 * cells * one
    )(anchor_index, clip_odd, clip_even, spatial, hidden, g3, temporal_w)
    clips = lax.axis_size("clip")
    powers = clips & (clips - 1) == 0
    if powers:
        routes = [[(i, i ^ s) for i in range(clips)] for s in range(1, clips, 2)]
    else:
        routes = [[(i, (i + s) % clips) for i in range(clips)] for s in range(1, clips)]
    arrived = [lax.ppermute(chosen, "clip", route) for route in routes]
    temporal, query, keyval = call(
        temporal_kernel,
        [(some, BF), (some, BF), ((frames, cells, 2 * channels), BF)],
        [VMEM] * 8,
        flops=6 * frames * cells * one,
        limit=32,
    )(clip_odd, clip_even, spatial, hidden, g3, temporal_w, w_query, w_keyval)
    maps = head_maps(frames, channels)
    split = frames // 2 if frames > 1 else frames

    def local(start, part, after):
        shape = (part, cells)
        return call(
            functools.partial(local_kernel, start),
            [(shape + (LANES,), F32)] * 2 + [(shape + (lanes_up,), F32), ((8, LANES), F32)],
            [VMEM] * 7,
            flops=10 * part * cells * one,
            limit=32,
        )(anchor_index, window, query, keyval, *maps, after)

    *early, after = local(0, split, order)
    if powers and clips > 2:
        *relayed, after = call(
            relay_kernel,
            [(chosen.shape, BF)] * (clips // 2 - 1) + [((8, LANES), F32)],
            [VMEM] * (clips // 2),
        )(after, *arrived[1:])
        arrived += [lax.ppermute(v, "clip", routes[0]) for v in relayed]
    *late, after = local(split, frames - split, after)
    pieces = 2
    state = [v for pair in zip(early, late) for v in pair]
    states = [((frames, cells, LANES), F32)] * 2 + [((frames, cells, lanes_up), F32)]
    to_lanes, _ = head_maps(1, channels, everywhere=True)
    _, to_channels = head_maps(2, channels)
    for arrival in arrived[:-1]:
        state = call(
            functools.partial(anchor_kernel, pieces),
            states,
            [VMEM] * (5 + 3 * pieces),
            flops=4 * frames * cells * one,
            limit=32,
        )(arrival, w_keyval, to_lanes, to_channels, query, *state)
        pieces = 1
    (out,) = call(
        last_kernel,
        [(latents.shape, BF)],
        [VMEM] * 10,
        [pltpu.VMEM(latents.shape, BF), sem((frames,))],
        flops=5 * frames * cells * one,
        limit=32,
        out_specs=(HBM,),
    )(arrived[-1], w_keyval, to_lanes, to_channels, query, *state, temporal, w_out)
    return out


def solution(mesh):
    return jax.shard_map(
        on_device,
        mesh=mesh,
        in_specs=(
            P(("groups", "clip"), "strip", None, None),
            P(("groups", "clip"), None),
            P(),
            P(),
            P(),
            P(),
            P(),
            P(),
            P(),
            P(),
            P(),
        ),
        out_specs=P(("groups", "clip"), "strip", None, None),
        check_vma=False,
    )
```

```python
import functools
import math

import jax
import jax.numpy as jnp
import numpy as np
from jax import lax
from jax.experimental import pallas as pl
from jax.experimental.pallas import tpu as pltpu
from jax.sharding import PartitionSpec as P

HEADS = 5
HEAD_DIM = 64
LANES = 128
BF = jnp.bfloat16
F32 = jnp.float32
VMEM = pl.BlockSpec(memory_space=pltpu.VMEM)
HBM = pl.BlockSpec(memory_space=pltpu.HBM)
MIB = 1 << 20


def call(body, outs, specs, scratch=(), flops=0, limit=24, out_specs=None):
    return pl.pallas_call(
        body,
        out_shape=tuple(jax.ShapeDtypeStruct(s, d) for s, d in outs),
        in_specs=specs,
        out_specs=out_specs or tuple(VMEM for _ in outs),
        scratch_shapes=list(scratch),
        cost_estimate=pl.CostEstimate(flops=flops, bytes_accessed=2 * MIB, transcendentals=0),
        compiler_params=pltpu.CompilerParams(vmem_limit_bytes=limit * MIB),
    )


def dot(a, b):
    return jnp.dot(a, b, preferred_element_type=F32)


def norm(v, gain_ref):
    wide = v.astype(F32)
    centred = wide - jnp.mean(wide, axis=-1, keepdims=True)
    variance = jnp.mean(centred * centred, axis=-1, keepdims=True)
    return centred * lax.rsqrt(variance + 1e-05) * gain_ref[...].reshape(1, v.shape[1])


def silu(u):
    half = 0.5 * u
    return half + half * jnp.tanh(half)


def pack_into(ref, h):
    cells, channels = h.shape
    full = channels // LANES
    for t in range(full):
        ref[t * cells : (t + 1) * cells, :] = h[:, t * LANES : (t + 1) * LANES]
    rest = channels - full * LANES
    if rest:
        share = LANES // rest
        part = cells // share
        ref[full * cells :, :] = jnp.concatenate(
            [h[s * part : (s + 1) * part, full * LANES :] for s in range(share)], axis=1
        )


def unpacked(p, channels):
    cells = p.shape[0] * LANES // channels
    full = channels // LANES
    pieces = [p[t * cells : (t + 1) * cells, :] for t in range(full)]
    rest = channels - full * LANES
    if rest:
        share = LANES // rest
        tail = p[full * cells :, :]
        pieces.append(
            jnp.concatenate([tail[:, s * rest : (s + 1) * rest] for s in range(share)], axis=0)
        )
    return jnp.concatenate(pieces, axis=1)


def columns(h, width):
    cells, channels = h.shape
    left = pltpu.roll(h, 1, 0)
    right = pltpu.roll(h, cells - 1, 0)
    place = lax.broadcasted_iota(jnp.int32, (8, channels), 0)
    lefts, rights = [], []
    for lo in range(0, cells, width):
        hi = lo + width
        lefts += [jnp.where(place == 0, 0.0, left[lo : lo + 8]), left[lo + 8 : hi]]
        rights += [right[lo : hi - 8], jnp.where(place == 7, 0.0, right[hi - 8 : hi])]
    sides = [jnp.concatenate(lefts, axis=0), h, jnp.concatenate(rights, axis=0)]
    return jnp.concatenate([v.astype(BF) for v in sides], axis=1)


def scalar(ref, n):
    values = ref[...].astype(F32)
    place = lax.broadcasted_iota(jnp.int32, values.shape, 1)
    return jnp.sum(jnp.where(place == n, values, 0.0)).astype(jnp.int32)


def at_odd(axis):
    return lax.rem(lax.axis_index(axis), 2) == 1


def sorted_pair(odd_ref, even_ref, axis):
    odd = at_odd(axis)
    first, second = odd_ref[...], even_ref[...]
    return jnp.where(odd, second, first), jnp.where(odd, first, second)


def edge_kernel(x_ref, odd_ref, even_ref):
    frames, height, width, channels = x_ref.shape
    odd = at_odd("strip")
    top = x_ref[:, 0].reshape(frames * width, channels)
    bottom = x_ref[:, height - 1].reshape(frames * width, channels)
    pack_into(odd_ref, jnp.where(odd, bottom, top))
    pack_into(even_ref, jnp.where(odd, top, bottom))


def rests_into(rem_ref, w_ref):
    full = w_ref.shape[2] // 256 * 256
    rest = w_ref.shape[2] - full
    for a in range(3):
        rem_ref[:, a * rest : (a + 1) * rest] = w_ref[a, :, full:]


def hidden_columns(v, g1_ref, width):
    return columns(silu(norm(v, g1_ref)), width)


def stacked_rows(col_ref, count, height, width, w_ref, rem_ref):
    cells = height * width
    rims = (col_ref.shape[0] - count * cells) // 2
    channels = w_ref.shape[2]
    full = channels // 256 * 256
    rest = channels - full
    size = count * cells
    above = dot(col_ref[: rims + size], w_ref[0, :, :full])
    centre = dot(col_ref[rims : rims + size], w_ref[1, :, :full])
    below = dot(col_ref[rims:], w_ref[2, :, :full])
    tails = dot(col_ref[...], rem_ref[...])

    def terms(place, row):
        own = place * cells + row * width
        wide = centre[own : own + width]
        tail = tails[rims + own : rims + own + width, rest : 2 * rest]
        if row > 0 or rims:
            at = rims + own - width if row > 0 else place * width
            wide = wide + above[at : at + width]
            tail = tail + tails[at : at + width, :rest]
        if row < height - 1 or rims:
            at = own + width if row < height - 1 else size + place * width
            wide = wide + below[at : at + width]
            tail = tail + tails[rims + at : rims + at + width, 2 * rest :]
        return jnp.concatenate([wide, tail], axis=1)

    return terms


def rim_rows(packed, frames, width, channels):
    rows = unpacked(packed, channels)
    return jnp.concatenate([rows[f * width : (f + 1) * width] for f in frames], axis=0)


def outer_kernel(x_ref, g1_ref, g2_ref, w_ref, mid_ref, mid2_ref, edge_ref, rem_ref, order_ref, col_ref):
    frames, height, width, channels = x_ref.shape
    cells = height * width
    order_ref[...] = jnp.zeros_like(order_ref)
    rests_into(rem_ref, w_ref)
    outer = (0, frames - 1)
    for s, f in enumerate(outer):
        x = x_ref[f].reshape(cells, channels)
        col_ref[s * cells : (s + 1) * cells] = hidden_columns(x, g1_ref, width)
    terms = stacked_rows(col_ref, 2, height, width, w_ref, rem_ref)
    for s, f in enumerate(outer):
        for row in range(height):
            total = x_ref[f, row].astype(F32) + terms(s, row)
            if 0 < row < height - 1:
                rounded = total.astype(BF)
                lo = (row - 1) * width
                mid_ref[s, lo : lo + width] = rounded
                mid2_ref[s, lo : lo + width] = silu(norm(rounded, g2_ref)).astype(BF)
            else:
                edge_ref[s, 0 if row == 0 else 1] = total


def outer_edge_kernel(
    frames, edge_ref, odd_ref, even_ref, order_ref, mid_ref, mid2_ref, g1_ref, g2_ref, w_ref, rem_ref,
    spatial_ref, hidden_ref, odd_clip_ref, even_clip_ref,
):
    _, cells, channels = spatial_ref.shape
    width = edge_ref.shape[2]
    full = channels // 256 * 256
    rest = channels - full
    spatial_ref[:, width : cells - width] = mid_ref[...]
    hidden_ref[:, width : cells - width] = mid2_ref[...]
    cols = [
        hidden_columns(rim_rows(packed, (0, frames - 1), width, channels), g1_ref, width)
        for packed in sorted_pair(odd_ref, even_ref, "strip")
    ]
    tails = dot(jnp.concatenate(cols, axis=0), rem_ref[...])
    size = 2 * width
    for side, lo in ((0, 0), (1, cells - width)):
        tail = tails[:size, :rest] if side == 0 else tails[size:, 2 * rest :]
        wide = dot(cols[side], w_ref[2 * side, :, :full])
        term = jnp.concatenate([wide, tail], axis=1)
        rounded = (edge_ref[:, side].reshape(size, channels) + term).astype(BF)
        hidden = silu(norm(rounded, g2_ref)).astype(BF)
        spatial_ref[:, lo : lo + width] = rounded.reshape(2, width, channels)
        hidden_ref[:, lo : lo + width] = hidden.reshape(2, width, channels)
    odd = at_odd("clip")
    pack_into(odd_clip_ref, jnp.where(odd, hidden_ref[1], hidden_ref[0]))
    pack_into(even_clip_ref, jnp.where(odd, hidden_ref[0], hidden_ref[1]))


def inner_kernel(
    x_ref, odd_ref, even_ref, g1_ref, g2_ref, w_ref, rem_ref, outer_spatial_ref, outer_hidden_ref,
    spatial_ref, hidden_ref, col_ref,
):
    frames, height, width, channels = x_ref.shape
    cells = height * width
    for s, f in ((0, 0), (1, frames - 1)):
        spatial_ref[f] = outer_spatial_ref[s]
        hidden_ref[f] = outer_hidden_ref[s]
    inside = range(1, frames - 1)
    above, below = sorted_pair(odd_ref, even_ref, "strip")
    rims = len(inside) * width
    end = rims + len(inside) * cells
    col_ref[:rims] = hidden_columns(rim_rows(above, inside, width, channels), g1_ref, width)
    for s, f in enumerate(inside):
        x = x_ref[f].reshape(cells, channels)
        lo = rims + s * cells
        col_ref[lo : lo + cells] = hidden_columns(x, g1_ref, width)
    col_ref[end:] = hidden_columns(rim_rows(below, inside, width, channels), g1_ref, width)
    terms = stacked_rows(col_ref, len(inside), height, width, w_ref, rem_ref)
    for s, f in enumerate(inside):
        for row in range(height):
            rounded = (x_ref[f, row].astype(F32) + terms(s, row)).astype(BF)
            lo = row * width
            spatial_ref[f, lo : lo + width] = rounded
            hidden_ref[f, lo : lo + width] = silu(norm(rounded, g2_ref)).astype(BF)


def chosen_kernel(
    picks_ref, odd_ref, even_ref, spatial_ref, hidden_ref, g3_ref, wt_ref, chosen_ref
):
    frames, cells, channels = spatial_ref.shape
    before, after = (unpacked(v, channels) for v in sorted_pair(odd_ref, even_ref, "clip"))
    for n in range(chosen_ref.shape[0]):
        pick = scalar(picks_ref, n)
        earlier = jnp.where(pick == 0, before, hidden_ref[jnp.maximum(pick - 1, 0)])
        later = jnp.where(pick == frames - 1, after, hidden_ref[jnp.minimum(pick + 1, frames - 1)])
        total = spatial_ref[pick].astype(F32) + dot(hidden_ref[pick], wt_ref[1])
        total = total + dot(earlier, wt_ref[0]) + dot(later, wt_ref[2])
        pack_into(chosen_ref.at[n], norm(total.astype(BF), g3_ref).astype(BF))


def temporal_kernel(
    odd_ref, even_ref, spatial_ref, hidden_ref, g3_ref, wt_ref, wq_ref, wkv_ref,
    temporal_ref, query_ref, keyval_ref,
):
    frames, cells, channels = spatial_ref.shape
    size = frames * cells
    before, after = (unpacked(v, channels) for v in sorted_pair(odd_ref, even_ref, "clip"))
    hidden = hidden_ref[...].reshape(size, channels)
    total = spatial_ref[...].reshape(size, channels).astype(F32) + dot(hidden, wt_ref[1])
    total = total + dot(jnp.concatenate([before, hidden[: size - cells]], axis=0), wt_ref[0])
    total = total + dot(jnp.concatenate([hidden[cells:], after], axis=0), wt_ref[2])
    temporal = total.astype(BF)
    temporal_ref[...] = temporal.reshape(frames, cells, channels)
    normed = norm(temporal, g3_ref).astype(BF)
    query_ref[...] = dot(normed, wq_ref[...]).astype(BF).reshape(frames, cells, channels)
    keyval_ref[...] = dot(normed, wkv_ref[...]).astype(BF).reshape(frames, cells, 2 * channels)


def head_maps(count, channels, everywhere=False):
    full = channels // LANES * LANES
    rest = channels - full
    stride = LANES // 4
    hits = np.zeros((count * channels, LANES), np.float32)
    for j in range(count):
        for c in range(channels):
            at = j * full + c if c < full else count * full + j * rest + c - full
            lanes = range(0, LANES, stride) if everywhere else (j * stride,)
            for lane in lanes:
                hits[at, lane + c // HEAD_DIM] = 1.0
    padded = np.zeros((-(-hits.shape[0] // LANES) * LANES, LANES), np.float32)
    padded[: hits.shape[0]] = hits
    blocks = padded.reshape(-1, LANES, LANES).transpose(0, 2, 1).reshape(-1, LANES)
    return jnp.asarray(hits / math.sqrt(HEAD_DIM), BF), jnp.asarray(blocks, BF)


def beside(ref):
    count = ref.shape[0] // LANES
    return jnp.concatenate([ref[b * LANES : (b + 1) * LANES] for b in range(count)], axis=1)


def local_kernel(
    start, picks_ref, window_ref, query_ref, keyval_ref, to_lanes_ref, to_channels_ref, order_ref,
    top_ref, sum_ref, mix_ref, next_ref,
):
    next_ref[...] = jnp.zeros_like(next_ref)
    frames, cells, channels = query_ref.shape
    count = picks_ref.shape[1]
    full = channels // LANES * LANES
    stride = LANES // 4
    part = top_ref.shape[0]
    queries = [query_ref[start + f] for f in range(part)]
    keyvals = [keyval_ref[f] for f in range(frames)]
    keys = [kv[:, :full] for kv in keyvals] + [
        jnp.concatenate([kv[:, full:channels] for kv in keyvals], axis=1)
    ]
    values = [kv[:, channels : channels + full].astype(F32) for kv in keyvals] + [
        jnp.concatenate([kv[:, channels + full :] for kv in keyvals], axis=1).astype(F32)
    ]
    products = []
    for q in queries:
        again = jnp.concatenate([q[:, full:]] * frames, axis=1)
        row = [q[:, :full] * k for k in keys[:frames]] + [again * keys[frames]]
        products.append(jnp.concatenate(row, axis=1))
    scores = dot(jnp.concatenate(products, axis=0), to_lanes_ref[...])
    source = lax.div(lax.broadcasted_iota(jnp.int32, (1, LANES), 1), stride)
    window = window_ref[...].reshape(1, 1)
    copies = jnp.zeros((1, LANES), F32)
    for n in range(count):
        copies = copies + jnp.where(source == picks_ref[:, n : n + 1], 1.0, 0.0)
    weights = []
    for i in range(part):
        times = copies + jnp.where(jnp.abs(source - (start + i)) < window, 1.0, 0.0)
        s = jnp.where(times > 0.0, scores[i * cells : (i + 1) * cells], -jnp.inf)
        top = jnp.maximum(s, pltpu.roll(s, stride, 1))
        top = jnp.maximum(top, pltpu.roll(top, 2 * stride, 1))
        w = jnp.exp(s - top) * times
        total = w + pltpu.roll(w, stride, 1)
        total = total + pltpu.roll(total, 2 * stride, 1)
        top_ref[i] = top
        sum_ref[i] = total
        weights.append(w.astype(BF))
    spread = dot(jnp.concatenate(weights, axis=0), beside(to_channels_ref))
    for i in range(part):
        share = spread[i * cells : (i + 1) * cells]
        wide = share[:, :full] * values[0]
        for j in range(1, frames):
            wide = wide + share[:, j * full : (j + 1) * full] * values[j]
        tail = share[:, frames * full :] * values[frames]
        tail = tail[:, :LANES] + tail[:, LANES:]
        tail = tail + pltpu.roll(tail, LANES // 2, 1)
        mix_ref[i] = jnp.concatenate([wide, tail], axis=1)


def keys_and_values(anchor_ref, wkv_ref, channels):
    return [
        dot(unpacked(anchor_ref[n], channels), wkv_ref[...]).astype(BF)
        for n in range(anchor_ref.shape[0])
    ]


def updated(keyvals, to_lanes_ref, to_channels_ref, query, top, total, mix, last):
    frames, cells, channels = query.shape
    full = channels // LANES * LANES
    size = frames * cells
    query, top, total, mix = (v.reshape(size, v.shape[-1]) for v in (query, top, total, mix))
    low = lax.broadcasted_iota(jnp.int32, (1, LANES), 1) < LANES // 4
    for n, keyval in enumerate(keyvals):
        key = jnp.concatenate([keyval[:, :channels]] * frames, axis=0)
        scores = dot(query * key, to_lanes_ref[...])
        higher = jnp.maximum(top, scores)
        weight = jnp.exp(scores - higher)
        fade = jnp.exp(top - higher)
        total = total * fade + weight
        both = jnp.where(low, weight, fade)
        if last and n == len(keyvals) - 1:
            both = both / total
        spread = dot(both.astype(BF), beside(to_channels_ref))
        value = keyval[:, channels:].astype(F32)
        value = jnp.concatenate([value] * frames, axis=0)
        wide = spread[:, :full] * value[:, :full] + spread[:, full : 2 * full] * mix[:, :full]
        tail = jnp.concatenate([value[:, full:], mix[:, full + LANES // 2 :]], axis=1)
        tail = spread[:, 2 * full :] * tail
        tail = tail + pltpu.roll(tail, LANES // 2, 1)
        mix = jnp.concatenate([wide, tail], axis=1)
        top = higher
    return top, total, mix


def copy_kernel(from_ref, to_ref):
    to_ref[...] = from_ref[...]


def relay_kernel(order_ref, *refs):
    count = len(refs) // 2
    for n in range(count):
        refs[count + n][...] = refs[n][...]
    refs[-1][...] = jnp.zeros_like(refs[-1])


def anchor_kernel(pieces, anchor_ref, wkv_ref, to_lanes_ref, to_channels_ref, query_ref, *refs):
    top, total, mix = (
        jnp.concatenate([ref[...] for ref in refs[v * pieces : (v + 1) * pieces]], axis=0)
        for v in range(3)
    )
    new = updated(
        keys_and_values(anchor_ref, wkv_ref, query_ref.shape[2]), to_lanes_ref, to_channels_ref,
        query_ref[...], top, total, mix, False,
    )
    for ref, v in zip(refs[3 * pieces :], new):
        ref[...] = v.reshape(ref.shape)


def last_kernel(
    anchor_ref, wkv_ref, to_lanes_ref, to_channels_ref, query_ref, top_ref, sum_ref, mix_ref,
    temporal_ref, wo_ref, out_ref, out_buf, sems,
):
    frames, cells, channels = query_ref.shape
    height, width = out_ref.shape[1:3]
    keyvals = keys_and_values(anchor_ref, wkv_ref, channels)
    copies = []
    group = 2 if frames % 2 == 0 else 1
    for lo in range(0, frames, group):
        at = slice(lo, lo + group)
        _, _, mix = updated(
            keyvals, to_lanes_ref, to_channels_ref,
            query_ref[at], top_ref[at], sum_ref[at], mix_ref[at], True,
        )
        result = dot(mix[:, :channels].astype(BF), wo_ref[...])
        total = temporal_ref[at].astype(F32) + result.reshape(group, cells, channels)
        out_buf[at] = total.astype(BF).reshape(group, height, width, channels)
        copies.append(pltpu.make_async_copy(out_buf.at[at], out_ref.at[at], sems.at[lo // group]))
        copies[-1].start()
    for copy in copies:
        copy.wait()


def swapped(odd, even, axis):
    count = lax.axis_size(axis)
    pairs = [[(i, i + 1) for i in range(start, count - 1, 2)] for start in (1, 0)]
    pairs = [up + [(j, i) for i, j in up] for up in pairs]
    return lax.ppermute(odd, axis, pairs[0]), lax.ppermute(even, axis, pairs[1])


def on_device(
    latents, anchor_index, window, gain_one, spatial_w, gain_two, temporal_w, gain_three,
    w_query, w_keyval, w_out,
):
    frames, height, width, channels = latents.shape
    cells = height * width
    count = anchor_index.shape[1]
    ws = spatial_w.reshape(3, 3 * channels, channels)
    one = 2 * channels * channels
    packed = cells * channels // LANES
    edge_packed = frames * width * channels // LANES
    lanes_up = (channels + LANES - 1) // LANES * LANES
    sem = pltpu.SemaphoreType.DMA
    some = (frames, cells, channels)

    x, g1, g2, g3, w = latents, gain_one, gain_two, gain_three, ws

    strip_odd, strip_even = call(
        edge_kernel, [((edge_packed, LANES), BF)] * 2, [VMEM], flops=8 * frames * cells * one
    )(x)
    strip_odd, strip_even = swapped(strip_odd, strip_even, "strip")
    outer_col = pltpu.VMEM((2 * cells, 3 * channels), BF)
    inner_col = pltpu.VMEM(((frames - 2) * (cells + 2 * width), 3 * channels), BF)
    middle = (2, cells - 2 * width, channels)
    mid, mid2, edge, w_rem, order = call(
        outer_kernel,
        [
            (middle, BF),
            (middle, BF),
            ((2, 2, width, channels), F32),
            ((3 * channels, 3 * (channels % 256)), BF),
            ((8, LANES), F32),
        ],
        [VMEM] * 4,
        [outer_col],
        flops=9 * 2 * cells * one,
    )(x, g1, g2, w)
    outer_spatial, outer_hidden, clip_odd, clip_even = call(
        functools.partial(outer_edge_kernel, frames),
        [((2, cells, channels), BF)] * 2 + [((packed, LANES), BF)] * 2,
        [VMEM] * 10,
        flops=6 * 2 * width * one,
    )(edge, strip_odd, strip_even, order, mid, mid2, g1, g2, w, w_rem)
    clip_odd, clip_even = swapped(clip_odd, clip_even, "clip")
    spatial, hidden = call(
        inner_kernel,
        [(some, BF), (some, BF)],
        [VMEM] * 9,
        [inner_col],
        flops=9 * (frames - 2) * cells * one,
    )(x, strip_odd, strip_even, g1, g2, w, w_rem, outer_spatial, outer_hidden)
    (chosen,) = call(
        chosen_kernel, [((count, packed, LANES), BF)], [VMEM] * 7, flops=3 * cells * one
    )(anchor_index, clip_odd, clip_even, spatial, hidden, g3, temporal_w)
    clips = lax.axis_size("clip")
    powers = clips & (clips - 1) == 0
    if powers:
        routes = [[(i, i ^ s) for i in range(clips)] for s in range(1, clips, 2)]
    else:
        routes = [[(i, (i + s) % clips) for i in range(clips)] for s in range(1, clips)]
    (near,) = call(copy_kernel, [(chosen.shape, BF)], [VMEM])(chosen)
    sent = [near] + [chosen] * (len(routes) - 1)
    arrived = [lax.ppermute(v, "clip", route) for v, route in zip(sent, routes)]
    temporal, query, keyval = call(
        temporal_kernel,
        [(some, BF), (some, BF), ((frames, cells, 2 * channels), BF)],
        [VMEM] * 8,
        flops=6 * frames * cells * one,
        limit=32,
    )(clip_odd, clip_even, spatial, hidden, g3, temporal_w, w_query, w_keyval)
    maps = head_maps(frames, channels)
    split = frames // 2 if frames > 1 else frames

    def local(start, part, after):
        shape = (part, cells)
        return call(
            functools.partial(local_kernel, start),
            [(shape + (LANES,), F32)] * 2 + [(shape + (lanes_up,), F32), ((8, LANES), F32)],
            [VMEM] * 7,
            flops=10 * part * cells * one,
            limit=32,
        )(anchor_index, window, query, keyval, *maps, after)

    *early, after = local(0, split, order)
    if powers and clips > 2:
        *relayed, after = call(
            relay_kernel,
            [(chosen.shape, BF)] * (clips // 2 - 1) + [((8, LANES), F32)],
            [VMEM] * (clips // 2),
        )(after, *arrived[1:])
        arrived += [lax.ppermute(v, "clip", routes[0]) for v in relayed]
    *late, after = local(split, frames - split, after)
    pieces = 2
    state = [v for pair in zip(early, late) for v in pair]
    states = [((frames, cells, LANES), F32)] * 2 + [((frames, cells, lanes_up), F32)]
    to_lanes, _ = head_maps(1, channels, everywhere=True)
    _, to_channels = head_maps(2, channels)
    for arrival in arrived[:-1]:
        state = call(
            functools.partial(anchor_kernel, pieces),
            states,
            [VMEM] * (5 + 3 * pieces),
            flops=4 * frames * cells * one,
            limit=32,
        )(arrival, w_keyval, to_lanes, to_channels, query, *state)
        pieces = 1
    (out,) = call(
        last_kernel,
        [(latents.shape, BF)],
        [VMEM] * 10,
        [pltpu.VMEM(latents.shape, BF), sem((frames,))],
        flops=5 * frames * cells * one,
        limit=32,
        out_specs=(HBM,),
    )(arrived[-1], w_keyval, to_lanes, to_channels, query, *state, temporal, w_out)
    return out


def solution(mesh):
    return jax.shard_map(
        on_device,
        mesh=mesh,
        in_specs=(
            P(("groups", "clip"), "strip", None, None),
            P(("groups", "clip"), None),
            P(),
            P(),
            P(),
            P(),
            P(),
            P(),
            P(),
            P(),
            P(),
        ),
        out_specs=P(("groups", "clip"), "strip", None, None),
        check_vma=False,
    )
```

```python
import functools
import math

import jax
import jax.numpy as jnp
import numpy as np
from jax import lax
from jax.experimental import pallas as pl
from jax.experimental.pallas import tpu as pltpu
from jax.sharding import PartitionSpec as P

HEADS = 5
HEAD_DIM = 64
LANES = 128
BF = jnp.bfloat16
F32 = jnp.float32
VMEM = pl.BlockSpec(memory_space=pltpu.VMEM)
HBM = pl.BlockSpec(memory_space=pltpu.HBM)
MIB = 1 << 20


def call(body, outs, specs, scratch=(), flops=0, limit=24, out_specs=None):
    return pl.pallas_call(
        body,
        out_shape=tuple(jax.ShapeDtypeStruct(s, d) for s, d in outs),
        in_specs=specs,
        out_specs=out_specs or tuple(VMEM for _ in outs),
        scratch_shapes=list(scratch),
        cost_estimate=pl.CostEstimate(flops=flops, bytes_accessed=2 * MIB, transcendentals=0),
        compiler_params=pltpu.CompilerParams(vmem_limit_bytes=limit * MIB),
    )


def dot(a, b):
    return jnp.dot(a, b, preferred_element_type=F32)


def norm(v, gain_ref):
    wide = v.astype(F32)
    centred = wide - jnp.mean(wide, axis=-1, keepdims=True)
    variance = jnp.mean(centred * centred, axis=-1, keepdims=True)
    return centred * lax.rsqrt(variance + 1e-05) * gain_ref[...].reshape(1, v.shape[1])


def silu(u):
    half = 0.5 * u
    return half + half * jnp.tanh(half)


def pack_into(ref, h):
    cells, channels = h.shape
    full = channels // LANES
    for t in range(full):
        ref[t * cells : (t + 1) * cells, :] = h[:, t * LANES : (t + 1) * LANES]
    rest = channels - full * LANES
    if rest:
        share = LANES // rest
        part = cells // share
        ref[full * cells :, :] = jnp.concatenate(
            [h[s * part : (s + 1) * part, full * LANES :] for s in range(share)], axis=1
        )


def unpacked(p, channels):
    cells = p.shape[0] * LANES // channels
    full = channels // LANES
    pieces = [p[t * cells : (t + 1) * cells, :] for t in range(full)]
    rest = channels - full * LANES
    if rest:
        share = LANES // rest
        tail = p[full * cells :, :]
        pieces.append(
            jnp.concatenate([tail[:, s * rest : (s + 1) * rest] for s in range(share)], axis=0)
        )
    return jnp.concatenate(pieces, axis=1)


def columns(h, width):
    cells, channels = h.shape
    left = pltpu.roll(h, 1, 0)
    right = pltpu.roll(h, cells - 1, 0)
    place = lax.broadcasted_iota(jnp.int32, (8, channels), 0)
    lefts, rights = [], []
    for lo in range(0, cells, width):
        hi = lo + width
        lefts += [jnp.where(place == 0, 0.0, left[lo : lo + 8]), left[lo + 8 : hi]]
        rights += [right[lo : hi - 8], jnp.where(place == 7, 0.0, right[hi - 8 : hi])]
    sides = [jnp.concatenate(lefts, axis=0), h, jnp.concatenate(rights, axis=0)]
    return jnp.concatenate([v.astype(BF) for v in sides], axis=1)


def scalar(ref, n):
    values = ref[...].astype(F32)
    place = lax.broadcasted_iota(jnp.int32, values.shape, 1)
    return jnp.sum(jnp.where(place == n, values, 0.0)).astype(jnp.int32)


def at_odd(axis):
    return lax.rem(lax.axis_index(axis), 2) == 1


def sorted_pair(odd_ref, even_ref, axis):
    odd = at_odd(axis)
    first, second = odd_ref[...], even_ref[...]
    return jnp.where(odd, second, first), jnp.where(odd, first, second)


def edge_kernel(x_ref, odd_ref, even_ref):
    frames, height, width, channels = x_ref.shape
    odd = at_odd("strip")
    top = x_ref[:, 0].reshape(frames * width, channels)
    bottom = x_ref[:, height - 1].reshape(frames * width, channels)
    pack_into(odd_ref, jnp.where(odd, bottom, top))
    pack_into(even_ref, jnp.where(odd, top, bottom))


def rests_into(rem_ref, w_ref):
    full = w_ref.shape[2] // 256 * 256
    rest = w_ref.shape[2] - full
    for a in range(3):
        rem_ref[:, a * rest : (a + 1) * rest] = w_ref[a, :, full:]


def hidden_columns(v, g1_ref, width):
    return columns(silu(norm(v, g1_ref)), width)


def stacked_rows(col_ref, count, height, width, w_ref, rem_ref):
    cells = height * width
    rims = (col_ref.shape[0] - count * cells) // 2
    channels = w_ref.shape[2]
    full = channels // 256 * 256
    rest = channels - full
    size = count * cells
    above = dot(col_ref[: rims + size], w_ref[0, :, :full])
    centre = dot(col_ref[rims : rims + size], w_ref[1, :, :full])
    below = dot(col_ref[rims:], w_ref[2, :, :full])
    tails = dot(col_ref[...], rem_ref[...])

    def terms(place, row):
        own = place * cells + row * width
        wide = centre[own : own + width]
        tail = tails[rims + own : rims + own + width, rest : 2 * rest]
        if row > 0 or rims:
            at = rims + own - width if row > 0 else place * width
            wide = wide + above[at : at + width]
            tail = tail + tails[at : at + width, :rest]
        if row < height - 1 or rims:
            at = own + width if row < height - 1 else size + place * width
            wide = wide + below[at : at + width]
            tail = tail + tails[rims + at : rims + at + width, 2 * rest :]
        return jnp.concatenate([wide, tail], axis=1)

    return terms


def rim_rows(packed, frames, width, channels):
    rows = unpacked(packed, channels)
    return jnp.concatenate([rows[f * width : (f + 1) * width] for f in frames], axis=0)


def outer_kernel(x_ref, g1_ref, g2_ref, w_ref, mid_ref, mid2_ref, edge_ref, rem_ref, order_ref, col_ref):
    frames, height, width, channels = x_ref.shape
    cells = height * width
    order_ref[...] = jnp.zeros_like(order_ref)
    rests_into(rem_ref, w_ref)
    outer = (0, frames - 1)
    for s, f in enumerate(outer):
        x = x_ref[f].reshape(cells, channels)
        col_ref[s * cells : (s + 1) * cells] = hidden_columns(x, g1_ref, width)
    terms = stacked_rows(col_ref, 2, height, width, w_ref, rem_ref)
    for s, f in enumerate(outer):
        for row in range(height):
            total = x_ref[f, row].astype(F32) + terms(s, row)
            if 0 < row < height - 1:
                rounded = total.astype(BF)
                lo = (row - 1) * width
                mid_ref[s, lo : lo + width] = rounded
                mid2_ref[s, lo : lo + width] = silu(norm(rounded, g2_ref)).astype(BF)
            else:
                edge_ref[s, 0 if row == 0 else 1] = total


def outer_edge_kernel(
    frames, edge_ref, odd_ref, even_ref, order_ref, mid_ref, mid2_ref, g1_ref, g2_ref, w_ref, rem_ref,
    spatial_ref, hidden_ref, even_clip_ref, odd_clip_ref,
):
    _, cells, channels = spatial_ref.shape
    width = edge_ref.shape[2]
    full = channels // 256 * 256
    rest = channels - full
    spatial_ref[:, width : cells - width] = mid_ref[...]
    hidden_ref[:, width : cells - width] = mid2_ref[...]
    cols = [
        hidden_columns(rim_rows(packed, (0, frames - 1), width, channels), g1_ref, width)
        for packed in sorted_pair(odd_ref, even_ref, "strip")
    ]
    tails = dot(jnp.concatenate(cols, axis=0), rem_ref[...])
    size = 2 * width
    for side, lo in ((0, 0), (1, cells - width)):
        tail = tails[:size, :rest] if side == 0 else tails[size:, 2 * rest :]
        wide = dot(cols[side], w_ref[2 * side, :, :full])
        term = jnp.concatenate([wide, tail], axis=1)
        rounded = (edge_ref[:, side].reshape(size, channels) + term).astype(BF)
        hidden = silu(norm(rounded, g2_ref)).astype(BF)
        spatial_ref[:, lo : lo + width] = rounded.reshape(2, width, channels)
        hidden_ref[:, lo : lo + width] = hidden.reshape(2, width, channels)
    odd = at_odd("clip")
    pack_into(odd_clip_ref, jnp.where(odd, hidden_ref[1], hidden_ref[0]))
    pack_into(even_clip_ref, jnp.where(odd, hidden_ref[0], hidden_ref[1]))


def inner_kernel(
    x_ref, odd_ref, even_ref, g1_ref, g2_ref, w_ref, rem_ref, outer_spatial_ref, outer_hidden_ref,
    spatial_ref, hidden_ref, col_ref,
):
    frames, height, width, channels = x_ref.shape
    cells = height * width
    for s, f in ((0, 0), (1, frames - 1)):
        spatial_ref[f] = outer_spatial_ref[s]
        hidden_ref[f] = outer_hidden_ref[s]
    inside = range(1, frames - 1)
    above, below = sorted_pair(odd_ref, even_ref, "strip")
    rims = len(inside) * width
    end = rims + len(inside) * cells
    col_ref[:rims] = hidden_columns(rim_rows(above, inside, width, channels), g1_ref, width)
    for s, f in enumerate(inside):
        x = x_ref[f].reshape(cells, channels)
        lo = rims + s * cells
        col_ref[lo : lo + cells] = hidden_columns(x, g1_ref, width)
    col_ref[end:] = hidden_columns(rim_rows(below, inside, width, channels), g1_ref, width)
    terms = stacked_rows(col_ref, len(inside), height, width, w_ref, rem_ref)
    for s, f in enumerate(inside):
        for row in range(height):
            rounded = (x_ref[f, row].astype(F32) + terms(s, row)).astype(BF)
            lo = row * width
            spatial_ref[f, lo : lo + width] = rounded
            hidden_ref[f, lo : lo + width] = silu(norm(rounded, g2_ref)).astype(BF)


def chosen_kernel(
    picks_ref, even_ref, odd_ref, spatial_ref, hidden_ref, g3_ref, wt_ref, chosen_ref
):
    frames, cells, channels = spatial_ref.shape
    before, after = (unpacked(v, channels) for v in sorted_pair(odd_ref, even_ref, "clip"))
    for n in range(chosen_ref.shape[0]):
        pick = scalar(picks_ref, n)
        earlier = jnp.where(pick == 0, before, hidden_ref[jnp.maximum(pick - 1, 0)])
        later = jnp.where(pick == frames - 1, after, hidden_ref[jnp.minimum(pick + 1, frames - 1)])
        total = spatial_ref[pick].astype(F32) + dot(hidden_ref[pick], wt_ref[1])
        total = total + dot(earlier, wt_ref[0]) + dot(later, wt_ref[2])
        pack_into(chosen_ref.at[n], norm(total.astype(BF), g3_ref).astype(BF))


def temporal_kernel(
    even_ref, odd_ref, spatial_ref, hidden_ref, g3_ref, wt_ref, wq_ref, wkv_ref,
    temporal_ref, query_ref, keyval_ref,
):
    frames, cells, channels = spatial_ref.shape
    size = frames * cells
    before, after = (unpacked(v, channels) for v in sorted_pair(odd_ref, even_ref, "clip"))
    hidden = hidden_ref[...].reshape(size, channels)
    total = spatial_ref[...].reshape(size, channels).astype(F32) + dot(hidden, wt_ref[1])
    total = total + dot(jnp.concatenate([before, hidden[: size - cells]], axis=0), wt_ref[0])
    total = total + dot(jnp.concatenate([hidden[cells:], after], axis=0), wt_ref[2])
    temporal = total.astype(BF)
    temporal_ref[...] = temporal.reshape(frames, cells, channels)
    normed = norm(temporal, g3_ref).astype(BF)
    query_ref[...] = dot(normed, wq_ref[...]).astype(BF).reshape(frames, cells, channels)
    keyval_ref[...] = dot(normed, wkv_ref[...]).astype(BF).reshape(frames, cells, 2 * channels)


def head_maps(count, channels, everywhere=False):
    full = channels // LANES * LANES
    rest = channels - full
    stride = LANES // 4
    hits = np.zeros((count * channels, LANES), np.float32)
    for j in range(count):
        for c in range(channels):
            at = j * full + c if c < full else count * full + j * rest + c - full
            lanes = range(0, LANES, stride) if everywhere else (j * stride,)
            for lane in lanes:
                hits[at, lane + c // HEAD_DIM] = 1.0
    padded = np.zeros((-(-hits.shape[0] // LANES) * LANES, LANES), np.float32)
    padded[: hits.shape[0]] = hits
    blocks = padded.reshape(-1, LANES, LANES).transpose(0, 2, 1).reshape(-1, LANES)
    return jnp.asarray(hits / math.sqrt(HEAD_DIM), BF), jnp.asarray(blocks, BF)


def beside(ref):
    count = ref.shape[0] // LANES
    return jnp.concatenate([ref[b * LANES : (b + 1) * LANES] for b in range(count)], axis=1)


def local_kernel(
    start, picks_ref, window_ref, query_ref, keyval_ref, to_lanes_ref, to_channels_ref, order_ref,
    top_ref, sum_ref, mix_ref, next_ref,
):
    next_ref[...] = jnp.zeros_like(next_ref)
    frames, cells, channels = query_ref.shape
    count = picks_ref.shape[1]
    full = channels // LANES * LANES
    stride = LANES // 4
    part = top_ref.shape[0]
    queries = [query_ref[start + f] for f in range(part)]
    keyvals = [keyval_ref[f] for f in range(frames)]
    keys = [kv[:, :full] for kv in keyvals] + [
        jnp.concatenate([kv[:, full:channels] for kv in keyvals], axis=1)
    ]
    values = [kv[:, channels : channels + full].astype(F32) for kv in keyvals] + [
        jnp.concatenate([kv[:, channels + full :] for kv in keyvals], axis=1).astype(F32)
    ]
    products = []
    for q in queries:
        again = jnp.concatenate([q[:, full:]] * frames, axis=1)
        row = [q[:, :full] * k for k in keys[:frames]] + [again * keys[frames]]
        products.append(jnp.concatenate(row, axis=1))
    scores = dot(jnp.concatenate(products, axis=0), to_lanes_ref[...])
    source = lax.div(lax.broadcasted_iota(jnp.int32, (1, LANES), 1), stride)
    window = window_ref[...].reshape(1, 1)
    copies = jnp.zeros((1, LANES), F32)
    for n in range(count):
        copies = copies + jnp.where(source == picks_ref[:, n : n + 1], 1.0, 0.0)
    weights = []
    for i in range(part):
        times = copies + jnp.where(jnp.abs(source - (start + i)) < window, 1.0, 0.0)
        s = jnp.where(times > 0.0, scores[i * cells : (i + 1) * cells], -jnp.inf)
        top = jnp.maximum(s, pltpu.roll(s, stride, 1))
        top = jnp.maximum(top, pltpu.roll(top, 2 * stride, 1))
        w = jnp.exp(s - top) * times
        total = w + pltpu.roll(w, stride, 1)
        total = total + pltpu.roll(total, 2 * stride, 1)
        top_ref[i] = top
        sum_ref[i] = total
        weights.append(w.astype(BF))
    spread = dot(jnp.concatenate(weights, axis=0), beside(to_channels_ref))
    for i in range(part):
        share = spread[i * cells : (i + 1) * cells]
        wide = share[:, :full] * values[0]
        for j in range(1, frames):
            wide = wide + share[:, j * full : (j + 1) * full] * values[j]
        tail = share[:, frames * full :] * values[frames]
        tail = tail[:, :LANES] + tail[:, LANES:]
        tail = tail + pltpu.roll(tail, LANES // 2, 1)
        mix_ref[i] = jnp.concatenate([wide, tail], axis=1)


def keys_and_values(anchor_ref, wkv_ref, channels):
    return [
        dot(unpacked(anchor_ref[n], channels), wkv_ref[...]).astype(BF)
        for n in range(anchor_ref.shape[0])
    ]


def updated(keyvals, to_lanes_ref, to_channels_ref, query, top, total, mix, last):
    frames, cells, channels = query.shape
    full = channels // LANES * LANES
    size = frames * cells
    query, top, total, mix = (v.reshape(size, v.shape[-1]) for v in (query, top, total, mix))
    low = lax.broadcasted_iota(jnp.int32, (1, LANES), 1) < LANES // 4
    for n, keyval in enumerate(keyvals):
        key = jnp.concatenate([keyval[:, :channels]] * frames, axis=0)
        scores = dot(query * key, to_lanes_ref[...])
        higher = jnp.maximum(top, scores)
        weight = jnp.exp(scores - higher)
        fade = jnp.exp(top - higher)
        total = total * fade + weight
        both = jnp.where(low, weight, fade)
        if last and n == len(keyvals) - 1:
            both = both / total
        spread = dot(both.astype(BF), beside(to_channels_ref))
        value = keyval[:, channels:].astype(F32)
        value = jnp.concatenate([value] * frames, axis=0)
        wide = spread[:, :full] * value[:, :full] + spread[:, full : 2 * full] * mix[:, :full]
        tail = jnp.concatenate([value[:, full:], mix[:, full + LANES // 2 :]], axis=1)
        tail = spread[:, 2 * full :] * tail
        tail = tail + pltpu.roll(tail, LANES // 2, 1)
        mix = jnp.concatenate([wide, tail], axis=1)
        top = higher
    return top, total, mix


def copy_kernel(from_ref, to_ref):
    to_ref[...] = from_ref[...]


def relay_kernel(order_ref, *refs):
    count = len(refs) // 2
    for n in range(count):
        refs[count + n][...] = refs[n][...]
    refs[-1][...] = jnp.zeros_like(refs[-1])


def anchor_kernel(pieces, anchor_ref, wkv_ref, to_lanes_ref, to_channels_ref, query_ref, *refs):
    top, total, mix = (
        jnp.concatenate([ref[...] for ref in refs[v * pieces : (v + 1) * pieces]], axis=0)
        for v in range(3)
    )
    new = updated(
        keys_and_values(anchor_ref, wkv_ref, query_ref.shape[2]), to_lanes_ref, to_channels_ref,
        query_ref[...], top, total, mix, False,
    )
    for ref, v in zip(refs[3 * pieces :], new):
        ref[...] = v.reshape(ref.shape)


def last_kernel(
    anchor_ref, wkv_ref, to_lanes_ref, to_channels_ref, query_ref, top_ref, sum_ref, mix_ref,
    temporal_ref, wo_ref, out_ref, out_buf, sems,
):
    frames, cells, channels = query_ref.shape
    height, width = out_ref.shape[1:3]
    keyvals = keys_and_values(anchor_ref, wkv_ref, channels)
    copies = []
    group = 2 if frames % 2 == 0 else 1
    for lo in range(0, frames, group):
        at = slice(lo, lo + group)
        _, _, mix = updated(
            keyvals, to_lanes_ref, to_channels_ref,
            query_ref[at], top_ref[at], sum_ref[at], mix_ref[at], True,
        )
        result = dot(mix[:, :channels].astype(BF), wo_ref[...])
        total = temporal_ref[at].astype(F32) + result.reshape(group, cells, channels)
        out_buf[at] = total.astype(BF).reshape(group, height, width, channels)
        copies.append(pltpu.make_async_copy(out_buf.at[at], out_ref.at[at], sems.at[lo // group]))
        copies[-1].start()
    for copy in copies:
        copy.wait()


def swapped(odd, even, axis, even_first):
    count = lax.axis_size(axis)
    pairs = [[(i, i + 1) for i in range(start, count - 1, 2)] for start in (1, 0)]
    pairs = [up + [(j, i) for i, j in up] for up in pairs]
    if even_first:
        even = lax.ppermute(even, axis, pairs[1])
        return lax.ppermute(odd, axis, pairs[0]), even
    odd = lax.ppermute(odd, axis, pairs[0])
    return odd, lax.ppermute(even, axis, pairs[1])


def on_device(
    latents, anchor_index, window, gain_one, spatial_w, gain_two, temporal_w, gain_three,
    w_query, w_keyval, w_out,
):
    frames, height, width, channels = latents.shape
    cells = height * width
    count = anchor_index.shape[1]
    ws = spatial_w.reshape(3, 3 * channels, channels)
    one = 2 * channels * channels
    packed = cells * channels // LANES
    edge_packed = frames * width * channels // LANES
    lanes_up = (channels + LANES - 1) // LANES * LANES
    sem = pltpu.SemaphoreType.DMA
    some = (frames, cells, channels)

    x, g1, g2, g3, w = latents, gain_one, gain_two, gain_three, ws

    strip_odd, strip_even = call(
        edge_kernel, [((edge_packed, LANES), BF)] * 2, [VMEM], flops=8 * frames * cells * one
    )(x)
    strip_odd, strip_even = swapped(strip_odd, strip_even, "strip", False)
    outer_col = pltpu.VMEM((2 * cells, 3 * channels), BF)
    inner_col = pltpu.VMEM(((frames - 2) * (cells + 2 * width), 3 * channels), BF)
    middle = (2, cells - 2 * width, channels)
    mid, mid2, edge, w_rem, order = call(
        outer_kernel,
        [
            (middle, BF),
            (middle, BF),
            ((2, 2, width, channels), F32),
            ((3 * channels, 3 * (channels % 256)), BF),
            ((8, LANES), F32),
        ],
        [VMEM] * 4,
        [outer_col],
        flops=9 * 2 * cells * one,
    )(x, g1, g2, w)
    outer_spatial, outer_hidden, clip_even, clip_odd = call(
        functools.partial(outer_edge_kernel, frames),
        [((2, cells, channels), BF)] * 2 + [((packed, LANES), BF)] * 2,
        [VMEM] * 10,
        flops=6 * 2 * width * one,
    )(edge, strip_odd, strip_even, order, mid, mid2, g1, g2, w, w_rem)
    clip_odd, clip_even = swapped(clip_odd, clip_even, "clip", True)
    spatial, hidden = call(
        inner_kernel,
        [(some, BF), (some, BF)],
        [VMEM] * 9,
        [inner_col],
        flops=9 * (frames - 2) * cells * one,
    )(x, strip_odd, strip_even, g1, g2, w, w_rem, outer_spatial, outer_hidden)
    (chosen,) = call(
        chosen_kernel, [((count, packed, LANES), BF)], [VMEM] * 7, flops=3 * cells * one
    )(anchor_index, clip_even, clip_odd, spatial, hidden, g3, temporal_w)
    clips = lax.axis_size("clip")
    powers = clips & (clips - 1) == 0
    if powers:
        routes = [[(i, i ^ s) for i in range(clips)] for s in range(1, clips, 2)]
    else:
        routes = [[(i, (i + s) % clips) for i in range(clips)] for s in range(1, clips)]
    (near,) = call(copy_kernel, [(chosen.shape, BF)], [VMEM])(chosen)
    sent = [near] + [chosen] * (len(routes) - 1)
    arrived = [lax.ppermute(v, "clip", route) for v, route in zip(sent, routes)]
    temporal, query, keyval = call(
        temporal_kernel,
        [(some, BF), (some, BF), ((frames, cells, 2 * channels), BF)],
        [VMEM] * 8,
        flops=6 * frames * cells * one,
        limit=32,
    )(clip_even, clip_odd, spatial, hidden, g3, temporal_w, w_query, w_keyval)
    maps = head_maps(frames, channels)
    split = frames // 2 if frames > 1 else frames

    def local(start, part, after):
        shape = (part, cells)
        return call(
            functools.partial(local_kernel, start),
            [(shape + (LANES,), F32)] * 2 + [(shape + (lanes_up,), F32), ((8, LANES), F32)],
            [VMEM] * 7,
            flops=10 * part * cells * one,
            limit=32,
        )(anchor_index, window, query, keyval, *maps, after)

    *early, after = local(0, split, order)
    if powers and clips > 2:
        *relayed, after = call(
            relay_kernel,
            [(chosen.shape, BF)] * (clips // 2 - 1) + [((8, LANES), F32)],
            [VMEM] * (clips // 2),
        )(after, *arrived[1:])
        arrived += [lax.ppermute(v, "clip", routes[0]) for v in relayed]
    *late, after = local(split, frames - split, after)
    pieces = 2
    state = [v for pair in zip(early, late) for v in pair]
    states = [((frames, cells, LANES), F32)] * 2 + [((frames, cells, lanes_up), F32)]
    to_lanes, _ = head_maps(1, channels, everywhere=True)
    _, to_channels = head_maps(2, channels)
    for arrival in arrived[:-1]:
        state = call(
            functools.partial(anchor_kernel, pieces),
            states,
            [VMEM] * (5 + 3 * pieces),
            flops=4 * frames * cells * one,
            limit=32,
        )(arrival, w_keyval, to_lanes, to_channels, query, *state)
        pieces = 1
    (out,) = call(
        last_kernel,
        [(latents.shape, BF)],
        [VMEM] * 10,
        [pltpu.VMEM(latents.shape, BF), sem((frames,))],
        flops=5 * frames * cells * one,
        limit=32,
        out_specs=(HBM,),
    )(arrived[-1], w_keyval, to_lanes, to_channels, query, *state, temporal, w_out)
    return out


def solution(mesh):
    return jax.shard_map(
        on_device,
        mesh=mesh,
        in_specs=(
            P(("groups", "clip"), "strip", None, None),
            P(("groups", "clip"), None),
            P(),
            P(),
            P(),
            P(),
            P(),
            P(),
            P(),
            P(),
            P(),
        ),
        out_specs=P(("groups", "clip"), "strip", None, None),
        check_vma=False,
    )
```

```python
import functools
import math

import jax
import jax.numpy as jnp
import numpy as np
from jax import lax
from jax.experimental import pallas as pl
from jax.experimental.pallas import tpu as pltpu
from jax.sharding import PartitionSpec as P

HEADS = 5
HEAD_DIM = 64
LANES = 128
BF = jnp.bfloat16
F32 = jnp.float32
VMEM = pl.BlockSpec(memory_space=pltpu.VMEM)
HBM = pl.BlockSpec(memory_space=pltpu.HBM)
MIB = 1 << 20


def call(body, outs, specs, scratch=(), flops=0, limit=24, out_specs=None):
    return pl.pallas_call(
        body,
        out_shape=tuple(jax.ShapeDtypeStruct(s, d) for s, d in outs),
        in_specs=specs,
        out_specs=out_specs or tuple(VMEM for _ in outs),
        scratch_shapes=list(scratch),
        cost_estimate=pl.CostEstimate(flops=flops, bytes_accessed=2 * MIB, transcendentals=0),
        compiler_params=pltpu.CompilerParams(vmem_limit_bytes=limit * MIB),
    )


def dot(a, b):
    return jnp.dot(a, b, preferred_element_type=F32)


def norm(v, gain_ref):
    wide = v.astype(F32)
    centred = wide - jnp.mean(wide, axis=-1, keepdims=True)
    variance = jnp.mean(centred * centred, axis=-1, keepdims=True)
    return centred * lax.rsqrt(variance + 1e-05) * gain_ref[...].reshape(1, v.shape[1])


def silu(u):
    half = 0.5 * u
    return half + half * jnp.tanh(half)


def pack_into(ref, h):
    cells, channels = h.shape
    full = channels // LANES
    for t in range(full):
        ref[t * cells : (t + 1) * cells, :] = h[:, t * LANES : (t + 1) * LANES]
    rest = channels - full * LANES
    if rest:
        share = LANES // rest
        part = cells // share
        ref[full * cells :, :] = jnp.concatenate(
            [h[s * part : (s + 1) * part, full * LANES :] for s in range(share)], axis=1
        )


def unpacked(p, channels):
    cells = p.shape[0] * LANES // channels
    full = channels // LANES
    pieces = [p[t * cells : (t + 1) * cells, :] for t in range(full)]
    rest = channels - full * LANES
    if rest:
        share = LANES // rest
        tail = p[full * cells :, :]
        pieces.append(
            jnp.concatenate([tail[:, s * rest : (s + 1) * rest] for s in range(share)], axis=0)
        )
    return jnp.concatenate(pieces, axis=1)


def columns(h, width):
    cells, channels = h.shape
    left = pltpu.roll(h, 1, 0)
    right = pltpu.roll(h, cells - 1, 0)
    place = lax.broadcasted_iota(jnp.int32, (8, channels), 0)
    lefts, rights = [], []
    for lo in range(0, cells, width):
        hi = lo + width
        lefts += [jnp.where(place == 0, 0.0, left[lo : lo + 8]), left[lo + 8 : hi]]
        rights += [right[lo : hi - 8], jnp.where(place == 7, 0.0, right[hi - 8 : hi])]
    sides = [jnp.concatenate(lefts, axis=0), h, jnp.concatenate(rights, axis=0)]
    return jnp.concatenate([v.astype(BF) for v in sides], axis=1)


def scalar(ref, n):
    values = ref[...].astype(F32)
    place = lax.broadcasted_iota(jnp.int32, values.shape, 1)
    return jnp.sum(jnp.where(place == n, values, 0.0)).astype(jnp.int32)


def at_odd(axis):
    return lax.rem(lax.axis_index(axis), 2) == 1


def sorted_pair(odd_ref, even_ref, axis):
    odd = at_odd(axis)
    first, second = odd_ref[...], even_ref[...]
    return jnp.where(odd, second, first), jnp.where(odd, first, second)


def edge_kernel(x_ref, odd_ref, even_ref):
    frames, height, width, channels = x_ref.shape
    odd = at_odd("strip")
    top = x_ref[:, 0].reshape(frames * width, channels)
    bottom = x_ref[:, height - 1].reshape(frames * width, channels)
    pack_into(odd_ref, jnp.where(odd, bottom, top))
    pack_into(even_ref, jnp.where(odd, top, bottom))


def rests_into(rem_ref, w_ref):
    full = w_ref.shape[2] // 256 * 256
    rest = w_ref.shape[2] - full
    for a in range(3):
        rem_ref[:, a * rest : (a + 1) * rest] = w_ref[a, :, full:]


def hidden_columns(v, g1_ref, width):
    return columns(silu(norm(v, g1_ref)), width)


def stacked_rows(col_ref, count, height, width, w_ref, rem_ref):
    cells = height * width
    rims = (col_ref.shape[0] - count * cells) // 2
    channels = w_ref.shape[2]
    full = channels // 256 * 256
    rest = channels - full
    size = count * cells
    above = dot(col_ref[: rims + size], w_ref[0, :, :full])
    centre = dot(col_ref[rims : rims + size], w_ref[1, :, :full])
    below = dot(col_ref[rims:], w_ref[2, :, :full])
    tails = dot(col_ref[...], rem_ref[...])

    def terms(place, row):
        own = place * cells + row * width
        wide = centre[own : own + width]
        tail = tails[rims + own : rims + own + width, rest : 2 * rest]
        if row > 0 or rims:
            at = rims + own - width if row > 0 else place * width
            wide = wide + above[at : at + width]
            tail = tail + tails[at : at + width, :rest]
        if row < height - 1 or rims:
            at = own + width if row < height - 1 else size + place * width
            wide = wide + below[at : at + width]
            tail = tail + tails[rims + at : rims + at + width, 2 * rest :]
        return jnp.concatenate([wide, tail], axis=1)

    return terms


def rim_rows(packed, frames, width, channels):
    rows = unpacked(packed, channels)
    return jnp.concatenate([rows[f * width : (f + 1) * width] for f in frames], axis=0)


def outer_kernel(x_ref, g1_ref, g2_ref, w_ref, mid_ref, mid2_ref, edge_ref, rem_ref, order_ref, col_ref):
    frames, height, width, channels = x_ref.shape
    cells = height * width
    order_ref[...] = jnp.zeros_like(order_ref)
    rests_into(rem_ref, w_ref)
    outer = (0, frames - 1)
    for s, f in enumerate(outer):
        x = x_ref[f].reshape(cells, channels)
        col_ref[s * cells : (s + 1) * cells] = hidden_columns(x, g1_ref, width)
    terms = stacked_rows(col_ref, 2, height, width, w_ref, rem_ref)
    for s, f in enumerate(outer):
        for row in range(height):
            total = x_ref[f, row].astype(F32) + terms(s, row)
            if 0 < row < height - 1:
                rounded = total.astype(BF)
                lo = (row - 1) * width
                mid_ref[s, lo : lo + width] = rounded
                mid2_ref[s, lo : lo + width] = silu(norm(rounded, g2_ref)).astype(BF)
            else:
                edge_ref[s, 0 if row == 0 else 1] = total


def outer_edge_kernel(
    frames, edge_ref, odd_ref, even_ref, order_ref, mid_ref, mid2_ref, g1_ref, g2_ref, w_ref, rem_ref,
    spatial_ref, hidden_ref, even_clip_ref, odd_clip_ref,
):
    _, cells, channels = spatial_ref.shape
    width = edge_ref.shape[2]
    full = channels // 256 * 256
    rest = channels - full
    spatial_ref[:, width : cells - width] = mid_ref[...]
    hidden_ref[:, width : cells - width] = mid2_ref[...]
    cols = [
        hidden_columns(rim_rows(packed, (0, frames - 1), width, channels), g1_ref, width)
        for packed in sorted_pair(odd_ref, even_ref, "strip")
    ]
    tails = dot(jnp.concatenate(cols, axis=0), rem_ref[...])
    size = 2 * width
    for side, lo in ((0, 0), (1, cells - width)):
        tail = tails[:size, :rest] if side == 0 else tails[size:, 2 * rest :]
        wide = dot(cols[side], w_ref[2 * side, :, :full])
        term = jnp.concatenate([wide, tail], axis=1)
        rounded = (edge_ref[:, side].reshape(size, channels) + term).astype(BF)
        hidden = silu(norm(rounded, g2_ref)).astype(BF)
        spatial_ref[:, lo : lo + width] = rounded.reshape(2, width, channels)
        hidden_ref[:, lo : lo + width] = hidden.reshape(2, width, channels)
    odd = at_odd("clip")
    pack_into(odd_clip_ref, jnp.where(odd, hidden_ref[1], hidden_ref[0]))
    pack_into(even_clip_ref, jnp.where(odd, hidden_ref[0], hidden_ref[1]))


def inner_kernel(
    x_ref, odd_ref, even_ref, g1_ref, g2_ref, w_ref, rem_ref, outer_spatial_ref, outer_hidden_ref,
    spatial_ref, hidden_ref, col_ref,
):
    frames, height, width, channels = x_ref.shape
    cells = height * width
    for s, f in ((0, 0), (1, frames - 1)):
        spatial_ref[f] = outer_spatial_ref[s]
        hidden_ref[f] = outer_hidden_ref[s]
    inside = range(1, frames - 1)
    above, below = sorted_pair(odd_ref, even_ref, "strip")
    rims = len(inside) * width
    end = rims + len(inside) * cells
    col_ref[:rims] = hidden_columns(rim_rows(above, inside, width, channels), g1_ref, width)
    for s, f in enumerate(inside):
        x = x_ref[f].reshape(cells, channels)
        lo = rims + s * cells
        col_ref[lo : lo + cells] = hidden_columns(x, g1_ref, width)
    col_ref[end:] = hidden_columns(rim_rows(below, inside, width, channels), g1_ref, width)
    terms = stacked_rows(col_ref, len(inside), height, width, w_ref, rem_ref)
    for s, f in enumerate(inside):
        for row in range(height):
            rounded = (x_ref[f, row].astype(F32) + terms(s, row)).astype(BF)
            lo = row * width
            spatial_ref[f, lo : lo + width] = rounded
            hidden_ref[f, lo : lo + width] = silu(norm(rounded, g2_ref)).astype(BF)


def chosen_kernel(
    picks_ref, even_ref, odd_ref, spatial_ref, hidden_ref, g3_ref, wt_ref, chosen_ref
):
    frames, cells, channels = spatial_ref.shape
    before, after = (unpacked(v, channels) for v in sorted_pair(odd_ref, even_ref, "clip"))
    for n in range(chosen_ref.shape[0]):
        pick = scalar(picks_ref, n)
        earlier = jnp.where(pick == 0, before, hidden_ref[jnp.maximum(pick - 1, 0)])
        later = jnp.where(pick == frames - 1, after, hidden_ref[jnp.minimum(pick + 1, frames - 1)])
        total = spatial_ref[pick].astype(F32) + dot(hidden_ref[pick], wt_ref[1])
        total = total + dot(earlier, wt_ref[0]) + dot(later, wt_ref[2])
        pack_into(chosen_ref.at[n], norm(total.astype(BF), g3_ref).astype(BF))


def temporal_kernel(
    even_ref, odd_ref, spatial_ref, hidden_ref, g3_ref, wt_ref, wq_ref, wkv_ref,
    temporal_ref, query_ref, keyval_ref,
):
    frames, cells, channels = spatial_ref.shape
    size = frames * cells
    before, after = (unpacked(v, channels) for v in sorted_pair(odd_ref, even_ref, "clip"))
    hidden = hidden_ref[...].reshape(size, channels)
    total = spatial_ref[...].reshape(size, channels).astype(F32) + dot(hidden, wt_ref[1])
    total = total + dot(jnp.concatenate([before, hidden[: size - cells]], axis=0), wt_ref[0])
    total = total + dot(jnp.concatenate([hidden[cells:], after], axis=0), wt_ref[2])
    temporal = total.astype(BF)
    temporal_ref[...] = temporal.reshape(frames, cells, channels)
    normed = norm(temporal, g3_ref).astype(BF)
    query_ref[...] = dot(normed, wq_ref[...]).astype(BF).reshape(frames, cells, channels)
    keyval_ref[...] = dot(normed, wkv_ref[...]).astype(BF).reshape(frames, cells, 2 * channels)


def head_maps(count, channels, everywhere=False):
    full = channels // LANES * LANES
    rest = channels - full
    stride = LANES // 4
    hits = np.zeros((count * channels, LANES), np.float32)
    for j in range(count):
        for c in range(channels):
            at = j * full + c if c < full else count * full + j * rest + c - full
            lanes = range(0, LANES, stride) if everywhere else (j * stride,)
            for lane in lanes:
                hits[at, lane + c // HEAD_DIM] = 1.0
    padded = np.zeros((-(-hits.shape[0] // LANES) * LANES, LANES), np.float32)
    padded[: hits.shape[0]] = hits
    blocks = padded.reshape(-1, LANES, LANES).transpose(0, 2, 1).reshape(-1, LANES)
    return jnp.asarray(hits / math.sqrt(HEAD_DIM), BF), jnp.asarray(blocks, BF)


def beside(ref):
    count = ref.shape[0] // LANES
    return jnp.concatenate([ref[b * LANES : (b + 1) * LANES] for b in range(count)], axis=1)


def local_kernel(
    start, picks_ref, window_ref, query_ref, keyval_ref, to_lanes_ref, to_channels_ref, order_ref,
    top_ref, sum_ref, mix_ref, next_ref,
):
    next_ref[...] = jnp.zeros_like(next_ref)
    frames, cells, channels = query_ref.shape
    count = picks_ref.shape[1]
    full = channels // LANES * LANES
    stride = LANES // 4
    part = top_ref.shape[0]
    queries = [query_ref[start + f] for f in range(part)]
    keyvals = [keyval_ref[f] for f in range(frames)]
    keys = [kv[:, :full] for kv in keyvals] + [
        jnp.concatenate([kv[:, full:channels] for kv in keyvals], axis=1)
    ]
    values = [kv[:, channels : channels + full].astype(F32) for kv in keyvals] + [
        jnp.concatenate([kv[:, channels + full :] for kv in keyvals], axis=1).astype(F32)
    ]
    products = []
    for q in queries:
        again = jnp.concatenate([q[:, full:]] * frames, axis=1)
        row = [q[:, :full] * k for k in keys[:frames]] + [again * keys[frames]]
        products.append(jnp.concatenate(row, axis=1))
    scores = dot(jnp.concatenate(products, axis=0), to_lanes_ref[...])
    source = lax.div(lax.broadcasted_iota(jnp.int32, (1, LANES), 1), stride)
    window = window_ref[...].reshape(1, 1)
    copies = jnp.zeros((1, LANES), F32)
    for n in range(count):
        copies = copies + jnp.where(source == picks_ref[:, n : n + 1], 1.0, 0.0)
    weights = []
    for i in range(part):
        times = copies + jnp.where(jnp.abs(source - (start + i)) < window, 1.0, 0.0)
        s = jnp.where(times > 0.0, scores[i * cells : (i + 1) * cells], -jnp.inf)
        top = jnp.maximum(s, pltpu.roll(s, stride, 1))
        top = jnp.maximum(top, pltpu.roll(top, 2 * stride, 1))
        w = jnp.exp(s - top) * times
        total = w + pltpu.roll(w, stride, 1)
        total = total + pltpu.roll(total, 2 * stride, 1)
        top_ref[i] = top
        sum_ref[i] = total
        weights.append(w.astype(BF))
    spread = dot(jnp.concatenate(weights, axis=0), beside(to_channels_ref))
    for i in range(part):
        share = spread[i * cells : (i + 1) * cells]
        wide = share[:, :full] * values[0]
        for j in range(1, frames):
            wide = wide + share[:, j * full : (j + 1) * full] * values[j]
        tail = share[:, frames * full :] * values[frames]
        tail = tail[:, :LANES] + tail[:, LANES:]
        tail = tail + pltpu.roll(tail, LANES // 2, 1)
        mix_ref[i] = jnp.concatenate([wide, tail], axis=1)


def keys_and_values(anchor_ref, wkv_ref, channels):
    return [
        dot(unpacked(anchor_ref[n], channels), wkv_ref[...]).astype(BF)
        for n in range(anchor_ref.shape[0])
    ]


def updated(keyvals, to_lanes_ref, to_channels_ref, query, top, total, mix, last):
    frames, cells, channels = query.shape
    full = channels // LANES * LANES
    size = frames * cells
    query, top, total, mix = (v.reshape(size, v.shape[-1]) for v in (query, top, total, mix))
    low = lax.broadcasted_iota(jnp.int32, (1, LANES), 1) < LANES // 4
    for n, keyval in enumerate(keyvals):
        key = jnp.concatenate([keyval[:, :channels]] * frames, axis=0)
        scores = dot(query * key, to_lanes_ref[...])
        higher = jnp.maximum(top, scores)
        weight = jnp.exp(scores - higher)
        fade = jnp.exp(top - higher)
        total = total * fade + weight
        both = jnp.where(low, weight, fade)
        if last and n == len(keyvals) - 1:
            both = both / total
        spread = dot(both.astype(BF), beside(to_channels_ref))
        value = keyval[:, channels:].astype(F32)
        value = jnp.concatenate([value] * frames, axis=0)
        wide = spread[:, :full] * value[:, :full] + spread[:, full : 2 * full] * mix[:, :full]
        tail = jnp.concatenate([value[:, full:], mix[:, full + LANES // 2 :]], axis=1)
        tail = spread[:, 2 * full :] * tail
        tail = tail + pltpu.roll(tail, LANES // 2, 1)
        mix = jnp.concatenate([wide, tail], axis=1)
        top = higher
    return top, total, mix


def copy_kernel(from_ref, order_ref, to_ref):
    to_ref[...] = from_ref[...]


def relay_kernel(order_ref, *refs):
    count = len(refs) // 2
    for n in range(count):
        refs[count + n][...] = refs[n][...]
    refs[-1][...] = jnp.zeros_like(refs[-1])


def anchor_kernel(pieces, anchor_ref, wkv_ref, to_lanes_ref, to_channels_ref, query_ref, *refs):
    top, total, mix = (
        jnp.concatenate([ref[...] for ref in refs[v * pieces : (v + 1) * pieces]], axis=0)
        for v in range(3)
    )
    new = updated(
        keys_and_values(anchor_ref, wkv_ref, query_ref.shape[2]), to_lanes_ref, to_channels_ref,
        query_ref[...], top, total, mix, False,
    )
    for ref, v in zip(refs[3 * pieces :], new):
        ref[...] = v.reshape(ref.shape)


def last_kernel(
    anchor_ref, wkv_ref, to_lanes_ref, to_channels_ref, query_ref, top_ref, sum_ref, mix_ref,
    temporal_ref, wo_ref, out_ref, out_buf, sems,
):
    frames, cells, channels = query_ref.shape
    height, width = out_ref.shape[1:3]
    keyvals = keys_and_values(anchor_ref, wkv_ref, channels)
    copies = []
    group = 2 if frames % 2 == 0 else 1
    for lo in range(0, frames, group):
        at = slice(lo, lo + group)
        _, _, mix = updated(
            keyvals, to_lanes_ref, to_channels_ref,
            query_ref[at], top_ref[at], sum_ref[at], mix_ref[at], True,
        )
        result = dot(mix[:, :channels].astype(BF), wo_ref[...])
        total = temporal_ref[at].astype(F32) + result.reshape(group, cells, channels)
        out_buf[at] = total.astype(BF).reshape(group, height, width, channels)
        copies.append(pltpu.make_async_copy(out_buf.at[at], out_ref.at[at], sems.at[lo // group]))
        copies[-1].start()
    for copy in copies:
        copy.wait()


def swapped(odd, even, axis, even_first):
    count = lax.axis_size(axis)
    pairs = [[(i, i + 1) for i in range(start, count - 1, 2)] for start in (1, 0)]
    pairs = [up + [(j, i) for i, j in up] for up in pairs]
    if even_first:
        even = lax.ppermute(even, axis, pairs[1])
        return lax.ppermute(odd, axis, pairs[0]), even
    odd = lax.ppermute(odd, axis, pairs[0])
    return odd, lax.ppermute(even, axis, pairs[1])


def on_device(
    latents, anchor_index, window, gain_one, spatial_w, gain_two, temporal_w, gain_three,
    w_query, w_keyval, w_out,
):
    frames, height, width, channels = latents.shape
    cells = height * width
    count = anchor_index.shape[1]
    ws = spatial_w.reshape(3, 3 * channels, channels)
    one = 2 * channels * channels
    packed = cells * channels // LANES
    edge_packed = frames * width * channels // LANES
    lanes_up = (channels + LANES - 1) // LANES * LANES
    sem = pltpu.SemaphoreType.DMA
    some = (frames, cells, channels)

    x, g1, g2, g3, w = latents, gain_one, gain_two, gain_three, ws

    strip_odd, strip_even = call(
        edge_kernel, [((edge_packed, LANES), BF)] * 2, [VMEM], flops=8 * frames * cells * one
    )(x)
    strip_odd, strip_even = swapped(strip_odd, strip_even, "strip", False)
    outer_col = pltpu.VMEM((2 * cells, 3 * channels), BF)
    inner_col = pltpu.VMEM(((frames - 2) * (cells + 2 * width), 3 * channels), BF)
    middle = (2, cells - 2 * width, channels)
    mid, mid2, edge, w_rem, order = call(
        outer_kernel,
        [
            (middle, BF),
            (middle, BF),
            ((2, 2, width, channels), F32),
            ((3 * channels, 3 * (channels % 256)), BF),
            ((8, LANES), F32),
        ],
        [VMEM] * 4,
        [outer_col],
        flops=9 * 2 * cells * one,
    )(x, g1, g2, w)
    outer_spatial, outer_hidden, clip_even, clip_odd = call(
        functools.partial(outer_edge_kernel, frames),
        [((2, cells, channels), BF)] * 2 + [((packed, LANES), BF)] * 2,
        [VMEM] * 10,
        flops=6 * 2 * width * one,
    )(edge, strip_odd, strip_even, order, mid, mid2, g1, g2, w, w_rem)
    clip_odd, clip_even = swapped(clip_odd, clip_even, "clip", True)
    spatial, hidden = call(
        inner_kernel,
        [(some, BF), (some, BF)],
        [VMEM] * 9,
        [inner_col],
        flops=9 * (frames - 2) * cells * one,
    )(x, strip_odd, strip_even, g1, g2, w, w_rem, outer_spatial, outer_hidden)
    (chosen,) = call(
        chosen_kernel, [((count, packed, LANES), BF)], [VMEM] * 7, flops=3 * cells * one
    )(anchor_index, clip_even, clip_odd, spatial, hidden, g3, temporal_w)
    clips = lax.axis_size("clip")
    powers = clips & (clips - 1) == 0
    if powers:
        routes = [[(i, i ^ s) for i in range(clips)] for s in range(1, clips, 2)]
    else:
        routes = [[(i, (i + s) % clips) for i in range(clips)] for s in range(1, clips)]
    far = [lax.ppermute(chosen, "clip", route) for route in routes[1:]]
    temporal, query, keyval = call(
        temporal_kernel,
        [(some, BF), (some, BF), ((frames, cells, 2 * channels), BF)],
        [VMEM] * 8,
        flops=6 * frames * cells * one,
        limit=32,
    )(clip_even, clip_odd, spatial, hidden, g3, temporal_w, w_query, w_keyval)
    (near,) = call(copy_kernel, [(chosen.shape, BF)], [VMEM] * 2)(chosen, temporal)
    arrived = [lax.ppermute(near, "clip", routes[0])] + far
    maps = head_maps(frames, channels)
    split = frames // 2 if frames > 1 else frames

    def local(start, part, after):
        shape = (part, cells)
        return call(
            functools.partial(local_kernel, start),
            [(shape + (LANES,), F32)] * 2 + [(shape + (lanes_up,), F32), ((8, LANES), F32)],
            [VMEM] * 7,
            flops=10 * part * cells * one,
            limit=32,
        )(anchor_index, window, query, keyval, *maps, after)

    *early, after = local(0, split, order)
    if powers and clips > 2:
        *relayed, after = call(
            relay_kernel,
            [(chosen.shape, BF)] * (clips // 2 - 1) + [((8, LANES), F32)],
            [VMEM] * (clips // 2),
        )(after, *arrived[1:])
        arrived += [lax.ppermute(v, "clip", routes[0]) for v in relayed]
    *late, after = local(split, frames - split, after)
    pieces = 2
    state = [v for pair in zip(early, late) for v in pair]
    states = [((frames, cells, LANES), F32)] * 2 + [((frames, cells, lanes_up), F32)]
    to_lanes, _ = head_maps(1, channels, everywhere=True)
    _, to_channels = head_maps(2, channels)
    for arrival in arrived[:-1]:
        state = call(
            functools.partial(anchor_kernel, pieces),
            states,
            [VMEM] * (5 + 3 * pieces),
            flops=4 * frames * cells * one,
            limit=32,
        )(arrival, w_keyval, to_lanes, to_channels, query, *state)
        pieces = 1
    (out,) = call(
        last_kernel,
        [(latents.shape, BF)],
        [VMEM] * 10,
        [pltpu.VMEM(latents.shape, BF), sem((frames,))],
        flops=5 * frames * cells * one,
        limit=32,
        out_specs=(HBM,),
    )(arrived[-1], w_keyval, to_lanes, to_channels, query, *state, temporal, w_out)
    return out


def solution(mesh):
    return jax.shard_map(
        on_device,
        mesh=mesh,
        in_specs=(
            P(("groups", "clip"), "strip", None, None),
            P(("groups", "clip"), None),
            P(),
            P(),
            P(),
            P(),
            P(),
            P(),
            P(),
            P(),
            P(),
        ),
        out_specs=P(("groups", "clip"), "strip", None, None),
        check_vma=False,
    )
```

```python
import functools
import math

import jax
import jax.numpy as jnp
import numpy as np
from jax import lax
from jax.experimental import pallas as pl
from jax.experimental.pallas import tpu as pltpu
from jax.sharding import PartitionSpec as P

HEADS = 5
HEAD_DIM = 64
LANES = 128
BF = jnp.bfloat16
F32 = jnp.float32
VMEM = pl.BlockSpec(memory_space=pltpu.VMEM)
HBM = pl.BlockSpec(memory_space=pltpu.HBM)
MIB = 1 << 20


def call(body, outs, specs, scratch=(), flops=0, limit=24, out_specs=None):
    return pl.pallas_call(
        body,
        out_shape=tuple(jax.ShapeDtypeStruct(s, d) for s, d in outs),
        in_specs=specs,
        out_specs=out_specs or tuple(VMEM for _ in outs),
        scratch_shapes=list(scratch),
        cost_estimate=pl.CostEstimate(flops=flops, bytes_accessed=2 * MIB, transcendentals=0),
        compiler_params=pltpu.CompilerParams(vmem_limit_bytes=limit * MIB),
    )


def dot(a, b):
    return jnp.dot(a, b, preferred_element_type=F32)


def norm(v, gain_ref):
    wide = v.astype(F32)
    centred = wide - jnp.mean(wide, axis=-1, keepdims=True)
    variance = jnp.mean(centred * centred, axis=-1, keepdims=True)
    return centred * lax.rsqrt(variance + 1e-05) * gain_ref[...].reshape(1, v.shape[1])


def silu(u):
    half = 0.5 * u
    return half + half * jnp.tanh(half)


def pack_into(ref, h):
    cells, channels = h.shape
    full = channels // LANES
    for t in range(full):
        ref[t * cells : (t + 1) * cells, :] = h[:, t * LANES : (t + 1) * LANES]
    rest = channels - full * LANES
    if rest:
        share = LANES // rest
        part = cells // share
        ref[full * cells :, :] = jnp.concatenate(
            [h[s * part : (s + 1) * part, full * LANES :] for s in range(share)], axis=1
        )


def unpacked(p, channels):
    cells = p.shape[0] * LANES // channels
    full = channels // LANES
    pieces = [p[t * cells : (t + 1) * cells, :] for t in range(full)]
    rest = channels - full * LANES
    if rest:
        share = LANES // rest
        tail = p[full * cells :, :]
        pieces.append(
            jnp.concatenate([tail[:, s * rest : (s + 1) * rest] for s in range(share)], axis=0)
        )
    return jnp.concatenate(pieces, axis=1)


def columns(h, width):
    cells, channels = h.shape
    left = pltpu.roll(h, 1, 0)
    right = pltpu.roll(h, cells - 1, 0)
    place = lax.broadcasted_iota(jnp.int32, (8, channels), 0)
    lefts, rights = [], []
    for lo in range(0, cells, width):
        hi = lo + width
        lefts += [jnp.where(place == 0, 0.0, left[lo : lo + 8]), left[lo + 8 : hi]]
        rights += [right[lo : hi - 8], jnp.where(place == 7, 0.0, right[hi - 8 : hi])]
    sides = [jnp.concatenate(lefts, axis=0), h, jnp.concatenate(rights, axis=0)]
    return jnp.concatenate([v.astype(BF) for v in sides], axis=1)


def scalar(ref, n):
    values = ref[...].astype(F32)
    place = lax.broadcasted_iota(jnp.int32, values.shape, 1)
    return jnp.sum(jnp.where(place == n, values, 0.0)).astype(jnp.int32)


def at_odd(axis):
    return lax.rem(lax.axis_index(axis), 2) == 1


def sorted_pair(odd_ref, even_ref, axis):
    odd = at_odd(axis)
    first, second = odd_ref[...], even_ref[...]
    return jnp.where(odd, second, first), jnp.where(odd, first, second)


def edge_kernel(x_ref, even_ref, odd_ref):
    frames, height, width, channels = x_ref.shape
    odd = at_odd("strip")
    top = x_ref[:, 0].reshape(frames * width, channels)
    bottom = x_ref[:, height - 1].reshape(frames * width, channels)
    pack_into(odd_ref, jnp.where(odd, bottom, top))
    pack_into(even_ref, jnp.where(odd, top, bottom))


def rests_into(rem_ref, w_ref):
    full = w_ref.shape[2] // 256 * 256
    rest = w_ref.shape[2] - full
    for a in range(3):
        rem_ref[:, a * rest : (a + 1) * rest] = w_ref[a, :, full:]


def hidden_columns(v, g1_ref, width):
    return columns(silu(norm(v, g1_ref)), width)


def stacked_rows(col_ref, count, height, width, w_ref, rem_ref):
    cells = height * width
    rims = (col_ref.shape[0] - count * cells) // 2
    channels = w_ref.shape[2]
    full = channels // 256 * 256
    rest = channels - full
    size = count * cells
    above = dot(col_ref[: rims + size], w_ref[0, :, :full])
    centre = dot(col_ref[rims : rims + size], w_ref[1, :, :full])
    below = dot(col_ref[rims:], w_ref[2, :, :full])
    tails = dot(col_ref[...], rem_ref[...])

    def terms(place, row):
        own = place * cells + row * width
        wide = centre[own : own + width]
        tail = tails[rims + own : rims + own + width, rest : 2 * rest]
        if row > 0 or rims:
            at = rims + own - width if row > 0 else place * width
            wide = wide + above[at : at + width]
            tail = tail + tails[at : at + width, :rest]
        if row < height - 1 or rims:
            at = own + width if row < height - 1 else size + place * width
            wide = wide + below[at : at + width]
            tail = tail + tails[rims + at : rims + at + width, 2 * rest :]
        return jnp.concatenate([wide, tail], axis=1)

    return terms


def rim_rows(packed, frames, width, channels):
    rows = unpacked(packed, channels)
    return jnp.concatenate([rows[f * width : (f + 1) * width] for f in frames], axis=0)


def outer_kernel(x_ref, g1_ref, g2_ref, w_ref, mid_ref, mid2_ref, edge_ref, rem_ref, order_ref, col_ref):
    frames, height, width, channels = x_ref.shape
    cells = height * width
    order_ref[...] = jnp.zeros_like(order_ref)
    rests_into(rem_ref, w_ref)
    outer = (0, frames - 1)
    for s, f in enumerate(outer):
        x = x_ref[f].reshape(cells, channels)
        col_ref[s * cells : (s + 1) * cells] = hidden_columns(x, g1_ref, width)
    terms = stacked_rows(col_ref, 2, height, width, w_ref, rem_ref)
    for s, f in enumerate(outer):
        for row in range(height):
            total = x_ref[f, row].astype(F32) + terms(s, row)
            if 0 < row < height - 1:
                rounded = total.astype(BF)
                lo = (row - 1) * width
                mid_ref[s, lo : lo + width] = rounded
                mid2_ref[s, lo : lo + width] = silu(norm(rounded, g2_ref)).astype(BF)
            else:
                edge_ref[s, 0 if row == 0 else 1] = total


def outer_edge_kernel(
    frames, edge_ref, even_ref, odd_ref, order_ref, mid_ref, mid2_ref, g1_ref, g2_ref, w_ref, rem_ref,
    spatial_ref, hidden_ref, even_clip_ref, odd_clip_ref,
):
    _, cells, channels = spatial_ref.shape
    width = edge_ref.shape[2]
    full = channels // 256 * 256
    rest = channels - full
    spatial_ref[:, width : cells - width] = mid_ref[...]
    hidden_ref[:, width : cells - width] = mid2_ref[...]
    cols = [
        hidden_columns(rim_rows(packed, (0, frames - 1), width, channels), g1_ref, width)
        for packed in sorted_pair(odd_ref, even_ref, "strip")
    ]
    tails = dot(jnp.concatenate(cols, axis=0), rem_ref[...])
    size = 2 * width
    for side, lo in ((0, 0), (1, cells - width)):
        tail = tails[:size, :rest] if side == 0 else tails[size:, 2 * rest :]
        wide = dot(cols[side], w_ref[2 * side, :, :full])
        term = jnp.concatenate([wide, tail], axis=1)
        rounded = (edge_ref[:, side].reshape(size, channels) + term).astype(BF)
        hidden = silu(norm(rounded, g2_ref)).astype(BF)
        spatial_ref[:, lo : lo + width] = rounded.reshape(2, width, channels)
        hidden_ref[:, lo : lo + width] = hidden.reshape(2, width, channels)
    odd = at_odd("clip")
    pack_into(odd_clip_ref, jnp.where(odd, hidden_ref[1], hidden_ref[0]))
    pack_into(even_clip_ref, jnp.where(odd, hidden_ref[0], hidden_ref[1]))


def inner_kernel(
    x_ref, even_ref, odd_ref, g1_ref, g2_ref, w_ref, rem_ref, outer_spatial_ref, outer_hidden_ref,
    spatial_ref, hidden_ref, col_ref,
):
    frames, height, width, channels = x_ref.shape
    cells = height * width
    for s, f in ((0, 0), (1, frames - 1)):
        spatial_ref[f] = outer_spatial_ref[s]
        hidden_ref[f] = outer_hidden_ref[s]
    inside = range(1, frames - 1)
    above, below = sorted_pair(odd_ref, even_ref, "strip")
    rims = len(inside) * width
    end = rims + len(inside) * cells
    col_ref[:rims] = hidden_columns(rim_rows(above, inside, width, channels), g1_ref, width)
    for s, f in enumerate(inside):
        x = x_ref[f].reshape(cells, channels)
        lo = rims + s * cells
        col_ref[lo : lo + cells] = hidden_columns(x, g1_ref, width)
    col_ref[end:] = hidden_columns(rim_rows(below, inside, width, channels), g1_ref, width)
    terms = stacked_rows(col_ref, len(inside), height, width, w_ref, rem_ref)
    for s, f in enumerate(inside):
        for row in range(height):
            rounded = (x_ref[f, row].astype(F32) + terms(s, row)).astype(BF)
            lo = row * width
            spatial_ref[f, lo : lo + width] = rounded
            hidden_ref[f, lo : lo + width] = silu(norm(rounded, g2_ref)).astype(BF)


def chosen_kernel(
    picks_ref, even_ref, odd_ref, spatial_ref, hidden_ref, g3_ref, wt_ref, chosen_ref
):
    frames, cells, channels = spatial_ref.shape
    before, after = (unpacked(v, channels) for v in sorted_pair(odd_ref, even_ref, "clip"))
    for n in range(chosen_ref.shape[0]):
        pick = scalar(picks_ref, n)
        earlier = jnp.where(pick == 0, before, hidden_ref[jnp.maximum(pick - 1, 0)])
        later = jnp.where(pick == frames - 1, after, hidden_ref[jnp.minimum(pick + 1, frames - 1)])
        total = spatial_ref[pick].astype(F32) + dot(hidden_ref[pick], wt_ref[1])
        total = total + dot(earlier, wt_ref[0]) + dot(later, wt_ref[2])
        pack_into(chosen_ref.at[n], norm(total.astype(BF), g3_ref).astype(BF))


def temporal_kernel(
    even_ref, odd_ref, spatial_ref, hidden_ref, g3_ref, wt_ref, wq_ref, wkv_ref,
    temporal_ref, query_ref, keyval_ref,
):
    frames, cells, channels = spatial_ref.shape
    size = frames * cells
    before, after = (unpacked(v, channels) for v in sorted_pair(odd_ref, even_ref, "clip"))
    hidden = hidden_ref[...].reshape(size, channels)
    total = spatial_ref[...].reshape(size, channels).astype(F32) + dot(hidden, wt_ref[1])
    total = total + dot(jnp.concatenate([before, hidden[: size - cells]], axis=0), wt_ref[0])
    total = total + dot(jnp.concatenate([hidden[cells:], after], axis=0), wt_ref[2])
    temporal = total.astype(BF)
    temporal_ref[...] = temporal.reshape(frames, cells, channels)
    normed = norm(temporal, g3_ref).astype(BF)
    query_ref[...] = dot(normed, wq_ref[...]).astype(BF).reshape(frames, cells, channels)
    keyval_ref[...] = dot(normed, wkv_ref[...]).astype(BF).reshape(frames, cells, 2 * channels)


def head_maps(count, channels, everywhere=False):
    full = channels // LANES * LANES
    rest = channels - full
    stride = LANES // 4
    hits = np.zeros((count * channels, LANES), np.float32)
    for j in range(count):
        for c in range(channels):
            at = j * full + c if c < full else count * full + j * rest + c - full
            lanes = range(0, LANES, stride) if everywhere else (j * stride,)
            for lane in lanes:
                hits[at, lane + c // HEAD_DIM] = 1.0
    padded = np.zeros((-(-hits.shape[0] // LANES) * LANES, LANES), np.float32)
    padded[: hits.shape[0]] = hits
    blocks = padded.reshape(-1, LANES, LANES).transpose(0, 2, 1).reshape(-1, LANES)
    return jnp.asarray(hits / math.sqrt(HEAD_DIM), BF), jnp.asarray(blocks, BF)


def beside(ref):
    count = ref.shape[0] // LANES
    return jnp.concatenate([ref[b * LANES : (b + 1) * LANES] for b in range(count)], axis=1)


def local_kernel(
    start, picks_ref, window_ref, query_ref, keyval_ref, to_lanes_ref, to_channels_ref, order_ref,
    top_ref, sum_ref, mix_ref, next_ref,
):
    next_ref[...] = jnp.zeros_like(next_ref)
    frames, cells, channels = query_ref.shape
    count = picks_ref.shape[1]
    full = channels // LANES * LANES
    stride = LANES // 4
    part = top_ref.shape[0]
    queries = [query_ref[start + f] for f in range(part)]
    keyvals = [keyval_ref[f] for f in range(frames)]
    keys = [kv[:, :full] for kv in keyvals] + [
        jnp.concatenate([kv[:, full:channels] for kv in keyvals], axis=1)
    ]
    values = [kv[:, channels : channels + full].astype(F32) for kv in keyvals] + [
        jnp.concatenate([kv[:, channels + full :] for kv in keyvals], axis=1).astype(F32)
    ]
    products = []
    for q in queries:
        again = jnp.concatenate([q[:, full:]] * frames, axis=1)
        row = [q[:, :full] * k for k in keys[:frames]] + [again * keys[frames]]
        products.append(jnp.concatenate(row, axis=1))
    scores = dot(jnp.concatenate(products, axis=0), to_lanes_ref[...])
    source = lax.div(lax.broadcasted_iota(jnp.int32, (1, LANES), 1), stride)
    window = window_ref[...].reshape(1, 1)
    copies = jnp.zeros((1, LANES), F32)
    for n in range(count):
        copies = copies + jnp.where(source == picks_ref[:, n : n + 1], 1.0, 0.0)
    weights = []
    for i in range(part):
        times = copies + jnp.where(jnp.abs(source - (start + i)) < window, 1.0, 0.0)
        s = jnp.where(times > 0.0, scores[i * cells : (i + 1) * cells], -jnp.inf)
        top = jnp.maximum(s, pltpu.roll(s, stride, 1))
        top = jnp.maximum(top, pltpu.roll(top, 2 * stride, 1))
        w = jnp.exp(s - top) * times
        total = w + pltpu.roll(w, stride, 1)
        total = total + pltpu.roll(total, 2 * stride, 1)
        top_ref[i] = top
        sum_ref[i] = total
        weights.append(w.astype(BF))
    spread = dot(jnp.concatenate(weights, axis=0), beside(to_channels_ref))
    for i in range(part):
        share = spread[i * cells : (i + 1) * cells]
        wide = share[:, :full] * values[0]
        for j in range(1, frames):
            wide = wide + share[:, j * full : (j + 1) * full] * values[j]
        tail = share[:, frames * full :] * values[frames]
        tail = tail[:, :LANES] + tail[:, LANES:]
        tail = tail + pltpu.roll(tail, LANES // 2, 1)
        mix_ref[i] = jnp.concatenate([wide, tail], axis=1)


def keys_and_values(anchor_ref, wkv_ref, channels):
    return [
        dot(unpacked(anchor_ref[n], channels), wkv_ref[...]).astype(BF)
        for n in range(anchor_ref.shape[0])
    ]


def updated(keyvals, to_lanes_ref, to_channels_ref, query, top, total, mix, last):
    frames, cells, channels = query.shape
    full = channels // LANES * LANES
    size = frames * cells
    query, top, total, mix = (v.reshape(size, v.shape[-1]) for v in (query, top, total, mix))
    low = lax.broadcasted_iota(jnp.int32, (1, LANES), 1) < LANES // 4
    for n, keyval in enumerate(keyvals):
        key = jnp.concatenate([keyval[:, :channels]] * frames, axis=0)
        scores = dot(query * key, to_lanes_ref[...])
        higher = jnp.maximum(top, scores)
        weight = jnp.exp(scores - higher)
        fade = jnp.exp(top - higher)
        total = total * fade + weight
        both = jnp.where(low, weight, fade)
        if last and n == len(keyvals) - 1:
            both = both / total
        spread = dot(both.astype(BF), beside(to_channels_ref))
        value = keyval[:, channels:].astype(F32)
        value = jnp.concatenate([value] * frames, axis=0)
        wide = spread[:, :full] * value[:, :full] + spread[:, full : 2 * full] * mix[:, :full]
        tail = jnp.concatenate([value[:, full:], mix[:, full + LANES // 2 :]], axis=1)
        tail = spread[:, 2 * full :] * tail
        tail = tail + pltpu.roll(tail, LANES // 2, 1)
        mix = jnp.concatenate([wide, tail], axis=1)
        top = higher
    return top, total, mix


def copy_kernel(from_ref, to_ref):
    to_ref[...] = from_ref[...]


def relay_kernel(order_ref, *refs):
    count = len(refs) // 2
    for n in range(count):
        refs[count + n][...] = refs[n][...]
    refs[-1][...] = jnp.zeros_like(refs[-1])


def anchor_kernel(pieces, anchor_ref, wkv_ref, to_lanes_ref, to_channels_ref, query_ref, *refs):
    top, total, mix = (
        jnp.concatenate([ref[...] for ref in refs[v * pieces : (v + 1) * pieces]], axis=0)
        for v in range(3)
    )
    new = updated(
        keys_and_values(anchor_ref, wkv_ref, query_ref.shape[2]), to_lanes_ref, to_channels_ref,
        query_ref[...], top, total, mix, False,
    )
    for ref, v in zip(refs[3 * pieces :], new):
        ref[...] = v.reshape(ref.shape)


def last_kernel(
    anchor_ref, wkv_ref, to_lanes_ref, to_channels_ref, query_ref, top_ref, sum_ref, mix_ref,
    temporal_ref, wo_ref, out_ref, out_buf, sems,
):
    frames, cells, channels = query_ref.shape
    height, width = out_ref.shape[1:3]
    keyvals = keys_and_values(anchor_ref, wkv_ref, channels)
    copies = []
    group = 2 if frames % 2 == 0 else 1
    for lo in range(0, frames, group):
        at = slice(lo, lo + group)
        _, _, mix = updated(
            keyvals, to_lanes_ref, to_channels_ref,
            query_ref[at], top_ref[at], sum_ref[at], mix_ref[at], True,
        )
        result = dot(mix[:, :channels].astype(BF), wo_ref[...])
        total = temporal_ref[at].astype(F32) + result.reshape(group, cells, channels)
        out_buf[at] = total.astype(BF).reshape(group, height, width, channels)
        copies.append(pltpu.make_async_copy(out_buf.at[at], out_ref.at[at], sems.at[lo // group]))
        copies[-1].start()
    for copy in copies:
        copy.wait()


def swapped(odd, even, axis, even_first):
    count = lax.axis_size(axis)
    pairs = [[(i, i + 1) for i in range(start, count - 1, 2)] for start in (1, 0)]
    pairs = [up + [(j, i) for i, j in up] for up in pairs]
    if even_first:
        even = lax.ppermute(even, axis, pairs[1])
        return lax.ppermute(odd, axis, pairs[0]), even
    odd = lax.ppermute(odd, axis, pairs[0])
    return odd, lax.ppermute(even, axis, pairs[1])


def on_device(
    latents, anchor_index, window, gain_one, spatial_w, gain_two, temporal_w, gain_three,
    w_query, w_keyval, w_out,
):
    frames, height, width, channels = latents.shape
    cells = height * width
    count = anchor_index.shape[1]
    ws = spatial_w.reshape(3, 3 * channels, channels)
    one = 2 * channels * channels
    packed = cells * channels // LANES
    edge_packed = frames * width * channels // LANES
    lanes_up = (channels + LANES - 1) // LANES * LANES
    sem = pltpu.SemaphoreType.DMA
    some = (frames, cells, channels)

    x, g1, g2, g3, w = latents, gain_one, gain_two, gain_three, ws

    strip_even, strip_odd = call(
        edge_kernel, [((edge_packed, LANES), BF)] * 2, [VMEM], flops=8 * frames * cells * one
    )(x)
    strip_odd, strip_even = swapped(strip_odd, strip_even, "strip", True)
    outer_col = pltpu.VMEM((2 * cells, 3 * channels), BF)
    inner_col = pltpu.VMEM(((frames - 2) * (cells + 2 * width), 3 * channels), BF)
    middle = (2, cells - 2 * width, channels)
    mid, mid2, edge, w_rem, order = call(
        outer_kernel,
        [
            (middle, BF),
            (middle, BF),
            ((2, 2, width, channels), F32),
            ((3 * channels, 3 * (channels % 256)), BF),
            ((8, LANES), F32),
        ],
        [VMEM] * 4,
        [outer_col],
        flops=9 * 2 * cells * one,
    )(x, g1, g2, w)
    outer_spatial, outer_hidden, clip_even, clip_odd = call(
        functools.partial(outer_edge_kernel, frames),
        [((2, cells, channels), BF)] * 2 + [((packed, LANES), BF)] * 2,
        [VMEM] * 10,
        flops=6 * 2 * width * one,
    )(edge, strip_even, strip_odd, order, mid, mid2, g1, g2, w, w_rem)
    clip_odd, clip_even = swapped(clip_odd, clip_even, "clip", True)
    spatial, hidden = call(
        inner_kernel,
        [(some, BF), (some, BF)],
        [VMEM] * 9,
        [inner_col],
        flops=9 * (frames - 2) * cells * one,
    )(x, strip_even, strip_odd, g1, g2, w, w_rem, outer_spatial, outer_hidden)
    (chosen,) = call(
        chosen_kernel, [((count, packed, LANES), BF)], [VMEM] * 7, flops=3 * cells * one
    )(anchor_index, clip_even, clip_odd, spatial, hidden, g3, temporal_w)
    clips = lax.axis_size("clip")
    powers = clips & (clips - 1) == 0
    if powers:
        routes = [[(i, i ^ s) for i in range(clips)] for s in range(1, clips, 2)]
    else:
        routes = [[(i, (i + s) % clips) for i in range(clips)] for s in range(1, clips)]
    (near,) = call(copy_kernel, [(chosen.shape, BF)], [VMEM])(chosen)
    sent = [near] + [chosen] * (len(routes) - 1)
    arrived = [lax.ppermute(v, "clip", route) for v, route in zip(sent, routes)]
    temporal, query, keyval = call(
        temporal_kernel,
        [(some, BF), (some, BF), ((frames, cells, 2 * channels), BF)],
        [VMEM] * 8,
        flops=6 * frames * cells * one,
        limit=32,
    )(clip_even, clip_odd, spatial, hidden, g3, temporal_w, w_query, w_keyval)
    maps = head_maps(frames, channels)
    split = frames // 2 if frames > 1 else frames

    def local(start, part, after):
        shape = (part, cells)
        return call(
            functools.partial(local_kernel, start),
            [(shape + (LANES,), F32)] * 2 + [(shape + (lanes_up,), F32), ((8, LANES), F32)],
            [VMEM] * 7,
            flops=10 * part * cells * one,
            limit=32,
        )(anchor_index, window, query, keyval, *maps, after)

    *early, after = local(0, split, order)
    if powers and clips > 2:
        *relayed, after = call(
            relay_kernel,
            [(chosen.shape, BF)] * (clips // 2 - 1) + [((8, LANES), F32)],
            [VMEM] * (clips // 2),
        )(after, *arrived[1:])
        arrived += [lax.ppermute(v, "clip", routes[0]) for v in relayed]
    *late, after = local(split, frames - split, after)
    pieces = 2
    state = [v for pair in zip(early, late) for v in pair]
    states = [((frames, cells, LANES), F32)] * 2 + [((frames, cells, lanes_up), F32)]
    to_lanes, _ = head_maps(1, channels, everywhere=True)
    _, to_channels = head_maps(2, channels)
    for arrival in arrived[:-1]:
        state = call(
            functools.partial(anchor_kernel, pieces),
            states,
            [VMEM] * (5 + 3 * pieces),
            flops=4 * frames * cells * one,
            limit=32,
        )(arrival, w_keyval, to_lanes, to_channels, query, *state)
        pieces = 1
    (out,) = call(
        last_kernel,
        [(latents.shape, BF)],
        [VMEM] * 10,
        [pltpu.VMEM(latents.shape, BF), sem((frames,))],
        flops=5 * frames * cells * one,
        limit=32,
        out_specs=(HBM,),
    )(arrived[-1], w_keyval, to_lanes, to_channels, query, *state, temporal, w_out)
    return out


def solution(mesh):
    return jax.shard_map(
        on_device,
        mesh=mesh,
        in_specs=(
            P(("groups", "clip"), "strip", None, None),
            P(("groups", "clip"), None),
            P(),
            P(),
            P(),
            P(),
            P(),
            P(),
            P(),
            P(),
            P(),
        ),
        out_specs=P(("groups", "clip"), "strip", None, None),
        check_vma=False,
    )
```

```python
import functools
import math

import jax
import jax.numpy as jnp
import numpy as np
from jax import lax
from jax.experimental import pallas as pl
from jax.experimental.pallas import tpu as pltpu
from jax.sharding import PartitionSpec as P

HEADS = 5
HEAD_DIM = 64
LANES = 128
BF = jnp.bfloat16
F32 = jnp.float32
VMEM = pl.BlockSpec(memory_space=pltpu.VMEM)
HBM = pl.BlockSpec(memory_space=pltpu.HBM)
MIB = 1 << 20


def call(body, outs, specs, scratch=(), flops=0, limit=24, out_specs=None):
    return pl.pallas_call(
        body,
        out_shape=tuple(jax.ShapeDtypeStruct(s, d) for s, d in outs),
        in_specs=specs,
        out_specs=out_specs or tuple(VMEM for _ in outs),
        scratch_shapes=list(scratch),
        cost_estimate=pl.CostEstimate(flops=flops, bytes_accessed=2 * MIB, transcendentals=0),
        compiler_params=pltpu.CompilerParams(vmem_limit_bytes=limit * MIB),
    )


def dot(a, b):
    return jnp.dot(a, b, preferred_element_type=F32)


def norm(v, gain_ref):
    wide = v.astype(F32)
    centred = wide - jnp.mean(wide, axis=-1, keepdims=True)
    variance = jnp.mean(centred * centred, axis=-1, keepdims=True)
    return centred * lax.rsqrt(variance + 1e-05) * gain_ref[...].reshape(1, v.shape[1])


def silu(u):
    half = 0.5 * u
    return half + half * jnp.tanh(half)


def pack_into(ref, h):
    cells, channels = h.shape
    full = channels // LANES
    for t in range(full):
        ref[t * cells : (t + 1) * cells, :] = h[:, t * LANES : (t + 1) * LANES]
    rest = channels - full * LANES
    if rest:
        share = LANES // rest
        part = cells // share
        ref[full * cells :, :] = jnp.concatenate(
            [h[s * part : (s + 1) * part, full * LANES :] for s in range(share)], axis=1
        )


def unpacked(p, channels):
    cells = p.shape[0] * LANES // channels
    full = channels // LANES
    pieces = [p[t * cells : (t + 1) * cells, :] for t in range(full)]
    rest = channels - full * LANES
    if rest:
        share = LANES // rest
        tail = p[full * cells :, :]
        pieces.append(
            jnp.concatenate([tail[:, s * rest : (s + 1) * rest] for s in range(share)], axis=0)
        )
    return jnp.concatenate(pieces, axis=1)


def columns(h, width):
    cells, channels = h.shape
    left = pltpu.roll(h, 1, 0)
    right = pltpu.roll(h, cells - 1, 0)
    place = lax.broadcasted_iota(jnp.int32, (8, channels), 0)
    lefts, rights = [], []
    for lo in range(0, cells, width):
        hi = lo + width
        lefts += [jnp.where(place == 0, 0.0, left[lo : lo + 8]), left[lo + 8 : hi]]
        rights += [right[lo : hi - 8], jnp.where(place == 7, 0.0, right[hi - 8 : hi])]
    sides = [jnp.concatenate(lefts, axis=0), h, jnp.concatenate(rights, axis=0)]
    return jnp.concatenate([v.astype(BF) for v in sides], axis=1)


def scalar(ref, n):
    values = ref[...].astype(F32)
    place = lax.broadcasted_iota(jnp.int32, values.shape, 1)
    return jnp.sum(jnp.where(place == n, values, 0.0)).astype(jnp.int32)


def at_odd(axis):
    return lax.rem(lax.axis_index(axis), 2) == 1


def sorted_pair(odd_ref, even_ref, axis):
    odd = at_odd(axis)
    first, second = odd_ref[...], even_ref[...]
    return jnp.where(odd, second, first), jnp.where(odd, first, second)


def edge_kernel(x_ref, even_ref, odd_ref):
    frames, height, width, channels = x_ref.shape
    odd = at_odd("strip")
    top = x_ref[:, 0].reshape(frames * width, channels)
    bottom = x_ref[:, height - 1].reshape(frames * width, channels)
    pack_into(odd_ref, jnp.where(odd, bottom, top))
    pack_into(even_ref, jnp.where(odd, top, bottom))


def rests_into(rem_ref, w_ref):
    full = w_ref.shape[2] // 256 * 256
    rest = w_ref.shape[2] - full
    for a in range(3):
        rem_ref[:, a * rest : (a + 1) * rest] = w_ref[a, :, full:]


def hidden_columns(v, g1_ref, width):
    return columns(silu(norm(v, g1_ref)), width)


def stacked_rows(col_ref, count, height, width, w_ref, rem_ref):
    cells = height * width
    rims = (col_ref.shape[0] - count * cells) // 2
    channels = w_ref.shape[2]
    full = channels // 256 * 256
    rest = channels - full
    size = count * cells
    above = dot(col_ref[: rims + size], w_ref[0, :, :full])
    centre = dot(col_ref[rims : rims + size], w_ref[1, :, :full])
    below = dot(col_ref[rims:], w_ref[2, :, :full])
    tails = dot(col_ref[...], rem_ref[...])

    def terms(place, row):
        own = place * cells + row * width
        wide = centre[own : own + width]
        tail = tails[rims + own : rims + own + width, rest : 2 * rest]
        if row > 0 or rims:
            at = rims + own - width if row > 0 else place * width
            wide = wide + above[at : at + width]
            tail = tail + tails[at : at + width, :rest]
        if row < height - 1 or rims:
            at = own + width if row < height - 1 else size + place * width
            wide = wide + below[at : at + width]
            tail = tail + tails[rims + at : rims + at + width, 2 * rest :]
        return jnp.concatenate([wide, tail], axis=1)

    return terms


def rim_rows(packed, frames, width, channels):
    rows = unpacked(packed, channels)
    return jnp.concatenate([rows[f * width : (f + 1) * width] for f in frames], axis=0)


def outer_kernel(x_ref, g1_ref, g2_ref, w_ref, mid_ref, mid2_ref, edge_ref, rem_ref, order_ref, col_ref):
    frames, height, width, channels = x_ref.shape
    cells = height * width
    order_ref[...] = jnp.zeros_like(order_ref)
    rests_into(rem_ref, w_ref)
    outer = (0, frames - 1)
    for s, f in enumerate(outer):
        x = x_ref[f].reshape(cells, channels)
        col_ref[s * cells : (s + 1) * cells] = hidden_columns(x, g1_ref, width)
    terms = stacked_rows(col_ref, 2, height, width, w_ref, rem_ref)
    for s, f in enumerate(outer):
        for row in range(height):
            total = x_ref[f, row].astype(F32) + terms(s, row)
            if 0 < row < height - 1:
                rounded = total.astype(BF)
                lo = (row - 1) * width
                mid_ref[s, lo : lo + width] = rounded
                mid2_ref[s, lo : lo + width] = silu(norm(rounded, g2_ref)).astype(BF)
            else:
                edge_ref[s, 0 if row == 0 else 1] = total


def outer_edge_kernel(
    frames, edge_ref, even_ref, odd_ref, order_ref, mid_ref, mid2_ref, g1_ref, g2_ref, w_ref, rem_ref,
    spatial_ref, hidden_ref, even_clip_ref, odd_clip_ref,
):
    _, cells, channels = spatial_ref.shape
    width = edge_ref.shape[2]
    full = channels // 256 * 256
    rest = channels - full
    spatial_ref[:, width : cells - width] = mid_ref[...]
    hidden_ref[:, width : cells - width] = mid2_ref[...]
    cols = [
        hidden_columns(rim_rows(packed, (0, frames - 1), width, channels), g1_ref, width)
        for packed in sorted_pair(odd_ref, even_ref, "strip")
    ]
    tails = dot(jnp.concatenate(cols, axis=0), rem_ref[...])
    size = 2 * width
    for side, lo in ((0, 0), (1, cells - width)):
        tail = tails[:size, :rest] if side == 0 else tails[size:, 2 * rest :]
        wide = dot(cols[side], w_ref[2 * side, :, :full])
        term = jnp.concatenate([wide, tail], axis=1)
        rounded = (edge_ref[:, side].reshape(size, channels) + term).astype(BF)
        hidden = silu(norm(rounded, g2_ref)).astype(BF)
        spatial_ref[:, lo : lo + width] = rounded.reshape(2, width, channels)
        hidden_ref[:, lo : lo + width] = hidden.reshape(2, width, channels)
    odd = at_odd("clip")
    pack_into(odd_clip_ref, jnp.where(odd, hidden_ref[1], hidden_ref[0]))
    pack_into(even_clip_ref, jnp.where(odd, hidden_ref[0], hidden_ref[1]))


def inner_kernel(
    x_ref, even_ref, odd_ref, g1_ref, g2_ref, w_ref, rem_ref, outer_spatial_ref, outer_hidden_ref,
    spatial_ref, hidden_ref, col_ref,
):
    frames, height, width, channels = x_ref.shape
    cells = height * width
    for s, f in ((0, 0), (1, frames - 1)):
        spatial_ref[f] = outer_spatial_ref[s]
        hidden_ref[f] = outer_hidden_ref[s]
    inside = range(1, frames - 1)
    above, below = sorted_pair(odd_ref, even_ref, "strip")
    rims = len(inside) * width
    end = rims + len(inside) * cells
    col_ref[:rims] = hidden_columns(rim_rows(above, inside, width, channels), g1_ref, width)
    for s, f in enumerate(inside):
        x = x_ref[f].reshape(cells, channels)
        lo = rims + s * cells
        col_ref[lo : lo + cells] = hidden_columns(x, g1_ref, width)
    col_ref[end:] = hidden_columns(rim_rows(below, inside, width, channels), g1_ref, width)
    terms = stacked_rows(col_ref, len(inside), height, width, w_ref, rem_ref)
    for s, f in enumerate(inside):
        for row in range(height):
            rounded = (x_ref[f, row].astype(F32) + terms(s, row)).astype(BF)
            lo = row * width
            spatial_ref[f, lo : lo + width] = rounded
            hidden_ref[f, lo : lo + width] = silu(norm(rounded, g2_ref)).astype(BF)


def chosen_kernel(
    picks_ref, even_ref, odd_ref, spatial_ref, hidden_ref, g3_ref, wt_ref, chosen_ref
):
    frames, cells, channels = spatial_ref.shape
    before, after = (unpacked(v, channels) for v in sorted_pair(odd_ref, even_ref, "clip"))
    for n in range(chosen_ref.shape[0]):
        pick = scalar(picks_ref, n)
        earlier = jnp.where(pick == 0, before, hidden_ref[jnp.maximum(pick - 1, 0)])
        later = jnp.where(pick == frames - 1, after, hidden_ref[jnp.minimum(pick + 1, frames - 1)])
        total = spatial_ref[pick].astype(F32) + dot(hidden_ref[pick], wt_ref[1])
        total = total + dot(earlier, wt_ref[0]) + dot(later, wt_ref[2])
        pack_into(chosen_ref.at[n], norm(total.astype(BF), g3_ref).astype(BF))


def temporal_kernel(
    even_ref, odd_ref, spatial_ref, hidden_ref, g3_ref, wt_ref, wq_ref, wkv_ref,
    temporal_ref, query_ref, keyval_ref,
):
    frames, cells, channels = spatial_ref.shape
    size = frames * cells
    before, after = (unpacked(v, channels) for v in sorted_pair(odd_ref, even_ref, "clip"))
    hidden = hidden_ref[...].reshape(size, channels)
    total = spatial_ref[...].reshape(size, channels).astype(F32) + dot(hidden, wt_ref[1])
    total = total + dot(jnp.concatenate([before, hidden[: size - cells]], axis=0), wt_ref[0])
    total = total + dot(jnp.concatenate([hidden[cells:], after], axis=0), wt_ref[2])
    temporal = total.astype(BF)
    temporal_ref[...] = temporal.reshape(frames, cells, channels)
    normed = norm(temporal, g3_ref).astype(BF)
    query_ref[...] = dot(normed, wq_ref[...]).astype(BF).reshape(frames, cells, channels)
    keyval_ref[...] = dot(normed, wkv_ref[...]).astype(BF).reshape(frames, cells, 2 * channels)


def head_maps(count, channels, everywhere=False):
    full = channels // LANES * LANES
    rest = channels - full
    stride = LANES // 4
    hits = np.zeros((count * channels, LANES), np.float32)
    for j in range(count):
        for c in range(channels):
            at = j * full + c if c < full else count * full + j * rest + c - full
            lanes = range(0, LANES, stride) if everywhere else (j * stride,)
            for lane in lanes:
                hits[at, lane + c // HEAD_DIM] = 1.0
    padded = np.zeros((-(-hits.shape[0] // LANES) * LANES, LANES), np.float32)
    padded[: hits.shape[0]] = hits
    blocks = padded.reshape(-1, LANES, LANES).transpose(0, 2, 1).reshape(-1, LANES)
    return jnp.asarray(hits / math.sqrt(HEAD_DIM), BF), jnp.asarray(blocks, BF)


def beside(ref):
    count = ref.shape[0] // LANES
    return jnp.concatenate([ref[b * LANES : (b + 1) * LANES] for b in range(count)], axis=1)


def local_kernel(
    start, picks_ref, window_ref, query_ref, keyval_ref, to_lanes_ref, to_channels_ref, order_ref,
    top_ref, sum_ref, mix_ref, next_ref,
):
    next_ref[...] = jnp.zeros_like(next_ref)
    frames, cells, channels = query_ref.shape
    count = picks_ref.shape[1]
    full = channels // LANES * LANES
    stride = LANES // 4
    part = top_ref.shape[0]
    queries = [query_ref[start + f] for f in range(part)]
    keyvals = [keyval_ref[f] for f in range(frames)]
    keys = [kv[:, :full] for kv in keyvals] + [
        jnp.concatenate([kv[:, full:channels] for kv in keyvals], axis=1)
    ]
    values = [kv[:, channels : channels + full].astype(F32) for kv in keyvals] + [
        jnp.concatenate([kv[:, channels + full :] for kv in keyvals], axis=1).astype(F32)
    ]
    products = []
    for q in queries:
        again = jnp.concatenate([q[:, full:]] * frames, axis=1)
        row = [q[:, :full] * k for k in keys[:frames]] + [again * keys[frames]]
        products.append(jnp.concatenate(row, axis=1))
    scores = dot(jnp.concatenate(products, axis=0), to_lanes_ref[...])
    source = lax.div(lax.broadcasted_iota(jnp.int32, (1, LANES), 1), stride)
    window = window_ref[...].reshape(1, 1)
    copies = jnp.zeros((1, LANES), F32)
    for n in range(count):
        copies = copies + jnp.where(source == picks_ref[:, n : n + 1], 1.0, 0.0)
    weights = []
    for i in range(part):
        times = copies + jnp.where(jnp.abs(source - (start + i)) < window, 1.0, 0.0)
        s = jnp.where(times > 0.0, scores[i * cells : (i + 1) * cells], -jnp.inf)
        top = jnp.maximum(s, pltpu.roll(s, stride, 1))
        top = jnp.maximum(top, pltpu.roll(top, 2 * stride, 1))
        w = jnp.exp(s - top) * times
        total = w + pltpu.roll(w, stride, 1)
        total = total + pltpu.roll(total, 2 * stride, 1)
        top_ref[i] = top
        sum_ref[i] = total
        weights.append(w.astype(BF))
    spread = dot(jnp.concatenate(weights, axis=0), beside(to_channels_ref))
    for i in range(part):
        share = spread[i * cells : (i + 1) * cells]
        wide = share[:, :full] * values[0]
        for j in range(1, frames):
            wide = wide + share[:, j * full : (j + 1) * full] * values[j]
        tail = share[:, frames * full :] * values[frames]
        tail = tail[:, :LANES] + tail[:, LANES:]
        tail = tail + pltpu.roll(tail, LANES // 2, 1)
        mix_ref[i] = jnp.concatenate([wide, tail], axis=1)


def keys_and_values(anchor_ref, wkv_ref, channels):
    return [
        dot(unpacked(anchor_ref[n], channels), wkv_ref[...]).astype(BF)
        for n in range(anchor_ref.shape[0])
    ]


def updated(keyvals, to_lanes_ref, to_channels_ref, query, top, total, mix, last):
    frames, cells, channels = query.shape
    full = channels // LANES * LANES
    size = frames * cells
    query, top, total, mix = (v.reshape(size, v.shape[-1]) for v in (query, top, total, mix))
    low = lax.broadcasted_iota(jnp.int32, (1, LANES), 1) < LANES // 4
    for n, keyval in enumerate(keyvals):
        key = jnp.concatenate([keyval[:, :channels]] * frames, axis=0)
        scores = dot(query * key, to_lanes_ref[...])
        higher = jnp.maximum(top, scores)
        weight = jnp.exp(scores - higher)
        fade = jnp.exp(top - higher)
        total = total * fade + weight
        both = jnp.where(low, weight, fade)
        if last and n == len(keyvals) - 1:
            both = both / total
        spread = dot(both.astype(BF), beside(to_channels_ref))
        value = keyval[:, channels:].astype(F32)
        value = jnp.concatenate([value] * frames, axis=0)
        wide = spread[:, :full] * value[:, :full] + spread[:, full : 2 * full] * mix[:, :full]
        tail = jnp.concatenate([value[:, full:], mix[:, full + LANES // 2 :]], axis=1)
        tail = spread[:, 2 * full :] * tail
        tail = tail + pltpu.roll(tail, LANES // 2, 1)
        mix = jnp.concatenate([wide, tail], axis=1)
        top = higher
    return top, total, mix


def copy_kernel(from_ref, order_ref, to_ref):
    to_ref[...] = from_ref[...]


def relay_kernel(order_ref, *refs):
    count = len(refs) // 2
    for n in range(count):
        refs[count + n][...] = refs[n][...]
    refs[-1][...] = jnp.zeros_like(refs[-1])


def anchor_kernel(pieces, anchor_ref, wkv_ref, to_lanes_ref, to_channels_ref, query_ref, *refs):
    top, total, mix = (
        jnp.concatenate([ref[...] for ref in refs[v * pieces : (v + 1) * pieces]], axis=0)
        for v in range(3)
    )
    new = updated(
        keys_and_values(anchor_ref, wkv_ref, query_ref.shape[2]), to_lanes_ref, to_channels_ref,
        query_ref[...], top, total, mix, False,
    )
    for ref, v in zip(refs[3 * pieces :], new):
        ref[...] = v.reshape(ref.shape)


def last_kernel(
    anchor_ref, wkv_ref, to_lanes_ref, to_channels_ref, query_ref, top_ref, sum_ref, mix_ref,
    temporal_ref, wo_ref, out_ref, out_buf, sems,
):
    frames, cells, channels = query_ref.shape
    height, width = out_ref.shape[1:3]
    keyvals = keys_and_values(anchor_ref, wkv_ref, channels)
    copies = []
    group = 2 if frames % 2 == 0 else 1
    for lo in range(0, frames, group):
        at = slice(lo, lo + group)
        _, _, mix = updated(
            keyvals, to_lanes_ref, to_channels_ref,
            query_ref[at], top_ref[at], sum_ref[at], mix_ref[at], True,
        )
        result = dot(mix[:, :channels].astype(BF), wo_ref[...])
        total = temporal_ref[at].astype(F32) + result.reshape(group, cells, channels)
        out_buf[at] = total.astype(BF).reshape(group, height, width, channels)
        copies.append(pltpu.make_async_copy(out_buf.at[at], out_ref.at[at], sems.at[lo // group]))
        copies[-1].start()
    for copy in copies:
        copy.wait()


def swapped(odd, even, axis, even_first):
    count = lax.axis_size(axis)
    pairs = [[(i, i + 1) for i in range(start, count - 1, 2)] for start in (1, 0)]
    pairs = [up + [(j, i) for i, j in up] for up in pairs]
    if even_first:
        even = lax.ppermute(even, axis, pairs[1])
        return lax.ppermute(odd, axis, pairs[0]), even
    odd = lax.ppermute(odd, axis, pairs[0])
    return odd, lax.ppermute(even, axis, pairs[1])


def on_device(
    latents, anchor_index, window, gain_one, spatial_w, gain_two, temporal_w, gain_three,
    w_query, w_keyval, w_out,
):
    frames, height, width, channels = latents.shape
    cells = height * width
    count = anchor_index.shape[1]
    ws = spatial_w.reshape(3, 3 * channels, channels)
    one = 2 * channels * channels
    packed = cells * channels // LANES
    edge_packed = frames * width * channels // LANES
    lanes_up = (channels + LANES - 1) // LANES * LANES
    sem = pltpu.SemaphoreType.DMA
    some = (frames, cells, channels)

    x, g1, g2, g3, w = latents, gain_one, gain_two, gain_three, ws

    strip_even, strip_odd = call(
        edge_kernel, [((edge_packed, LANES), BF)] * 2, [VMEM], flops=8 * frames * cells * one
    )(x)
    strip_odd, strip_even = swapped(strip_odd, strip_even, "strip", True)
    outer_col = pltpu.VMEM((2 * cells, 3 * channels), BF)
    inner_col = pltpu.VMEM(((frames - 2) * (cells + 2 * width), 3 * channels), BF)
    middle = (2, cells - 2 * width, channels)
    mid, mid2, edge, w_rem, order = call(
        outer_kernel,
        [
            (middle, BF),
            (middle, BF),
            ((2, 2, width, channels), F32),
            ((3 * channels, 3 * (channels % 256)), BF),
            ((8, LANES), F32),
        ],
        [VMEM] * 4,
        [outer_col],
        flops=9 * 2 * cells * one,
    )(x, g1, g2, w)
    outer_spatial, outer_hidden, clip_even, clip_odd = call(
        functools.partial(outer_edge_kernel, frames),
        [((2, cells, channels), BF)] * 2 + [((packed, LANES), BF)] * 2,
        [VMEM] * 10,
        flops=6 * 2 * width * one,
    )(edge, strip_even, strip_odd, order, mid, mid2, g1, g2, w, w_rem)
    clip_odd, clip_even = swapped(clip_odd, clip_even, "clip", True)
    spatial, hidden = call(
        inner_kernel,
        [(some, BF), (some, BF)],
        [VMEM] * 9,
        [inner_col],
        flops=9 * (frames - 2) * cells * one,
    )(x, strip_even, strip_odd, g1, g2, w, w_rem, outer_spatial, outer_hidden)
    (chosen,) = call(
        chosen_kernel, [((count, packed, LANES), BF)], [VMEM] * 7, flops=3 * cells * one
    )(anchor_index, clip_even, clip_odd, spatial, hidden, g3, temporal_w)
    clips = lax.axis_size("clip")
    powers = clips & (clips - 1) == 0
    if powers:
        routes = [[(i, i ^ s) for i in range(clips)] for s in range(1, clips, 2)]
    else:
        routes = [[(i, (i + s) % clips) for i in range(clips)] for s in range(1, clips)]
    far = [lax.ppermute(chosen, "clip", route) for route in routes[1:]]
    temporal, query, keyval = call(
        temporal_kernel,
        [(some, BF), (some, BF), ((frames, cells, 2 * channels), BF)],
        [VMEM] * 8,
        flops=6 * frames * cells * one,
        limit=32,
    )(clip_even, clip_odd, spatial, hidden, g3, temporal_w, w_query, w_keyval)
    (near,) = call(copy_kernel, [(chosen.shape, BF)], [VMEM] * 2)(chosen, temporal)
    arrived = [lax.ppermute(near, "clip", routes[0])] + far
    maps = head_maps(frames, channels)
    split = frames // 2 if frames > 1 else frames

    def local(start, part, after):
        shape = (part, cells)
        return call(
            functools.partial(local_kernel, start),
            [(shape + (LANES,), F32)] * 2 + [(shape + (lanes_up,), F32), ((8, LANES), F32)],
            [VMEM] * 7,
            flops=10 * part * cells * one,
            limit=32,
        )(anchor_index, window, query, keyval, *maps, after)

    *early, after = local(0, split, order)
    if powers and clips > 2:
        *relayed, after = call(
            relay_kernel,
            [(chosen.shape, BF)] * (clips // 2 - 1) + [((8, LANES), F32)],
            [VMEM] * (clips // 2),
        )(after, *arrived[1:])
        arrived += [lax.ppermute(v, "clip", routes[0]) for v in relayed]
    *late, after = local(split, frames - split, after)
    pieces = 2
    state = [v for pair in zip(early, late) for v in pair]
    states = [((frames, cells, LANES), F32)] * 2 + [((frames, cells, lanes_up), F32)]
    to_lanes, _ = head_maps(1, channels, everywhere=True)
    _, to_channels = head_maps(2, channels)
    for arrival in arrived[:-1]:
        state = call(
            functools.partial(anchor_kernel, pieces),
            states,
            [VMEM] * (5 + 3 * pieces),
            flops=4 * frames * cells * one,
            limit=32,
        )(arrival, w_keyval, to_lanes, to_channels, query, *state)
        pieces = 1
    (out,) = call(
        last_kernel,
        [(latents.shape, BF)],
        [VMEM] * 10,
        [pltpu.VMEM(latents.shape, BF), sem((frames,))],
        flops=5 * frames * cells * one,
        limit=32,
        out_specs=(HBM,),
    )(arrived[-1], w_keyval, to_lanes, to_channels, query, *state, temporal, w_out)
    return out


def solution(mesh):
    return jax.shard_map(
        on_device,
        mesh=mesh,
        in_specs=(
            P(("groups", "clip"), "strip", None, None),
            P(("groups", "clip"), None),
            P(),
            P(),
            P(),
            P(),
            P(),
            P(),
            P(),
            P(),
            P(),
        ),
        out_specs=P(("groups", "clip"), "strip", None, None),
        check_vma=False,
    )
```

```python
import functools
import math

import jax
import jax.numpy as jnp
import numpy as np
from jax import lax
from jax.experimental import pallas as pl
from jax.experimental.pallas import tpu as pltpu
from jax.sharding import PartitionSpec as P

HEADS = 5
HEAD_DIM = 64
LANES = 128
BF = jnp.bfloat16
F32 = jnp.float32
VMEM = pl.BlockSpec(memory_space=pltpu.VMEM)
HBM = pl.BlockSpec(memory_space=pltpu.HBM)
MIB = 1 << 20


def call(body, outs, specs, scratch=(), flops=0, limit=24, out_specs=None):
    return pl.pallas_call(
        body,
        out_shape=tuple(jax.ShapeDtypeStruct(s, d) for s, d in outs),
        in_specs=specs,
        out_specs=out_specs or tuple(VMEM for _ in outs),
        scratch_shapes=list(scratch),
        cost_estimate=pl.CostEstimate(flops=flops, bytes_accessed=2 * MIB, transcendentals=0),
        compiler_params=pltpu.CompilerParams(vmem_limit_bytes=limit * MIB),
    )


def dot(a, b):
    return jnp.dot(a, b, preferred_element_type=F32)


def norm(v, gain_ref):
    wide = v.astype(F32)
    centred = wide - jnp.mean(wide, axis=-1, keepdims=True)
    variance = jnp.mean(centred * centred, axis=-1, keepdims=True)
    return centred * lax.rsqrt(variance + 1e-05) * gain_ref[...].reshape(1, v.shape[1])


def silu(u):
    half = 0.5 * u
    return half + half * jnp.tanh(half)


def pack_into(ref, h):
    cells, channels = h.shape
    full = channels // LANES
    for t in range(full):
        ref[t * cells : (t + 1) * cells, :] = h[:, t * LANES : (t + 1) * LANES]
    rest = channels - full * LANES
    if rest:
        share = LANES // rest
        part = cells // share
        ref[full * cells :, :] = jnp.concatenate(
            [h[s * part : (s + 1) * part, full * LANES :] for s in range(share)], axis=1
        )


def unpacked(p, channels):
    cells = p.shape[0] * LANES // channels
    full = channels // LANES
    pieces = [p[t * cells : (t + 1) * cells, :] for t in range(full)]
    rest = channels - full * LANES
    if rest:
        share = LANES // rest
        tail = p[full * cells :, :]
        pieces.append(
            jnp.concatenate([tail[:, s * rest : (s + 1) * rest] for s in range(share)], axis=0)
        )
    return jnp.concatenate(pieces, axis=1)


def columns(h, width):
    cells, channels = h.shape
    left = pltpu.roll(h, 1, 0)
    right = pltpu.roll(h, cells - 1, 0)
    place = lax.broadcasted_iota(jnp.int32, (8, channels), 0)
    lefts, rights = [], []
    for lo in range(0, cells, width):
        hi = lo + width
        lefts += [jnp.where(place == 0, 0.0, left[lo : lo + 8]), left[lo + 8 : hi]]
        rights += [right[lo : hi - 8], jnp.where(place == 7, 0.0, right[hi - 8 : hi])]
    sides = [jnp.concatenate(lefts, axis=0), h, jnp.concatenate(rights, axis=0)]
    return jnp.concatenate([v.astype(BF) for v in sides], axis=1)


def scalar(ref, n):
    values = ref[...].astype(F32)
    place = lax.broadcasted_iota(jnp.int32, values.shape, 1)
    return jnp.sum(jnp.where(place == n, values, 0.0)).astype(jnp.int32)


def at_odd(axis):
    return lax.rem(lax.axis_index(axis), 2) == 1


def sorted_pair(odd_ref, even_ref, axis):
    odd = at_odd(axis)
    first, second = odd_ref[...], even_ref[...]
    return jnp.where(odd, second, first), jnp.where(odd, first, second)


def edge_kernel(x_ref, even_ref, odd_ref):
    frames, height, width, channels = x_ref.shape
    odd = at_odd("strip")
    top = x_ref[:, 0].reshape(frames * width, channels)
    bottom = x_ref[:, height - 1].reshape(frames * width, channels)
    pack_into(odd_ref, jnp.where(odd, bottom, top))
    pack_into(even_ref, jnp.where(odd, top, bottom))


def rests_into(rem_ref, w_ref):
    full = w_ref.shape[2] // 256 * 256
    rest = w_ref.shape[2] - full
    for a in range(3):
        rem_ref[:, a * rest : (a + 1) * rest] = w_ref[a, :, full:]


def hidden_columns(v, g1_ref, width):
    return columns(silu(norm(v, g1_ref)), width)


def stacked_rows(col_ref, count, height, width, w_ref, rem_ref):
    cells = height * width
    rims = (col_ref.shape[0] - count * cells) // 2
    channels = w_ref.shape[2]
    full = channels // 256 * 256
    rest = channels - full
    size = count * cells
    above = dot(col_ref[: rims + size], w_ref[0, :, :full])
    centre = dot(col_ref[rims : rims + size], w_ref[1, :, :full])
    below = dot(col_ref[rims:], w_ref[2, :, :full])
    tails = dot(col_ref[...], rem_ref[...])

    def terms(place, row):
        own = place * cells + row * width
        wide = centre[own : own + width]
        tail = tails[rims + own : rims + own + width, rest : 2 * rest]
        if row > 0 or rims:
            at = rims + own - width if row > 0 else place * width
            wide = wide + above[at : at + width]
            tail = tail + tails[at : at + width, :rest]
        if row < height - 1 or rims:
            at = own + width if row < height - 1 else size + place * width
            wide = wide + below[at : at + width]
            tail = tail + tails[rims + at : rims + at + width, 2 * rest :]
        return jnp.concatenate([wide, tail], axis=1)

    return terms


def rim_rows(packed, frames, width, channels):
    rows = unpacked(packed, channels)
    return jnp.concatenate([rows[f * width : (f + 1) * width] for f in frames], axis=0)


def outer_kernel(x_ref, g1_ref, g2_ref, w_ref, mid_ref, mid2_ref, edge_ref, rem_ref, order_ref, col_ref):
    frames, height, width, channels = x_ref.shape
    cells = height * width
    order_ref[...] = jnp.zeros_like(order_ref)
    rests_into(rem_ref, w_ref)
    outer = (0, frames - 1)
    for s, f in enumerate(outer):
        x = x_ref[f].reshape(cells, channels)
        col_ref[s * cells : (s + 1) * cells] = hidden_columns(x, g1_ref, width)
    terms = stacked_rows(col_ref, 2, height, width, w_ref, rem_ref)
    for s, f in enumerate(outer):
        for row in range(height):
            total = x_ref[f, row].astype(F32) + terms(s, row)
            if 0 < row < height - 1:
                rounded = total.astype(BF)
                lo = (row - 1) * width
                mid_ref[s, lo : lo + width] = rounded
                mid2_ref[s, lo : lo + width] = silu(norm(rounded, g2_ref)).astype(BF)
            else:
                edge_ref[s, 0 if row == 0 else 1] = total


def outer_edge_kernel(
    frames, edge_ref, even_ref, odd_ref, order_ref, mid_ref, mid2_ref, g1_ref, g2_ref, w_ref, rem_ref,
    spatial_ref, hidden_ref, even_clip_ref, odd_clip_ref,
):
    _, cells, channels = spatial_ref.shape
    width = edge_ref.shape[2]
    full = channels // 256 * 256
    rest = channels - full
    spatial_ref[:, width : cells - width] = mid_ref[...]
    hidden_ref[:, width : cells - width] = mid2_ref[...]
    cols = [
        hidden_columns(rim_rows(packed, (0, frames - 1), width, channels), g1_ref, width)
        for packed in sorted_pair(odd_ref, even_ref, "strip")
    ]
    tails = dot(jnp.concatenate(cols, axis=0), rem_ref[...])
    size = 2 * width
    for side, lo in ((0, 0), (1, cells - width)):
        tail = tails[:size, :rest] if side == 0 else tails[size:, 2 * rest :]
        wide = dot(cols[side], w_ref[2 * side, :, :full])
        term = jnp.concatenate([wide, tail], axis=1)
        rounded = (edge_ref[:, side].reshape(size, channels) + term).astype(BF)
        hidden = silu(norm(rounded, g2_ref)).astype(BF)
        spatial_ref[:, lo : lo + width] = rounded.reshape(2, width, channels)
        hidden_ref[:, lo : lo + width] = hidden.reshape(2, width, channels)
    odd = at_odd("clip")
    pack_into(odd_clip_ref, jnp.where(odd, hidden_ref[1], hidden_ref[0]))
    pack_into(even_clip_ref, jnp.where(odd, hidden_ref[0], hidden_ref[1]))


def inner_kernel(
    x_ref, even_ref, odd_ref, g1_ref, g2_ref, w_ref, rem_ref, outer_spatial_ref, outer_hidden_ref,
    spatial_ref, hidden_ref, col_ref,
):
    frames, height, width, channels = x_ref.shape
    cells = height * width
    for s, f in ((0, 0), (1, frames - 1)):
        spatial_ref[f] = outer_spatial_ref[s]
        hidden_ref[f] = outer_hidden_ref[s]
    inside = range(1, frames - 1)
    above, below = sorted_pair(odd_ref, even_ref, "strip")
    rims = len(inside) * width
    end = rims + len(inside) * cells
    col_ref[:rims] = hidden_columns(rim_rows(above, inside, width, channels), g1_ref, width)
    for s, f in enumerate(inside):
        x = x_ref[f].reshape(cells, channels)
        lo = rims + s * cells
        col_ref[lo : lo + cells] = hidden_columns(x, g1_ref, width)
    col_ref[end:] = hidden_columns(rim_rows(below, inside, width, channels), g1_ref, width)
    terms = stacked_rows(col_ref, len(inside), height, width, w_ref, rem_ref)
    for s, f in enumerate(inside):
        for row in range(height):
            rounded = (x_ref[f, row].astype(F32) + terms(s, row)).astype(BF)
            lo = row * width
            spatial_ref[f, lo : lo + width] = rounded
            hidden_ref[f, lo : lo + width] = silu(norm(rounded, g2_ref)).astype(BF)


def chosen_kernel(
    picks_ref, even_ref, odd_ref, spatial_ref, hidden_ref, g3_ref, wt_ref, chosen_ref
):
    frames, cells, channels = spatial_ref.shape
    before, after = (unpacked(v, channels) for v in sorted_pair(odd_ref, even_ref, "clip"))
    for n in range(chosen_ref.shape[0]):
        pick = scalar(picks_ref, n)
        earlier = jnp.where(pick == 0, before, hidden_ref[jnp.maximum(pick - 1, 0)])
        later = jnp.where(pick == frames - 1, after, hidden_ref[jnp.minimum(pick + 1, frames - 1)])
        total = spatial_ref[pick].astype(F32) + dot(hidden_ref[pick], wt_ref[1])
        total = total + dot(earlier, wt_ref[0]) + dot(later, wt_ref[2])
        pack_into(chosen_ref.at[n], norm(total.astype(BF), g3_ref).astype(BF))


def temporal_kernel(
    even_ref, odd_ref, spatial_ref, hidden_ref, g3_ref, wt_ref, wq_ref, wkv_ref,
    temporal_ref, query_ref, keyval_ref,
):
    frames, cells, channels = spatial_ref.shape
    size = frames * cells
    before, after = (unpacked(v, channels) for v in sorted_pair(odd_ref, even_ref, "clip"))
    hidden = hidden_ref[...].reshape(size, channels)
    total = spatial_ref[...].reshape(size, channels).astype(F32) + dot(hidden, wt_ref[1])
    total = total + dot(jnp.concatenate([before, hidden[: size - cells]], axis=0), wt_ref[0])
    total = total + dot(jnp.concatenate([hidden[cells:], after], axis=0), wt_ref[2])
    temporal = total.astype(BF)
    temporal_ref[...] = temporal.reshape(frames, cells, channels)
    normed = norm(temporal, g3_ref).astype(BF)
    query_ref[...] = dot(normed, wq_ref[...]).astype(BF).reshape(frames, cells, channels)
    keyval_ref[...] = dot(normed, wkv_ref[...]).astype(BF).reshape(frames, cells, 2 * channels)


def head_maps(count, channels, everywhere=False):
    full = channels // LANES * LANES
    rest = channels - full
    stride = LANES // 4
    hits = np.zeros((count * channels, LANES), np.float32)
    for j in range(count):
        for c in range(channels):
            at = j * full + c if c < full else count * full + j * rest + c - full
            lanes = range(0, LANES, stride) if everywhere else (j * stride,)
            for lane in lanes:
                hits[at, lane + c // HEAD_DIM] = 1.0
    padded = np.zeros((-(-hits.shape[0] // LANES) * LANES, LANES), np.float32)
    padded[: hits.shape[0]] = hits
    blocks = padded.reshape(-1, LANES, LANES).transpose(0, 2, 1).reshape(-1, LANES)
    return jnp.asarray(hits / math.sqrt(HEAD_DIM), BF), jnp.asarray(blocks, BF)


def beside(ref):
    count = ref.shape[0] // LANES
    return jnp.concatenate([ref[b * LANES : (b + 1) * LANES] for b in range(count)], axis=1)


def local_kernel(
    start, picks_ref, window_ref, query_ref, keyval_ref, to_lanes_ref, to_channels_ref, order_ref,
    top_ref, sum_ref, mix_ref, next_ref,
):
    next_ref[...] = jnp.zeros_like(next_ref)
    frames, cells, channels = query_ref.shape
    count = picks_ref.shape[1]
    full = channels // LANES * LANES
    stride = LANES // 4
    part = top_ref.shape[0]
    queries = [query_ref[start + f] for f in range(part)]
    keyvals = [keyval_ref[f] for f in range(frames)]
    keys = [kv[:, :full] for kv in keyvals] + [
        jnp.concatenate([kv[:, full:channels] for kv in keyvals], axis=1)
    ]
    values = [kv[:, channels : channels + full].astype(F32) for kv in keyvals] + [
        jnp.concatenate([kv[:, channels + full :] for kv in keyvals], axis=1).astype(F32)
    ]
    products = []
    for q in queries:
        again = jnp.concatenate([q[:, full:]] * frames, axis=1)
        row = [q[:, :full] * k for k in keys[:frames]] + [again * keys[frames]]
        products.append(jnp.concatenate(row, axis=1))
    scores = dot(jnp.concatenate(products, axis=0), to_lanes_ref[...])
    source = lax.div(lax.broadcasted_iota(jnp.int32, (1, LANES), 1), stride)
    window = window_ref[...].reshape(1, 1)
    copies = jnp.zeros((1, LANES), F32)
    for n in range(count):
        copies = copies + jnp.where(source == picks_ref[:, n : n + 1], 1.0, 0.0)
    weights = []
    for i in range(part):
        times = copies + jnp.where(jnp.abs(source - (start + i)) < window, 1.0, 0.0)
        s = jnp.where(times > 0.0, scores[i * cells : (i + 1) * cells], -jnp.inf)
        top = jnp.maximum(s, pltpu.roll(s, stride, 1))
        top = jnp.maximum(top, pltpu.roll(top, 2 * stride, 1))
        w = jnp.exp(s - top) * times
        total = w + pltpu.roll(w, stride, 1)
        total = total + pltpu.roll(total, 2 * stride, 1)
        top_ref[i] = top
        sum_ref[i] = total
        weights.append(w.astype(BF))
    spread = dot(jnp.concatenate(weights, axis=0), beside(to_channels_ref))
    for i in range(part):
        share = spread[i * cells : (i + 1) * cells]
        wide = share[:, :full] * values[0]
        for j in range(1, frames):
            wide = wide + share[:, j * full : (j + 1) * full] * values[j]
        tail = share[:, frames * full :] * values[frames]
        tail = tail[:, :LANES] + tail[:, LANES:]
        tail = tail + pltpu.roll(tail, LANES // 2, 1)
        mix_ref[i] = jnp.concatenate([wide, tail], axis=1)


def keys_and_values(anchor_ref, wkv_ref, channels):
    return [
        dot(unpacked(anchor_ref[n], channels), wkv_ref[...]).astype(BF)
        for n in range(anchor_ref.shape[0])
    ]


def updated(keyvals, to_lanes_ref, to_channels_ref, query, top, total, mix, last):
    frames, cells, channels = query.shape
    full = channels // LANES * LANES
    size = frames * cells
    query, top, total, mix = (v.reshape(size, v.shape[-1]) for v in (query, top, total, mix))
    low = lax.broadcasted_iota(jnp.int32, (1, LANES), 1) < LANES // 4
    for n, keyval in enumerate(keyvals):
        key = jnp.concatenate([keyval[:, :channels]] * frames, axis=0)
        scores = dot(query * key, to_lanes_ref[...])
        higher = jnp.maximum(top, scores)
        weight = jnp.exp(scores - higher)
        fade = jnp.exp(top - higher)
        total = total * fade + weight
        both = jnp.where(low, weight, fade)
        if last and n == len(keyvals) - 1:
            both = both / total
        spread = dot(both.astype(BF), beside(to_channels_ref))
        value = keyval[:, channels:].astype(F32)
        value = jnp.concatenate([value] * frames, axis=0)
        wide = spread[:, :full] * value[:, :full] + spread[:, full : 2 * full] * mix[:, :full]
        tail = jnp.concatenate([value[:, full:], mix[:, full + LANES // 2 :]], axis=1)
        tail = spread[:, 2 * full :] * tail
        tail = tail + pltpu.roll(tail, LANES // 2, 1)
        mix = jnp.concatenate([wide, tail], axis=1)
        top = higher
    return top, total, mix


def copy_kernel(from_ref, to_ref):
    to_ref[...] = from_ref[...]


def relay_kernel(order_ref, *refs):
    count = len(refs) // 2
    for n in range(count):
        refs[count + n][...] = refs[n][...]
    refs[-1][...] = jnp.zeros_like(refs[-1])


def anchor_kernel(pieces, anchor_ref, wkv_ref, to_lanes_ref, to_channels_ref, query_ref, *refs):
    top, total, mix = (
        jnp.concatenate([ref[...] for ref in refs[v * pieces : (v + 1) * pieces]], axis=0)
        for v in range(3)
    )
    new = updated(
        keys_and_values(anchor_ref, wkv_ref, query_ref.shape[2]), to_lanes_ref, to_channels_ref,
        query_ref[...], top, total, mix, False,
    )
    for ref, v in zip(refs[3 * pieces :], new):
        ref[...] = v.reshape(ref.shape)


def last_kernel(
    anchor_ref, wkv_ref, to_lanes_ref, to_channels_ref, query_ref, top_ref, sum_ref, mix_ref,
    temporal_ref, wo_ref, out_ref, out_buf, sems,
):
    frames, cells, channels = query_ref.shape
    height, width = out_ref.shape[1:3]
    keyvals = keys_and_values(anchor_ref, wkv_ref, channels)
    copies = []
    group = 2 if frames % 2 == 0 else 1
    for lo in range(0, frames, group):
        at = slice(lo, lo + group)
        _, _, mix = updated(
            keyvals, to_lanes_ref, to_channels_ref,
            query_ref[at], top_ref[at], sum_ref[at], mix_ref[at], True,
        )
        result = dot(mix[:, :channels].astype(BF), wo_ref[...])
        total = temporal_ref[at].astype(F32) + result.reshape(group, cells, channels)
        out_buf[at] = total.astype(BF).reshape(group, height, width, channels)
        copies.append(pltpu.make_async_copy(out_buf.at[at], out_ref.at[at], sems.at[lo // group]))
        copies[-1].start()
    for copy in copies:
        copy.wait()


def swapped(odd, even, axis, even_first):
    count = lax.axis_size(axis)
    pairs = [[(i, i + 1) for i in range(start, count - 1, 2)] for start in (1, 0)]
    pairs = [up + [(j, i) for i, j in up] for up in pairs]
    if even_first:
        even = lax.ppermute(even, axis, pairs[1])
        return lax.ppermute(odd, axis, pairs[0]), even
    odd = lax.ppermute(odd, axis, pairs[0])
    return odd, lax.ppermute(even, axis, pairs[1])


def on_device(
    latents, anchor_index, window, gain_one, spatial_w, gain_two, temporal_w, gain_three,
    w_query, w_keyval, w_out,
):
    frames, height, width, channels = latents.shape
    cells = height * width
    count = anchor_index.shape[1]
    ws = spatial_w.reshape(3, 3 * channels, channels)
    one = 2 * channels * channels
    packed = cells * channels // LANES
    edge_packed = frames * width * channels // LANES
    lanes_up = (channels + LANES - 1) // LANES * LANES
    sem = pltpu.SemaphoreType.DMA
    some = (frames, cells, channels)

    x, g1, g2, g3, w = latents, gain_one, gain_two, gain_three, ws

    strip_even, strip_odd = call(
        edge_kernel, [((edge_packed, LANES), BF)] * 2, [VMEM], flops=8 * frames * cells * one
    )(x)
    strip_odd, strip_even = swapped(strip_odd, strip_even, "strip", True)
    outer_col = pltpu.VMEM((2 * cells, 3 * channels), BF)
    inner_col = pltpu.VMEM(((frames - 2) * (cells + 2 * width), 3 * channels), BF)
    middle = (2, cells - 2 * width, channels)
    mid, mid2, edge, w_rem, order = call(
        outer_kernel,
        [
            (middle, BF),
            (middle, BF),
            ((2, 2, width, channels), F32),
            ((3 * channels, 3 * (channels % 256)), BF),
            ((8, LANES), F32),
        ],
        [VMEM] * 4,
        [outer_col],
        flops=9 * 2 * cells * one,
    )(x, g1, g2, w)
    outer_spatial, outer_hidden, clip_even, clip_odd = call(
        functools.partial(outer_edge_kernel, frames),
        [((2, cells, channels), BF)] * 2 + [((packed, LANES), BF)] * 2,
        [VMEM] * 10,
        flops=6 * 2 * width * one,
    )(edge, strip_even, strip_odd, order, mid, mid2, g1, g2, w, w_rem)
    clip_odd, clip_even = swapped(clip_odd, clip_even, "clip", True)
    spatial, hidden = call(
        inner_kernel,
        [(some, BF), (some, BF)],
        [VMEM] * 9,
        [inner_col],
        flops=9 * (frames - 2) * cells * one,
    )(x, strip_even, strip_odd, g1, g2, w, w_rem, outer_spatial, outer_hidden)
    (chosen,) = call(
        chosen_kernel, [((count, packed, LANES), BF)], [VMEM] * 7, flops=3 * cells * one
    )(anchor_index, clip_even, clip_odd, spatial, hidden, g3, temporal_w)
    clips = lax.axis_size("clip")
    powers = clips & (clips - 1) == 0
    if powers:
        routes = [[(i, i ^ s) for i in range(clips)] for s in range(1, clips, 2)]
    else:
        routes = [[(i, (i + s) % clips) for i in range(clips)] for s in range(1, clips)]
    (near,) = call(copy_kernel, [(chosen.shape, BF)], [VMEM])(chosen)
    sent = [near] + [chosen] * (len(routes) - 1)
    arrived = [lax.ppermute(v, "clip", route) for v, route in zip(sent, routes)]
    temporal, query, keyval = call(
        temporal_kernel,
        [(some, BF), (some, BF), ((frames, cells, 2 * channels), BF)],
        [VMEM] * 8,
        flops=6 * frames * cells * one,
        limit=32,
    )(clip_even, clip_odd, spatial, hidden, g3, temporal_w, w_query, w_keyval)
    maps = head_maps(frames, channels)
    split = max(frames - 1, 1)

    def local(start, part, after):
        shape = (part, cells)
        return call(
            functools.partial(local_kernel, start),
            [(shape + (LANES,), F32)] * 2 + [(shape + (lanes_up,), F32), ((8, LANES), F32)],
            [VMEM] * 7,
            flops=10 * part * cells * one,
            limit=32,
        )(anchor_index, window, query, keyval, *maps, after)

    *early, after = local(0, split, order)
    if powers and clips > 2:
        *relayed, after = call(
            relay_kernel,
            [(chosen.shape, BF)] * (clips // 2 - 1) + [((8, LANES), F32)],
            [VMEM] * (clips // 2),
        )(after, *arrived[1:])
        arrived += [lax.ppermute(v, "clip", routes[0]) for v in relayed]
    *late, after = local(split, frames - split, after)
    pieces = 2
    state = [v for pair in zip(early, late) for v in pair]
    states = [((frames, cells, LANES), F32)] * 2 + [((frames, cells, lanes_up), F32)]
    to_lanes, _ = head_maps(1, channels, everywhere=True)
    _, to_channels = head_maps(2, channels)
    for arrival in arrived[:-1]:
        state = call(
            functools.partial(anchor_kernel, pieces),
            states,
            [VMEM] * (5 + 3 * pieces),
            flops=4 * frames * cells * one,
            limit=32,
        )(arrival, w_keyval, to_lanes, to_channels, query, *state)
        pieces = 1
    (out,) = call(
        last_kernel,
        [(latents.shape, BF)],
        [VMEM] * 10,
        [pltpu.VMEM(latents.shape, BF), sem((frames,))],
        flops=5 * frames * cells * one,
        limit=32,
        out_specs=(HBM,),
    )(arrived[-1], w_keyval, to_lanes, to_channels, query, *state, temporal, w_out)
    return out


def solution(mesh):
    return jax.shard_map(
        on_device,
        mesh=mesh,
        in_specs=(
            P(("groups", "clip"), "strip", None, None),
            P(("groups", "clip"), None),
            P(),
            P(),
            P(),
            P(),
            P(),
            P(),
            P(),
            P(),
            P(),
        ),
        out_specs=P(("groups", "clip"), "strip", None, None),
        check_vma=False,
    )
```
